32 devices in a mesh: dp: 8 (over z, x), expert: 4 (over y, core).
Axes of the slice: x: 2, y: 2, z: 4, core: 2. Of those that a mesh axis runs over, the one named last changes fastest.
Arguments:
- tokens: bfloat16 [32, 1024, 1024], P(('dp', 'expert')), may hold values from -6 to 6
- cotangent: bfloat16 [32, 1024, 1024], P(('dp', 'expert')), may hold values from -6 to 6
- routes: int32 [32, 1024, 8], P(('dp', 'expert')), may hold values from 0 to 15, all different within a row; in each aligned block of 1024 rows (0 to 1023, 1024 to 2047, ..., all dimensions but the last counted through in order) at most 576 rows name the same one
- prefix: int32 [32], P(('dp', 'expert')), may hold values from 102 to 512
- w_query: bfloat16 [1024, 1024], P('dp'), may hold values from -0.1875 to 0.1875
- keyvalue_weight: bfloat16 [1024, 1024], P('dp'), may hold values from -0.1875 to 0.1875
- w_out: bfloat16 [1024, 1024], P('dp'), may hold values from -3 to 3
- w_router: bfloat16 [1024, 16], P('dp'), may hold values from -0.09375 to 0.09375
- gain_attn: bfloat16 [1024], P('dp'), may hold values from 0.5 to 1.5
- gain_mlp: bfloat16 [1024], P('dp'), may hold values from 0.5 to 1.5
- expert_gate: bfloat16 [16, 1024, 512], P('expert'), may hold values from -0.1875 to 0.1875
- expert_up: bfloat16 [16, 1024, 512], P('expert'), may hold values from -0.1875 to 0.1875
- expert_down: bfloat16 [16, 512, 1024], P('expert'), may hold values from -0.75 to 0.75
- query_logit_cap: float32 [16], replicated, may hold values from 3.5 to 8
Outputs:
- block_out: bfloat16 [32, 1024, 1024], P(('dp', 'expert'))
- grad_tokens: float32 [32, 1024, 1024], P(('dp', 'expert'))
- grad_query: float32 [1024, 1024], P('dp')
- grad_keyval: float32 [1024, 1024], P('dp')
- grad_out: float32 [1024, 1024], P('dp')
- grad_router: float32 [1024, 16], P('dp')
- grad_gain_attn: float32 [1024], P('dp')
- grad_gain_mlp: float32 [1024], P('dp')
- grad_gate: float32 [16, 1024, 512], P('expert', 'dp')
- grad_up: float32 [16, 1024, 512], P('expert', 'dp')
- grad_down: float32 [16, 512, 1024], P('expert', 'dp')
- clipped_query: bfloat16 [1024, 1024], P('dp')
- clipped_keyval: bfloat16 [1024, 1024], P('dp')
- head_logit_peak: float32 [16], replicated
The draws below stay inside these ranges and needn't reach their ends.
Inputs may be any that keep to these rules, and one draw needn't show every extreme that they name: `routes`: each token names 8 different experts; among the 1024 tokens of one device (aligned blocks of 1 sequence) no expert is named more than 576 times, a bound that some block reaches.
All inputs are finite; a program needn't handle non-finite values.
Results may differ from the reference program's by a relative error of at most 0.022.
Values may be sent and summed in bfloat16 or wider, within the bound.
A program may use at most 512 MiB of HBM per device.

```python
import math
import jax
import jax.numpy as jnp
import numpy as np
from jax import lax

MODEL_DIM = 1024
QUERY_HEADS = 16
KEY_VALUE_HEADS = 8
HEAD_DIM = 64
FF = 512
TOP = 8
SEQUENCE_LENGTH = 1024
SEQ_DEV = 1
EXPERTS = 16
TOK_DEV = 1024
SEQS = 32
CAP = 576


def with_ends(entries, rng, smallest, high):
    longest = entries.shape.index(max(entries.shape))
    spots = []
    for shift in (0, 1):
        where = [jax.random.randint(jax.random.fold_in(rng, axis), (), 0, length) for axis, length in enumerate(entries.shape)]
        where[longest] = (where[longest] + shift) % entries.shape[longest]
        spots.append(tuple(where))
    return entries.at[spots[0]].set(smallest).at[spots[1]].set(high)


def shard_levels(rng, extent, cuts, least, largest):
    gain = 1.0
    for axis_at, blocks in cuts:
        heights = jax.random.uniform(jax.random.fold_in(jax.random.fold_in(rng, 6), axis_at), (blocks,), jnp.float32, least / len(cuts), largest / len(cuts))
        gain = gain * jnp.repeat(jnp.exp(heights), extent[axis_at] // blocks).reshape((-1,) + (1,) * (len(extent) - 1 - axis_at))
    return gain


def routed_block(rng, own, number, rows, amount, top, limit, lean):
    sequence = jax.random.permutation(rng, amount)
    heavy_load, usual = portions_of(amount, rows * top, limit, lean, True), portions_of(amount, rows * top, limit, lean, False)
    places = jnp.arange(amount)

    def named(lengths, rotation):
        used = int((lengths > 0).sum())
        fixed = max(1, used // 4)
        passed = fixed + (places - fixed + rotation * (used - fixed)) % max(1, amount - fixed)
        return jnp.zeros((amount,), jnp.int32).at[sequence[jnp.where(places < fixed, places, passed)]].set(jnp.asarray(lengths, jnp.int32))

    lengths = jnp.where(number % 4 == 0, named(heavy_load, number // 4), named(usual, number - number // 4 - 1))
    mixed = jax.random.permutation(jax.random.fold_in(own, 3), amount)
    source_of, receiver = mixed[0:amount // 2 * 2:2], mixed[1:amount // 2 * 2:2]
    room = jnp.minimum(lengths[source_of] - 1, limit - lengths[receiver]) // 2
    room = jnp.where((source_of == sequence[0]) | (receiver == sequence[0]) | (lengths[receiver] == 0), 0, jnp.maximum(room, 0))
    passed = jax.random.randint(jax.random.fold_in(own, 4), (amount // 2,), 0, 1 << 20) % (room + 1)
    lengths = lengths.at[source_of].add(-passed).at[receiver].add(passed)
    labels = jnp.searchsorted(jnp.cumsum(lengths), jnp.arange(rows * top), side="right").astype(jnp.int32)
    listing = labels.reshape(top, rows).T
    listing = listing[jax.random.permutation(jax.random.fold_in(own, 1), rows)]
    rotation = jax.random.randint(jax.random.fold_in(own, 2), (rows, 1), 0, top)
    return jnp.take_along_axis(listing, (jnp.arange(top)[None, :] + rotation) % top, axis=1)


def portions_of(count, total, bound, slope, full):
    weights = [(1 << 20) // math.isqrt(grade ** slope) + 1 for grade in range(1, count + 1)]
    largest = bound if full else min(bound, max(-(-total // count), total * weights[0] // sum(weights)))
    least = 1 if total - largest >= count - 1 else 0
    given, rest = [largest] + [least] * (count - 1), total - largest - least * (count - 1)
    while rest > 0:
        free = [i for i in range(1, count) if given[i] < largest] or [i for i in range(1, count) if given[i] < bound]
        pool, left = sum([weights[i] for i in free]), rest
        for i in free:
            more = min(bound - given[i], max(1, left * weights[i] // pool), rest)
            given[i] = given[i] + more
            rest = rest - more
    return np.array(given)


def centred(stream_key, extent, deviation, most, cuts=(), kind=jnp.bfloat16):
    drawn = jax.random.normal(stream_key, extent, jnp.float32) * deviation
    if len(cuts) > 0:
        drawn = shard_levels(stream_key, extent, cuts, -0.22, 0.18) * drawn
    return jnp.clip(drawn, min=-most, max=most).astype(kind)


def setup_inputs(seed: int = 0) -> dict:
    key_list = jax.random.split(jax.random.key(seed), 15)
    tokens = centred(key_list[0], (SEQS, SEQUENCE_LENGTH, MODEL_DIM), 1.0, 6.0, ((0, 32),))
    cotangent = centred(key_list[1], (SEQS, SEQUENCE_LENGTH, MODEL_DIM), 1.0, 6.0, ((0, 32),))
    routes_keys = jax.random.split(jax.random.fold_in(key_list[2], 1), SEQS * SEQUENCE_LENGTH // TOK_DEV)
    routes_turns = jax.random.permutation(jax.random.fold_in(key_list[2], 3), SEQS * SEQUENCE_LENGTH // TOK_DEV)
    routes = jax.vmap(lambda own, number: routed_block(jax.random.fold_in(key_list[2], 2), own, number, TOK_DEV, EXPERTS, TOP, CAP, 1))(routes_keys, routes_turns).reshape((SEQS, SEQUENCE_LENGTH, TOP))
    prefix = with_ends(jax.random.randint(key_list[3], (SEQS,), SEQUENCE_LENGTH // 10, SEQUENCE_LENGTH // 2 + 1), jax.random.fold_in(key_list[3], 1), SEQUENCE_LENGTH // 10, (SEQUENCE_LENGTH // 2 + 1) - 1).astype(jnp.int32)
    w_query = centred(key_list[4], (MODEL_DIM, QUERY_HEADS * HEAD_DIM), MODEL_DIM ** -0.5, 0.1875, ((0, 8),))
    keyvalue_weight = centred(key_list[5], (MODEL_DIM, 2 * KEY_VALUE_HEADS * HEAD_DIM), MODEL_DIM ** -0.5, 0.1875, ((0, 8),))
    w_out = centred(key_list[6], (QUERY_HEADS * HEAD_DIM, MODEL_DIM), (max(QUERY_HEADS * HEAD_DIM * 4 // SEQUENCE_LENGTH, 1)) ** -0.5, 3.0, ((0, 8),))
    w_router = centred(key_list[7], (MODEL_DIM, EXPERTS), (4 * MODEL_DIM) ** -0.5, 0.09375, ((0, 8),))
    gain_attn = jnp.clip(1.0 + 0.1 * jax.random.normal(key_list[8], (MODEL_DIM,), jnp.float32), 0.5, 1.5).astype(jnp.bfloat16)
    gain_mlp = jnp.clip(1.0 + 0.1 * jax.random.normal(key_list[9], (MODEL_DIM,), jnp.float32), 0.5, 1.5).astype(jnp.bfloat16)
    expert_gate = centred(key_list[10], (EXPERTS, MODEL_DIM, FF), MODEL_DIM ** -0.5, 0.1875, ((0, 4),))
    expert_up = centred(key_list[11], (EXPERTS, MODEL_DIM, FF), MODEL_DIM ** -0.5, 0.1875, ((0, 4),))
    expert_down = centred(key_list[12], (EXPERTS, FF, MODEL_DIM), (FF // 8) ** -0.5, 0.75, ((0, 4),))
    query_logit_cap = jnp.clip(jax.random.uniform(key_list[13], (QUERY_HEADS,), jnp.float32, 3.5, 8.0), 3.5, 8.0)
    return {"tokens": tokens, "cotangent": cotangent, "routes": routes, "prefix": prefix, "w_query": w_query, "keyvalue_weight": keyvalue_weight, "w_out": w_out, "w_router": w_router, "gain_attn": gain_attn, "gain_mlp": gain_mlp, "expert_gate": expert_gate, "expert_up": expert_up, "expert_down": expert_down, "query_logit_cap": query_logit_cap}


epsilon = 1e-05
rope_base = 10000.0
highest = lax.Precision.HIGHEST

@jax.custom_vjp
def low(v):
    return lax.optimization_barrier(v.astype(jnp.bfloat16)).astype(jnp.float32)

@jax.custom_vjp
def low_back(v):
    return v

def low_keep(v):
    return (low(v), None)

def low_pass(kept, grad):
    return (grad,)

def back_keep(v):
    return (v, None)

def back_low(kept, grad):
    return (low(grad),)
low.defvjp(low_keep, low_pass)
low_back.defvjp(back_keep, back_low)

def rope_tables(length, head_size):
    half_size = head_size // 2
    frequency = rope_base ** (-(jnp.arange(half_size, dtype=jnp.float32) * 2.0 / head_size))
    angles = jnp.arange(length, dtype=jnp.float32)[:, None] * frequency[None, :]
    return (jnp.cos(angles), jnp.sin(angles))

def rotate(values_in, cosine, sine_part):
    half_size = values_in.shape[-1] // 2
    first_half = values_in[..., :half_size]
    second_half = values_in[..., half_size:]
    cos_cols = cosine[:, None, :]
    sin_cols = sine_part[:, None, :]
    return jnp.concatenate([first_half * cos_cols - second_half * sin_cols, first_half * sin_cols + second_half * cos_cols], axis=-1)

def norm_rows(values_in, gain_vec):
    return values_in * lax.rsqrt(lax.optimization_barrier(jnp.mean(values_in * values_in, axis=-1, keepdims=True)) + epsilon) * gain_vec

def matrix_product(left_side, right_side):
    return jnp.dot(left_side, right_side, preferred_element_type=jnp.float32, precision=highest)

def attend(queries, keys_rot, values_low, prefix_len):
    length = queries.shape[0]
    queries_per_group = queries.shape[1] // keys_rot.shape[1]
    key_full = jnp.repeat(keys_rot, queries_per_group, axis=1)
    value_full = jnp.repeat(values_low, queries_per_group, axis=1)
    scores = low_back(jnp.einsum('qhd,khd->hqk', queries, key_full, precision=highest) * queries.shape[2] ** (-0.5))
    query_pos = jnp.arange(length, dtype=jnp.int32)[:, None]
    key_pos = jnp.arange(length, dtype=jnp.int32)[None, :]
    allowed = (key_pos <= query_pos) | (key_pos < prefix_len)
    masked = jnp.where(allowed[None], scores, -1e+30)
    row_max = lax.optimization_barrier(jnp.max(masked, axis=-1, keepdims=True))
    weights = jnp.exp(masked - row_max)
    weights = weights / lax.optimization_barrier(jnp.sum(weights, axis=-1, keepdims=True))
    context = jnp.einsum('hqk,khd->qhd', low(weights), value_full, precision=highest)
    return (context, lax.optimization_barrier(jnp.max(masked, axis=(1, 2))))

def run_experts(normed_two, route_rows, gate_w, up_w, down_w):
    route_flat = route_rows.reshape(-1)
    num_routes = route_flat.shape[0]
    one_hot = (route_flat[:, None] == jnp.arange(EXPERTS, dtype=jnp.int32)[None, :]).astype(jnp.int32)
    rank_in = lax.optimization_barrier(jnp.sum((jnp.cumsum(one_hot, axis=0) - one_hot) * one_hot, axis=1)).astype(jnp.int32)
    slot_index = route_flat * CAP + rank_in
    fillers = jnp.zeros((EXPERTS * CAP,), jnp.int32).at[slot_index].set(jnp.arange(num_routes, dtype=jnp.int32) + 1)
    slot_used = (fillers > 0)[:, None]
    source_row = jnp.maximum(fillers - 1, 0) // TOP
    inputs = low_back(jnp.where(slot_used, normed_two[source_row], 0.0)).reshape(EXPERTS, CAP, MODEL_DIM)
    gate_pre = low_back(jnp.einsum('ecd,edf->ecf', inputs, gate_w, precision=highest))
    up_pre = low_back(jnp.einsum('ecd,edf->ecf', inputs, up_w, precision=highest))
    hidden = low(jax.nn.silu(gate_pre) * up_pre)
    result = low_back(low(jnp.einsum('ecf,efd->ecd', hidden, down_w, precision=highest)))
    return result.reshape(EXPERTS * CAP, MODEL_DIM)[slot_index].reshape(route_rows.shape[0], TOP, MODEL_DIM)

def forward(params, tokens_in, route_rows, prefix_len):
    w_query, keyvalue_weight, w_out, w_router, gain_attn, gain_mlp, gate_w, up_w, down_w = params
    sequence_count = tokens_in.shape[0]
    num_rows = sequence_count * SEQUENCE_LENGTH
    cosine, sine_part = rope_tables(SEQUENCE_LENGTH, HEAD_DIM)
    resid_in = tokens_in.reshape(num_rows, MODEL_DIM)
    attention_normed = low(norm_rows(resid_in, gain_attn))
    query_raw = low_back(matrix_product(attention_normed, w_query)).reshape(sequence_count, SEQUENCE_LENGTH, QUERY_HEADS, HEAD_DIM)
    unrotated_keyval = low_back(matrix_product(attention_normed, keyvalue_weight)).reshape(sequence_count, SEQUENCE_LENGTH, 2, KEY_VALUE_HEADS, HEAD_DIM)
    queries = low(rotate(query_raw, cosine, sine_part))
    keys_rot = low(rotate(unrotated_keyval[:, :, 0], cosine, sine_part))
    values_low = low(unrotated_keyval[:, :, 1])
    contexts, head_peaks = jax.vmap(attend)(queries, keys_rot, values_low, prefix_len)
    context_low = low_back(low(contexts.reshape(num_rows, QUERY_HEADS * HEAD_DIM)))
    attn_out = low_back(matrix_product(context_low, w_out))
    resid_mid = resid_in + attn_out
    normed_two = low(norm_rows(resid_mid, gain_mlp))
    logits = low_back(matrix_product(normed_two, w_router))
    flat_routes = route_rows.reshape(num_rows, TOP)
    gate_probs = jax.nn.softmax(jnp.take_along_axis(logits, flat_routes, axis=1), axis=-1)
    route_out = run_experts(normed_two, flat_routes, gate_w, up_w, down_w)
    block_out = resid_mid + lax.optimization_barrier(jnp.sum(gate_probs[:, :, None] * route_out, axis=1))
    return (block_out.reshape(sequence_count, SEQUENCE_LENGTH, MODEL_DIM), lax.optimization_barrier(jnp.max(head_peaks, axis=0)))

def reference(tokens, cotangent, routes, prefix, w_query, keyvalue_weight, w_out, w_router, gain_attn, gain_mlp, expert_gate, expert_up, expert_down, query_logit_cap):
    params = tuple((weight_arr.astype(jnp.float32) for weight_arr in (w_query, keyvalue_weight, w_out, w_router, gain_attn, gain_mlp, expert_gate, expert_up, expert_down)))
    num_blocks = SEQS // SEQ_DEV
    token_blocks = tokens.astype(jnp.float32).reshape(num_blocks, SEQ_DEV, SEQUENCE_LENGTH, MODEL_DIM)
    grad_blocks = cotangent.astype(jnp.float32).reshape(num_blocks, SEQ_DEV, SEQUENCE_LENGTH, MODEL_DIM)
    route_blocks = routes.reshape(num_blocks, SEQ_DEV, SEQUENCE_LENGTH, TOP)
    prefix_blocks = prefix.reshape(num_blocks, SEQ_DEV)

    def step_block(carry, operands):
        grad_sum, peak_sum = carry
        tokens_in, cot_in, route_in, prefix_in = operands

        def forward_block(param_set, token_set):
            return forward(param_set, token_set, route_in, prefix_in)
        block_res, pull_back, peaks = jax.vjp(forward_block, params, tokens_in, has_aux=True)
        param_grads, token_grads = pull_back(cot_in)
        grad_sum = jax.tree.map(jnp.add, grad_sum, param_grads)
        return ((grad_sum, jnp.maximum(peak_sum, peaks)), (block_res.astype(jnp.bfloat16), token_grads))
    start_state = (jax.tree.map(jnp.zeros_like, params), jnp.full((QUERY_HEADS,), -1e+30, jnp.float32))
    (grad_sum, head_logit_peak), (out_blocks, tok_grads) = lax.scan(step_block, start_state, (token_blocks, grad_blocks, route_blocks, prefix_blocks))
    queries_per_group = QUERY_HEADS // KEY_VALUE_HEADS
    query_factor = jnp.sqrt(query_logit_cap / jnp.maximum(head_logit_peak, query_logit_cap))
    paired_logit_peak = lax.optimization_barrier(jnp.max(head_logit_peak.reshape(KEY_VALUE_HEADS, queries_per_group), axis=1))
    paired_logit_cap = lax.optimization_barrier(jnp.min(query_logit_cap.reshape(KEY_VALUE_HEADS, queries_per_group), axis=1))
    key_rescale = jnp.sqrt(paired_logit_cap / jnp.maximum(paired_logit_peak, paired_logit_cap))
    clipped_query = (w_query.astype(jnp.float32) * jnp.repeat(query_factor, HEAD_DIM)[None, :]).astype(jnp.bfloat16)
    key_column_set = jnp.concatenate([jnp.repeat(key_rescale, HEAD_DIM), jnp.ones((KEY_VALUE_HEADS * HEAD_DIM,), jnp.float32)])
    clipped_keyval = (keyvalue_weight.astype(jnp.float32) * key_column_set[None, :]).astype(jnp.bfloat16)
    return (out_blocks.reshape(SEQS, SEQUENCE_LENGTH, MODEL_DIM), tok_grads.reshape(SEQS, SEQUENCE_LENGTH, MODEL_DIM), grad_sum[0], grad_sum[1], grad_sum[2], grad_sum[3], grad_sum[4], grad_sum[5], grad_sum[6], grad_sum[7], grad_sum[8], clipped_query, clipped_keyval, head_logit_peak)
```

```python
import functools

import jax
import jax.numpy as jnp
import numpy as np
from jax import lax
from jax.experimental import pallas as pl
from jax.experimental.pallas import tpu as pltpu
from jax.sharding import PartitionSpec as P

EPS = 1e-05
ROPE_BASE = 10000.0
F32 = jnp.float32
BF16 = jnp.bfloat16
NEG = -1e30
MIB = 1 << 20


def dot(a, b):
    return lax.dot_general(a, b, (((1,), (0,)), ((), ())), preferred_element_type=F32)


def dot_t(a, b):
    return lax.dot_general(a, b, (((1,), (1,)), ((), ())), preferred_element_type=F32)


def params(vmem_mib, n=1):
    return pltpu.CompilerParams(
        dimension_semantics=("arbitrary",) * n, vmem_limit_bytes=vmem_mib * MIB
    )


def cost(flops, nbytes, trans=0):
    return pl.CostEstimate(flops=int(flops), bytes_accessed=int(nbytes), transcendentals=int(trans))


def spec(shape, index):
    return pl.BlockSpec(shape, index)


def whole(shape):
    zeros = (0,) * len(shape)
    return pl.BlockSpec(shape, lambda *_: zeros)


def rope_tables(length, head):
    half = head // 2
    freq = np.float32(ROPE_BASE) ** (
        -(np.arange(half, dtype=np.float32) * np.float32(2.0) / np.float32(head))
    )
    ang = np.arange(length, dtype=np.float32)[:, None] * freq.astype(np.float32)[None, :]
    ang = ang.astype(np.float32)
    return np.cos(ang).astype(np.float32), np.sin(ang).astype(np.float32)


def lane_half(shape, width):
    return (lax.broadcasted_iota(jnp.int32, shape, 1) % width) < (width // 2)


def rope_lanes(x, cos, sin, first):
    partner = jnp.where(first, pltpu.roll(x, 96, 1), pltpu.roll(x, 32, 1))
    return x * cos + partner * sin


def qkv_kernel(tok_ref, gain_ref, w_ref, cos_ref, sin_ref, h_ref, q_ref, kd_ref, vd_ref):
    x = tok_ref[...].astype(F32)
    d = x.shape[1]
    r = lax.rsqrt(jnp.mean(x * x, axis=1, keepdims=True) + EPS)
    h = (x * r * gain_ref[...].astype(F32)).astype(BF16)
    h_ref[...] = h
    cos, sin = cos_ref[...], sin_ref[...]
    rows = x.shape[0]
    first = lane_half((rows, 128), 64)
    low = lane_half((rows, 128), 128)
    nq = q_ref.shape[1]
    nk = kd_ref.shape[1] // 2
    q = dot(h, w_ref[:, :nq])
    for c in range(0, nq, 128):
        q_ref[:, c : c + 128] = (rope_lanes(q[:, c : c + 128], cos, sin, first) * 0.125).astype(
            BF16
        )
    k = dot(h, w_ref[:, nq : nq + nk])
    for c in range(0, nk, 128):
        kk = rope_lanes(k[:, c : c + 128], cos, sin, first)
        sw = pltpu.roll(kk, 64, 1)
        kd_ref[:, 2 * c : 2 * c + 128] = jnp.where(low, kk, sw).astype(BF16)
        kd_ref[:, 2 * c + 128 : 2 * c + 256] = jnp.where(low, sw, kk).astype(BF16)
    v = dot(h, w_ref[:, nq + nk : nq + 2 * nk])
    for c in range(0, nk, 128):
        vv = v[:, c : c + 128]
        sw = pltpu.roll(vv, 64, 1)
        vd_ref[:, 2 * c : 2 * c + 128] = jnp.where(low, vv, sw).astype(BF16)
        vd_ref[:, 2 * c + 128 : 2 * c + 256] = jnp.where(low, sw, vv).astype(BF16)


def run_qkv(tok, gain, w_qkv, cos, sin, nq):
    length, d = tok.shape
    b = 256
    row = lambda i: (i, 0)
    return pl.pallas_call(
        qkv_kernel,
        grid=(length // b,),
        in_specs=[
            spec((b, d), row),
            whole((1, d)),
            spec((d, 2 * nq), lambda i: (0, 0)),
            spec((b, 128), row),
            spec((b, 128), row),
        ],
        out_specs=[spec((b, d), row)] + [spec((b, nq), row)] * 3,
        out_shape=[jax.ShapeDtypeStruct((length, d), BF16)]
        + [jax.ShapeDtypeStruct((length, nq), BF16)] * 3,
        compiler_params=params(40),
        cost_estimate=cost(2 * length * d * 2 * nq, 16 * MIB),
        name="qkv",
    )(tok, gain, w_qkv, cos, sin)


def mask_bias(prefix, q0, k0, nq, nk, q_axis):
    shape = (nq, nk) if q_axis == 0 else (nk, nq)
    qpos = q0 + lax.broadcasted_iota(jnp.int32, shape, q_axis)
    kpos = k0 + lax.broadcasted_iota(jnp.int32, shape, 1 - q_axis)
    return jnp.where((kpos <= qpos) | (kpos < prefix), 0.0, NEG).astype(F32)


def two_heads(pair, low):
    zero = jnp.zeros_like(pair)
    return jnp.concatenate([jnp.where(low, pair, zero), jnp.where(low, zero, pair)], axis=0)


def attn_fwd_kernel(prefix_ref, q_ref, kd_ref, vd_ref, ctx_ref, lse_ref, peak_ref):
    length = q_ref.shape[0]
    b = 256
    prefix = prefix_ref[0]
    low_b = lane_half((b, 128), 128)
    lane = lax.broadcasted_iota(jnp.int32, (b, 128), 1)
    peak = jnp.full((8, 128), NEG, F32)
    peak_lane = lax.broadcasted_iota(jnp.int32, (8, 128), 1)
    for i in range(length // b):
        nk = max((i + 1) * b, length // 2)
        free = i * b
        bias = mask_bias(prefix, i * b, free, b, nk - free, 0)
        bias = jnp.concatenate([bias, bias], axis=0)
        lse_cols = jnp.zeros((b, 128), F32)
        for j in range(2):
            cols = slice(j * 128, (j + 1) * 128)
            q2 = two_heads(q_ref[i * b : (i + 1) * b, cols], low_b)
            s_hi = dot_t(q2, kd_ref[free:nk, cols]) + bias
            m = jnp.max(s_hi, axis=1, keepdims=True)
            if free:
                s_lo = dot_t(q2, kd_ref[:free, cols])
                m = jnp.maximum(m, jnp.max(s_lo, axis=1, keepdims=True))
            p_hi = jnp.exp(s_hi - m)
            total = jnp.sum(p_hi, axis=1, keepdims=True)
            ctx = dot(p_hi.astype(BF16), vd_ref[free:nk, cols])
            if free:
                p_lo = jnp.exp(s_lo - m)
                total = total + jnp.sum(p_lo, axis=1, keepdims=True)
                ctx = ctx + dot(p_lo.astype(BF16), vd_ref[:free, cols])
            ctx = ctx * (1.0 / total)
            ctx_ref[i * b : (i + 1) * b, cols] = jnp.where(low_b, ctx[:b], ctx[b:]).astype(BF16)
            lse = m + jnp.log(total)
            for g in range(2):
                lse_cols = jnp.where(lane == 2 * j + g, lse[g * b : (g + 1) * b], lse_cols)
                top = jnp.max(m[g * b : (g + 1) * b], axis=0, keepdims=True)
                peak = jnp.where(peak_lane == 2 * j + g, jnp.maximum(peak, top), peak)
        lse_ref[0, :, i * b : (i + 1) * b] = lse_cols.T[:8]
    peak_ref[0] = peak


def run_attn_fwd(prefix, q, kd, vd):
    length, nq = q.shape
    groups = nq // 256
    col = lambda g: (0, g)
    return pl.pallas_call(
        attn_fwd_kernel,
        grid=(groups,),
        in_specs=[pl.BlockSpec(memory_space=pltpu.SMEM)] + [spec((length, 256), col)] * 3,
        out_specs=[
            spec((length, 256), col),
            spec((1, 8, length), lambda g: (g, 0, 0)),
            spec((1, 8, 128), lambda g: (g, 0, 0)),
        ],
        out_shape=[
            jax.ShapeDtypeStruct((length, nq), BF16),
            jax.ShapeDtypeStruct((groups, 8, length), F32),
            jax.ShapeDtypeStruct((groups, 8, 128), F32),
        ],
        compiler_params=params(48),
        cost_estimate=cost(25e9, 9 * MIB),
        name="attn_fwd",
    )(prefix, q, kd, vd)


def attn_bwd_kernel(
    prefix_ref, q_ref, kd_ref, vd_ref, do_ref, ctx_ref, lse_ref, cos_ref, sin_ref, cost_ref, sint_ref,
    dq_ref, dk_ref, dv_ref, dk_acc, dv_acc, kt_ref,
):
    length = q_ref.shape[0]
    b = 256
    prefix = prefix_ref[0]
    low_b = lane_half((b, 128), 128)
    for j in range(2):
        cols = slice(j * 128, (j + 1) * 128)
        kt_ref[j] = kd_ref[:, cols].T
    dk_acc[...] = jnp.zeros_like(dk_acc)
    dv_acc[...] = jnp.zeros_like(dv_acc)
    for i in range(length // b):
        rows = slice(i * b, (i + 1) * b)
        nk = max((i + 1) * b, length // 2)
        free = i * b
        bias = mask_bias(prefix, i * b, free, b, nk - free, 1)
        bias = jnp.concatenate([bias, bias], axis=1)
        for j in range(2):
            cols = slice(j * 128, (j + 1) * 128)
            do = do_ref[rows, cols]
            q2 = two_heads(q_ref[rows, cols], low_b)
            do2 = two_heads(do, low_b)
            prod = (do.astype(F32) * ctx_ref[rows, cols].astype(F32)).T
            delta = jnp.concatenate(
                [
                    jnp.sum(prod[:64], axis=0, keepdims=True),
                    jnp.sum(prod[64:], axis=0, keepdims=True),
                ],
                axis=1,
            )
            lse = jnp.concatenate(
                [lse_ref[0, 2 * j : 2 * j + 1, rows], lse_ref[0, 2 * j + 1 : 2 * j + 2, rows]],
                axis=1,
            )
            dq_t = None
            parts = [(0, free)] if free else []
            for k0, k1 in parts + [(free, nk)]:
                keys = slice(k0, k1)
                s = dot_t(kd_ref[keys, cols], q2)
                if k0 == free:
                    s = s + bias
                p = jnp.exp(s - lse)
                dp = dot_t(vd_ref[keys, cols], do2)
                ds = (p * (dp - delta)).astype(BF16)
                dv_acc[j, keys, :] += dot(p.astype(BF16), do2)
                dk_acc[j, keys, :] += dot(ds, q2)
                part = dot(kt_ref[j, :, keys], ds)
                dq_t = part if dq_t is None else dq_t + part
            cos_t, sin_t = cost_ref[:, rows], sint_ref[:, rows]
            a0, b0 = dq_t[0:32, :b], dq_t[32:64, :b]
            a1, b1 = dq_t[64:96, b:], dq_t[96:128, b:]
            full = jnp.concatenate(
                [
                    a0 * cos_t + b0 * sin_t,
                    b0 * cos_t - a0 * sin_t,
                    a1 * cos_t + b1 * sin_t,
                    b1 * cos_t - a1 * sin_t,
                ],
                axis=0,
            )
            dq_ref[rows, cols] = (full * 0.125).T.astype(BF16)
    low = lane_half((length, 128), 128)
    first = lane_half((length, 128), 64)
    sums = []
    for acc in (dk_acc, dv_acc):
        even = acc[0] + pltpu.roll(acc[0], 64, 1)
        odd = acc[1] + pltpu.roll(acc[1], 64, 1)
        sums.append(jnp.where(low, even, odd))
    dk_ref[...] = rope_lanes(sums[0], cos_ref[...], -sin_ref[...], first).astype(BF16)
    dv_ref[...] = sums[1].astype(BF16)


def run_attn_bwd(prefix, q, kd, vd, d_ctx, ctx, lse, cos, sin, cos_t, sin_t):
    length, nq = q.shape
    groups = nq // 256
    col = lambda g: (0, g)
    wide = spec((length, 256), col)
    return pl.pallas_call(
        attn_bwd_kernel,
        grid=(groups,),
        in_specs=[pl.BlockSpec(memory_space=pltpu.SMEM)]
        + [wide] * 5
        + [spec((1, 8, length), lambda g: (g, 0, 0))]
        + [whole((length, 128))] * 2
        + [whole((cos_t.shape[0], length))] * 2,
        out_specs=[wide, spec((length, 128), col), spec((length, 128), col)],
        out_shape=[
            jax.ShapeDtypeStruct((length, nq), BF16),
            jax.ShapeDtypeStruct((length, nq // 2), BF16),
            jax.ShapeDtypeStruct((length, nq // 2), BF16),
        ],
        scratch_shapes=[
            pltpu.VMEM((2, length, 128), F32),
            pltpu.VMEM((2, length, 128), F32),
            pltpu.VMEM((2, 128, length), BF16),
        ],
        compiler_params=params(56),
        cost_estimate=cost(60e9, 16 * MIB),
        name="attn_bwd",
    )(prefix, q, kd, vd, d_ctx, ctx, lse, cos, sin, cos_t, sin_t)


def mid_kernel(tok_ref, ctx_ref, w_ref, gain_ref, res_ref, x_ref):
    res = tok_ref[...].astype(F32) + dot(ctx_ref[...], w_ref[...])
    res_ref[...] = res
    r = lax.rsqrt(jnp.mean(res * res, axis=1, keepdims=True) + EPS)
    x_ref[...] = (res * r * gain_ref[...].astype(F32)).astype(BF16)


def run_mid(tok, ctx, w_out, gain):
    length, d = tok.shape
    b = 256
    row = lambda i: (i, 0)
    return pl.pallas_call(
        mid_kernel,
        grid=(length // b,),
        in_specs=[
            spec((b, d), row),
            spec((b, ctx.shape[1]), row),
            whole(w_out.shape),
            whole((1, d)),
        ],
        out_specs=[spec((b, d), row)] * 2,
        out_shape=[
            jax.ShapeDtypeStruct((length, d), F32),
            jax.ShapeDtypeStruct((length, d), BF16),
        ],
        compiler_params=params(40),
        cost_estimate=cost(2 * length * d * d, 12 * MIB),
        name="mid",
    )(tok, ctx, w_out, gain)


def gates_of(x, router, mask):
    logits = dot(x, router)
    logits = jnp.where(mask > 0, logits, NEG)
    e = jnp.exp(logits - jnp.max(logits, axis=1, keepdims=True))
    e = jnp.where(mask > 0, e, 0.0)
    return e / jnp.sum(e, axis=1, keepdims=True)


def expert_kernel(
    me_ref, x_ref, c_ref, mask_ref, router_ref, wg_ref, wu_ref, wd_ref,
    out_ref, dx_ref, dg_ref, hs_ref, dgate_ref, dup_ref, xt_ref, ct_ref, out_acc, dx_acc, gp_ref, dgc_ref,
):
    e = pl.program_id(1)
    local = pl.num_programs(1)
    x, c = x_ref[...], c_ref[...]
    b = x.shape[0]
    lane = lax.broadcasted_iota(jnp.int32, (b, 128), 1)

    @pl.when(e == 0)
    def _():
        gp_ref[...] = gates_of(x, router_ref[...], mask_ref[...].astype(F32))
        xt_ref[...] = x.T
        ct_ref[...] = c.T

    gp = jnp.sum(
        jnp.where(lane == me_ref[0] * local + e, gp_ref[...], 0.0), axis=1, keepdims=True
    )
    gate = dot(x, wg_ref[e])
    up = dot(x, wu_ref[e])
    grad = dot_t(c, wd_ref[e])
    sig = 0.5 * jnp.tanh(0.5 * gate) + 0.5
    act = gate * sig
    hidden = (act * up).astype(BF16).astype(F32)
    dg = jnp.sum(hidden * grad, axis=1, keepdims=True)
    hs = (hidden * gp).astype(BF16)
    dh = grad * gp
    dup = (dh * act).astype(BF16)
    dgate = (dh * up * (sig + act * (1.0 - sig))).astype(BF16)
    hs_ref[...] = hs
    dup_ref[...] = dup
    dgate_ref[...] = dgate
    out = dot(hs, wd_ref[e])
    dx = dot_t(dgate, wg_ref[e]) + dot_t(dup, wu_ref[e])
    dg_col = jnp.where(lane == e, dg, 0.0)

    @pl.when(e == 0)
    def _():
        out_acc[...] = out
        dx_acc[...] = dx
        dgc_ref[...] = dg_col

    @pl.when((e > 0) & (e < local - 1))
    def _():
        out_acc[...] += out
        dx_acc[...] += dx
        dgc_ref[...] += dg_col

    @pl.when(e == local - 1)
    def _():
        out_ref[...] = (out_acc[...] + out).astype(BF16)
        dx_ref[...] = (dx_acc[...] + dx).astype(BF16)
        dg_ref[...] = (dgc_ref[...] + dg_col).T[:8]


def run_expert(me, x, c, mask, router, wg, wu, wd):
    length, d = x.shape
    local, _, ff = wg.shape
    b = 512
    row = lambda i, e: (i, 0)
    colT = lambda i, e: (0, i)
    once = lambda shape: pl.BlockSpec(
        shape, lambda i, e: (0,) * len(shape), pipeline_mode=pl.Buffered(1)
    )
    return pl.pallas_call(
        expert_kernel,
        grid=(length // b, local),
        in_specs=[
            pl.BlockSpec(memory_space=pltpu.SMEM),
            spec((b, d), row),
            spec((b, d), row),
            spec((b, 128), row),
            once(router.shape),
            once(wg.shape),
            once(wu.shape),
            once(wd.shape),
        ],
        out_specs=[
            spec((b, d), row),
            spec((b, d), row),
            spec((8, b), colT),
            spec((b, ff), lambda i, e: (i, e)),
            spec((b, ff), lambda i, e: (i, e)),
            spec((b, ff), lambda i, e: (i, e)),
            spec((d, b), colT),
            spec((d, b), colT),
        ],
        out_shape=[
            jax.ShapeDtypeStruct((length, d), BF16),
            jax.ShapeDtypeStruct((length, d), BF16),
            jax.ShapeDtypeStruct((8, length), F32),
            jax.ShapeDtypeStruct((length, local * ff), BF16),
            jax.ShapeDtypeStruct((length, local * ff), BF16),
            jax.ShapeDtypeStruct((length, local * ff), BF16),
            jax.ShapeDtypeStruct((d, length), BF16),
            jax.ShapeDtypeStruct((d, length), BF16),
        ],
        scratch_shapes=[
            pltpu.VMEM((b, d), F32),
            pltpu.VMEM((b, d), F32),
            pltpu.VMEM((b, 128), F32),
            pltpu.VMEM((b, 128), F32),
        ],
        compiler_params=params(58, 2),
        cost_estimate=cost(12 * length * d * ff * local, 40 * MIB, length * ff * local),
        name="experts",
    )(me, x, c, mask, router, wg, wu, wd)


def weight_grad_kernel(n, transpose, *refs):
    lefts, rights, out_ref = refs[:n], refs[n : 2 * n], refs[2 * n]
    d = lefts[0].shape[0]
    for m in range(0, d, 256):
        acc = None
        for left, right in zip(lefts, rights):
            part = dot(left[m : m + 256, :], right[...])
            acc = part if acc is None else acc + part
        if transpose:
            out_ref[0, :, m : m + 256] = acc.T.astype(BF16)
        else:
            out_ref[0, m : m + 256, :] = acc.astype(BF16)


def run_weight_grad(lefts, rights, local, transpose):
    n = len(lefts)
    d, length = lefts[0].shape
    ff = rights[0].shape[1] // local
    shape = (ff, d) if transpose else (d, ff)
    return pl.pallas_call(
        functools.partial(weight_grad_kernel, n, transpose),
        grid=(local,),
        in_specs=[
            pl.BlockSpec((d, length), lambda e: (0, 0), pipeline_mode=pl.Buffered(1))
            for _ in lefts
        ]
        + [spec((length, ff), lambda e: (0, e)) for _ in rights],
        out_specs=spec((1,) + shape, lambda e: (e, 0, 0)),
        out_shape=jax.ShapeDtypeStruct((local,) + shape, BF16),
        compiler_params=params(56),
        cost_estimate=cost(2 * n * length * d * ff * local, (n * 6 + 4) * MIB),
        name="weight_grad",
    )(*lefts, *rights)


def back_mid_kernel(n, *refs):
    (res_ref, cot_ref, mask_ref, x_ref, router_ref, dg_ref, gain_ref, w_ref) = refs[:8]
    dx_refs = refs[8 : 8 + n]
    dres_ref, dattn_ref, dctx_ref, dlog_ref, ggain_ref = refs[8 + n :]
    gp = gates_of(x_ref[...], router_ref[...], mask_ref[...].astype(F32))
    dg = dg_ref[...]
    d_logits = (gp * (dg - jnp.sum(gp * dg, axis=1, keepdims=True))).astype(BF16)
    dlog_ref[...] = d_logits
    d_norm = dot_t(d_logits, router_ref[...])
    for ref in dx_refs:
        d_norm = d_norm + ref[...].astype(F32)
    res = res_ref[...]
    r = lax.rsqrt(jnp.mean(res * res, axis=1, keepdims=True) + EPS)
    xr = res * r
    part = jnp.sum(d_norm * xr, axis=0, keepdims=True)

    @pl.when(pl.program_id(0) == 0)
    def _():
        ggain_ref[...] = jnp.zeros_like(ggain_ref)

    ggain_ref[...] += part
    u = d_norm * gain_ref[...].astype(F32)
    d_res = (
        cot_ref[...].astype(F32) + r * u - xr * (r * r) * jnp.mean(u * res, axis=1, keepdims=True)
    )
    dres_ref[...] = d_res
    d_attn = d_res.astype(BF16)
    dattn_ref[...] = d_attn
    dctx_ref[...] = dot_t(d_attn, w_ref[...]).astype(BF16)


def run_back_mid(res, cot, mask, x, router, dg, gain, w_out, dxs):
    length, d = res.shape
    b = 256
    row = lambda i: (i, 0)
    n = len(dxs)
    return pl.pallas_call(
        functools.partial(back_mid_kernel, n),
        grid=(length // b,),
        in_specs=[
            spec((b, d), row),
            spec((b, d), row),
            spec((b, 128), row),
            spec((b, d), row),
            whole(router.shape),
            spec((b, 128), row),
            whole((1, d)),
            whole(w_out.shape),
        ]
        + [spec((b, d), row)] * n,
        out_specs=[
            spec((b, d), row),
            spec((b, d), row),
            spec((b, w_out.shape[0]), row),
            spec((b, 128), row),
            whole((1, d)),
        ],
        out_shape=[
            jax.ShapeDtypeStruct((length, d), F32),
            jax.ShapeDtypeStruct((length, d), BF16),
            jax.ShapeDtypeStruct((length, w_out.shape[0]), BF16),
            jax.ShapeDtypeStruct((length, 128), BF16),
            jax.ShapeDtypeStruct((1, d), F32),
        ],
        compiler_params=params(48),
        cost_estimate=cost(2 * length * d * d, 26 * MIB),
        name="back_mid",
    )(res, cot, mask, x, router, dg, gain, w_out, *dxs)


def back_in_kernel(dq_ref, dk_ref, dv_ref, w_ref, tok_ref, gain_ref, dres_ref, gt_ref, ggain_ref):
    nq, nk = dq_ref.shape[1], dk_ref.shape[1]
    d_norm = dot_t(dq_ref[...], w_ref[:, :nq])
    d_norm = d_norm + dot_t(dk_ref[...], w_ref[:, nq : nq + nk])
    d_norm = d_norm + dot_t(dv_ref[...], w_ref[:, nq + nk : nq + 2 * nk])
    x = tok_ref[...].astype(F32)
    r = lax.rsqrt(jnp.mean(x * x, axis=1, keepdims=True) + EPS)
    xr = x * r
    part = jnp.sum(d_norm * xr, axis=0, keepdims=True)

    @pl.when(pl.program_id(0) == 0)
    def _():
        ggain_ref[...] = jnp.zeros_like(ggain_ref)

    ggain_ref[...] += part
    u = d_norm * gain_ref[...].astype(F32)
    gt_ref[...] = dres_ref[...] + r * u - xr * (r * r) * jnp.mean(u * x, axis=1, keepdims=True)


def run_back_in(dq, dk, dv, w_qkv, tok, gain, d_res):
    length, d = tok.shape
    b = 256
    row = lambda i: (i, 0)
    nq = dq.shape[1]
    return pl.pallas_call(
        back_in_kernel,
        grid=(length // b,),
        in_specs=[
            spec((b, nq), row),
            spec((b, dk.shape[1]), row),
            spec((b, dv.shape[1]), row),
            spec((d, 2 * nq), lambda i: (0, 0)),
            spec((b, d), row),
            whole((1, d)),
            spec((b, d), row),
        ],
        out_specs=[spec((b, d), row), whole((1, d))],
        out_shape=[jax.ShapeDtypeStruct((length, d), F32), jax.ShapeDtypeStruct((1, d), F32)],
        compiler_params=params(48),
        cost_estimate=cost(4 * length * d * nq, 20 * MIB),
        name="back_in",
    )(dq, dk, dv, w_qkv, tok, gain, d_res)


def after(value, *deps):
    return lax.optimization_barrier((value,) + deps)[0]


def on_device(
    n_dp, n_ex, tokens, cotangent, routes, prefix, w_query, keyvalue_weight, w_out, w_router,
    gain_attn, gain_mlp, expert_gate, expert_up, expert_down, query_logit_cap,
):
    length, d = tokens.shape[1], tokens.shape[2]
    tok = tokens.reshape(length, d)
    cot = cotangent.reshape(length, d)
    heads = query_logit_cap.shape[0]
    nq = w_query.shape[1]
    head = nq // heads
    kv_heads = keyvalue_weight.shape[1] // (2 * head)
    num_experts = w_router.shape[1]
    local = expert_gate.shape[0]
    rows = w_query.shape[0]
    ex = lax.axis_index("expert")

    def swap(value, step, axis="expert", n=n_ex):
        return lax.ppermute(value, axis, [(i, i ^ step) for i in range(n)])

    part = rows // n_ex
    small = jnp.concatenate(
        [
            w_router,
            gain_attn[:, None],
            gain_mlp[:, None],
            jnp.zeros((rows, 128 - num_experts - 2), BF16),
        ],
        axis=1,
    )
    packed = jnp.concatenate([w_query, keyvalue_weight, w_out, small], axis=1)
    mine = lax.dynamic_slice_in_dim(packed, ex * part, part, axis=0)
    every = lax.all_gather(mine, ("dp", "expert"), axis=0, tiled=True)
    w_all = every
    width = 2 * nq
    full_out = every[:, width : width + d]
    extra = every[:, width + d :]
    lanes = lax.broadcasted_iota(jnp.int32, extra.shape, 1)
    router = jnp.where(lanes < num_experts, extra, jnp.zeros((), BF16))
    gain_one = extra[:, num_experts].reshape(1, d)
    gain_two = extra[:, num_experts + 1].reshape(1, d)

    routes_t = routes.reshape(length, -1).T
    cots, masks = {0: cot}, {}
    route_set = {0: routes_t}
    cot_late = after(cot, every)
    for step in range(1, n_ex):
        if step == 1:
            cots[1] = swap(cot_late, 1)
        elif step % 2 == 0:
            cots[step] = swap(cot_late, step)
        else:
            cots[step] = swap(cots[step - 1], 1)
        route_set[step] = swap(routes_t, step)
    columns = jnp.arange(128, dtype=jnp.int32)
    for step in range(n_ex):
        hit = route_set[step].T[:, :, None] == columns[None, None, :]
        masks[step] = jnp.any(hit, axis=1).astype(BF16)

    cos_np, sin_np = rope_tables(length, head)
    cos_l = jnp.asarray(np.concatenate([cos_np] * 4, axis=1))
    sin_l = jnp.asarray(np.concatenate([-sin_np, sin_np] * 2, axis=1))
    cos_t = jnp.asarray(np.ascontiguousarray(cos_np.T))
    sin_t = jnp.asarray(np.ascontiguousarray(sin_np.T))

    normed_one, q, kd, vd = run_qkv(tok, gain_one, w_all, cos_l, sin_l, nq)
    ctx, lse, peaks = run_attn_fwd(prefix, q, kd, vd)
    resid, normed_two = run_mid(tok, ctx, full_out, gain_two)

    me = ex.reshape(1).astype(jnp.int32)
    xs = {0: normed_two}
    for step in range(1, n_ex):
        if step == 1 or step % 2 == 0:
            xs[step] = swap(normed_two, step)
        else:
            xs[step] = swap(xs[step - 1], 1)
    res = {}
    for step in range(n_ex):
        res[step] = run_expert(
            me, xs[step], cots[step], masks[step], router, expert_gate, expert_up, expert_down
        )

    def collect(index, dep=None):
        got = [res[0][index]]
        first = res[1][index]
        if dep is not None:
            first = after(first, dep)
        got.append(swap(first, 1))
        for step in range(2, n_ex, 2):
            other = res[step + 1][index]
            if dep is not None:
                other = after(other, dep)
            both = (res[step][index].astype(F32) + swap(other, 1).astype(F32)).astype(BF16)
            got.append(swap(both, step))
        return got

    dxs = collect(1)
    dg_parts = [res[0][2]] + [swap(res[step][2], step) for step in range(1, n_ex)]
    stacked = jnp.stack([piece[:local] for piece in dg_parts])
    owner = jnp.arange(n_ex, dtype=jnp.int32)
    dg = sum(
        jnp.where(((owner ^ step) == ex)[:, None, None], stacked[step][None], 0.0)
        for step in range(n_ex)
    )
    dg = dg.reshape(num_experts, length).T
    dg = jnp.pad(dg, ((0, 0), (0, 128 - num_experts)))

    order = list(range(n_ex))
    d_down = run_weight_grad(
        [res[s][7] for s in order], [res[s][3] for s in order], local, True
    )
    d_gate = run_weight_grad(
        [res[s][6] for s in order], [res[s][4] for s in order], local, False
    )
    d_up = run_weight_grad([res[s][6] for s in order], [res[s][5] for s in order], local, False)
    grad_down = lax.psum_scatter(d_down, "dp", scatter_dimension=1, tiled=True).astype(F32)
    grad_gate = lax.psum_scatter(d_gate, "dp", scatter_dimension=1, tiled=True).astype(F32)
    grad_up = lax.psum_scatter(d_up, "dp", scatter_dimension=1, tiled=True).astype(F32)

    d_res, d_attn, d_ctx, d_logits, d_gain_two = run_back_mid(
        resid, cot, masks[0], normed_two, router, dg, gain_two, full_out, dxs
    )
    outs = collect(0, d_ctx)
    block = resid
    for piece in outs:
        block = block + piece.astype(F32)
    block_out = block.astype(BF16).reshape(tokens.shape)

    d_out_w = jnp.einsum("rc,rd->cd", ctx, d_attn, preferred_element_type=F32).astype(BF16)
    d_router_w = jnp.einsum("rd,re->de", normed_two, d_logits, preferred_element_type=F32)

    dq, dk, dv = run_attn_bwd(
        prefix, q, kd, vd, d_ctx, ctx, lse, cos_l, sin_l, cos_t, sin_t
    )
    grad_tok, d_gain_one = run_back_in(dq, dk, dv, w_all, tok, gain_one, d_res)
    d_query_w = jnp.einsum("rd,rc->dc", normed_one, dq, preferred_element_type=F32).astype(BF16)
    d_key_w = jnp.einsum("rd,rc->dc", normed_one, dk, preferred_element_type=F32).astype(BF16)
    d_val_w = jnp.einsum("rd,rc->dc", normed_one, dv, preferred_element_type=F32).astype(BF16)

    small_grad = jnp.concatenate(
        [
            d_router_w[:, :num_experts].astype(BF16),
            d_gain_one.reshape(d, 1).astype(BF16),
            d_gain_two.reshape(d, 1).astype(BF16),
            jnp.zeros((d, 128 - num_experts - 2), BF16),
        ],
        axis=1,
    )

    def reduce_all(value):
        value = value.reshape(n_dp, n_ex, value.shape[0] // (n_dp * n_ex), value.shape[1])
        value = lax.psum_scatter(value, "expert", scatter_dimension=1, tiled=True)
        value = lax.psum_scatter(
            value.reshape(n_dp * value.shape[2], value.shape[3]),
            "dp",
            scatter_dimension=0,
            tiled=True,
        )
        return lax.all_gather(value, "expert", axis=0, tiled=True).astype(F32)

    grad_out = reduce_all(d_out_w)
    rest = reduce_all(jnp.concatenate([d_query_w, d_key_w, d_val_w, small_grad], axis=1))
    grad_query = rest[:, :nq]
    grad_keyval = rest[:, nq : 2 * nq]
    grad_router = rest[:, 2 * nq : 2 * nq + num_experts]
    grad_gain_one = rest[:, 2 * nq + num_experts]
    grad_gain_two = rest[:, 2 * nq + num_experts + 1]

    top = peaks[:, :, :4]
    step = 1
    while step < n_ex:
        top = jnp.maximum(top, swap(top, step))
        step *= 2
    step = 1
    while step < n_dp:
        top = jnp.maximum(top, swap(top, step, "dp", n_dp))
        step *= 2
    head_logit_peak = top[:, 0, :].reshape(heads)
    per_group = heads // kv_heads
    query_factor = jnp.sqrt(query_logit_cap / jnp.maximum(head_logit_peak, query_logit_cap))
    pair_peak = jnp.max(head_logit_peak.reshape(kv_heads, per_group), axis=1)
    pair_cap = jnp.min(query_logit_cap.reshape(kv_heads, per_group), axis=1)
    key_factor = jnp.sqrt(pair_cap / jnp.maximum(pair_peak, pair_cap))
    clipped_query = (w_query.astype(F32) * jnp.repeat(query_factor, head)[None, :]).astype(BF16)
    key_cols = jnp.concatenate(
        [jnp.repeat(key_factor, head), jnp.ones((kv_heads * head,), F32)]
    )
    clipped_keyval = (keyvalue_weight.astype(F32) * key_cols[None, :]).astype(BF16)
    return (
        block_out,
        grad_tok.reshape(tokens.shape),
        grad_query,
        grad_keyval,
        grad_out,
        grad_router,
        grad_gain_one,
        grad_gain_two,
        grad_gate,
        grad_up,
        grad_down,
        clipped_query,
        clipped_keyval,
        head_logit_peak,
    )


def solution(mesh):
    rows3 = P(("dp", "expert"), None, None)
    in_specs = (
        rows3,
        rows3,
        rows3,
        P(("dp", "expert")),
        P("dp", None),
        P("dp", None),
        P("dp", None),
        P("dp", None),
        P("dp"),
        P("dp"),
        P("expert", None, None),
        P("expert", None, None),
        P("expert", None, None),
        P(),
    )
    out_specs = (
        rows3,
        rows3,
        P("dp", None),
        P("dp", None),
        P("dp", None),
        P("dp", None),
        P("dp"),
        P("dp"),
        P("expert", "dp", None),
        P("expert", "dp", None),
        P("expert", "dp", None),
        P("dp", None),
        P("dp", None),
        P(),
    )
    return jax.shard_map(
        functools.partial(on_device, mesh.shape["dp"], mesh.shape["expert"]),
        mesh=mesh,
        in_specs=in_specs,
        out_specs=out_specs,
        check_vma=False,
    )
```

```python
import functools

import jax
import jax.numpy as jnp
import numpy as np
from jax import lax
from jax.experimental import pallas as pl
from jax.experimental.pallas import tpu as pltpu
from jax.sharding import PartitionSpec as P

EPS = 1e-05
ROPE_BASE = 10000.0
F32 = jnp.float32
BF16 = jnp.bfloat16
NEG = -1e30
MIB = 1 << 20
SCALE = 0.5


def dot(a, b):
    return lax.dot_general(a, b, (((1,), (0,)), ((), ())), preferred_element_type=F32)


def dot_t(a, b):
    return lax.dot_general(a, b, (((1,), (1,)), ((), ())), preferred_element_type=F32)


def params(vmem_mib, n=1):
    return pltpu.CompilerParams(
        dimension_semantics=("arbitrary",) * n, vmem_limit_bytes=vmem_mib * MIB
    )


def took(us):
    return pl.CostEstimate(flops=int(us * SCALE * 1e9), bytes_accessed=1000, transcendentals=0)


def spec(shape, index):
    return pl.BlockSpec(shape, index)


def whole(shape):
    zeros = (0,) * len(shape)
    return pl.BlockSpec(shape, lambda *_: zeros)


def rope_tables(length, head):
    half = head // 2
    freq = np.float32(ROPE_BASE) ** (
        -(np.arange(half, dtype=np.float32) * np.float32(2.0) / np.float32(head))
    )
    ang = np.arange(length, dtype=np.float32)[:, None] * freq.astype(np.float32)[None, :]
    ang = ang.astype(np.float32)
    return np.cos(ang).astype(np.float32), np.sin(ang).astype(np.float32)


def lane_half(shape, width):
    return (lax.broadcasted_iota(jnp.int32, shape, 1) % width) < (width // 2)


def rope_lanes(x, cos, sin, first):
    partner = jnp.where(first, pltpu.roll(x, 96, 1), pltpu.roll(x, 32, 1))
    return x * cos + partner * sin


def qkv_kernel(tok_ref, gain_ref, w_ref, cos_ref, sin_ref, ht_ref, q_ref, kd_ref, vd_ref):
    x = tok_ref[...].astype(F32)
    d = x.shape[1]
    r = lax.rsqrt(jnp.mean(x * x, axis=1, keepdims=True) + EPS)
    h = (x * r * gain_ref[...].astype(F32)).astype(BF16)
    ht_ref[...] = h.T
    cos, sin = cos_ref[...], sin_ref[...]
    rows = x.shape[0]
    first = lane_half((rows, 128), 64)
    low = lane_half((rows, 128), 128)
    nq = q_ref.shape[1]
    nk = kd_ref.shape[1] // 2
    q = dot(h, w_ref[:, :nq])
    for c in range(0, nq, 128):
        q_ref[:, c : c + 128] = (rope_lanes(q[:, c : c + 128], cos, sin, first) * 0.125).astype(
            BF16
        )
    k = dot(h, w_ref[:, nq : nq + nk])
    for c in range(0, nk, 128):
        kk = rope_lanes(k[:, c : c + 128], cos, sin, first)
        sw = pltpu.roll(kk, 64, 1)
        kd_ref[:, 2 * c : 2 * c + 128] = jnp.where(low, kk, sw).astype(BF16)
        kd_ref[:, 2 * c + 128 : 2 * c + 256] = jnp.where(low, sw, kk).astype(BF16)
    v = dot(h, w_ref[:, nq + nk : nq + 2 * nk])
    for c in range(0, nk, 128):
        vv = v[:, c : c + 128]
        sw = pltpu.roll(vv, 64, 1)
        vd_ref[:, 2 * c : 2 * c + 128] = jnp.where(low, vv, sw).astype(BF16)
        vd_ref[:, 2 * c + 128 : 2 * c + 256] = jnp.where(low, sw, vv).astype(BF16)


def run_qkv(tok, gain, w_qkv, cos, sin, nq):
    length, d = tok.shape
    b = 256
    row = lambda i: (i, 0)
    return pl.pallas_call(
        qkv_kernel,
        grid=(length // b,),
        in_specs=[
            spec((b, d), row),
            whole((1, d)),
            spec((d, 2 * nq), lambda i: (0, 0)),
            spec((b, 128), row),
            spec((b, 128), row),
        ],
        out_specs=[spec((d, b), lambda i: (0, i))] + [spec((b, nq), row)] * 3,
        out_shape=[jax.ShapeDtypeStruct((d, length), BF16)]
        + [jax.ShapeDtypeStruct((length, nq), BF16)] * 3,
        compiler_params=params(60),
        cost_estimate=took(9),
        name="qkv",
    )(tok, gain, w_qkv, cos, sin)


def mask_bias(prefix, q0, k0, nq, nk, q_axis):
    shape = (nq, nk) if q_axis == 0 else (nk, nq)
    qpos = q0 + lax.broadcasted_iota(jnp.int32, shape, q_axis)
    kpos = k0 + lax.broadcasted_iota(jnp.int32, shape, 1 - q_axis)
    return jnp.where((kpos <= qpos) | (kpos < prefix), 0.0, NEG).astype(F32)


def two_heads(pair, low):
    zero = jnp.zeros_like(pair)
    return jnp.concatenate([jnp.where(low, pair, zero), jnp.where(low, zero, pair)], axis=0)


def attn_fwd_kernel(prefix_ref, q_ref, kd_ref, vd_ref, ctx_ref, lse_ref, peak_ref):
    length = q_ref.shape[0]
    b = 256
    prefix = prefix_ref[0]
    low_b = lane_half((b, 128), 128)
    lane = lax.broadcasted_iota(jnp.int32, (b, 128), 1)
    peak = jnp.full((8, 128), NEG, F32)
    peak_lane = lax.broadcasted_iota(jnp.int32, (8, 128), 1)
    for i in range(length // b):
        nk = max((i + 1) * b, length // 2)
        free = i * b
        bias = mask_bias(prefix, i * b, free, b, nk - free, 0)
        bias = jnp.concatenate([bias, bias], axis=0)
        lse_cols = jnp.zeros((b, 128), F32)
        for j in range(2):
            cols = slice(j * 128, (j + 1) * 128)
            q2 = two_heads(q_ref[i * b : (i + 1) * b, cols], low_b)
            s_hi = dot_t(q2, kd_ref[free:nk, cols]) + bias
            m = jnp.max(s_hi, axis=1, keepdims=True)
            if free:
                s_lo = dot_t(q2, kd_ref[:free, cols])
                m = jnp.maximum(m, jnp.max(s_lo, axis=1, keepdims=True))
            p_hi = jnp.exp(s_hi - m)
            total = jnp.sum(p_hi, axis=1, keepdims=True)
            ctx = dot(p_hi.astype(BF16), vd_ref[free:nk, cols])
            if free:
                p_lo = jnp.exp(s_lo - m)
                total = total + jnp.sum(p_lo, axis=1, keepdims=True)
                ctx = ctx + dot(p_lo.astype(BF16), vd_ref[:free, cols])
            ctx = ctx * (1.0 / total)
            ctx_ref[i * b : (i + 1) * b, cols] = jnp.where(low_b, ctx[:b], ctx[b:]).astype(BF16)
            lse = m + jnp.log(total)
            for g in range(2):
                lse_cols = jnp.where(lane == 2 * j + g, lse[g * b : (g + 1) * b], lse_cols)
                top = jnp.max(m[g * b : (g + 1) * b], axis=0, keepdims=True)
                peak = jnp.where(peak_lane == 2 * j + g, jnp.maximum(peak, top), peak)
        lse_ref[0, :, i * b : (i + 1) * b] = lse_cols.T[:8]
    peak_ref[0] = peak


def run_attn_fwd(prefix, q, kd, vd):
    length, nq = q.shape
    groups = nq // 256
    col = lambda g: (0, g)
    return pl.pallas_call(
        attn_fwd_kernel,
        grid=(groups,),
        in_specs=[pl.BlockSpec(memory_space=pltpu.SMEM)] + [spec((length, 256), col)] * 3,
        out_specs=[
            spec((length, 256), col),
            spec((1, 8, length), lambda g: (g, 0, 0)),
            spec((1, 8, 128), lambda g: (g, 0, 0)),
        ],
        out_shape=[
            jax.ShapeDtypeStruct((length, nq), BF16),
            jax.ShapeDtypeStruct((groups, 8, length), F32),
            jax.ShapeDtypeStruct((groups, 8, 128), F32),
        ],
        compiler_params=params(60),
        cost_estimate=took(21),
        name="attn_fwd",
    )(prefix, q, kd, vd)


def attn_bwd_kernel(
    prefix_ref, q_ref, kd_ref, vd_ref, do_ref, ctx_ref, lse_ref, cos_ref, sin_ref, cost_ref, sint_ref,
    dq_ref, dk_ref, dv_ref, dk_acc, dv_acc, kt_ref,
):
    length = q_ref.shape[0]
    b = 256
    prefix = prefix_ref[0]
    low_b = lane_half((b, 128), 128)
    for j in range(2):
        cols = slice(j * 128, (j + 1) * 128)
        kt_ref[j] = kd_ref[:, cols].T
    dk_acc[...] = jnp.zeros_like(dk_acc)
    dv_acc[...] = jnp.zeros_like(dv_acc)
    for i in range(length // b):
        rows = slice(i * b, (i + 1) * b)
        nk = max((i + 1) * b, length // 2)
        free = i * b
        bias = mask_bias(prefix, i * b, free, b, nk - free, 1)
        bias = jnp.concatenate([bias, bias], axis=1)
        for j in range(2):
            cols = slice(j * 128, (j + 1) * 128)
            do = do_ref[rows, cols]
            q2 = two_heads(q_ref[rows, cols], low_b)
            do2 = two_heads(do, low_b)
            prod = (do.astype(F32) * ctx_ref[rows, cols].astype(F32)).T
            delta = jnp.concatenate(
                [
                    jnp.sum(prod[:64], axis=0, keepdims=True),
                    jnp.sum(prod[64:], axis=0, keepdims=True),
                ],
                axis=1,
            )
            lse = jnp.concatenate(
                [lse_ref[0, 2 * j : 2 * j + 1, rows], lse_ref[0, 2 * j + 1 : 2 * j + 2, rows]],
                axis=1,
            )
            dq_t = None
            parts = [(0, free)] if free else []
            for k0, k1 in parts + [(free, nk)]:
                keys = slice(k0, k1)
                s = dot_t(kd_ref[keys, cols], q2)
                if k0 == free:
                    s = s + bias
                p = jnp.exp(s - lse)
                dp = dot_t(vd_ref[keys, cols], do2)
                ds = (p * (dp - delta)).astype(BF16)
                dv_acc[j, keys, :] += dot(p.astype(BF16), do2)
                dk_acc[j, keys, :] += dot(ds, q2)
                part = dot(kt_ref[j, :, keys], ds)
                dq_t = part if dq_t is None else dq_t + part
            cos_t, sin_t = cost_ref[:, rows], sint_ref[:, rows]
            a0, b0 = dq_t[0:32, :b], dq_t[32:64, :b]
            a1, b1 = dq_t[64:96, b:], dq_t[96:128, b:]
            full = jnp.concatenate(
                [
                    a0 * cos_t + b0 * sin_t,
                    b0 * cos_t - a0 * sin_t,
                    a1 * cos_t + b1 * sin_t,
                    b1 * cos_t - a1 * sin_t,
                ],
                axis=0,
            )
            dq_ref[rows, cols] = (full * 0.125).T.astype(BF16)
    low = lane_half((length, 128), 128)
    first = lane_half((length, 128), 64)
    sums = []
    for acc in (dk_acc, dv_acc):
        even = acc[0] + pltpu.roll(acc[0], 64, 1)
        odd = acc[1] + pltpu.roll(acc[1], 64, 1)
        sums.append(jnp.where(low, even, odd))
    dk_ref[...] = rope_lanes(sums[0], cos_ref[...], -sin_ref[...], first).astype(BF16)
    dv_ref[...] = sums[1].astype(BF16)


def run_attn_bwd(prefix, q, kd, vd, d_ctx, ctx, lse, cos, sin, cos_t, sin_t):
    length, nq = q.shape
    groups = nq // 256
    col = lambda g: (0, g)
    wide = spec((length, 256), col)
    return pl.pallas_call(
        attn_bwd_kernel,
        grid=(groups,),
        in_specs=[pl.BlockSpec(memory_space=pltpu.SMEM)]
        + [wide] * 5
        + [spec((1, 8, length), lambda g: (g, 0, 0))]
        + [whole((length, 128))] * 2
        + [whole((cos_t.shape[0], length))] * 2,
        out_specs=[wide, spec((length, 128), col), spec((length, 128), col)],
        out_shape=[
            jax.ShapeDtypeStruct((length, nq), BF16),
            jax.ShapeDtypeStruct((length, nq // 2), BF16),
            jax.ShapeDtypeStruct((length, nq // 2), BF16),
        ],
        scratch_shapes=[
            pltpu.VMEM((2, length, 128), F32),
            pltpu.VMEM((2, length, 128), F32),
            pltpu.VMEM((2, 128, length), BF16),
        ],
        compiler_params=params(60),
        cost_estimate=took(33),
        name="attn_bwd",
    )(prefix, q, kd, vd, d_ctx, ctx, lse, cos, sin, cos_t, sin_t)


def mid_kernel(tok_ref, ctx_ref, w_ref, gain_ref, res_ref, x_ref):
    res = tok_ref[...].astype(F32) + dot(ctx_ref[...], w_ref[...])
    res_ref[...] = res
    r = lax.rsqrt(jnp.mean(res * res, axis=1, keepdims=True) + EPS)
    x_ref[...] = (res * r * gain_ref[...].astype(F32)).astype(BF16)


def run_mid(tok, ctx, w_out, gain):
    length, d = tok.shape
    b = 256
    row = lambda i: (i, 0)
    return pl.pallas_call(
        mid_kernel,
        grid=(length // b,),
        in_specs=[
            spec((b, d), row),
            spec((b, ctx.shape[1]), row),
            whole(w_out.shape),
            whole((1, d)),
        ],
        out_specs=[spec((b, d), row)] * 2,
        out_shape=[
            jax.ShapeDtypeStruct((length, d), F32),
            jax.ShapeDtypeStruct((length, d), BF16),
        ],
        compiler_params=params(60),
        cost_estimate=took(4),
        name="mid",
    )(tok, ctx, w_out, gain)


def gates_of(x, router, routes_t):
    logits = dot(x, router).T
    expert = lax.broadcasted_iota(jnp.int32, logits.shape, 0)
    hit = expert == routes_t[0:1]
    for k in range(1, routes_t.shape[0]):
        hit = hit | (expert == routes_t[k : k + 1])
    logits = jnp.where(hit, logits, NEG)
    e = jnp.exp(logits - jnp.max(logits, axis=0, keepdims=True))
    e = jnp.where(hit, e, 0.0)
    return e / jnp.sum(e, axis=0, keepdims=True)


def expert_kernel(
    first_expert, local, with_init, me_ref, x_ref, c_ref, route_ref, router_ref, wg_ref, wu_ref, wd_ref, *refs
):
    if with_init:
        out_in, dx_in, dg_in, refs = refs[0], refs[1], refs[2], refs[3:]
        out_ref, dx_ref, dg_ref, hs_ref, dgate_ref, dup_ref, out_acc, dx_acc, gp_ref, dgc_ref = refs
    else:
        out_ref, dx_ref, dg_ref, hs_ref, dgate_ref, dup_ref, xt_ref, ct_ref, out_acc, dx_acc, gp_ref, dgc_ref = refs
    e = pl.program_id(1)
    last = pl.num_programs(1) - 1
    x, c = x_ref[...], c_ref[...]
    b = x.shape[0]
    lane = lax.broadcasted_iota(jnp.int32, (b, 128), 1)

    @pl.when(e == 0)
    def _():
        gp_ref[...] = gates_of(x, router_ref[...], route_ref[...]).T
        dgc_ref[...] = jnp.zeros_like(dgc_ref)
        if with_init:
            out_acc[...] = out_in[...].astype(F32)
            dx_acc[...] = dx_in[...].astype(F32)
        else:
            out_acc[...] = jnp.zeros_like(out_acc)
            dx_acc[...] = jnp.zeros_like(dx_acc)
            xt_ref[...] = x.T
            ct_ref[...] = c.T

    gp = jnp.sum(
        jnp.where(lane == me_ref[0] * local + first_expert + e, gp_ref[...], 0.0),
        axis=1,
        keepdims=True,
    )
    gate = dot(x, wg_ref[e])
    up = dot(x, wu_ref[e])
    grad = dot_t(c, wd_ref[e])
    sig = 0.5 * jnp.tanh(0.5 * gate) + 0.5
    act = gate * sig
    hidden = (act * up).astype(BF16).astype(F32)
    dg = jnp.sum(hidden * grad, axis=1, keepdims=True)
    hs = (hidden * gp).astype(BF16)
    dh = grad * gp
    dup = (dh * act).astype(BF16)
    dgate = (dh * up * (sig + act * (1.0 - sig))).astype(BF16)
    hs_ref[...] = hs
    dup_ref[...] = dup
    dgate_ref[...] = dgate
    out = dot(hs, wd_ref[e])
    dx = dot_t(dgate, wg_ref[e]) + dot_t(dup, wu_ref[e])
    dgc_ref[...] += jnp.where(lane == first_expert + e, dg, 0.0)

    @pl.when(e < last)
    def _():
        out_acc[...] += out
        dx_acc[...] += dx

    @pl.when(e == last)
    def _():
        out_ref[...] = (out_acc[...] + out).astype(BF16)
        dx_ref[...] = (dx_acc[...] + dx).astype(BF16)
        dg_t = dgc_ref[...].T[:8]
        dg_ref[...] = dg_t + dg_in[...] if with_init else dg_t


def run_expert(me, x, c, routes_t, router, wg, wu, wd, first, count, init=None):
    length, d = x.shape
    local, _, ff = wg.shape
    b = 512
    top = routes_t.shape[0]
    row = lambda i, e: (i, 0)
    col_t = lambda i, e: (0, i)
    pick = lambda shape: pl.BlockSpec(
        (count,) + shape[1:],
        lambda i, e: (first // count, 0, 0),
        pipeline_mode=pl.Buffered(1),
    )
    wide = jax.ShapeDtypeStruct((length, count * ff), BF16)
    full = jax.ShapeDtypeStruct((length, d), BF16)
    turned = jax.ShapeDtypeStruct((d, length), BF16)
    wide_spec = spec((b, ff), lambda i, e: (i, e))
    with_init = init is not None
    return pl.pallas_call(
        functools.partial(expert_kernel, first, local, with_init),
        grid=(length // b, count),
        in_specs=[
            pl.BlockSpec(memory_space=pltpu.SMEM),
            spec((b, d), row),
            spec((b, d), row),
            spec((top, b), col_t),
            pl.BlockSpec(router.shape, lambda i, e: (0, 0), pipeline_mode=pl.Buffered(1)),
            pick(wg.shape),
            pick(wu.shape),
            pick(wd.shape),
        ]
        + ([spec((b, d), row)] * 2 + [spec((8, b), col_t)] if with_init else []),
        out_specs=[spec((b, d), row)] * 2
        + [spec((8, b), col_t)]
        + [wide_spec] * 3
        + ([] if with_init else [spec((d, b), col_t)] * 2),
        out_shape=[full, full, jax.ShapeDtypeStruct((8, length), F32), wide, wide, wide]
        + ([] if with_init else [turned, turned]),
        scratch_shapes=[
            pltpu.VMEM((b, d), F32),
            pltpu.VMEM((b, d), F32),
            pltpu.VMEM((b, 128), F32),
            pltpu.VMEM((b, 128), F32),
        ],
        compiler_params=params(60, 2),
        cost_estimate=took(12 * count),
        name="experts",
    )(me, x, c, routes_t, router, wg, wu, wd, *(init if with_init else ()))


def weight_grad_kernel(n, *refs):
    xt, ct, dgate, dup, hs = (refs[k * n : (k + 1) * n] for k in range(5))
    gate_ref, up_ref, down_ref = refs[5 * n :]

    def total(lefts, rights):
        acc = None
        for left, right in zip(lefts, rights):
            part = dot(left[...], right[...])
            acc = part if acc is None else acc + part
        return acc

    down = total(ct, hs).T.astype(BF16)
    gate = total(xt, dgate).astype(BF16)
    up = total(xt, dup).astype(BF16)
    for p in range(down_ref.shape[0]):
        rows = down_ref.shape[3]
        down_ref[p, 0, 0] = down[p * rows : (p + 1) * rows]
    for p in range(gate_ref.shape[0]):
        rows = gate_ref.shape[2]
        gate_ref[p, 0] = gate[p * rows : (p + 1) * rows]
        up_ref[p, 0] = up[p * rows : (p + 1) * rows]


def run_weight_grad(xt, ct, dgate, dup, hs, count, skips, n_dp):
    n = len(xt)
    d, length = xt[0].shape
    ff = hs[-1].shape[1] // count
    m = 256
    left = spec((m, length), lambda e, i: (i, 0))
    rights = [
        spec((length, ff), functools.partial(lambda skip, e, i: (0, e + skip), skip))
        for skip in skips
    ]
    per = d // n_dp
    rows = jax.ShapeDtypeStruct((n_dp, count, per, ff), BF16)
    row_spec = spec((m // per, 1, per, ff), lambda e, i: (i, e, 0, 0))
    return pl.pallas_call(
        functools.partial(weight_grad_kernel, n),
        grid=(count, d // m),
        in_specs=[left] * (2 * n) + rights * 3,
        out_specs=[
            row_spec,
            row_spec,
            spec((n_dp, 1, 1, ff // n_dp, m), lambda e, i: (0, e, i // (ff // m), 0, i % (ff // m))),
        ],
        out_shape=[
            rows,
            rows,
            jax.ShapeDtypeStruct((n_dp, count, d // ff, ff // n_dp, ff), BF16),
        ],
        compiler_params=params(60, 2),
        cost_estimate=took(37),
        name="weight_grad",
    )(*xt, *ct, *dgate, *dup, *hs)


def back_mid_kernel(n, n_ex, local, *refs):
    (me_ref, res_ref, cot_ref, route_ref, x_ref, router_ref, gain_ref, w_ref) = refs[:8]
    dx_refs, dg_refs = refs[8 : 8 + n], refs[8 + n : 8 + n + n_ex]
    dres_ref, dattn_ref, dctx_ref, dlog_ref, ggain_ref = refs[8 + n + n_ex :]
    gp = gates_of(x_ref[...], router_ref[...], route_ref[...])
    parts = [ref[...][:local] for ref in dg_refs]
    owners = []
    for owner in range(n_ex):
        own = jnp.zeros_like(parts[0])
        for step in range(n_ex):
            own = jnp.where((owner ^ step) == me_ref[0], parts[step], own)
        owners.append(own)
    dg = jnp.concatenate(owners, axis=0)
    gp = gp[: dg.shape[0]]
    d_logits = gp * (dg - jnp.sum(gp * dg, axis=0, keepdims=True))
    fill = jnp.zeros((128 - dg.shape[0], dg.shape[1]), F32)
    d_logits = jnp.concatenate([d_logits, fill], axis=0).T.astype(BF16)
    dlog_ref[...] = d_logits
    d_norm = dot_t(d_logits, router_ref[...])
    for ref in dx_refs:
        d_norm = d_norm + ref[...].astype(F32)
    res = res_ref[...]
    r = lax.rsqrt(jnp.mean(res * res, axis=1, keepdims=True) + EPS)
    xr = res * r
    part = jnp.sum(d_norm * xr, axis=0, keepdims=True)

    @pl.when(pl.program_id(0) == 0)
    def _():
        ggain_ref[...] = jnp.zeros_like(ggain_ref)

    ggain_ref[...] += part
    u = d_norm * gain_ref[...].astype(F32)
    d_res = (
        cot_ref[...].astype(F32) + r * u - xr * (r * r) * jnp.mean(u * res, axis=1, keepdims=True)
    )
    dres_ref[...] = d_res
    d_attn = d_res.astype(BF16)
    dattn_ref[...] = d_attn
    dctx_ref[...] = dot_t(d_attn, w_ref[...]).astype(BF16)


def run_back_mid(me, res, cot, routes_t, x, router, gain, w_out, dxs, dgs, local):
    length, d = res.shape
    b = 256
    row = lambda i: (i, 0)
    n, n_ex = len(dxs), len(dgs)
    return pl.pallas_call(
        functools.partial(back_mid_kernel, n, n_ex, local),
        grid=(length // b,),
        in_specs=[
            pl.BlockSpec(memory_space=pltpu.SMEM),
            spec((b, d), row),
            spec((b, d), row),
            spec((routes_t.shape[0], b), lambda i: (0, i)),
            spec((b, d), row),
            whole(router.shape),
            whole((1, d)),
            whole(w_out.shape),
        ]
        + [spec((b, d), row)] * n
        + [spec((8, b), lambda i: (0, i))] * n_ex,
        out_specs=[
            spec((b, d), row),
            spec((b, d), row),
            spec((b, w_out.shape[0]), row),
            spec((b, 128), row),
            whole((1, d)),
        ],
        out_shape=[
            jax.ShapeDtypeStruct((length, d), F32),
            jax.ShapeDtypeStruct((length, d), BF16),
            jax.ShapeDtypeStruct((length, w_out.shape[0]), BF16),
            jax.ShapeDtypeStruct((length, 128), BF16),
            jax.ShapeDtypeStruct((1, d), F32),
        ],
        compiler_params=params(60),
        cost_estimate=took(11),
        name="back_mid",
    )(me, res, cot, routes_t, x, router, gain, w_out, *dxs, *dgs)


def back_in_kernel(dq_ref, dk_ref, dv_ref, w_ref, tok_ref, gain_ref, dres_ref, gt_ref, ggain_ref):
    nq, nk = dq_ref.shape[1], dk_ref.shape[1]
    d_norm = dot_t(dq_ref[...], w_ref[:, :nq])
    d_norm = d_norm + dot_t(dk_ref[...], w_ref[:, nq : nq + nk])
    d_norm = d_norm + dot_t(dv_ref[...], w_ref[:, nq + nk : nq + 2 * nk])
    x = tok_ref[...].astype(F32)
    r = lax.rsqrt(jnp.mean(x * x, axis=1, keepdims=True) + EPS)
    xr = x * r
    part = jnp.sum(d_norm * xr, axis=0, keepdims=True)

    @pl.when(pl.program_id(0) == 0)
    def _():
        ggain_ref[...] = jnp.zeros_like(ggain_ref)

    ggain_ref[...] += part
    u = d_norm * gain_ref[...].astype(F32)
    gt_ref[...] = dres_ref[...] + r * u - xr * (r * r) * jnp.mean(u * x, axis=1, keepdims=True)


def run_back_in(dq, dk, dv, w_qkv, tok, gain, d_res):
    length, d = tok.shape
    b = 256
    row = lambda i: (i, 0)
    nq = dq.shape[1]
    return pl.pallas_call(
        back_in_kernel,
        grid=(length // b,),
        in_specs=[
            spec((b, nq), row),
            spec((b, dk.shape[1]), row),
            spec((b, dv.shape[1]), row),
            spec((d, 2 * nq), lambda i: (0, 0)),
            spec((b, d), row),
            whole((1, d)),
            spec((b, d), row),
        ],
        out_specs=[spec((b, d), row), whole((1, d))],
        out_shape=[jax.ShapeDtypeStruct((length, d), F32), jax.ShapeDtypeStruct((1, d), F32)],
        compiler_params=params(60),
        cost_estimate=took(10),
        name="back_in",
    )(dq, dk, dv, w_qkv, tok, gain, d_res)


def finish_kernel(
    ht_ref, dq_ref, dk_ref, dv_ref, dout_ref, small_ref, out_ref,
    b1, r1, s1, r2, s2, r3, s3, r4, sem_s, sem_r,
):
    dp, ex = lax.axis_index("dp"), lax.axis_index("expert")
    z, x, y, c = dp // 2, dp % 2, ex // 2, ex % 2
    core = [(dp, ex ^ 1)]
    plane = [(dp ^ 1, ex), (dp, ex ^ 2), (dp ^ 1, ex ^ 2)]
    line = [(dp ^ (2 * k), ex) for k in (1, 2, 3)]
    group = [(dp, ex ^ k) for k in (1, 2, 3)]
    barrier = pltpu.get_barrier_semaphore()
    peers = core + plane + line + group[2:]
    for peer in peers:
        pl.semaphore_signal(barrier, inc=1, device_id=peer, device_id_type=pl.DeviceIdType.MESH)
    pl.semaphore_wait(barrier, len(peers))

    n = b1.shape[0]
    widths = [dout_ref.shape[1], dq_ref.shape[1], dk_ref.shape[1] + dv_ref.shape[1], 128]
    starts = [sum(widths[:k]) for k in range(n)]
    started = {}

    def send(k, slot, src, dst, peer):
        copy = pltpu.make_async_remote_copy(
            src_ref=src,
            dst_ref=dst,
            send_sem=sem_s.at[k, slot],
            recv_sem=sem_r.at[k, slot],
            device_id=peer,
            device_id_type=pl.DeviceIdType.MESH,
        )
        copy.start()
        started[k, slot] = copy

    def arrive(k, slots):
        for slot in slots:
            started[k, slot].wait()

    def place(k, lanes, value):
        for p in range(8):
            for e in range(4):
                row = 128 * p + 32 * e
                b1[k, e % 2, e // 2, p % 2, p // 2, :, lanes] = value[row : row + 32]

    def step0(k):
        if k == 0:
            place(k, slice(0, widths[k]), dout_ref[...])
        elif k == 1:
            for col in range(0, widths[1], 512):
                part = dot(ht_ref[...], dq_ref[:, col : col + 512])
                place(k, slice(col, col + 512), part.astype(BF16))
        elif k == 2:
            half = dk_ref.shape[1]
            place(k, slice(0, half), dot(ht_ref[...], dk_ref[...]).astype(BF16))
            place(k, slice(half, 2 * half), dot(ht_ref[...], dv_ref[...]).astype(BF16))
        else:
            place(k, slice(0, 128), small_ref[...])
        w = slice(0, widths[k])
        send(k, 0, b1.at[k, 1 - c, :, :, :, :, w], r1.at[k, :, :, :, :, w], core[0])

    def step1(k):
        arrive(k, [0])
        w = slice(0, widths[k])
        for yy in range(2):
            for xx in range(2):
                for zz in range(4):
                    s1[k, yy, xx, zz, :, w] = (
                        b1[k, c, yy, xx, zz, :, w].astype(F32)
                        + r1[k, yy, xx, zz, :, w].astype(F32)
                    ).astype(BF16)
        for i, (dy, dx) in enumerate([(0, 1), (1, 0), (1, 1)]):
            send(k, 1 + i, s1.at[k, y ^ dy, x ^ dx, :, :, w], r2.at[k, i, :, :, w], plane[i])

    def step2(k):
        arrive(k, [1, 2, 3])
        w = slice(0, widths[k])
        for zz in range(4):
            total = s1[k, y, x, zz, :, w].astype(F32)
            for i in range(3):
                total = total + r2[k, i, zz, :, w].astype(F32)
            s2[k, zz, :, w] = total.astype(BF16)
        for i in range(3):
            send(k, 4 + i, s2.at[k, z ^ (i + 1), :, w], r3.at[k, i, :, w], line[i])

    def step3(k):
        arrive(k, [4, 5, 6])
        w = slice(0, widths[k])
        total = s2[k, z, :, w].astype(F32)
        for i in range(3):
            total = total + r3[k, i, :, w].astype(F32)
        s3[k, :, w] = total.astype(BF16)
        for i in range(3):
            send(k, 7 + i, s3.at[k, :, w], r4.at[k, i, :, w], group[i])

    def step4(k):
        arrive(k, [7, 8, 9])
        w, o = slice(0, widths[k]), slice(starts[k], starts[k] + widths[k])
        out_ref[pl.ds(pl.multiple_of(ex * 32, 32), 32), o] = s3[k, :, w].astype(F32)
        for i in range(3):
            rows = pl.ds(pl.multiple_of((ex ^ (i + 1)) * 32, 32), 32)
            out_ref[rows, o] = r4[k, i, :, w].astype(F32)

    steps = (step0, step1, step2, step3, step4)
    order = [3, 0, 1, 2]
    for turn in range(n + len(steps) - 1):
        for place_in, k in enumerate(order):
            at = turn - place_in
            if 0 <= at < len(steps):
                steps[at](k)


def run_finish(ht, dq, dk, dv, d_out, small):
    d = ht.shape[0]
    n, w = 4, d
    columns = d_out.shape[1] + dq.shape[1] + dk.shape[1] + dv.shape[1] + small.shape[1]
    return pl.pallas_call(
        finish_kernel,
        in_specs=[pl.BlockSpec(memory_space=pltpu.VMEM)] * 6,
        out_specs=pl.BlockSpec(memory_space=pltpu.VMEM),
        out_shape=jax.ShapeDtypeStruct((128, columns), F32),
        scratch_shapes=[
            pltpu.VMEM((n, 2, 2, 2, 4, 32, w), BF16),
            pltpu.VMEM((n, 2, 2, 4, 32, w), BF16),
            pltpu.VMEM((n, 2, 2, 4, 32, w), BF16),
            pltpu.VMEM((n, 3, 4, 32, w), BF16),
            pltpu.VMEM((n, 4, 32, w), BF16),
            pltpu.VMEM((n, 3, 32, w), BF16),
            pltpu.VMEM((n, 32, w), BF16),
            pltpu.VMEM((n, 3, 32, w), BF16),
            pltpu.SemaphoreType.DMA((n, 10)),
            pltpu.SemaphoreType.DMA((n, 10)),
        ],
        compiler_params=pltpu.CompilerParams(
            vmem_limit_bytes=60 * MIB, collective_id=1, has_side_effects=True
        ),
        cost_estimate=took(60),
        name="finish",
    )(ht, dq, dk, dv, d_out, small)


def after(value, *deps):
    return lax.optimization_barrier((value,) + deps)[0]


def on_device(
    n_dp, n_ex, tokens, cotangent, routes, prefix, w_query, keyvalue_weight, w_out, w_router,
    gain_attn, gain_mlp, expert_gate, expert_up, expert_down, query_logit_cap,
):
    length, d = tokens.shape[1], tokens.shape[2]
    tok = tokens.reshape(length, d)
    cot = cotangent.reshape(length, d)
    heads = query_logit_cap.shape[0]
    nq = w_query.shape[1]
    head = nq // heads
    kv_heads = keyvalue_weight.shape[1] // (2 * head)
    num_experts = w_router.shape[1]
    local = expert_gate.shape[0]
    rows = w_query.shape[0]
    ex = lax.axis_index("expert")

    def swap(value, step, axis="expert", n=n_ex):
        return lax.ppermute(value, axis, [(i, i ^ step) for i in range(n)])

    part = rows // n_ex
    small = jnp.concatenate(
        [
            w_router,
            gain_attn[:, None],
            gain_mlp[:, None],
            jnp.zeros((rows, 128 - num_experts - 2), BF16),
        ],
        axis=1,
    )
    packed = jnp.concatenate([w_query, keyvalue_weight, w_out, small], axis=1)
    mine = lax.dynamic_slice_in_dim(packed, ex * part, part, axis=0)
    every = lax.all_gather(mine, ("dp", "expert"), axis=0, tiled=True)
    w_all = every
    width = 2 * nq
    full_out = every[:, width : width + d]
    extra = every[:, width + d :]
    lanes = lax.broadcasted_iota(jnp.int32, extra.shape, 1)
    router = jnp.where(lanes < num_experts, extra, jnp.zeros((), BF16))
    gain_one = extra[:, num_experts].reshape(1, d)
    gain_two = extra[:, num_experts + 1].reshape(1, d)

    routes_t = routes.reshape(length, -1).T
    cots = {0: cot}
    route_set = {0: routes_t}
    for step in range(1, n_ex):
        route_set[step] = swap(routes_t, step)
    cot_late = after(cot, every, *route_set.values())
    for step in range(1, n_ex):
        if step == 1 or step % 2 == 0:
            cots[step] = swap(cot_late, step)

    cos_np, sin_np = rope_tables(length, head)
    cos_l = jnp.asarray(np.concatenate([cos_np] * 4, axis=1))
    sin_l = jnp.asarray(np.concatenate([-sin_np, sin_np] * 2, axis=1))
    cos_t = jnp.asarray(np.ascontiguousarray(cos_np.T))
    sin_t = jnp.asarray(np.ascontiguousarray(sin_np.T))

    normed_one_t, q, kd, vd = run_qkv(tok, gain_one, w_all, cos_l, sin_l, nq)
    ctx, lse, peaks = run_attn_fwd(prefix, q, kd, vd)
    for step in range(3, n_ex, 2):
        cots[step] = swap(after(cots[step - 1], ctx), 1)
    resid, normed_two = run_mid(tok, after(ctx, *cots.values()), full_out, gain_two)

    me = ex.reshape(1).astype(jnp.int32)
    xs = {0: normed_two}
    for step in range(1, n_ex):
        if step == 1 or step % 2 == 0:
            xs[step] = swap(normed_two, step)
        else:
            xs[step] = swap(xs[step - 1], 1)
    tops = [peaks[:, :, :4]]
    bits = [("expert", n_ex, 1 << i) for i in range(n_ex.bit_length() - 1)]
    bits += [("dp", n_dp, 1 << i) for i in range(n_dp.bit_length() - 1)]

    def widen_top():
        if len(tops) <= len(bits):
            axis, n, step = bits[len(tops) - 1]
            top = after(tops[-1], chain)
            tops.append(jnp.maximum(top, swap(top, step, axis, n)))

    weights = (expert_gate, expert_up, expert_down)
    half = local // 2

    def scatter(made):
        if n_dp != 8:
            done = [
                lax.psum_scatter(g, "dp", scatter_dimension=0, tiled=True)[0].astype(F32)
                for g in made
            ]
            for _ in range(4):
                yield made[0]
            yield done
            return
        at = lax.axis_index("dp")
        z, x = at // 2, at % 2

        def side(which):
            return jnp.concatenate(
                [
                    lax.dynamic_index_in_dim(
                        g.reshape(4, 2, -1, ff_lanes), which, axis=1, keepdims=False
                    )
                    for g in made
                ],
                axis=1,
            )

        sent = side(1 - x)
        yield sent
        got = lax.ppermute(sent, "dp", [(i, i ^ 1) for i in range(8)])
        total = (side(x).astype(F32) + got.astype(F32)).astype(BF16)
        upper = z // 2
        far = lax.dynamic_slice_in_dim(total, 2 * (1 - upper), 2, axis=0)
        near = lax.dynamic_slice_in_dim(total, 2 * upper, 2, axis=0)
        yield far
        got = lax.ppermute(far, "dp", [(0, 2), (1, 3), (6, 4), (7, 5)])
        far = (far.astype(F32) + got.astype(F32)).astype(BF16)
        yield far
        got = lax.ppermute(far, "dp", [(2, 4), (3, 5), (4, 2), (5, 3)])
        near = (near.astype(F32) + got.astype(F32)).astype(BF16)
        yield near
        got = lax.ppermute(
            lax.dynamic_index_in_dim(near, 1 - z % 2, axis=0, keepdims=False),
            "dp",
            [(i, i ^ 2) for i in range(8)],
        )
        own = lax.dynamic_index_in_dim(near, z % 2, axis=0, keepdims=False)
        own = own.astype(F32) + got.astype(F32)
        done, begin = [], 0
        for g in made:
            size = g.size // (8 * ff_lanes)
            done.append(own[begin : begin + size].reshape(g.shape[1:]))
            begin += size
        yield done

    ff_lanes = expert_gate.shape[2]
    res = {}
    chain = xs[1]

    def experts(step, first, count, init=None):
        x = after(xs[step], chain)
        return run_expert(
            me, x, cots[step], route_set[step], router, *weights, first, count, init
        )

    def grads(first):
        skips = [first if step < 2 else 0 for step in range(n_ex)]
        pieces = [
            [res[step, 0 if step < 2 else first][k] for step in range(n_ex)] for k in (4, 5, 3)
        ]
        turned = [[res[step, 0][k] for step in range(n_ex)] for k in (6, 7)]
        turned[0][0] = after(turned[0][0], chain)
        made = None
        for at in range(0, n_ex, 4):
            some = [group[at : at + 4] for group in turned + pieces]
            part = run_weight_grad(*some, half, skips[at : at + 4], n_dp)
            if made is None:
                made = part
            else:
                made = [(a.astype(F32) + b.astype(F32)).astype(BF16) for a, b in zip(made, part)]
        return made

    for step in range(2):
        res[step, 0] = experts(step, 0, local)
        chain = res[step, 0][0]
    odd, even = range(3, n_ex, 2), range(2, n_ex, 2)
    for step in odd:
        res[step, 0] = experts(step, 0, half)
        chain = res[step, 0][0]
        res[step, half] = experts(step, half, half, res[step, 0][:3])
        chain = (res[step, half][0], tops[-1])
        widen_top()
    partner = {step - 1: [swap(res[step, half][k], 1) for k in (0, 1)] for step in odd}
    for step in even:
        res[step, 0] = experts(step, 0, half)
        chain = (res[step, 0][0], tops[-1])
        widen_top()
    made = grads(0)
    one = scatter(made)
    chain = (next(one), tops[-1])
    widen_top()
    for step in even:
        init = [
            (a.astype(F32) + b.astype(F32)).astype(BF16)
            for a, b in zip(res[step, 0][:2], partner[step])
        ]
        res[step, half] = experts(step, half, half, init + [res[step, 0][2]])
        chain = (res[step, half][0], tops[-1])
        widen_top()
    made = grads(half)
    two = scatter(made)
    chain = (next(two), next(one), tops[-1])
    while len(tops) <= len(bits):
        widen_top()
    top = tops[-1]

    last = [res[step, 0 if step < 2 else half] for step in range(n_ex)]
    dxs = [last[0][1], swap(last[1][1], 1)] + [swap(last[step][1], step) for step in even]
    dgs = [last[0][2]] + [swap(last[step][2], step) for step in range(1, n_ex)]
    d_res, d_attn, d_ctx, d_logits, d_gain_two = run_back_mid(
        me,
        after(resid, chain),
        cot,
        routes_t,
        normed_two,
        router,
        gain_two,
        full_out,
        dxs,
        dgs,
        local,
    )
    outs = [last[0][0], swap(last[1][0], 1)]
    outs += [swap(after(last[step][0], dxs), step) for step in even]
    block = resid
    for piece in outs:
        block = block + piece.astype(F32)
    block_out = block.astype(BF16).reshape(tokens.shape)

    d_out_w = jnp.einsum("rc,rd->cd", ctx, d_attn, preferred_element_type=F32).astype(BF16)
    d_router_w = jnp.einsum("rd,re->de", normed_two, d_logits, preferred_element_type=F32)

    dq, dk, dv = run_attn_bwd(
        prefix, after(q, next(one), top), kd, vd, d_ctx, ctx, lse, cos_l, sin_l, cos_t, sin_t
    )
    grad_tok, d_gain_one = run_back_in(
        after(dq, next(two), next(one), block_out), dk, dv, w_all, tok, gain_one, d_res
    )
    small_grad = jnp.concatenate(
        [
            d_router_w[:, :num_experts].astype(BF16),
            d_gain_one.reshape(d, 1).astype(BF16),
            d_gain_two.reshape(d, 1).astype(BF16),
            jnp.zeros((d, 128 - num_experts - 2), BF16),
        ],
        axis=1,
    )

    def reduce_all(value, order):
        shape = (n_dp, n_ex, value.shape[0] // (n_dp * n_ex), value.shape[1])
        names = []
        dims = []
        for axis, n in (("dp", n_dp), ("expert", n_ex)):
            count = n.bit_length() - 1
            names += [(axis, n, 1 << (count - 1 - i)) for i in range(count)]
            dims += [2] * count
        value = value.reshape(*dims, *shape[2:])
        for bit in order:
            at = names.index(bit)
            axis, n, step = bit
            mine = (lax.axis_index(axis) // step) % 2
            keep = lax.dynamic_slice_in_dim(value, mine, 1, axis=at)
            send = lax.dynamic_slice_in_dim(value, 1 - mine, 1, axis=at)
            value = (keep.astype(F32) + swap(send, step, axis, n).astype(F32)).astype(BF16)
        return value.reshape(shape[2:])

    def share(value):
        return lax.all_gather(value, "expert", axis=0, tiled=True).astype(F32)

    core = [("expert", n_ex, 1)]
    y_bits = [("expert", n_ex, 1 << i) for i in range(1, n_ex.bit_length() - 1)][::-1]
    dp_bits = [("dp", n_dp, 1 << i) for i in range(n_dp.bit_length() - 1)]
    next(two), next(two)
    ends = [next(one), next(two)]
    grad_gate, grad_up, grad_down = (
        jnp.concatenate([ends[0][k], ends[1][k]], axis=0) for k in range(3)
    )
    grad_down = jnp.swapaxes(grad_down, 1, 2).reshape(local, -1, d)

    if n_dp == 8 and n_ex == 4 and d == 1024:
        every_grad = run_finish(normed_one_t, dq, dk, dv, d_out_w, small_grad)
    else:

        def product(right):
            return jnp.dot(normed_one_t, right, preferred_element_type=F32).astype(BF16)

        every_grad = jnp.concatenate(
            [d_out_w, product(dq), product(dk), product(dv), small_grad], axis=1
        )
        every_grad = share(reduce_all(every_grad, core + y_bits + dp_bits[::-1]))
    grad_out = every_grad[:, :d]
    grad_query = every_grad[:, d : d + nq]
    grad_keyval = every_grad[:, d + nq : d + 2 * nq]
    grad_router = every_grad[:, d + 2 * nq : d + 2 * nq + num_experts]
    grad_gain_one = every_grad[:, d + 2 * nq + num_experts]
    grad_gain_two = every_grad[:, d + 2 * nq + num_experts + 1]

    head_logit_peak = top[:, 0, :].reshape(heads)
    per_group = heads // kv_heads
    query_factor = jnp.sqrt(query_logit_cap / jnp.maximum(head_logit_peak, query_logit_cap))
    pair_peak = jnp.max(head_logit_peak.reshape(kv_heads, per_group), axis=1)
    pair_cap = jnp.min(query_logit_cap.reshape(kv_heads, per_group), axis=1)
    key_factor = jnp.sqrt(pair_cap / jnp.maximum(pair_peak, pair_cap))
    clipped_query = (w_query.astype(F32) * jnp.repeat(query_factor, head)[None, :]).astype(BF16)
    key_cols = jnp.concatenate(
        [jnp.repeat(key_factor, head), jnp.ones((kv_heads * head,), F32)]
    )
    clipped_keyval = (keyvalue_weight.astype(F32) * key_cols[None, :]).astype(BF16)
    return (
        block_out,
        grad_tok.reshape(tokens.shape),
        grad_query,
        grad_keyval,
        grad_out,
        grad_router,
        grad_gain_one,
        grad_gain_two,
        grad_gate,
        grad_up,
        grad_down,
        clipped_query,
        clipped_keyval,
        head_logit_peak,
    )


def solution(mesh):
    rows3 = P(("dp", "expert"), None, None)
    in_specs = (
        rows3,
        rows3,
        rows3,
        P(("dp", "expert")),
        P("dp", None),
        P("dp", None),
        P("dp", None),
        P("dp", None),
        P("dp"),
        P("dp"),
        P("expert", None, None),
        P("expert", None, None),
        P("expert", None, None),
        P(),
    )
    out_specs = (
        rows3,
        rows3,
        P("dp", None),
        P("dp", None),
        P("dp", None),
        P("dp", None),
        P("dp"),
        P("dp"),
        P("expert", "dp", None),
        P("expert", "dp", None),
        P("expert", "dp", None),
        P("dp", None),
        P("dp", None),
        P(),
    )
    return jax.shard_map(
        functools.partial(on_device, mesh.shape["dp"], mesh.shape["expert"]),
        mesh=mesh,
        in_specs=in_specs,
        out_specs=out_specs,
        check_vma=False,
    )
```

```python
import functools

import jax
import jax.numpy as jnp
import numpy as np
from jax import lax
from jax.experimental import pallas as pl
from jax.experimental.pallas import tpu as pltpu
from jax.sharding import PartitionSpec as P

EPS = 1e-05
ROPE_BASE = 10000.0
F32 = jnp.float32
BF16 = jnp.bfloat16
NEG = -1e30
MIB = 1 << 20
SCALE = 0.5


def dot(a, b):
    return lax.dot_general(a, b, (((1,), (0,)), ((), ())), preferred_element_type=F32)


def dot_t(a, b):
    return lax.dot_general(a, b, (((1,), (1,)), ((), ())), preferred_element_type=F32)


def params(vmem_mib, n=1):
    return pltpu.CompilerParams(
        dimension_semantics=("arbitrary",) * n, vmem_limit_bytes=vmem_mib * MIB
    )


def took(us):
    return pl.CostEstimate(flops=int(us * SCALE * 1e9), bytes_accessed=1000, transcendentals=0)


def spec(shape, index):
    return pl.BlockSpec(shape, index)


def whole(shape):
    zeros = (0,) * len(shape)
    return pl.BlockSpec(shape, lambda *_: zeros)


def rope_tables(length, head):
    half = head // 2
    freq = np.float32(ROPE_BASE) ** (
        -(np.arange(half, dtype=np.float32) * np.float32(2.0) / np.float32(head))
    )
    ang = np.arange(length, dtype=np.float32)[:, None] * freq.astype(np.float32)[None, :]
    ang = ang.astype(np.float32)
    return np.cos(ang).astype(np.float32), np.sin(ang).astype(np.float32)


def lane_half(shape, width):
    return (lax.broadcasted_iota(jnp.int32, shape, 1) % width) < (width // 2)


def rope_lanes(x, cos, sin, first):
    partner = jnp.where(first, pltpu.roll(x, 96, 1), pltpu.roll(x, 32, 1))
    return x * cos + partner * sin


def qkv_kernel(tok_ref, gain_ref, w_ref, cos_ref, sin_ref, ht_ref, q_ref, kd_ref, vd_ref):
    x = tok_ref[...].astype(F32)
    d = x.shape[1]
    r = lax.rsqrt(jnp.mean(x * x, axis=1, keepdims=True) + EPS)
    h = (x * r * gain_ref[...].astype(F32)).astype(BF16)
    ht_ref[...] = h.T
    cos, sin = cos_ref[...], sin_ref[...]
    rows = x.shape[0]
    first = lane_half((rows, 128), 64)
    low = lane_half((rows, 128), 128)
    nq = q_ref.shape[1]
    nk = kd_ref.shape[1] // 2
    q = dot(h, w_ref[:, :nq])
    for c in range(0, nq, 128):
        q_ref[:, c : c + 128] = (rope_lanes(q[:, c : c + 128], cos, sin, first) * 0.125).astype(
            BF16
        )
    k = dot(h, w_ref[:, nq : nq + nk])
    for c in range(0, nk, 128):
        kk = rope_lanes(k[:, c : c + 128], cos, sin, first)
        sw = pltpu.roll(kk, 64, 1)
        kd_ref[:, 2 * c : 2 * c + 128] = jnp.where(low, kk, sw).astype(BF16)
        kd_ref[:, 2 * c + 128 : 2 * c + 256] = jnp.where(low, sw, kk).astype(BF16)
    v = dot(h, w_ref[:, nq + nk : nq + 2 * nk])
    for c in range(0, nk, 128):
        vv = v[:, c : c + 128]
        sw = pltpu.roll(vv, 64, 1)
        vd_ref[:, 2 * c : 2 * c + 128] = jnp.where(low, vv, sw).astype(BF16)
        vd_ref[:, 2 * c + 128 : 2 * c + 256] = jnp.where(low, sw, vv).astype(BF16)


def run_qkv(tok, gain, w_qkv, cos, sin, nq):
    length, d = tok.shape
    b = 256
    row = lambda i: (i, 0)
    return pl.pallas_call(
        qkv_kernel,
        grid=(length // b,),
        in_specs=[
            spec((b, d), row),
            whole((1, d)),
            spec((d, 2 * nq), lambda i: (0, 0)),
            spec((b, 128), row),
            spec((b, 128), row),
        ],
        out_specs=[spec((d, b), lambda i: (0, i))] + [spec((b, nq), row)] * 3,
        out_shape=[jax.ShapeDtypeStruct((d, length), BF16)]
        + [jax.ShapeDtypeStruct((length, nq), BF16)] * 3,
        compiler_params=params(60),
        cost_estimate=took(9),
        name="qkv",
    )(tok, gain, w_qkv, cos, sin)


def mask_bias(prefix, q0, k0, nq, nk, q_axis):
    shape = (nq, nk) if q_axis == 0 else (nk, nq)
    qpos = q0 + lax.broadcasted_iota(jnp.int32, shape, q_axis)
    kpos = k0 + lax.broadcasted_iota(jnp.int32, shape, 1 - q_axis)
    return jnp.where((kpos <= qpos) | (kpos < prefix), 0.0, NEG).astype(F32)


def two_heads(pair, low):
    zero = jnp.zeros_like(pair)
    return jnp.concatenate([jnp.where(low, pair, zero), jnp.where(low, zero, pair)], axis=0)


def attn_fwd_kernel(prefix_ref, q_ref, kd_ref, vd_ref, ctx_ref, lse_ref, peak_ref):
    length = q_ref.shape[0]
    b = 256
    prefix = prefix_ref[0]
    low_b = lane_half((b, 128), 128)
    lane = lax.broadcasted_iota(jnp.int32, (b, 128), 1)
    peak = jnp.full((8, 128), NEG, F32)
    peak_lane = lax.broadcasted_iota(jnp.int32, (8, 128), 1)
    for i in range(length // b):
        nk = max((i + 1) * b, length // 2)
        free = i * b
        bias = mask_bias(prefix, i * b, free, b, nk - free, 0)
        bias = jnp.concatenate([bias, bias], axis=0)
        lse_cols = jnp.zeros((b, 128), F32)
        for j in range(2):
            cols = slice(j * 128, (j + 1) * 128)
            q2 = two_heads(q_ref[i * b : (i + 1) * b, cols], low_b)
            s_hi = dot_t(q2, kd_ref[free:nk, cols]) + bias
            m = jnp.max(s_hi, axis=1, keepdims=True)
            if free:
                s_lo = dot_t(q2, kd_ref[:free, cols])
                m = jnp.maximum(m, jnp.max(s_lo, axis=1, keepdims=True))
            p_hi = jnp.exp(s_hi - m)
            total = jnp.sum(p_hi, axis=1, keepdims=True)
            ctx = dot(p_hi.astype(BF16), vd_ref[free:nk, cols])
            if free:
                p_lo = jnp.exp(s_lo - m)
                total = total + jnp.sum(p_lo, axis=1, keepdims=True)
                ctx = ctx + dot(p_lo.astype(BF16), vd_ref[:free, cols])
            ctx = ctx * (1.0 / total)
            ctx_ref[i * b : (i + 1) * b, cols] = jnp.where(low_b, ctx[:b], ctx[b:]).astype(BF16)
            lse = m + jnp.log(total)
            for g in range(2):
                lse_cols = jnp.where(lane == 2 * j + g, lse[g * b : (g + 1) * b], lse_cols)
                top = jnp.max(m[g * b : (g + 1) * b], axis=0, keepdims=True)
                peak = jnp.where(peak_lane == 2 * j + g, jnp.maximum(peak, top), peak)
        lse_ref[0, :, i * b : (i + 1) * b] = lse_cols.T[:8]
    peak_ref[0] = peak


def run_attn_fwd(prefix, q, kd, vd):
    length, nq = q.shape
    groups = nq // 256
    col = lambda g: (0, g)
    return pl.pallas_call(
        attn_fwd_kernel,
        grid=(groups,),
        in_specs=[pl.BlockSpec(memory_space=pltpu.SMEM)] + [spec((length, 256), col)] * 3,
        out_specs=[
            spec((length, 256), col),
            spec((1, 8, length), lambda g: (g, 0, 0)),
            spec((1, 8, 128), lambda g: (g, 0, 0)),
        ],
        out_shape=[
            jax.ShapeDtypeStruct((length, nq), BF16),
            jax.ShapeDtypeStruct((groups, 8, length), F32),
            jax.ShapeDtypeStruct((groups, 8, 128), F32),
        ],
        compiler_params=params(60),
        cost_estimate=took(21),
        name="attn_fwd",
    )(prefix, q, kd, vd)


def attn_bwd_kernel(
    prefix_ref, q_ref, kd_ref, vd_ref, do_ref, ctx_ref, lse_ref, cos_ref, sin_ref, cost_ref, sint_ref,
    dq_ref, dk_ref, dv_ref, dk_acc, dv_acc, kt_ref,
):
    length = q_ref.shape[0]
    b = 256
    prefix = prefix_ref[0]
    low_b = lane_half((b, 128), 128)
    for j in range(2):
        cols = slice(j * 128, (j + 1) * 128)
        kt_ref[j] = kd_ref[:, cols].T
    dk_acc[...] = jnp.zeros_like(dk_acc)
    dv_acc[...] = jnp.zeros_like(dv_acc)
    for i in range(length // b):
        rows = slice(i * b, (i + 1) * b)
        nk = max((i + 1) * b, length // 2)
        free = i * b
        bias = mask_bias(prefix, i * b, free, b, nk - free, 1)
        bias = jnp.concatenate([bias, bias], axis=1)
        for j in range(2):
            cols = slice(j * 128, (j + 1) * 128)
            do = do_ref[rows, cols]
            q2 = two_heads(q_ref[rows, cols], low_b)
            do2 = two_heads(do, low_b)
            prod = (do.astype(F32) * ctx_ref[rows, cols].astype(F32)).T
            delta = jnp.concatenate(
                [
                    jnp.sum(prod[:64], axis=0, keepdims=True),
                    jnp.sum(prod[64:], axis=0, keepdims=True),
                ],
                axis=1,
            )
            lse = jnp.concatenate(
                [lse_ref[0, 2 * j : 2 * j + 1, rows], lse_ref[0, 2 * j + 1 : 2 * j + 2, rows]],
                axis=1,
            )
            dq_t = None
            parts = [(0, free)] if free else []
            for k0, k1 in parts + [(free, nk)]:
                keys = slice(k0, k1)
                s = dot_t(kd_ref[keys, cols], q2)
                if k0 == free:
                    s = s + bias
                p = jnp.exp(s - lse)
                dp = dot_t(vd_ref[keys, cols], do2)
                ds = (p * (dp - delta)).astype(BF16)
                dv_acc[j, keys, :] += dot(p.astype(BF16), do2)
                dk_acc[j, keys, :] += dot(ds, q2)
                part = dot(kt_ref[j, :, keys], ds)
                dq_t = part if dq_t is None else dq_t + part
            cos_t, sin_t = cost_ref[:, rows], sint_ref[:, rows]
            a0, b0 = dq_t[0:32, :b], dq_t[32:64, :b]
            a1, b1 = dq_t[64:96, b:], dq_t[96:128, b:]
            full = jnp.concatenate(
                [
                    a0 * cos_t + b0 * sin_t,
                    b0 * cos_t - a0 * sin_t,
                    a1 * cos_t + b1 * sin_t,
                    b1 * cos_t - a1 * sin_t,
                ],
                axis=0,
            )
            dq_ref[rows, cols] = (full * 0.125).T.astype(BF16)
    low = lane_half((length, 128), 128)
    first = lane_half((length, 128), 64)
    sums = []
    for acc in (dk_acc, dv_acc):
        even = acc[0] + pltpu.roll(acc[0], 64, 1)
        odd = acc[1] + pltpu.roll(acc[1], 64, 1)
        sums.append(jnp.where(low, even, odd))
    dk_ref[...] = rope_lanes(sums[0], cos_ref[...], -sin_ref[...], first).astype(BF16)
    dv_ref[...] = sums[1].astype(BF16)


def run_attn_bwd(prefix, q, kd, vd, d_ctx, ctx, lse, cos, sin, cos_t, sin_t):
    length, nq = q.shape
    groups = nq // 256
    col = lambda g: (0, g)
    wide = spec((length, 256), col)
    return pl.pallas_call(
        attn_bwd_kernel,
        grid=(groups,),
        in_specs=[pl.BlockSpec(memory_space=pltpu.SMEM)]
        + [wide] * 5
        + [spec((1, 8, length), lambda g: (g, 0, 0))]
        + [whole((length, 128))] * 2
        + [whole((cos_t.shape[0], length))] * 2,
        out_specs=[wide, spec((length, 128), col), spec((length, 128), col)],
        out_shape=[
            jax.ShapeDtypeStruct((length, nq), BF16),
            jax.ShapeDtypeStruct((length, nq // 2), BF16),
            jax.ShapeDtypeStruct((length, nq // 2), BF16),
        ],
        scratch_shapes=[
            pltpu.VMEM((2, length, 128), F32),
            pltpu.VMEM((2, length, 128), F32),
            pltpu.VMEM((2, 128, length), BF16),
        ],
        compiler_params=params(60),
        cost_estimate=took(33),
        name="attn_bwd",
    )(prefix, q, kd, vd, d_ctx, ctx, lse, cos, sin, cos_t, sin_t)


def mid_kernel(tok_ref, ctx_ref, w_ref, gain_ref, res_ref, x_ref):
    res = tok_ref[...].astype(F32) + dot(ctx_ref[...], w_ref[...])
    res_ref[...] = res
    r = lax.rsqrt(jnp.mean(res * res, axis=1, keepdims=True) + EPS)
    x_ref[...] = (res * r * gain_ref[...].astype(F32)).astype(BF16)


def run_mid(tok, ctx, w_out, gain):
    length, d = tok.shape
    b = 256
    row = lambda i: (i, 0)
    return pl.pallas_call(
        mid_kernel,
        grid=(length // b,),
        in_specs=[
            spec((b, d), row),
            spec((b, ctx.shape[1]), row),
            whole(w_out.shape),
            whole((1, d)),
        ],
        out_specs=[spec((b, d), row)] * 2,
        out_shape=[
            jax.ShapeDtypeStruct((length, d), F32),
            jax.ShapeDtypeStruct((length, d), BF16),
        ],
        compiler_params=params(60),
        cost_estimate=took(4),
        name="mid",
    )(tok, ctx, w_out, gain)


def gates_of(x, router, routes_t, num_experts):
    logits = dot(x, router).T[: 16 * pl.cdiv(num_experts, 16)]
    expert = lax.broadcasted_iota(jnp.int32, logits.shape, 0)
    hit = expert == routes_t[0:1]
    for k in range(1, routes_t.shape[0]):
        hit = hit | (expert == routes_t[k : k + 1])
    logits = jnp.where(hit, logits, NEG)
    e = jnp.exp(logits - jnp.max(logits, axis=0, keepdims=True))
    e = jnp.where(hit, e, 0.0)
    return e / jnp.sum(e, axis=0, keepdims=True)


def expert_kernel(
    first_expert, local, num_experts, with_init, me_ref, x_ref, c_ref, route_ref, router_ref, wg_ref, wu_ref, wd_ref, *refs
):
    if with_init:
        out_in, dx_in, dg_in, refs = refs[0], refs[1], refs[2], refs[3:]
        out_ref, dx_ref, dg_ref, hs_ref, dgate_ref, dup_ref, out_acc, dx_acc, gp_ref, dgc_ref = refs
    else:
        out_ref, dx_ref, dg_ref, hs_ref, dgate_ref, dup_ref, xt_ref, ct_ref, out_acc, dx_acc, gp_ref, dgc_ref = refs
    e = pl.program_id(1)
    last = pl.num_programs(1) - 1
    x, c = x_ref[...], c_ref[...]
    b = x.shape[0]
    lane = lax.broadcasted_iota(jnp.int32, (b, 128), 1)

    @pl.when(e == 0)
    def _():
        gates = gates_of(x, router_ref[...], route_ref[...], num_experts)
        fill = jnp.zeros((128 - gates.shape[0], b), F32)
        gp_ref[...] = jnp.concatenate([gates, fill], axis=0).T
        dgc_ref[...] = jnp.zeros_like(dgc_ref)
        if with_init:
            out_acc[...] = out_in[...].astype(F32)
            dx_acc[...] = dx_in[...].astype(F32)
        else:
            out_acc[...] = jnp.zeros_like(out_acc)
            dx_acc[...] = jnp.zeros_like(dx_acc)
            xt_ref[...] = x.T
            ct_ref[...] = c.T

    gp = jnp.sum(
        jnp.where(lane == me_ref[0] * local + first_expert + e, gp_ref[...], 0.0),
        axis=1,
        keepdims=True,
    )
    gate = dot(x, wg_ref[e])
    up = dot(x, wu_ref[e])
    grad = dot_t(c, wd_ref[e])
    sig = 0.5 * jnp.tanh(0.5 * gate) + 0.5
    act = gate * sig
    hidden = (act * up).astype(BF16).astype(F32)
    dg = jnp.sum(hidden * grad, axis=1, keepdims=True)
    hs = (hidden * gp).astype(BF16)
    dh = grad * gp
    dup = (dh * act).astype(BF16)
    dgate = (dh * up * (sig + act * (1.0 - sig))).astype(BF16)
    hs_ref[...] = hs
    dup_ref[...] = dup
    dgate_ref[...] = dgate
    out = dot(hs, wd_ref[e])
    dx = dot_t(dgate, wg_ref[e]) + dot_t(dup, wu_ref[e])
    dgc_ref[...] += jnp.where(lane == first_expert + e, dg, 0.0)

    @pl.when(e < last)
    def _():
        out_acc[...] += out
        dx_acc[...] += dx

    @pl.when(e == last)
    def _():
        out_ref[...] = (out_acc[...] + out).astype(BF16)
        dx_ref[...] = (dx_acc[...] + dx).astype(BF16)
        dg_t = dgc_ref[...].T[:8]
        dg_ref[...] = dg_t + dg_in[...] if with_init else dg_t


def run_expert(me, x, c, routes_t, router, wg, wu, wd, first, count, num_experts, init=None):
    length, d = x.shape
    local, _, ff = wg.shape
    b = 512
    top = routes_t.shape[0]
    row = lambda i, e: (i, 0)
    col_t = lambda i, e: (0, i)
    pick = lambda shape: pl.BlockSpec(
        (count,) + shape[1:],
        lambda i, e: (first // count, 0, 0),
        pipeline_mode=pl.Buffered(1),
    )
    wide = jax.ShapeDtypeStruct((length, count * ff), BF16)
    full = jax.ShapeDtypeStruct((length, d), BF16)
    turned = jax.ShapeDtypeStruct((d, length), BF16)
    wide_spec = spec((b, ff), lambda i, e: (i, e))
    with_init = init is not None
    return pl.pallas_call(
        functools.partial(expert_kernel, first, local, num_experts, with_init),
        grid=(length // b, count),
        in_specs=[
            pl.BlockSpec(memory_space=pltpu.SMEM),
            spec((b, d), row),
            spec((b, d), row),
            spec((top, b), col_t),
            pl.BlockSpec(router.shape, lambda i, e: (0, 0), pipeline_mode=pl.Buffered(1)),
            pick(wg.shape),
            pick(wu.shape),
            pick(wd.shape),
        ]
        + ([spec((b, d), row)] * 2 + [spec((8, b), col_t)] if with_init else []),
        out_specs=[spec((b, d), row)] * 2
        + [spec((8, b), col_t)]
        + [wide_spec] * 3
        + ([] if with_init else [spec((d, b), col_t)] * 2),
        out_shape=[full, full, jax.ShapeDtypeStruct((8, length), F32), wide, wide, wide]
        + ([] if with_init else [turned, turned]),
        scratch_shapes=[
            pltpu.VMEM((b, d), F32),
            pltpu.VMEM((b, d), F32),
            pltpu.VMEM((b, 128), F32),
            pltpu.VMEM((b, 128), F32),
        ],
        compiler_params=params(60, 2),
        cost_estimate=took(12 * count),
        name="experts",
    )(me, x, c, routes_t, router, wg, wu, wd, *(init if with_init else ()))


def weight_grad_kernel(n, paired, dp_ref, *refs):
    xt, ct, dgate, dup, hs = (refs[k * n : (k + 1) * n] for k in range(5))

    def total(lefts, rights):
        acc = None
        for left, right in zip(lefts, rights):
            part = dot(left[...], right[...])
            acc = part if acc is None else acc + part
        return acc

    down = total(ct, hs).T.astype(BF16)
    gate = total(xt, dgate).astype(BF16)
    up = total(xt, dup).astype(BF16)
    if paired:
        keep_ref, send_ref, down_keep_ref, down_send_ref = refs[5 * n :]
        first = dp_ref[0] % 2 == 0
        half = gate.shape[0] // 2
        for k, value in enumerate((gate, up)):
            keep_ref[0, k, 0] = jnp.where(first, value[:half], value[half:])
            send_ref[0, k, 0] = jnp.where(first, value[half:], value[:half])
        rows = down_keep_ref.shape[3]
        for z in range(down_keep_ref.shape[0]):
            even = down[2 * z * rows : (2 * z + 1) * rows]
            odd = down[(2 * z + 1) * rows : (2 * z + 2) * rows]
            down_keep_ref[z, 0, 0] = jnp.where(first, even, odd)
            down_send_ref[z, 0, 0] = jnp.where(first, odd, even)
        return
    gate_ref, up_ref, down_ref = refs[5 * n :]
    for p in range(down_ref.shape[0]):
        rows = down_ref.shape[3]
        down_ref[p, 0, 0] = down[p * rows : (p + 1) * rows]
    for p in range(gate_ref.shape[0]):
        rows = gate_ref.shape[2]
        gate_ref[p, 0] = gate[p * rows : (p + 1) * rows]
        up_ref[p, 0] = up[p * rows : (p + 1) * rows]


def run_weight_grad(dp, xt, ct, dgate, dup, hs, count, skips, n_dp, paired):
    n = len(xt)
    d, length = xt[0].shape
    ff = hs[-1].shape[1] // count
    m = 256
    left = spec((m, length), lambda e, i: (i, 0))
    rights = [
        spec((length, ff), functools.partial(lambda skip, e, i: (0, e + skip), skip))
        for skip in skips
    ]
    per = d // n_dp
    down_at = lambda e, i: (0, e, i // (ff // m), 0, i % (ff // m))
    if paired:
        row_spec = spec((1, 2, 1, per, ff), lambda e, i: (i, 0, e, 0, 0))
        rows = jax.ShapeDtypeStruct((n_dp // 2, 2, count, per, ff), BF16)
        down_spec = spec((n_dp // 2, 1, 1, ff // n_dp, m), down_at)
        down = jax.ShapeDtypeStruct((n_dp // 2, count, d // ff, ff // n_dp, ff), BF16)
        out_specs, out_shape = [row_spec] * 2 + [down_spec] * 2, [rows] * 2 + [down] * 2
    else:
        row_spec = spec((m // per, 1, per, ff), lambda e, i: (i, e, 0, 0))
        rows = jax.ShapeDtypeStruct((n_dp, count, per, ff), BF16)
        down_spec = spec((n_dp, 1, 1, ff // n_dp, m), down_at)
        down = jax.ShapeDtypeStruct((n_dp, count, d // ff, ff // n_dp, ff), BF16)
        out_specs, out_shape = [row_spec] * 2 + [down_spec], [rows] * 2 + [down]
    return pl.pallas_call(
        functools.partial(weight_grad_kernel, n, paired),
        grid=(count, d // m),
        in_specs=[pl.BlockSpec(memory_space=pltpu.SMEM)] + [left] * (2 * n) + rights * 3,
        out_specs=out_specs,
        out_shape=out_shape,
        compiler_params=params(60, 2),
        cost_estimate=took(37),
        name="weight_grad",
    )(dp, *xt, *ct, *dgate, *dup, *hs)


def back_mid_kernel(n, n_ex, local, *refs):
    (me_ref, res_ref, cot_ref, route_ref, x_ref, router_ref, gain_ref, w_ref) = refs[:8]
    dx_refs, dg_refs = refs[8 : 8 + n], refs[8 + n : 8 + n + n_ex]
    dres_ref, dattn_ref, dctx_ref, dlog_ref, ggain_ref = refs[8 + n + n_ex :]
    gp = gates_of(x_ref[...], router_ref[...], route_ref[...], n_ex * local)
    parts = [ref[...][:local] for ref in dg_refs]
    owners = []
    for owner in range(n_ex):
        own = jnp.zeros_like(parts[0])
        for step in range(n_ex):
            own = jnp.where((owner ^ step) == me_ref[0], parts[step], own)
        owners.append(own)
    dg = jnp.concatenate(owners, axis=0)
    d_logits = gp * (dg - jnp.sum(gp * dg, axis=0, keepdims=True))
    fill = jnp.zeros((128 - dg.shape[0], dg.shape[1]), F32)
    d_logits = jnp.concatenate([d_logits, fill], axis=0).T.astype(BF16)
    dlog_ref[...] = d_logits
    d_norm = dot_t(d_logits, router_ref[...])
    for ref in dx_refs:
        d_norm = d_norm + ref[...].astype(F32)
    res = res_ref[...]
    r = lax.rsqrt(jnp.mean(res * res, axis=1, keepdims=True) + EPS)
    xr = res * r
    part = jnp.sum(d_norm * xr, axis=0, keepdims=True)

    @pl.when(pl.program_id(0) == 0)
    def _():
        ggain_ref[...] = jnp.zeros_like(ggain_ref)

    ggain_ref[...] += part
    u = d_norm * gain_ref[...].astype(F32)
    d_res = (
        cot_ref[...].astype(F32) + r * u - xr * (r * r) * jnp.mean(u * res, axis=1, keepdims=True)
    )
    dres_ref[...] = d_res
    d_attn = d_res.astype(BF16)
    dattn_ref[...] = d_attn
    dctx_ref[...] = dot_t(d_attn, w_ref[...]).astype(BF16)


def run_back_mid(me, res, cot, routes_t, x, router, gain, w_out, dxs, dgs, local):
    length, d = res.shape
    b = 256
    row = lambda i: (i, 0)
    n, n_ex = len(dxs), len(dgs)
    return pl.pallas_call(
        functools.partial(back_mid_kernel, n, n_ex, local),
        grid=(length // b,),
        in_specs=[
            pl.BlockSpec(memory_space=pltpu.SMEM),
            spec((b, d), row),
            spec((b, d), row),
            spec((routes_t.shape[0], b), lambda i: (0, i)),
            spec((b, d), row),
            whole(router.shape),
            whole((1, d)),
            whole(w_out.shape),
        ]
        + [spec((b, d), row)] * n
        + [spec((8, b), lambda i: (0, i))] * n_ex,
        out_specs=[
            spec((b, d), row),
            spec((b, d), row),
            spec((b, w_out.shape[0]), row),
            spec((b, 128), row),
            whole((1, d)),
        ],
        out_shape=[
            jax.ShapeDtypeStruct((length, d), F32),
            jax.ShapeDtypeStruct((length, d), BF16),
            jax.ShapeDtypeStruct((length, w_out.shape[0]), BF16),
            jax.ShapeDtypeStruct((length, 128), BF16),
            jax.ShapeDtypeStruct((1, d), F32),
        ],
        compiler_params=params(60),
        cost_estimate=took(11),
        name="back_mid",
    )(me, res, cot, routes_t, x, router, gain, w_out, *dxs, *dgs)


def back_in_kernel(dq_ref, dk_ref, dv_ref, w_ref, tok_ref, gain_ref, dres_ref, gt_ref, ggain_ref):
    nq, nk = dq_ref.shape[1], dk_ref.shape[1]
    d_norm = dot_t(dq_ref[...], w_ref[:, :nq])
    d_norm = d_norm + dot_t(dk_ref[...], w_ref[:, nq : nq + nk])
    d_norm = d_norm + dot_t(dv_ref[...], w_ref[:, nq + nk : nq + 2 * nk])
    x = tok_ref[...].astype(F32)
    r = lax.rsqrt(jnp.mean(x * x, axis=1, keepdims=True) + EPS)
    xr = x * r
    part = jnp.sum(d_norm * xr, axis=0, keepdims=True)

    @pl.when(pl.program_id(0) == 0)
    def _():
        ggain_ref[...] = jnp.zeros_like(ggain_ref)

    ggain_ref[...] += part
    u = d_norm * gain_ref[...].astype(F32)
    gt_ref[...] = dres_ref[...] + r * u - xr * (r * r) * jnp.mean(u * x, axis=1, keepdims=True)


def run_back_in(dq, dk, dv, w_qkv, tok, gain, d_res):
    length, d = tok.shape
    b = 256
    row = lambda i: (i, 0)
    nq = dq.shape[1]
    return pl.pallas_call(
        back_in_kernel,
        grid=(length // b,),
        in_specs=[
            spec((b, nq), row),
            spec((b, dk.shape[1]), row),
            spec((b, dv.shape[1]), row),
            spec((d, 2 * nq), lambda i: (0, 0)),
            spec((b, d), row),
            whole((1, d)),
            spec((b, d), row),
        ],
        out_specs=[spec((b, d), row), whole((1, d))],
        out_shape=[jax.ShapeDtypeStruct((length, d), F32), jax.ShapeDtypeStruct((1, d), F32)],
        compiler_params=params(60),
        cost_estimate=took(10),
        name="back_in",
    )(dq, dk, dv, w_qkv, tok, gain, d_res)


CHUNKS = (3, 0, 1, 2)


def add_rows(dst, srcs, step=64):
    def body(i, carry):
        at = pl.ds(pl.multiple_of(i * step, step), step)
        total = srcs[0][at, :].astype(F32)
        for src in srcs[1:]:
            total = total + src[at, :].astype(F32)
        dst[at, :] = total.astype(dst.dtype)
        return carry

    lax.fori_loop(0, dst.shape[0] // step, body, 0)


def finish_kernel(
    ht_ref, dq_ref, dk_ref, dv_ref, dout_ref, small_ref,
    keep_a, got_a, down_keep_a, down_got_a, keep_b, send_b, down_keep_b, down_send_b,
    out_ref, gate_ref, up_ref, down_ref, *scratch,
):
    n = len(CHUNKS)
    lists = [scratch[k * n : (k + 1) * n] for k in range(8)]
    b1, r1, s1, r2, s2, r3, s3, r4 = lists
    tot, rx, rx_down, rz1, rz2, rz3, sem_s, sem_r, sem_es, sem_er, sem_l = scratch[8 * n :]
    dp, ex = lax.axis_index("dp"), lax.axis_index("expert")
    z, x, y, c = dp // 2, dp % 2, ex // 2, ex % 2
    over_core, over_y, over_x = (dp, ex ^ 1), (dp, ex ^ 2), (dp ^ 1, ex)
    line = [(dp ^ (2 * k), ex) for k in (1, 2, 3)]
    group = [over_core, over_y, (dp, ex ^ 3)]
    barrier = pltpu.get_barrier_semaphore()
    peers = group + [over_x] + line
    for peer in peers:
        pl.semaphore_signal(barrier, inc=1, device_id=peer, device_id_type=pl.DeviceIdType.MESH)
    pl.semaphore_wait(barrier, len(peers))

    widths = [dout_ref.shape[1], dq_ref.shape[1], dk_ref.shape[1] + dv_ref.shape[1], 128]
    starts = [sum(widths[:k]) for k in range(n)]
    started = {}

    def remote(key, src, dst, send_sem, recv_sem, peer):
        copy = pltpu.make_async_remote_copy(
            src_ref=src,
            dst_ref=dst,
            send_sem=send_sem,
            recv_sem=recv_sem,
            device_id=peer,
            device_id_type=pl.DeviceIdType.MESH,
        )
        started[key] = copy
        return copy

    def send(k, slot, src, dst, peer):
        remote((k, slot), src, dst, sem_s.at[k, slot], sem_r.at[k, slot], peer).start()

    def kind_of(which, keep_like, down_like):
        return down_like if which == 2 else keep_like.at[:, which]

    def rx_of(ch):
        return rx_down.at[ch // 3] if ch % 3 == 2 else rx.at[ch // 3, :, ch % 3]

    for ch in range(3, 6):
        src = kind_of(ch - 3, send_b, down_send_b)
        remote(("x", ch), src, rx_of(ch), sem_es.at[ch, 0], sem_er.at[ch, 0], over_x).start()
    loads = {}
    for ch in range(3):
        copy = pltpu.make_async_copy(
            kind_of(ch, got_a, down_got_a), rx_of(ch), sem_l.at[ch]
        )
        copy.start()
        loads[ch] = [copy]
    for ch in range(6):
        keep, down_keep = (keep_a, down_keep_a) if ch < 3 else (keep_b, down_keep_b)
        for zz in range(4):
            for e in range(2):
                if ch % 3 < 2:
                    copy = pltpu.make_async_copy(
                        keep.at[zz, ch % 3, e],
                        tot.at[ch, zz, e * 128 : (e + 1) * 128],
                        sem_l.at[6 + (ch * 4 + zz) * 4 + e * 2],
                    )
                    copy.start()
                    loads.setdefault(ch, []).append(copy)
                    continue
                for h in range(2):
                    at = e * 128 + h * 64
                    copy = pltpu.make_async_copy(
                        down_keep.at[zz, e, h],
                        tot.at[ch, zz, at : at + 64],
                        sem_l.at[6 + (ch * 4 + zz) * 4 + e * 2 + h],
                    )
                    copy.start()
                    loads.setdefault(ch, []).append(copy)

    upper = z // 2
    outer = (z == 0) | (z == 3)
    inner = jnp.logical_not(outer)

    def z_copy(ch, stage):
        if stage == 1:
            src, dst = tot.at[ch, pl.ds(2 * (1 - upper), 2)], rz1.at[ch]
            peer = (dp ^ 2, ex)
        elif stage == 2:
            src, dst = tot.at[ch, pl.ds(2 * (1 - upper), 2)], rz2.at[ch]
            peer = (dp ^ 6, ex)
        else:
            src, dst = tot.at[ch, 2 * upper + 1 - z % 2], rz3.at[ch]
            peer = (dp ^ 2, ex)
        key = ("z", ch, stage)
        if key in started:
            return started[key]
        return remote(key, src, dst, sem_es.at[ch, stage], sem_er.at[ch, stage], peer)

    def exp_x(ch):
        for copy in loads[ch]:
            copy.wait()
        if ch >= 3:
            started["x", ch].wait()
        for zz in range(4):
            for e in range(2):
                if ch % 3 < 2:
                    dst = tot.at[ch, zz, e * 128 : (e + 1) * 128]
                    add_rows(dst, [dst, rx.at[ch // 3, zz, ch % 3, e]])
                else:
                    for h in range(2):
                        at = e * 128 + h * 64
                        dst = tot.at[ch, zz, at : at + 64]
                        add_rows(dst, [dst, rx_down.at[ch // 3, zz, e, h]])
        one, three = z_copy(ch, 1), z_copy(ch, 3)

        @pl.when(outer)
        def _():
            one.start()
            three.start()

    def exp_1(ch):
        two = z_copy(ch, 2)

        @pl.when(inner)
        def _():
            z_copy(ch, 1).wait_recv()
            for p in range(2):
                dst = tot.at[ch, 2 * (1 - upper) + p]
                add_rows(dst, [dst, rz1.at[ch, p]])
            two.start()

    def exp_2(ch):
        @pl.when(inner)
        def _():
            z_copy(ch, 2).wait()
            for p in range(2):
                dst = tot.at[ch, 2 * upper + p]
                add_rows(dst, [dst, rz2.at[ch, p]])
            z_copy(ch, 3).start()

        @pl.when(outer)
        def _():
            z_copy(ch, 1).wait_send()

    def exp_3(ch):
        z_copy(ch, 3).wait()
        for e in range(2):
            at = 2 * (ch // 3) + e
            if ch % 3 < 2:
                rows = slice(e * 128, (e + 1) * 128)
                dst = (gate_ref, up_ref)[ch % 3].at[at]
                add_rows(dst, [tot.at[ch, z, rows], rz3.at[ch, rows]])
            else:
                for h in range(2):
                    rows = slice(e * 128 + h * 64, e * 128 + (h + 1) * 64)
                    dst = down_ref.at[at, :, h * 512 : (h + 1) * 512]
                    add_rows(dst, [tot.at[ch, z, rows], rz3.at[ch, rows]])

    def place(k, lanes, value):
        for p in range(8):
            for e in range(4):
                row = 128 * p + 32 * e
                b1[k][e % 2, e // 2, p % 2, p // 2, :, lanes] = value[row : row + 32]

    def step0(k):
        if k == 0:
            place(k, slice(0, widths[k]), dout_ref[...])
        elif k == 1:
            for col in range(0, widths[1], 512):
                part = dot(ht_ref[...], dq_ref[:, col : col + 512])
                place(k, slice(col, col + 512), part.astype(BF16))
        elif k == 2:
            half = dk_ref.shape[1]
            place(k, slice(0, half), dot(ht_ref[...], dk_ref[...]).astype(BF16))
            place(k, slice(half, 2 * half), dot(ht_ref[...], dv_ref[...]).astype(BF16))
        else:
            place(k, slice(0, 128), small_ref[...])
        send(k, 0, b1[k].at[1 - c], r1[k], over_core)

    def step1(k):
        started[k, 0].wait()
        for yy in range(2):
            for xx in range(2):
                for zz in range(4):
                    s1[k][yy, xx, zz] = (
                        b1[k][c, yy, xx, zz].astype(F32) + r1[k][yy, xx, zz].astype(F32)
                    ).astype(BF16)
        send(k, 1, s1[k].at[1 - y], r2[k], over_y)

    def step2(k):
        started[k, 1].wait()
        for xx in range(2):
            for zz in range(4):
                s2[k][xx, zz] = (
                    s1[k][y, xx, zz].astype(F32) + r2[k][xx, zz].astype(F32)
                ).astype(BF16)
        send(k, 2, s2[k].at[1 - x], r3[k].at[0], over_x)

    def step3(k):
        started[k, 2].wait()
        for zz in range(4):
            s3[k][zz] = (s2[k][x, zz].astype(F32) + r3[k][0, zz].astype(F32)).astype(BF16)
        for i in range(3):
            send(k, 3 + i, s3[k].at[z ^ (i + 1)], r3[k].at[1, i], line[i])

    def step4(k):
        for i in range(3):
            started[k, 3 + i].wait()
        total = s3[k][z].astype(F32)
        for i in range(3):
            total = total + r3[k][1, i].astype(F32)
        r4[k][3] = total.astype(BF16)
        for i in range(3):
            send(k, 6 + i, r4[k].at[3], r4[k].at[i], group[i])

    def step5(k):
        o = slice(starts[k], starts[k] + widths[k])
        out_ref[pl.ds(pl.multiple_of(ex * 32, 32), 32), o] = r4[k][3].astype(F32)
        for i in range(3):
            started[k, 6 + i].wait()
            rows = pl.ds(pl.multiple_of((ex ^ (i + 1)) * 32, 32), 32)
            out_ref[rows, o] = r4[k][i].astype(F32)

    def dense(step, chunks=CHUNKS):
        for k in chunks:
            step(k)

    dense(step0, CHUNKS[:2])
    for ch in range(3):
        exp_x(ch)
    dense(step0, CHUNKS[2:])
    dense(step1)
    for ch in range(3):
        exp_1(ch)
    exp_x(3)
    dense(step2)
    for ch in range(3):
        exp_2(ch)
    exp_1(3)
    exp_x(4)
    dense(step3)
    for ch in range(3):
        exp_3(ch)
    exp_1(4)
    exp_2(3)
    exp_x(5)
    dense(step4)
    exp_3(3)
    exp_1(5)
    exp_2(4)
    dense(step5)
    exp_3(4)
    exp_2(5)
    exp_3(5)


def run_finish(ht, dq, dk, dv, d_out, small, experts):
    d = ht.shape[0]
    widths = [d_out.shape[1], dq.shape[1], dk.shape[1] + dv.shape[1], small.shape[1]]
    keep_a, _, down_keep_a, _ = experts[0], None, experts[2], None
    _, kinds, count, per, ff = keep_a.shape
    down_rows = down_keep_a.shape[3]
    vmem = pl.BlockSpec(memory_space=pltpu.VMEM)
    hbm = pl.BlockSpec(memory_space=pl.ANY)
    shapes = [
        (2, 2, 2, 4, 32), (2, 2, 4, 32), (2, 2, 4, 32), (2, 4, 32), (2, 4, 32), (2, 4, 32), (4, 32), (4, 32),
    ]
    scratch = [pltpu.VMEM(shape + (w,), BF16) for shape in shapes for w in widths]
    rows = count * per
    scratch += [
        pltpu.VMEM((6, 4, rows, ff), BF16),
        pltpu.VMEM((2, 4, 2, count, per, ff), BF16),
        pltpu.VMEM((2,) + down_keep_a.shape, BF16),
        pltpu.VMEM((6, 2, rows, ff), BF16),
        pltpu.VMEM((6, 2, rows, ff), BF16),
        pltpu.VMEM((6, rows, ff), BF16),
        pltpu.SemaphoreType.DMA((len(widths), 9)),
        pltpu.SemaphoreType.DMA((len(widths), 9)),
        pltpu.SemaphoreType.DMA((6, 4)),
        pltpu.SemaphoreType.DMA((6, 4)),
        pltpu.SemaphoreType.DMA((6 + 96,)),
    ]
    return pl.pallas_call(
        finish_kernel,
        in_specs=[vmem] * 6 + [hbm] * 8,
        out_specs=[vmem] * 4,
        out_shape=[
            jax.ShapeDtypeStruct((128, sum(widths)), F32),
            jax.ShapeDtypeStruct((2 * count, per, ff), F32),
            jax.ShapeDtypeStruct((2 * count, per, ff), F32),
            jax.ShapeDtypeStruct((2 * count, down_rows, d), F32),
        ],
        scratch_shapes=scratch,
        compiler_params=pltpu.CompilerParams(
            vmem_limit_bytes=62 * MIB, collective_id=1, has_side_effects=True
        ),
        cost_estimate=took(60),
        name="finish",
    )(ht, dq, dk, dv, d_out, small, *experts)


def gather_kernel(mine_ref, out_ref, sem_s, sem_r, sem_l):
    dp, ex = lax.axis_index("dp"), lax.axis_index("expert")
    z = dp // 2
    core, over_y, over_x = (dp, ex ^ 1), (dp, ex ^ 2), (dp ^ 1, ex)
    line = [None] + [(dp ^ (2 * k), ex) for k in (1, 2, 3)]
    barrier = pltpu.get_barrier_semaphore()
    peers = [core, over_y, over_x] + line[1:]
    for peer in peers:
        pl.semaphore_signal(barrier, inc=1, device_id=peer, device_id_type=pl.DeviceIdType.MESH)
    pl.semaphore_wait(barrier, len(peers))
    rows = mine_ref.shape[0]
    width = mine_ref.shape[1]
    cut = (width // 256 + 1) * 128
    halves = [pl.ds(0, cut), pl.ds(cut, width - cut)]
    started = {}

    def block(k, dx, dy):
        at = (((z ^ k) * 2 + (dp % 2 ^ dx)) * 4 + (ex ^ (2 * dy))) * rows
        return pl.ds(pl.multiple_of(at, rows), rows)

    def send(key, k, dx, dy, peer, src=None, lanes=None):
        index = len(started)
        at = block(k, dx, dy)
        dst = out_ref.at[at] if lanes is None else out_ref.at[at, lanes]
        copy = pltpu.make_async_remote_copy(
            src_ref=dst if src is None else src,
            dst_ref=dst,
            send_sem=sem_s.at[index],
            recv_sem=sem_r.at[index],
            device_id=peer,
            device_id_type=pl.DeviceIdType.MESH,
        )
        copy.start()
        started[key] = copy

    for k in (3, 2, 1):
        send(("z", k), 0, 0, 0, line[k], mine_ref)
    send(("x", 0), 0, 0, 0, over_x, mine_ref)
    send(("y", 0), 0, 0, 0, over_y, mine_ref)
    send(("c", 0), 0, 0, 0, core, mine_ref)
    own = pltpu.make_async_copy(mine_ref, out_ref.at[block(0, 0, 0)], sem_l)
    own.start()

    def onward(k):
        started["x", k].wait_recv()
        send(("dy", k), k, 1, 0, over_y, None, halves[0])
        send(("cx", k), k, 1, 0, core)
        started["y", k].wait_recv()
        send(("dx", k), k, 0, 1, over_x, None, halves[1])
        send(("cy", k), k, 0, 1, core)

    def last(k):
        started["dy", k].wait_recv()
        started["dx", k].wait_recv()
        send(("cd", k), k, 1, 1, core)

    onward(0)
    for k in (1, 2, 3):
        started["z", k].wait_recv()
        send(("x", k), k, 0, 0, over_x)
        send(("y", k), k, 0, 0, over_y)
        send(("c", k), k, 0, 0, core)
    last(0)
    for k in (1, 2, 3):
        onward(k)
    for k in (1, 2, 3):
        last(k)
    for key, copy in started.items():
        copy.wait_send()
        if key[0] in ("c", "cx", "cy", "cd"):
            copy.wait_recv()
    own.wait()


def run_gather(mine, total):
    hbm = pl.BlockSpec(memory_space=pl.ANY)
    return pl.pallas_call(
        gather_kernel,
        in_specs=[hbm],
        out_specs=hbm,
        out_shape=jax.ShapeDtypeStruct((total, mine.shape[1]), BF16),
        scratch_shapes=[
            pltpu.SemaphoreType.DMA((40,)),
            pltpu.SemaphoreType.DMA((40,)),
            pltpu.SemaphoreType.DMA,
        ],
        compiler_params=pltpu.CompilerParams(collective_id=2, has_side_effects=True),
        cost_estimate=took(40),
        name="gather",
    )(mine)


def after(value, *deps):
    return lax.optimization_barrier((value,) + deps)[0]


def on_device(
    n_dp, n_ex, tokens, cotangent, routes, prefix, w_query, keyvalue_weight, w_out, w_router,
    gain_attn, gain_mlp, expert_gate, expert_up, expert_down, query_logit_cap,
):
    length, d = tokens.shape[1], tokens.shape[2]
    tok = tokens.reshape(length, d)
    cot = cotangent.reshape(length, d)
    heads = query_logit_cap.shape[0]
    nq = w_query.shape[1]
    head = nq // heads
    kv_heads = keyvalue_weight.shape[1] // (2 * head)
    num_experts = w_router.shape[1]
    local = expert_gate.shape[0]
    rows = w_query.shape[0]
    ex = lax.axis_index("expert")

    def swap(value, step, axis="expert", n=n_ex):
        return lax.ppermute(value, axis, [(i, i ^ step) for i in range(n)])

    part = rows // n_ex
    small = jnp.concatenate(
        [
            w_router,
            gain_attn[:, None],
            gain_mlp[:, None],
            jnp.zeros((rows, 128 - num_experts - 2), BF16),
        ],
        axis=1,
    )
    packed = jnp.concatenate([w_query, keyvalue_weight, w_out, small], axis=1)
    mine = lax.dynamic_slice_in_dim(packed, ex * part, part, axis=0)
    local = expert_gate.shape[0]
    fast = n_dp == 8 and n_ex == 4 and d == 1024 and local == 4 and expert_gate.shape[2] == 512
    if fast:
        every = run_gather(mine, d)
    else:
        every = lax.all_gather(mine, ("dp", "expert"), axis=0, tiled=True)
    w_all = every
    width = 2 * nq
    full_out = every[:, width : width + d]
    extra = every[:, width + d :]
    lanes = lax.broadcasted_iota(jnp.int32, extra.shape, 1)
    router = jnp.where(lanes < num_experts, extra, jnp.zeros((), BF16))
    gain_one = extra[:, num_experts].reshape(1, d)
    gain_two = extra[:, num_experts + 1].reshape(1, d)

    routes_t = after(routes.reshape(length, -1).T, every)
    cots = {0: cot}
    route_set = {0: routes_t}
    for step in range(1, n_ex):
        route_set[step] = swap(routes_t, step)
    cot_late = after(cot, every, *route_set.values())
    for step in range(1, n_ex):
        if step == 1 or step % 2 == 0:
            cots[step] = swap(cot_late, step)

    cos_np, sin_np = rope_tables(length, head)
    cos_l = jnp.asarray(np.concatenate([cos_np] * 4, axis=1))
    sin_l = jnp.asarray(np.concatenate([-sin_np, sin_np] * 2, axis=1))
    cos_t = jnp.asarray(np.ascontiguousarray(cos_np.T))
    sin_t = jnp.asarray(np.ascontiguousarray(sin_np.T))

    normed_one_t, q, kd, vd = run_qkv(tok, gain_one, w_all, cos_l, sin_l, nq)
    ctx, lse, peaks = run_attn_fwd(prefix, q, kd, vd)
    for step in range(3, n_ex, 2):
        cots[step] = swap(after(cots[step - 1], ctx), 1)
    resid, normed_two = run_mid(tok, after(ctx, *cots.values()), full_out, gain_two)

    me = ex.reshape(1).astype(jnp.int32)
    xs = {0: normed_two}
    for step in range(1, n_ex):
        if step == 1 or step % 2 == 0:
            xs[step] = swap(normed_two, step)
        else:
            xs[step] = swap(xs[step - 1], 1)
    tops = [peaks[:, :, :4]]
    bits = [("expert", n_ex, 1 << i) for i in range(n_ex.bit_length() - 1)]
    bits += [("dp", n_dp, 1 << i) for i in range(n_dp.bit_length() - 1)]

    def widen_top():
        if len(tops) <= len(bits):
            axis, n, step = bits[len(tops) - 1]
            top = after(tops[-1], chain)
            tops.append(jnp.maximum(top, swap(top, step, axis, n)))

    weights = (expert_gate, expert_up, expert_down)
    half = local // 2

    dp = lax.axis_index("dp").reshape(1).astype(jnp.int32)

    res = {}
    chain = xs[1]

    def experts(step, first, count, init=None):
        x = after(xs[step], chain)
        return run_expert(
            me, x, cots[step], route_set[step], router, *weights, first, count, num_experts, init
        )

    def grads(first):
        skips = [first if step < 2 else 0 for step in range(n_ex)]
        pieces = [
            [res[step, 0 if step < 2 else first][k] for step in range(n_ex)] for k in (4, 5, 3)
        ]
        turned = [[res[step, 0][k] for step in range(n_ex)] for k in (6, 7)]
        turned[0][0] = after(turned[0][0], chain)
        made = None
        for at in range(0, n_ex, 4):
            some = [group[at : at + 4] for group in turned + pieces]
            part = run_weight_grad(dp, *some, half, skips[at : at + 4], n_dp, fast)
            if made is None:
                made = part
            else:
                made = [(a.astype(F32) + b.astype(F32)).astype(BF16) for a, b in zip(made, part)]
        return made

    for step in range(2):
        res[step, 0] = experts(step, 0, local)
        chain = res[step, 0][0]
    odd, even = range(3, n_ex, 2), range(2, n_ex, 2)
    for step in odd:
        res[step, 0] = experts(step, 0, half)
        chain = res[step, 0][0]
        res[step, half] = experts(step, half, half, res[step, 0][:3])
        chain = (res[step, half][0], tops[-1])
        widen_top()
    partner = {step - 1: [swap(res[step, half][k], 1) for k in (0, 1)] for step in odd}
    for step in even:
        res[step, 0] = experts(step, 0, half)
        chain = (res[step, 0][0], tops[-1])
        widen_top()
    made_one = grads(0)
    chain = (made_one[0], tops[-1])
    got_one = [swap(made_one[k], 1, "dp", n_dp) for k in (1, 3)] if fast else []
    widen_top()
    for step in even:
        init = [
            (a.astype(F32) + b.astype(F32)).astype(BF16)
            for a, b in zip(res[step, 0][:2], partner[step])
        ]
        res[step, half] = experts(step, half, half, init + [res[step, 0][2]])
        chain = (res[step, half][0], tops[-1])
        widen_top()
    made_two = grads(half)
    chain = (made_two[0], got_one, tops[-1])
    while len(tops) <= len(bits):
        widen_top()
    top = tops[-1]

    last = [res[step, 0 if step < 2 else half] for step in range(n_ex)]
    dxs = [last[0][1], swap(last[1][1], 1)] + [swap(last[step][1], step) for step in even]
    dgs = [last[0][2]] + [swap(last[step][2], step) for step in range(1, n_ex)]
    d_res, d_attn, d_ctx, d_logits, d_gain_two = run_back_mid(
        me,
        after(resid, chain),
        cot,
        routes_t,
        normed_two,
        router,
        gain_two,
        full_out,
        dxs,
        dgs,
        local,
    )
    outs = [last[0][0], swap(last[1][0], 1)]
    outs += [swap(after(last[step][0], dxs), step) for step in even]
    block = resid
    for piece in outs:
        block = block + piece.astype(F32)
    block_out = block.astype(BF16).reshape(tokens.shape)

    d_out_w = jnp.einsum("rc,rd->cd", ctx, d_attn, preferred_element_type=F32).astype(BF16)
    d_router_w = jnp.einsum("rd,re->de", normed_two, d_logits, preferred_element_type=F32)

    dq, dk, dv = run_attn_bwd(
        prefix, after(q, top), kd, vd, d_ctx, ctx, lse, cos_l, sin_l, cos_t, sin_t
    )
    grad_tok, d_gain_one = run_back_in(
        after(dq, block_out), dk, dv, w_all, tok, gain_one, d_res
    )
    small_grad = jnp.concatenate(
        [
            d_router_w[:, :num_experts].astype(BF16),
            d_gain_one.reshape(d, 1).astype(BF16),
            d_gain_two.reshape(d, 1).astype(BF16),
            jnp.zeros((d, 128 - num_experts - 2), BF16),
        ],
        axis=1,
    )

    def reduce_all(value, order):
        shape = (n_dp, n_ex, value.shape[0] // (n_dp * n_ex), value.shape[1])
        names = []
        dims = []
        for axis, n in (("dp", n_dp), ("expert", n_ex)):
            count = n.bit_length() - 1
            names += [(axis, n, 1 << (count - 1 - i)) for i in range(count)]
            dims += [2] * count
        value = value.reshape(*dims, *shape[2:])
        for bit in order:
            at = names.index(bit)
            axis, n, step = bit
            mine = (lax.axis_index(axis) // step) % 2
            keep = lax.dynamic_slice_in_dim(value, mine, 1, axis=at)
            send = lax.dynamic_slice_in_dim(value, 1 - mine, 1, axis=at)
            value = (keep.astype(F32) + swap(send, step, axis, n).astype(F32)).astype(BF16)
        return value.reshape(shape[2:])

    def share(value):
        return lax.all_gather(value, "expert", axis=0, tiled=True).astype(F32)

    core = [("expert", n_ex, 1)]
    y_bits = [("expert", n_ex, 1 << i) for i in range(1, n_ex.bit_length() - 1)][::-1]
    dp_bits = [("dp", n_dp, 1 << i) for i in range(n_dp.bit_length() - 1)]
    if fast:
        keep_a, _, down_keep_a, _ = made_one
        keep_b, send_b, down_keep_b, down_send_b = made_two
        every_grad, grad_gate, grad_up, grad_down = run_finish(
            normed_one_t,
            dq,
            dk,
            dv,
            d_out_w,
            small_grad,
            [keep_a, got_one[0], down_keep_a, got_one[1], keep_b, send_b, down_keep_b, down_send_b],
        )
    else:
        ends = [
            [
                lax.psum_scatter(g, "dp", scatter_dimension=0, tiled=True)[0].astype(F32)
                for g in made
            ]
            for made in (made_one, made_two)
        ]
        grad_gate, grad_up, grad_down = (
            jnp.concatenate([ends[0][k], ends[1][k]], axis=0) for k in range(3)
        )
        grad_down = jnp.swapaxes(grad_down, 1, 2).reshape(local, -1, d)

        def product(right):
            return jnp.dot(normed_one_t, right, preferred_element_type=F32).astype(BF16)

        every_grad = jnp.concatenate(
            [d_out_w, product(dq), product(dk), product(dv), small_grad], axis=1
        )
        every_grad = share(reduce_all(every_grad, core + y_bits + dp_bits[::-1]))
    grad_out = every_grad[:, :d]
    grad_query = every_grad[:, d : d + nq]
    grad_keyval = every_grad[:, d + nq : d + 2 * nq]
    grad_router = every_grad[:, d + 2 * nq : d + 2 * nq + num_experts]
    grad_gain_one = every_grad[:, d + 2 * nq + num_experts]
    grad_gain_two = every_grad[:, d + 2 * nq + num_experts + 1]

    head_logit_peak = top[:, 0, :].reshape(heads)
    per_group = heads // kv_heads
    query_factor = jnp.sqrt(query_logit_cap / jnp.maximum(head_logit_peak, query_logit_cap))
    pair_peak = jnp.max(head_logit_peak.reshape(kv_heads, per_group), axis=1)
    pair_cap = jnp.min(query_logit_cap.reshape(kv_heads, per_group), axis=1)
    key_factor = jnp.sqrt(pair_cap / jnp.maximum(pair_peak, pair_cap))
    clipped_query = (w_query.astype(F32) * jnp.repeat(query_factor, head)[None, :]).astype(BF16)
    key_cols = jnp.concatenate(
        [jnp.repeat(key_factor, head), jnp.ones((kv_heads * head,), F32)]
    )
    clipped_keyval = (keyvalue_weight.astype(F32) * key_cols[None, :]).astype(BF16)
    return (
        block_out,
        grad_tok.reshape(tokens.shape),
        grad_query,
        grad_keyval,
        grad_out,
        grad_router,
        grad_gain_one,
        grad_gain_two,
        grad_gate,
        grad_up,
        grad_down,
        clipped_query,
        clipped_keyval,
        head_logit_peak,
    )


def solution(mesh):
    rows3 = P(("dp", "expert"), None, None)
    in_specs = (
        rows3,
        rows3,
        rows3,
        P(("dp", "expert")),
        P("dp", None),
        P("dp", None),
        P("dp", None),
        P("dp", None),
        P("dp"),
        P("dp"),
        P("expert", None, None),
        P("expert", None, None),
        P("expert", None, None),
        P(),
    )
    out_specs = (
        rows3,
        rows3,
        P("dp", None),
        P("dp", None),
        P("dp", None),
        P("dp", None),
        P("dp"),
        P("dp"),
        P("expert", "dp", None),
        P("expert", "dp", None),
        P("expert", "dp", None),
        P("dp", None),
        P("dp", None),
        P(),
    )
    return jax.shard_map(
        functools.partial(on_device, mesh.shape["dp"], mesh.shape["expert"]),
        mesh=mesh,
        in_specs=in_specs,
        out_specs=out_specs,
        check_vma=False,
    )
```

```python
import functools

import jax
import jax.numpy as jnp
import numpy as np
from jax import lax
from jax.experimental import pallas as pl
from jax.experimental.pallas import tpu as pltpu
from jax.sharding import PartitionSpec as P

EPS = 1e-05
ROPE_BASE = 10000.0
F32 = jnp.float32
BF16 = jnp.bfloat16
NEG = -1e30
MIB = 1 << 20
SCALE = 0.5


def dot(a, b):
    return lax.dot_general(a, b, (((1,), (0,)), ((), ())), preferred_element_type=F32)


def dot_t(a, b):
    return lax.dot_general(a, b, (((1,), (1,)), ((), ())), preferred_element_type=F32)


def params(vmem_mib, n=1):
    return pltpu.CompilerParams(
        dimension_semantics=("arbitrary",) * n, vmem_limit_bytes=vmem_mib * MIB
    )


def took(us):
    return pl.CostEstimate(flops=int(us * SCALE * 1e9), bytes_accessed=1000, transcendentals=0)


def spec(shape, index):
    return pl.BlockSpec(shape, index)


def whole(shape):
    zeros = (0,) * len(shape)
    return pl.BlockSpec(shape, lambda *_: zeros)


def rope_tables(length, head):
    half = head // 2
    freq = np.float32(ROPE_BASE) ** (
        -(np.arange(half, dtype=np.float32) * np.float32(2.0) / np.float32(head))
    )
    ang = np.arange(length, dtype=np.float32)[:, None] * freq.astype(np.float32)[None, :]
    ang = ang.astype(np.float32)
    return np.cos(ang).astype(np.float32), np.sin(ang).astype(np.float32)


def lane_half(shape, width):
    return (lax.broadcasted_iota(jnp.int32, shape, 1) % width) < (width // 2)


def rope_lanes(x, cos, sin, first):
    partner = jnp.where(first, pltpu.roll(x, 96, 1), pltpu.roll(x, 32, 1))
    return x * cos + partner * sin


def qkv_kernel(tok_ref, gain_ref, w_ref, cos_ref, sin_ref, ht_ref, q_ref, kd_ref, vd_ref):
    x = tok_ref[...].astype(F32)
    d = x.shape[1]
    r = lax.rsqrt(jnp.mean(x * x, axis=1, keepdims=True) + EPS)
    h = (x * r * gain_ref[...].astype(F32)).astype(BF16)
    ht_ref[...] = h.T
    cos, sin = cos_ref[...], sin_ref[...]
    rows = x.shape[0]
    first = lane_half((rows, 128), 64)
    low = lane_half((rows, 128), 128)
    nq = q_ref.shape[1]
    nk = kd_ref.shape[1] // 2
    q = dot(h, w_ref[:, :nq])
    for c in range(0, nq, 128):
        q_ref[:, c : c + 128] = (rope_lanes(q[:, c : c + 128], cos, sin, first) * 0.125).astype(
            BF16
        )
    k = dot(h, w_ref[:, nq : nq + nk])
    for c in range(0, nk, 128):
        kk = rope_lanes(k[:, c : c + 128], cos, sin, first)
        sw = pltpu.roll(kk, 64, 1)
        kd_ref[:, 2 * c : 2 * c + 128] = jnp.where(low, kk, sw).astype(BF16)
        kd_ref[:, 2 * c + 128 : 2 * c + 256] = jnp.where(low, sw, kk).astype(BF16)
    v = dot(h, w_ref[:, nq + nk : nq + 2 * nk])
    for c in range(0, nk, 128):
        vv = v[:, c : c + 128]
        sw = pltpu.roll(vv, 64, 1)
        vd_ref[:, 2 * c : 2 * c + 128] = jnp.where(low, vv, sw).astype(BF16)
        vd_ref[:, 2 * c + 128 : 2 * c + 256] = jnp.where(low, sw, vv).astype(BF16)


def run_qkv(tok, gain, w_qkv, cos, sin, nq):
    length, d = tok.shape
    b = 256
    row = lambda i: (i, 0)
    return pl.pallas_call(
        qkv_kernel,
        grid=(length // b,),
        in_specs=[
            spec((b, d), row),
            whole((1, d)),
            spec((d, 2 * nq), lambda i: (0, 0)),
            spec((b, 128), row),
            spec((b, 128), row),
        ],
        out_specs=[spec((d, b), lambda i: (0, i))] + [spec((b, nq), row)] * 3,
        out_shape=[jax.ShapeDtypeStruct((d, length), BF16)]
        + [jax.ShapeDtypeStruct((length, nq), BF16)] * 3,
        compiler_params=params(60),
        cost_estimate=took(9),
        name="qkv",
    )(tok, gain, w_qkv, cos, sin)


def mask_bias(prefix, q0, k0, nq, nk, q_axis):
    shape = (nq, nk) if q_axis == 0 else (nk, nq)
    qpos = q0 + lax.broadcasted_iota(jnp.int32, shape, q_axis)
    kpos = k0 + lax.broadcasted_iota(jnp.int32, shape, 1 - q_axis)
    return jnp.where((kpos <= qpos) | (kpos < prefix), 0.0, NEG).astype(F32)


def two_heads(pair, low):
    zero = jnp.zeros_like(pair)
    return jnp.concatenate([jnp.where(low, pair, zero), jnp.where(low, zero, pair)], axis=0)


def attn_fwd_kernel(prefix_ref, q_ref, kd_ref, vd_ref, ctx_ref, lse_ref, peak_ref):
    length = q_ref.shape[0]
    b = 256
    prefix = prefix_ref[0]
    low_b = lane_half((b, 128), 128)
    lane = lax.broadcasted_iota(jnp.int32, (b, 128), 1)
    peak = jnp.full((8, 128), NEG, F32)
    peak_lane = lax.broadcasted_iota(jnp.int32, (8, 128), 1)
    for i in range(length // b):
        nk = max((i + 1) * b, length // 2)
        free = i * b
        bias = mask_bias(prefix, i * b, free, b, nk - free, 0)
        bias = jnp.concatenate([bias, bias], axis=0)
        lse_cols = jnp.zeros((b, 128), F32)
        for j in range(2):
            cols = slice(j * 128, (j + 1) * 128)
            q2 = two_heads(q_ref[i * b : (i + 1) * b, cols], low_b)
            s_hi = dot_t(q2, kd_ref[free:nk, cols]) + bias
            m = jnp.max(s_hi, axis=1, keepdims=True)
            if free:
                s_lo = dot_t(q2, kd_ref[:free, cols])
                m = jnp.maximum(m, jnp.max(s_lo, axis=1, keepdims=True))
            p_hi = jnp.exp(s_hi - m)
            total = jnp.sum(p_hi, axis=1, keepdims=True)
            ctx = dot(p_hi.astype(BF16), vd_ref[free:nk, cols])
            if free:
                p_lo = jnp.exp(s_lo - m)
                total = total + jnp.sum(p_lo, axis=1, keepdims=True)
                ctx = ctx + dot(p_lo.astype(BF16), vd_ref[:free, cols])
            ctx = ctx * (1.0 / total)
            ctx_ref[i * b : (i + 1) * b, cols] = jnp.where(low_b, ctx[:b], ctx[b:]).astype(BF16)
            lse = m + jnp.log(total)
            for g in range(2):
                lse_cols = jnp.where(lane == 2 * j + g, lse[g * b : (g + 1) * b], lse_cols)
                top = jnp.max(m[g * b : (g + 1) * b], axis=0, keepdims=True)
                peak = jnp.where(peak_lane == 2 * j + g, jnp.maximum(peak, top), peak)
        lse_ref[0, :, i * b : (i + 1) * b] = lse_cols.T[:8]
    peak_ref[0] = peak


def run_attn_fwd(prefix, q, kd, vd):
    length, nq = q.shape
    groups = nq // 256
    col = lambda g: (0, g)
    return pl.pallas_call(
        attn_fwd_kernel,
        grid=(groups,),
        in_specs=[pl.BlockSpec(memory_space=pltpu.SMEM)] + [spec((length, 256), col)] * 3,
        out_specs=[
            spec((length, 256), col),
            spec((1, 8, length), lambda g: (g, 0, 0)),
            spec((1, 8, 128), lambda g: (g, 0, 0)),
        ],
        out_shape=[
            jax.ShapeDtypeStruct((length, nq), BF16),
            jax.ShapeDtypeStruct((groups, 8, length), F32),
            jax.ShapeDtypeStruct((groups, 8, 128), F32),
        ],
        compiler_params=params(60),
        cost_estimate=took(21),
        name="attn_fwd",
    )(prefix, q, kd, vd)


def add_rows(dst, srcs, step=64):
    def body(i, carry):
        at = pl.ds(pl.multiple_of(i * step, step), step)
        total = srcs[0][at, :].astype(F32)
        for src in srcs[1:]:
            total = total + src[at, :].astype(F32)
        dst[at, :] = total.astype(dst.dtype)
        return carry

    lax.fori_loop(0, dst.shape[0] // step, body, 0)


def greet(peers):
    barrier = pltpu.get_barrier_semaphore()
    for peer in peers:
        pl.semaphore_signal(barrier, inc=1, device_id=peer, device_id_type=pl.DeviceIdType.MESH)
    pl.semaphore_wait(barrier, len(peers))


class Line:
    def __init__(self, tot, rz1, rz2, rz3, sem_s, sem_r):
        self.tot, self.rz1, self.rz2, self.rz3 = tot, rz1, rz2, rz3
        self.sem_s, self.sem_r = sem_s, sem_r
        dp, ex = lax.axis_index("dp"), lax.axis_index("expert")
        self.z = dp // 2
        self.upper = self.z // 2
        self.outer = (self.z == 0) | (self.z == 3)
        self.inner = jnp.logical_not(self.outer)
        self.near, self.middle = (dp ^ 2, ex), (dp ^ 6, ex)

    def copy(self, ch, stage):
        if stage == 3:
            src, dst = self.tot.at[ch, 2 * self.upper + 1 - self.z % 2], self.rz3.at[ch]
        else:
            src = self.tot.at[ch, pl.ds(2 * (1 - self.upper), 2)]
            dst = (self.rz1 if stage == 1 else self.rz2).at[ch]
        return pltpu.make_async_remote_copy(
            src_ref=src,
            dst_ref=dst,
            send_sem=self.sem_s.at[ch, stage],
            recv_sem=self.sem_r.at[ch, stage],
            device_id=self.middle if stage == 2 else self.near,
            device_id_type=pl.DeviceIdType.MESH,
        )

    def add(self, ch, first, other):
        for p in range(2):
            for e in range(2):
                dst = self.tot.at[ch, first + p, e]
                add_rows(dst, [dst, other.at[ch, p, e]])

    def ends(self, ch, inward):
        @pl.when(self.outer)
        def _():
            if inward:
                self.copy(ch, 1).start()
            self.copy(ch, 3).start()

    def middle_sends(self, ch, inward):
        @pl.when(self.inner)
        def _():
            if inward:
                self.copy(ch, 1).wait_recv()
            self.add(ch, 2 * (1 - self.upper), self.rz1)
            self.copy(ch, 2).start()

    def middle_adds(self, ch, inward):
        @pl.when(self.inner)
        def _():
            self.copy(ch, 2).wait()
            self.add(ch, 2 * self.upper, self.rz2)
            self.copy(ch, 3).start()

        if inward:

            @pl.when(self.outer)
            def _():
                self.copy(ch, 1).wait_send()

    def result(self, ch, refs):
        self.copy(ch, 3).wait()
        for e in range(2):
            own, got = self.tot.at[ch, self.z, e], self.rz3.at[ch, e]
            if ch < 2:
                add_rows(refs[ch].at[e], [own, got])
            else:
                rows, lanes = refs[2].shape[1], own.shape[1]
                for h in range(2):
                    at = slice(h * rows, (h + 1) * rows)
                    dst = refs[2].at[e, :, h * lanes : (h + 1) * lanes]
                    add_rows(dst, [own.at[at], got.at[at]])


def line_scratch(shape):
    return [
        pltpu.VMEM((3,) + shape, BF16),
        pltpu.VMEM((3, 2) + shape[1:], BF16),
        pltpu.VMEM((3, 2) + shape[1:], BF16),
        pltpu.VMEM((3,) + shape[1:], BF16),
        pltpu.SemaphoreType.DMA((3, 4)),
        pltpu.SemaphoreType.DMA((3, 4)),
    ]


def attn_bwd_kernel(*refs):
    attn_bwd_body(*refs)


def attn_bwd_sum_kernel(*refs):
    ins, (tot_a, far_a, keep_a, got_a) = refs[:11], refs[11:15]
    outs, (gate_ref, up_ref, down_ref) = refs[15:18], refs[18:21]
    scratch, line_refs, (rx, sem_l) = refs[21:24], refs[24:30], refs[30:]
    step = pl.program_id(0)
    line = Line(*line_refs)
    loads = []
    for k in range(2):
        loads.append([pltpu.make_async_copy(tot_a.at[:, k], line.tot.at[k], sem_l.at[2 * k])])
        loads[-1].append(
            pltpu.make_async_copy(far_a.at[:, k], line.rz1.at[k], sem_l.at[2 * k + 1])
        )
    loads.append(
        [
            pltpu.make_async_copy(keep_a, line.tot.at[2], sem_l.at[4]),
            pltpu.make_async_copy(got_a, rx, sem_l.at[5]),
        ]
    )
    @pl.when(step == 0)
    def _():
        for group in loads:
            for copy in group:
                copy.start()
        greet([line.near, line.middle])
        for copy in loads[2]:
            copy.wait()
        for zz in range(4):
            for e in range(2):
                dst = line.tot.at[2, zz, e]
                add_rows(dst, [dst, rx.at[zz, e]])
        line.ends(2, True)
        for k in range(2):
            for copy in loads[k]:
                copy.wait()
            line.ends(k, False)
            line.middle_sends(k, False)

    attn_bwd_body(*ins, *outs, *scratch)

    @pl.when(step == 1)
    def _():
        line.middle_sends(2, True)
        line.middle_adds(0, False)

    @pl.when(step == 2)
    def _():
        line.middle_adds(1, False)

    @pl.when(step == 3)
    def _():
        line.middle_adds(2, True)
        for ch in range(3):
            line.result(ch, (gate_ref, up_ref, down_ref))


def attn_bwd_body(
    prefix_ref, q_ref, kd_ref, vd_ref, do_ref, ctx_ref, lse_ref, cos_ref, sin_ref, cost_ref, sint_ref,
    dq_ref, dk_ref, dv_ref, dk_acc, dv_acc, kt_ref,
):
    length = q_ref.shape[0]
    b = 256
    prefix = prefix_ref[0]
    low_b = lane_half((b, 128), 128)
    for j in range(2):
        cols = slice(j * 128, (j + 1) * 128)
        kt_ref[j] = kd_ref[:, cols].T
    dk_acc[...] = jnp.zeros_like(dk_acc)
    dv_acc[...] = jnp.zeros_like(dv_acc)
    for i in range(length // b):
        rows = slice(i * b, (i + 1) * b)
        nk = max((i + 1) * b, length // 2)
        free = i * b
        bias = mask_bias(prefix, i * b, free, b, nk - free, 1)
        bias = jnp.concatenate([bias, bias], axis=1)
        for j in range(2):
            cols = slice(j * 128, (j + 1) * 128)
            do = do_ref[rows, cols]
            q2 = two_heads(q_ref[rows, cols], low_b)
            do2 = two_heads(do, low_b)
            prod = (do.astype(F32) * ctx_ref[rows, cols].astype(F32)).T
            delta = jnp.concatenate(
                [
                    jnp.sum(prod[:64], axis=0, keepdims=True),
                    jnp.sum(prod[64:], axis=0, keepdims=True),
                ],
                axis=1,
            )
            lse = jnp.concatenate(
                [lse_ref[0, 2 * j : 2 * j + 1, rows], lse_ref[0, 2 * j + 1 : 2 * j + 2, rows]],
                axis=1,
            )
            dq_t = None
            parts = [(0, free)] if free else []
            for k0, k1 in parts + [(free, nk)]:
                keys = slice(k0, k1)
                s = dot_t(kd_ref[keys, cols], q2)
                if k0 == free:
                    s = s + bias
                p = jnp.exp(s - lse)
                dp = dot_t(vd_ref[keys, cols], do2)
                ds = (p * (dp - delta)).astype(BF16)
                dv_acc[j, keys, :] += dot(p.astype(BF16), do2)
                dk_acc[j, keys, :] += dot(ds, q2)
                part = dot(kt_ref[j, :, keys], ds)
                dq_t = part if dq_t is None else dq_t + part
            cos_t, sin_t = cost_ref[:, rows], sint_ref[:, rows]
            a0, b0 = dq_t[0:32, :b], dq_t[32:64, :b]
            a1, b1 = dq_t[64:96, b:], dq_t[96:128, b:]
            full = jnp.concatenate(
                [
                    a0 * cos_t + b0 * sin_t,
                    b0 * cos_t - a0 * sin_t,
                    a1 * cos_t + b1 * sin_t,
                    b1 * cos_t - a1 * sin_t,
                ],
                axis=0,
            )
            dq_ref[rows, cols] = (full * 0.125).T.astype(BF16)
    low = lane_half((length, 128), 128)
    first = lane_half((length, 128), 64)
    sums = []
    for acc in (dk_acc, dv_acc):
        even = acc[0] + pltpu.roll(acc[0], 64, 1)
        odd = acc[1] + pltpu.roll(acc[1], 64, 1)
        sums.append(jnp.where(low, even, odd))
    dk_ref[...] = rope_lanes(sums[0], cos_ref[...], -sin_ref[...], first).astype(BF16)
    dv_ref[...] = sums[1].astype(BF16)


def run_attn_bwd(prefix, q, kd, vd, d_ctx, ctx, lse, cos, sin, cos_t, sin_t, sums=None):
    length, nq = q.shape
    groups = nq // 256
    col = lambda g: (0, g)
    wide = spec((length, 256), col)
    in_specs = [pl.BlockSpec(memory_space=pltpu.SMEM)] + [wide] * 5
    in_specs += [spec((1, 8, length), lambda g: (g, 0, 0))]
    in_specs += [whole((length, 128))] * 2 + [whole((cos_t.shape[0], length))] * 2
    out_specs = [wide, spec((length, 128), col), spec((length, 128), col)]
    out_shape = [
        jax.ShapeDtypeStruct((length, nq), BF16),
        jax.ShapeDtypeStruct((length, nq // 2), BF16),
        jax.ShapeDtypeStruct((length, nq // 2), BF16),
    ]
    scratch = [
        pltpu.VMEM((2, length, 128), F32),
        pltpu.VMEM((2, length, 128), F32),
        pltpu.VMEM((2, 128, length), BF16),
    ]
    args = (prefix, q, kd, vd, d_ctx, ctx, lse, cos, sin, cos_t, sin_t)
    kernel, extra = attn_bwd_kernel, {}
    if sums is not None:
        kernel, extra = attn_bwd_sum_kernel, {"collective_id": 3, "has_side_effects": True}
        hbm = pl.BlockSpec(memory_space=pl.ANY)
        keep_a = sums[2]
        _, count, rows, lanes = keep_a.shape
        made = [(count, rows, lanes)] * 2 + [(count, rows // 2, 2 * lanes)]
        in_specs += [hbm] * 4
        out_specs += [whole(shape) for shape in made]
        out_shape += [jax.ShapeDtypeStruct(shape, F32) for shape in made]
        scratch += line_scratch(keep_a.shape)
        scratch += [
            pltpu.VMEM(keep_a.shape, BF16),
            pltpu.SemaphoreType.DMA((6,)),
        ]
        args += tuple(sums)
    return pl.pallas_call(
        kernel,
        grid=(groups,),
        in_specs=in_specs,
        out_specs=out_specs,
        out_shape=out_shape,
        scratch_shapes=scratch,
        compiler_params=pltpu.CompilerParams(
            dimension_semantics=("arbitrary",), vmem_limit_bytes=60 * MIB, **extra
        ),
        cost_estimate=took(33),
        name="attn_bwd",
    )(*args)


def mid_kernel(tok_ref, ctx_ref, w_ref, gain_ref, res_ref, x_ref):
    res = tok_ref[...].astype(F32) + dot(ctx_ref[...], w_ref[...])
    res_ref[...] = res
    r = lax.rsqrt(jnp.mean(res * res, axis=1, keepdims=True) + EPS)
    x_ref[...] = (res * r * gain_ref[...].astype(F32)).astype(BF16)


def run_mid(tok, ctx, w_all, gain, at):
    length, d = tok.shape
    b = 256
    row = lambda i: (i, 0)
    return pl.pallas_call(
        mid_kernel,
        grid=(length // b,),
        in_specs=[
            spec((b, d), row),
            spec((b, ctx.shape[1]), row),
            spec((w_all.shape[0], d), lambda i: (0, at)),
            whole((1, d)),
        ],
        out_specs=[spec((b, d), row)] * 2,
        out_shape=[
            jax.ShapeDtypeStruct((length, d), F32),
            jax.ShapeDtypeStruct((length, d), BF16),
        ],
        compiler_params=params(60),
        cost_estimate=took(4),
        name="mid",
    )(tok, ctx, w_all, gain)


def gates_of(x, router, routes_t, num_experts):
    logits = dot(x, router).T[: 16 * pl.cdiv(num_experts, 16)]
    expert = lax.broadcasted_iota(jnp.int32, logits.shape, 0)
    hit = expert == routes_t[0:1]
    for k in range(1, routes_t.shape[0]):
        hit = hit | (expert == routes_t[k : k + 1])
    logits = jnp.where(hit, logits, NEG)
    e = jnp.exp(logits - jnp.max(logits, axis=0, keepdims=True))
    e = jnp.where(hit, e, 0.0)
    return e / jnp.sum(e, axis=0, keepdims=True)


def expert_kernel(
    first_expert, local, num_experts, with_init, me_ref, x_ref, c_ref, route_ref, router_ref, wg_ref, wu_ref, wd_ref, *refs
):
    if with_init:
        out_in, dx_in, dg_in, refs = refs[0], refs[1], refs[2], refs[3:]
        out_ref, dx_ref, dg_ref, hs_ref, dgate_ref, dup_ref, out_acc, dx_acc, gp_ref, dgc_ref = refs
    else:
        out_ref, dx_ref, dg_ref, hs_ref, dgate_ref, dup_ref, xt_ref, ct_ref, out_acc, dx_acc, gp_ref, dgc_ref = refs
    e = pl.program_id(1)
    last = pl.num_programs(1) - 1
    x, c = x_ref[...], c_ref[...]
    b = x.shape[0]
    lane = lax.broadcasted_iota(jnp.int32, (b, 128), 1)

    @pl.when(e == 0)
    def _():
        gates = gates_of(x, router_ref[...], route_ref[...], num_experts)
        fill = jnp.zeros((128 - gates.shape[0], b), F32)
        gp_ref[...] = jnp.concatenate([gates, fill], axis=0).T
        dgc_ref[...] = jnp.zeros_like(dgc_ref)
        if with_init:
            out_acc[...] = out_in[...].astype(F32)
            dx_acc[...] = dx_in[...].astype(F32)
        else:
            out_acc[...] = jnp.zeros_like(out_acc)
            dx_acc[...] = jnp.zeros_like(dx_acc)
            xt_ref[...] = x.T
            ct_ref[...] = c.T

    gp = jnp.sum(
        jnp.where(lane == me_ref[0] * local + first_expert + e, gp_ref[...], 0.0),
        axis=1,
        keepdims=True,
    )
    gate = dot(x, wg_ref[0])
    up = dot(x, wu_ref[0])
    grad = dot_t(c, wd_ref[0])
    sig = 0.5 * jnp.tanh(0.5 * gate) + 0.5
    act = gate * sig
    hidden = (act * up).astype(BF16).astype(F32)
    dg = jnp.sum(hidden * grad, axis=1, keepdims=True)
    hs = (hidden * gp).astype(BF16)
    dh = grad * gp
    dup = (dh * act).astype(BF16)
    dgate = (dh * up * (sig + act * (1.0 - sig))).astype(BF16)
    hs_ref[...] = hs
    dup_ref[...] = dup
    dgate_ref[...] = dgate
    out = dot(hs, wd_ref[0])
    dx = dot_t(dgate, wg_ref[0]) + dot_t(dup, wu_ref[0])
    dgc_ref[...] += jnp.where(lane == first_expert + e, dg, 0.0)

    @pl.when(e < last)
    def _():
        out_acc[...] += out
        dx_acc[...] += dx

    @pl.when(e == last)
    def _():
        out_ref[...] = (out_acc[...] + out).astype(BF16)
        dx_ref[...] = (dx_acc[...] + dx).astype(BF16)
        dg_t = dgc_ref[...].T[:8]
        dg_ref[...] = dg_t + dg_in[...] if with_init else dg_t


def run_expert(me, x, c, routes_t, router, wg, wu, wd, first, count, num_experts, init=None):
    length, d = x.shape
    local, _, ff = wg.shape
    b = 512
    top = routes_t.shape[0]
    row = lambda i, e: (i, 0)
    col_t = lambda i, e: (0, i)
    pick = lambda shape: pl.BlockSpec((1,) + shape[1:], lambda i, e: (first + e, 0, 0))
    wide = jax.ShapeDtypeStruct((length, count * ff), BF16)
    full = jax.ShapeDtypeStruct((length, d), BF16)
    turned = jax.ShapeDtypeStruct((d, length), BF16)
    wide_spec = spec((b, ff), lambda i, e: (i, e))
    with_init = init is not None
    return pl.pallas_call(
        functools.partial(expert_kernel, first, local, num_experts, with_init),
        grid=(length // b, count),
        in_specs=[
            pl.BlockSpec(memory_space=pltpu.SMEM),
            spec((b, d), row),
            spec((b, d), row),
            spec((top, b), col_t),
            pl.BlockSpec(
                (d, 128),
                lambda i, e: (0, router.shape[1] // 128 - 1),
                pipeline_mode=pl.Buffered(1),
            ),
            pick(wg.shape),
            pick(wu.shape),
            pick(wd.shape),
        ]
        + ([spec((b, d), row)] * 2 + [spec((8, b), col_t)] if with_init else []),
        out_specs=[spec((b, d), row)] * 2
        + [spec((8, b), col_t)]
        + [wide_spec] * 3
        + ([] if with_init else [spec((d, b), col_t)] * 2),
        out_shape=[full, full, jax.ShapeDtypeStruct((8, length), F32), wide, wide, wide]
        + ([] if with_init else [turned, turned]),
        scratch_shapes=[
            pltpu.VMEM((b, d), F32),
            pltpu.VMEM((b, d), F32),
            pltpu.VMEM((b, 128), F32),
            pltpu.VMEM((b, 128), F32),
        ],
        compiler_params=params(60, 2),
        cost_estimate=took(12 * count),
        name="experts",
    )(me, x, c, routes_t, router, wg, wu, wd, *(init if with_init else ()))


def weight_grad_kernel(n, paired, dp_ref, *refs):
    xt, ct, dgate, dup, hs = (refs[k * n : (k + 1) * n] for k in range(5))

    def total(lefts, rights):
        acc = None
        for left, right in zip(lefts, rights):
            part = dot(left[...], right[...])
            acc = part if acc is None else acc + part
        return acc

    down = total(ct, hs).T.astype(BF16)
    gate = total(xt, dgate).astype(BF16)
    up = total(xt, dup).astype(BF16)
    if paired:
        keep_ref, send_ref, down_keep_ref, down_send_ref = refs[5 * n :]
        first = dp_ref[0] % 2 == 0

        def parts(value, z, rows):
            even = value[2 * z * rows : (2 * z + 1) * rows]
            odd = value[(2 * z + 1) * rows : (2 * z + 2) * rows]
            return jnp.where(first, even, odd), jnp.where(first, odd, even)

        for z in range(keep_ref.shape[0]):
            for k, value in enumerate((gate, up)):
                keep_ref[z, k, 0], send_ref[z, k, 0] = parts(value, z, keep_ref.shape[3])
        for z in range(down_keep_ref.shape[0]):
            rows = down_keep_ref.shape[2]
            down_keep_ref[z, 0], down_send_ref[z, 0] = parts(down, z, rows)
        return
    gate_ref, up_ref, down_ref = refs[5 * n :]
    for p in range(down_ref.shape[0]):
        rows = down_ref.shape[3]
        down_ref[p, 0, 0] = down[p * rows : (p + 1) * rows]
    for p in range(gate_ref.shape[0]):
        rows = gate_ref.shape[2]
        gate_ref[p, 0] = gate[p * rows : (p + 1) * rows]
        up_ref[p, 0] = up[p * rows : (p + 1) * rows]


def run_weight_grad(dp, xt, ct, dgate, dup, hs, count, skips, n_dp, paired):
    n = len(xt)
    d, length = xt[0].shape
    ff = hs[-1].shape[1] // count
    m = 512 if paired else 256
    left = spec((m, length), lambda e, i: (i, 0))
    rights = [
        spec((length, ff), functools.partial(lambda skip, e, i: (0, e + skip), skip))
        for skip in skips
    ]
    per = d // n_dp
    down_at = lambda e, i: (0, e, i // (ff // m), 0, i % (ff // m))
    if paired:
        row_spec = spec((m // (2 * per), 2, 1, per, ff), lambda e, i: (i, 0, e, 0, 0))
        rows = jax.ShapeDtypeStruct((n_dp // 2, 2, count, per, ff), BF16)
        down_spec = spec((n_dp // 2, 1, ff // n_dp, m), lambda e, i: (0, e, i, 0))
        down = jax.ShapeDtypeStruct((n_dp // 2, count, ff // n_dp * (d // ff), ff), BF16)
        out_specs, out_shape = [row_spec] * 2 + [down_spec] * 2, [rows] * 2 + [down] * 2
    else:
        row_spec = spec((m // per, 1, per, ff), lambda e, i: (i, e, 0, 0))
        rows = jax.ShapeDtypeStruct((n_dp, count, per, ff), BF16)
        down_spec = spec((n_dp, 1, 1, ff // n_dp, m), down_at)
        down = jax.ShapeDtypeStruct((n_dp, count, d // ff, ff // n_dp, ff), BF16)
        out_specs, out_shape = [row_spec] * 2 + [down_spec], [rows] * 2 + [down]
    return pl.pallas_call(
        functools.partial(weight_grad_kernel, n, paired),
        grid=(count, d // m),
        in_specs=[pl.BlockSpec(memory_space=pltpu.SMEM)] + [left] * (2 * n) + rights * 3,
        out_specs=out_specs,
        out_shape=out_shape,
        compiler_params=params(60, 2),
        cost_estimate=took(37),
        name="weight_grad",
    )(dp, *xt, *ct, *dgate, *dup, *hs)


def back_mid_kernel(n, n_ex, local, *refs):
    (me_ref, res_ref, cot_ref, route_ref, x_ref, router_ref, gain_ref, w_ref) = refs[:8]
    dx_refs, dg_refs = refs[8 : 8 + n], refs[8 + n : 8 + n + n_ex]
    dres_ref, dattn_ref, dctx_ref, dlog_ref, ggain_ref = refs[8 + n + n_ex :]
    gp = gates_of(x_ref[...], router_ref[...], route_ref[...], n_ex * local)
    parts = [ref[...][:local] for ref in dg_refs]
    owners = []
    for owner in range(n_ex):
        own = jnp.zeros_like(parts[0])
        for step in range(n_ex):
            own = jnp.where((owner ^ step) == me_ref[0], parts[step], own)
        owners.append(own)
    dg = jnp.concatenate(owners, axis=0)
    d_logits = gp * (dg - jnp.sum(gp * dg, axis=0, keepdims=True))
    fill = jnp.zeros((128 - dg.shape[0], dg.shape[1]), F32)
    d_logits = jnp.concatenate([d_logits, fill], axis=0).T.astype(BF16)
    dlog_ref[...] = d_logits
    d_norm = dot_t(d_logits, router_ref[...])
    for ref in dx_refs:
        d_norm = d_norm + ref[...].astype(F32)
    res = res_ref[...]
    r = lax.rsqrt(jnp.mean(res * res, axis=1, keepdims=True) + EPS)
    xr = res * r
    part = jnp.sum(d_norm * xr, axis=0, keepdims=True)

    @pl.when(pl.program_id(0) == 0)
    def _():
        ggain_ref[...] = jnp.zeros_like(ggain_ref)

    ggain_ref[...] += part
    u = d_norm * gain_ref[...].astype(F32)
    d_res = (
        cot_ref[...].astype(F32) + r * u - xr * (r * r) * jnp.mean(u * res, axis=1, keepdims=True)
    )
    dres_ref[...] = d_res
    d_attn = d_res.astype(BF16)
    dattn_ref[...] = d_attn
    dctx_ref[...] = dot_t(d_attn, w_ref[...]).astype(BF16)


def run_back_mid(me, res, cot, routes_t, x, w_all, gain, at, dxs, dgs, local):
    length, d = res.shape
    b = 256
    row = lambda i: (i, 0)
    n, n_ex = len(dxs), len(dgs)
    return pl.pallas_call(
        functools.partial(back_mid_kernel, n, n_ex, local),
        grid=(length // b,),
        in_specs=[
            pl.BlockSpec(memory_space=pltpu.SMEM),
            spec((b, d), row),
            spec((b, d), row),
            spec((routes_t.shape[0], b), lambda i: (0, i)),
            spec((b, d), row),
            spec((d, 128), lambda i: (0, w_all.shape[1] // 128 - 1)),
            whole((1, d)),
            spec((d, d), lambda i: (0, at)),
        ]
        + [spec((b, d), row)] * n
        + [spec((8, b), lambda i: (0, i))] * n_ex,
        out_specs=[
            spec((b, d), row),
            spec((b, d), row),
            spec((b, d), row),
            spec((b, 128), row),
            whole((1, d)),
        ],
        out_shape=[
            jax.ShapeDtypeStruct((length, d), F32),
            jax.ShapeDtypeStruct((length, d), BF16),
            jax.ShapeDtypeStruct((length, d), BF16),
            jax.ShapeDtypeStruct((length, 128), BF16),
            jax.ShapeDtypeStruct((1, d), F32),
        ],
        compiler_params=params(60),
        cost_estimate=took(11),
        name="back_mid",
    )(me, res, cot, routes_t, x, w_all, gain, w_all, *dxs, *dgs)


def back_in_kernel(dq_ref, dk_ref, dv_ref, w_ref, tok_ref, gain_ref, dres_ref, gt_ref, ggain_ref):
    nq, nk = dq_ref.shape[1], dk_ref.shape[1]
    d_norm = dot_t(dq_ref[...], w_ref[:, :nq])
    d_norm = d_norm + dot_t(dk_ref[...], w_ref[:, nq : nq + nk])
    d_norm = d_norm + dot_t(dv_ref[...], w_ref[:, nq + nk : nq + 2 * nk])
    x = tok_ref[...].astype(F32)
    r = lax.rsqrt(jnp.mean(x * x, axis=1, keepdims=True) + EPS)
    xr = x * r
    part = jnp.sum(d_norm * xr, axis=0, keepdims=True)

    @pl.when(pl.program_id(0) == 0)
    def _():
        ggain_ref[...] = jnp.zeros_like(ggain_ref)

    ggain_ref[...] += part
    u = d_norm * gain_ref[...].astype(F32)
    gt_ref[...] = dres_ref[...] + r * u - xr * (r * r) * jnp.mean(u * x, axis=1, keepdims=True)


def run_back_in(dq, dk, dv, w_qkv, tok, gain, d_res):
    length, d = tok.shape
    b = 256
    row = lambda i: (i, 0)
    nq = dq.shape[1]
    return pl.pallas_call(
        back_in_kernel,
        grid=(length // b,),
        in_specs=[
            spec((b, nq), row),
            spec((b, dk.shape[1]), row),
            spec((b, dv.shape[1]), row),
            spec((d, 2 * nq), lambda i: (0, 0)),
            spec((b, d), row),
            whole((1, d)),
            spec((b, d), row),
        ],
        out_specs=[spec((b, d), row), whole((1, d))],
        out_shape=[jax.ShapeDtypeStruct((length, d), F32), jax.ShapeDtypeStruct((1, d), F32)],
        compiler_params=params(60),
        cost_estimate=took(10),
        name="back_in",
    )(dq, dk, dv, w_qkv, tok, gain, d_res)


CHUNKS = (3, 0, 1, 2)


def finish_kernel(
    ht_ref, dq_ref, dk_ref, dv_ref, dout_ref, small_ref, keep_ref, got_ref, down_keep_ref, down_got_ref,
    out_ref, gate_ref, up_ref, down_ref, *scratch,
):
    n = len(CHUNKS)
    lists = [scratch[k * n : (k + 1) * n] for k in range(8)]
    b1, r1, s1, r2, s2, r3, s3, r4 = lists
    sem_s, sem_r = scratch[8 * n : 8 * n + 2]
    line = Line(*scratch[8 * n + 2 : 8 * n + 8])
    rx, sem_l = scratch[8 * n + 8 :]
    dp, ex = lax.axis_index("dp"), lax.axis_index("expert")
    z, x, y, c = dp // 2, dp % 2, ex // 2, ex % 2
    over_core, over_y, over_x = (dp, ex ^ 1), (dp, ex ^ 2), (dp ^ 1, ex)
    along = [(dp ^ (2 * k), ex) for k in (1, 2, 3)]
    group = [over_core, over_y, (dp, ex ^ 3)]
    loads = []
    for k in range(3):
        keep, got = (down_keep_ref, down_got_ref) if k == 2 else (keep_ref.at[:, k], got_ref.at[:, k])
        loads.append(
            [
                pltpu.make_async_copy(keep, line.tot.at[k], sem_l.at[2 * k]),
                pltpu.make_async_copy(got, rx.at[k], sem_l.at[2 * k + 1]),
            ]
        )
        for copy in loads[k]:
            copy.start()
    greet(group + [over_x] + along)

    widths = [dout_ref.shape[1], dq_ref.shape[1], dk_ref.shape[1] + dv_ref.shape[1], 128]
    starts = [sum(widths[:k]) for k in range(n)]
    started = {}

    def send(k, slot, src, dst, peer):
        copy = pltpu.make_async_remote_copy(
            src_ref=src,
            dst_ref=dst,
            send_sem=sem_s.at[k, slot],
            recv_sem=sem_r.at[k, slot],
            device_id=peer,
            device_id_type=pl.DeviceIdType.MESH,
        )
        copy.start()
        started[k, slot] = copy

    def begin(k):
        for copy in loads[k]:
            copy.wait()
        for zz in range(4):
            for e in range(2):
                dst = line.tot.at[k, zz, e]
                add_rows(dst, [dst, rx.at[k, zz, e]])
        line.ends(k, True)

    def place(k, lanes, value):
        for p in range(8):
            for e in range(4):
                row = 128 * p + 32 * e
                b1[k][e % 2, e // 2, p % 2, p // 2, :, lanes] = value[row : row + 32]

    def step0(k):
        if k == 0:
            place(k, slice(0, widths[k]), dout_ref[...])
        elif k == 1:
            for col in range(0, widths[1], 512):
                part = dot(ht_ref[...], dq_ref[:, col : col + 512])
                place(k, slice(col, col + 512), part.astype(BF16))
        elif k == 2:
            half = dk_ref.shape[1]
            place(k, slice(0, half), dot(ht_ref[...], dk_ref[...]).astype(BF16))
            place(k, slice(half, 2 * half), dot(ht_ref[...], dv_ref[...]).astype(BF16))
        else:
            place(k, slice(0, 128), small_ref[...])
        send(k, 0, b1[k].at[1 - c], r1[k], over_core)

    def step1(k):
        started[k, 0].wait()
        for yy in range(2):
            for xx in range(2):
                for zz in range(4):
                    s1[k][yy, xx, zz] = (
                        b1[k][c, yy, xx, zz].astype(F32) + r1[k][yy, xx, zz].astype(F32)
                    ).astype(BF16)
        send(k, 1, s1[k].at[1 - y], r2[k], over_y)

    def step2(k):
        started[k, 1].wait()
        for xx in range(2):
            for zz in range(4):
                s2[k][xx, zz] = (
                    s1[k][y, xx, zz].astype(F32) + r2[k][xx, zz].astype(F32)
                ).astype(BF16)
        send(k, 2, s2[k].at[1 - x], r3[k].at[0], over_x)

    def step3(k):
        started[k, 2].wait()
        for zz in range(4):
            s3[k][zz] = (s2[k][x, zz].astype(F32) + r3[k][0, zz].astype(F32)).astype(BF16)
        for i in range(3):
            send(k, 3 + i, s3[k].at[z ^ (i + 1)], r3[k].at[1, i], along[i])

    def step4(k):
        for i in range(3):
            started[k, 3 + i].wait()
        total = s3[k][z].astype(F32)
        for i in range(3):
            total = total + r3[k][1, i].astype(F32)
        r4[k][3] = total.astype(BF16)
        for i in range(3):
            send(k, 6 + i, r4[k].at[3], r4[k].at[i], group[i])

    def step5(k):
        o = slice(starts[k], starts[k] + widths[k])
        out_ref[pl.ds(pl.multiple_of(ex * 32, 32), 32), o] = r4[k][3].astype(F32)
        for i in range(3):
            started[k, 6 + i].wait()
            rows = pl.ds(pl.multiple_of((ex ^ (i + 1)) * 32, 32), 32)
            out_ref[rows, o] = r4[k][i].astype(F32)

    done = (gate_ref, up_ref, down_ref)
    step0(3)
    step0(0)
    begin(0)
    step1(3)
    step1(0)
    step0(1)
    begin(1)
    step1(1)
    step0(2)
    begin(2)
    step1(2)
    step2(3)
    step2(0)
    line.middle_sends(0, True)
    step2(1)
    step3(3)
    step3(0)
    line.middle_sends(1, True)
    line.middle_adds(0, True)
    step2(2)
    step3(1)
    line.middle_sends(2, True)
    line.middle_adds(1, True)
    step4(3)
    step4(0)
    step3(2)
    line.result(0, done)
    line.middle_adds(2, True)
    step4(1)
    step5(3)
    step5(0)
    step4(2)
    line.result(1, done)
    line.result(2, done)
    step5(1)
    step5(2)


def run_finish(ht, dq, dk, dv, d_out, small, experts):
    widths = [d_out.shape[1], dq.shape[1], dk.shape[1] + dv.shape[1], small.shape[1]]
    chunk = experts[2].shape
    _, count, rows, lanes = chunk
    vmem = pl.BlockSpec(memory_space=pltpu.VMEM)
    hbm = pl.BlockSpec(memory_space=pl.ANY)
    shapes = [
        (2, 2, 2, 4, 32), (2, 2, 4, 32), (2, 2, 4, 32), (2, 4, 32), (2, 4, 32), (2, 4, 32), (4, 32), (4, 32),
    ]
    scratch = [pltpu.VMEM(shape + (w,), BF16) for shape in shapes for w in widths]
    scratch += [pltpu.SemaphoreType.DMA((len(widths), 9))] * 2
    scratch += line_scratch(chunk)
    scratch += [pltpu.VMEM((3,) + chunk, BF16), pltpu.SemaphoreType.DMA((6,))]
    return pl.pallas_call(
        finish_kernel,
        in_specs=[vmem] * 6 + [hbm] * 4,
        out_specs=[vmem] * 4,
        out_shape=[
            jax.ShapeDtypeStruct((128, sum(widths)), F32),
            jax.ShapeDtypeStruct((count, rows, lanes), F32),
            jax.ShapeDtypeStruct((count, rows, lanes), F32),
            jax.ShapeDtypeStruct((count, rows // 2, 2 * lanes), F32),
        ],
        scratch_shapes=scratch,
        compiler_params=pltpu.CompilerParams(
            vmem_limit_bytes=60 * MIB, collective_id=1, has_side_effects=True
        ),
        cost_estimate=took(60),
        name="finish",
    )(ht, dq, dk, dv, d_out, small, *experts)


def gather_kernel(mine_ref, out_ref, sem_s, sem_r, sem_l):
    dp, ex = lax.axis_index("dp"), lax.axis_index("expert")
    z = dp // 2
    core, over_y, over_x = (dp, ex ^ 1), (dp, ex ^ 2), (dp ^ 1, ex)
    line = [None] + [(dp ^ (2 * k), ex) for k in (1, 2, 3)]
    barrier = pltpu.get_barrier_semaphore()
    peers = [core, over_y, over_x] + line[1:]
    for peer in peers:
        pl.semaphore_signal(barrier, inc=1, device_id=peer, device_id_type=pl.DeviceIdType.MESH)
    pl.semaphore_wait(barrier, len(peers))
    rows = mine_ref.shape[0]
    width = mine_ref.shape[1]
    cut = (width // 256 + 1) * 128
    halves = [pl.ds(0, cut), pl.ds(cut, width - cut)]
    started = {}

    def block(k, dx, dy):
        at = (((z ^ k) * 2 + (dp % 2 ^ dx)) * 4 + (ex ^ (2 * dy))) * rows
        return pl.ds(pl.multiple_of(at, rows), rows)

    def send(key, k, dx, dy, peer, src=None, lanes=None):
        index = len(started)
        at = block(k, dx, dy)
        dst = out_ref.at[at] if lanes is None else out_ref.at[at, lanes]
        copy = pltpu.make_async_remote_copy(
            src_ref=dst if src is None else src,
            dst_ref=dst,
            send_sem=sem_s.at[index],
            recv_sem=sem_r.at[index],
            device_id=peer,
            device_id_type=pl.DeviceIdType.MESH,
        )
        copy.start()
        started[key] = copy

    for k in (3, 2, 1):
        send(("z", k), 0, 0, 0, line[k], mine_ref)
    send(("x", 0), 0, 0, 0, over_x, mine_ref)
    send(("y", 0), 0, 0, 0, over_y, mine_ref)
    send(("c", 0), 0, 0, 0, core, mine_ref)
    own = pltpu.make_async_copy(mine_ref, out_ref.at[block(0, 0, 0)], sem_l)
    own.start()

    def onward(k):
        started["x", k].wait_recv()
        send(("dy", k), k, 1, 0, over_y, None, halves[0])
        send(("cx", k), k, 1, 0, core)
        started["y", k].wait_recv()
        send(("dx", k), k, 0, 1, over_x, None, halves[1])
        send(("cy", k), k, 0, 1, core)

    def last(k):
        started["dy", k].wait_recv()
        started["dx", k].wait_recv()
        send(("cd", k), k, 1, 1, core)

    onward(0)
    for k in (1, 2, 3):
        started["z", k].wait_recv()
        send(("x", k), k, 0, 0, over_x)
        send(("y", k), k, 0, 0, over_y)
        send(("c", k), k, 0, 0, core)
    last(0)
    for k in (1, 2, 3):
        onward(k)
    for k in (1, 2, 3):
        last(k)
    for key, copy in started.items():
        copy.wait_send()
        if key[0] in ("c", "cx", "cy", "cd"):
            copy.wait_recv()
    own.wait()


def run_gather(mine, total):
    hbm = pl.BlockSpec(memory_space=pl.ANY)
    return pl.pallas_call(
        gather_kernel,
        in_specs=[hbm],
        out_specs=hbm,
        out_shape=jax.ShapeDtypeStruct((total, mine.shape[1]), BF16),
        scratch_shapes=[
            pltpu.SemaphoreType.DMA((40,)),
            pltpu.SemaphoreType.DMA((40,)),
            pltpu.SemaphoreType.DMA,
        ],
        compiler_params=pltpu.CompilerParams(collective_id=2, has_side_effects=True),
        cost_estimate=took(40),
        name="gather",
    )(mine)


def after(value, *deps):
    return lax.optimization_barrier((value,) + deps)[0]


def on_device(
    n_dp, n_ex, tokens, cotangent, routes, prefix, w_query, keyvalue_weight, w_out, w_router,
    gain_attn, gain_mlp, expert_gate, expert_up, expert_down, query_logit_cap,
):
    length, d = tokens.shape[1], tokens.shape[2]
    tok = tokens.reshape(length, d)
    cot = cotangent.reshape(length, d)
    heads = query_logit_cap.shape[0]
    nq = w_query.shape[1]
    head = nq // heads
    kv_heads = keyvalue_weight.shape[1] // (2 * head)
    num_experts = w_router.shape[1]
    local = expert_gate.shape[0]
    rows = w_query.shape[0]
    ex = lax.axis_index("expert")

    def swap(value, step, axis="expert", n=n_ex):
        return lax.ppermute(value, axis, [(i, i ^ step) for i in range(n)])

    part = rows // n_ex
    small = jnp.concatenate(
        [
            w_router,
            gain_attn[:, None],
            gain_mlp[:, None],
            jnp.zeros((rows, 128 - num_experts - 2), BF16),
        ],
        axis=1,
    )
    packed = jnp.concatenate([w_query, keyvalue_weight, w_out, small], axis=1)
    mine = lax.dynamic_slice_in_dim(packed, ex * part, part, axis=0)
    local = expert_gate.shape[0]
    fast = n_dp == 8 and n_ex == 4 and d == 1024 and local == 4 and expert_gate.shape[2] == 512
    if fast:
        every = run_gather(mine, d)
    else:
        every = lax.all_gather(mine, ("dp", "expert"), axis=0, tiled=True)
    w_all = every
    width = 2 * nq
    extra = every[:, width + d :]
    gain_one = extra[:, num_experts].reshape(1, d)
    gain_two = extra[:, num_experts + 1].reshape(1, d)

    routes_t = after(routes.reshape(length, -1).T, every)
    cots = {0: cot}
    route_set = {0: routes_t}
    for step in range(1, n_ex):
        route_set[step] = swap(routes_t, step)
    cot_late = after(cot, every, *route_set.values())
    for step in range(1, n_ex):
        if step == 1 or step % 2 == 0:
            cots[step] = swap(cot_late, step)

    cos_np, sin_np = rope_tables(length, head)
    cos_l = jnp.asarray(np.concatenate([cos_np] * 4, axis=1))
    sin_l = jnp.asarray(np.concatenate([-sin_np, sin_np] * 2, axis=1))
    cos_t = jnp.asarray(np.ascontiguousarray(cos_np.T))
    sin_t = jnp.asarray(np.ascontiguousarray(sin_np.T))

    normed_one_t, q, kd, vd = run_qkv(tok, gain_one, w_all, cos_l, sin_l, nq)
    ctx, lse, peaks = run_attn_fwd(prefix, q, kd, vd)
    resid, normed_two = run_mid(tok, ctx, w_all, gain_two, width // d)

    me = ex.reshape(1).astype(jnp.int32)
    xs = {0: normed_two}
    for step in range(1, n_ex):
        if step == 1 or step % 2 == 0:
            xs[step] = swap(normed_two, step)
    tops = [peaks[:, :, :4]]
    bits = [("expert", n_ex, 1 << i) for i in range(n_ex.bit_length() - 1)]
    bits += [("dp", n_dp, 1 << i) for i in range(n_dp.bit_length() - 1)]

    def widen_top():
        if len(tops) <= len(bits):
            axis, n, step = bits[len(tops) - 1]
            top = after(tops[-1], chain)
            tops.append(jnp.maximum(top, swap(top, step, axis, n)))

    weights = (expert_gate, expert_up, expert_down)
    half = local // 2

    dp = lax.axis_index("dp").reshape(1).astype(jnp.int32)

    res = {}
    chain = (normed_two, [cots[step] for step in range(2, n_ex, 2)])

    def experts(step, first, count, init=None):
        x = after(xs[step], chain)
        return run_expert(
            me, x, cots[step], route_set[step], w_all, *weights, first, count, num_experts, init
        )

    def grads(first):
        skips = [first if step < 2 else 0 for step in range(n_ex)]
        pieces = [
            [res[step, 0 if step < 2 else first][k] for step in range(n_ex)] for k in (4, 5, 3)
        ]
        turned = [[res[step, 0][k] for step in range(n_ex)] for k in (6, 7)]
        turned[0][0] = after(turned[0][0], chain)
        made = None
        for at in range(0, n_ex, 4):
            some = [group[at : at + 4] for group in turned + pieces]
            part = run_weight_grad(dp, *some, half, skips[at : at + 4], n_dp, fast)
            if made is None:
                made = part
            else:
                made = [(a.astype(F32) + b.astype(F32)).astype(BF16) for a, b in zip(made, part)]
        return made

    for step in range(2):
        res[step, 0] = experts(step, 0, local)
        chain = (res[step, 0][0], tops[-1])
        widen_top()
        if step == 0:
            for other in range(3, n_ex, 2):
                cots[other] = swap(after(cots[other - 1], chain), 1)
                xs[other] = swap(after(xs[other - 1], chain), 1)
    odd, even = range(3, n_ex, 2), range(2, n_ex, 2)
    for step in [*odd, *even]:
        res[step, 0] = experts(step, 0, half)
        chain = (res[step, 0][0], tops[-1])
        widen_top()
    made_one = grads(0)
    chain = (made_one[0], tops[-1])
    got_one = [swap(made_one[k], 1, "dp", n_dp) for k in (1, 3)] if fast else []
    widen_top()
    for step in odd:
        res[step, half] = experts(step, half, half, res[step, 0][:3])
        chain = (res[step, half][0], tops[-1])
        widen_top()
    partner = {step - 1: [swap(res[step, half][k], 1) for k in (0, 1)] for step in odd}
    for step in even:
        res[step, half] = experts(step, half, half, res[step, 0][:3])
        chain = (res[step, half][0], tops[-1])
        widen_top()

    def with_partner(step, index):
        own, other = res[step, half][index], partner[step][index]
        return (own.astype(F32) + other.astype(F32)).astype(BF16)

    to_send = {step: with_partner(step, 1) for step in even}
    chain = (chain, list(to_send.values()))
    sums, got_two = None, []
    if fast:
        tot_one = (made_one[0].astype(F32) + got_one[0].astype(F32)).astype(BF16)
        far_one = lax.dynamic_slice_in_dim(tot_one, 2 * (1 - dp[0] // 4), 2, axis=0)
        chain = (chain, far_one)
        far_one = lax.ppermute(far_one, "dp", [(0, 2), (1, 3), (6, 4), (7, 5)])
    made_two = grads(half)
    chain = (made_two[0], got_one, tops[-1])
    if fast:
        chain = (chain, far_one)
        sums = [tot_one, far_one, made_one[2], got_one[1]]
        got_two = [swap(made_two[k], 1, "dp", n_dp) for k in (1, 3)]
    while len(tops) <= len(bits):
        widen_top()
    top = tops[-1]

    last = [res[step, 0 if step < 2 else half] for step in range(n_ex)]
    dxs = [last[0][1], swap(last[1][1], 1)] + [swap(to_send[step], step) for step in even]
    dgs = [last[0][2]] + [swap(last[step][2], step) for step in range(1, n_ex)]
    d_res, d_attn, d_ctx, d_logits, d_gain_two = run_back_mid(
        me,
        after(resid, chain),
        cot,
        routes_t,
        normed_two,
        w_all,
        gain_two,
        width // d,
        dxs,
        dgs,
        local,
    )
    outs = [last[0][0], swap(last[1][0], 1)]
    outs += [swap(after(with_partner(step, 0), dxs), step) for step in even]
    block = resid
    for piece in outs:
        block = block + piece.astype(F32)
    block_out = block.astype(BF16).reshape(tokens.shape)

    d_out_w = jnp.einsum("rc,rd->cd", ctx, d_attn, preferred_element_type=F32).astype(BF16)
    d_router_w = jnp.einsum("rd,re->de", normed_two, d_logits, preferred_element_type=F32)

    dq, dk, dv, *halves = run_attn_bwd(
        prefix, after(q, top), kd, vd, d_ctx, ctx, lse, cos_l, sin_l, cos_t, sin_t, sums
    )
    grad_tok, d_gain_one = run_back_in(
        after(dq, block_out, got_two), dk, dv, w_all, tok, gain_one, d_res
    )
    small_grad = jnp.concatenate(
        [
            d_router_w[:, :num_experts].astype(BF16),
            d_gain_one.reshape(d, 1).astype(BF16),
            d_gain_two.reshape(d, 1).astype(BF16),
            jnp.zeros((d, 128 - num_experts - 2), BF16),
        ],
        axis=1,
    )

    def reduce_all(value, order):
        shape = (n_dp, n_ex, value.shape[0] // (n_dp * n_ex), value.shape[1])
        names = []
        dims = []
        for axis, n in (("dp", n_dp), ("expert", n_ex)):
            count = n.bit_length() - 1
            names += [(axis, n, 1 << (count - 1 - i)) for i in range(count)]
            dims += [2] * count
        value = value.reshape(*dims, *shape[2:])
        for bit in order:
            at = names.index(bit)
            axis, n, step = bit
            mine = (lax.axis_index(axis) // step) % 2
            keep = lax.dynamic_slice_in_dim(value, mine, 1, axis=at)
            send = lax.dynamic_slice_in_dim(value, 1 - mine, 1, axis=at)
            value = (keep.astype(F32) + swap(send, step, axis, n).astype(F32)).astype(BF16)
        return value.reshape(shape[2:])

    def share(value):
        return lax.all_gather(value, "expert", axis=0, tiled=True).astype(F32)

    core = [("expert", n_ex, 1)]
    y_bits = [("expert", n_ex, 1 << i) for i in range(1, n_ex.bit_length() - 1)][::-1]
    dp_bits = [("dp", n_dp, 1 << i) for i in range(n_dp.bit_length() - 1)]
    if fast:
        every_grad, *others = run_finish(
            normed_one_t,
            dq,
            dk,
            dv,
            d_out_w,
            small_grad,
            [made_two[0], got_two[0], made_two[2], got_two[1]],
        )
        grad_gate, grad_up, grad_down = (
            jnp.concatenate([halves[k], others[k]], axis=0) for k in range(3)
        )
    else:
        ends = [
            [
                lax.psum_scatter(g, "dp", scatter_dimension=0, tiled=True)[0].astype(F32)
                for g in made
            ]
            for made in (made_one, made_two)
        ]
        grad_gate, grad_up, grad_down = (
            jnp.concatenate([ends[0][k], ends[1][k]], axis=0) for k in range(3)
        )
        grad_down = jnp.swapaxes(grad_down, 1, 2).reshape(local, -1, d)

        def product(right):
            return jnp.dot(normed_one_t, right, preferred_element_type=F32).astype(BF16)

        every_grad = jnp.concatenate(
            [d_out_w, product(dq), product(dk), product(dv), small_grad], axis=1
        )
        every_grad = share(reduce_all(every_grad, core + y_bits + dp_bits[::-1]))
    grad_out = every_grad[:, :d]
    grad_query = every_grad[:, d : d + nq]
    grad_keyval = every_grad[:, d + nq : d + 2 * nq]
    grad_router = every_grad[:, d + 2 * nq : d + 2 * nq + num_experts]
    grad_gain_one = every_grad[:, d + 2 * nq + num_experts]
    grad_gain_two = every_grad[:, d + 2 * nq + num_experts + 1]

    head_logit_peak = top[:, 0, :].reshape(heads)
    per_group = heads // kv_heads
    query_factor = jnp.sqrt(query_logit_cap / jnp.maximum(head_logit_peak, query_logit_cap))
    pair_peak = jnp.max(head_logit_peak.reshape(kv_heads, per_group), axis=1)
    pair_cap = jnp.min(query_logit_cap.reshape(kv_heads, per_group), axis=1)
    key_factor = jnp.sqrt(pair_cap / jnp.maximum(pair_peak, pair_cap))
    clipped_query = (w_query.astype(F32) * jnp.repeat(query_factor, head)[None, :]).astype(BF16)
    key_cols = jnp.concatenate(
        [jnp.repeat(key_factor, head), jnp.ones((kv_heads * head,), F32)]
    )
    clipped_keyval = (keyvalue_weight.astype(F32) * key_cols[None, :]).astype(BF16)
    return (
        block_out,
        grad_tok.reshape(tokens.shape),
        grad_query,
        grad_keyval,
        grad_out,
        grad_router,
        grad_gain_one,
        grad_gain_two,
        grad_gate,
        grad_up,
        grad_down,
        clipped_query,
        clipped_keyval,
        head_logit_peak,
    )


def solution(mesh):
    rows3 = P(("dp", "expert"), None, None)
    in_specs = (
        rows3,
        rows3,
        rows3,
        P(("dp", "expert")),
        P("dp", None),
        P("dp", None),
        P("dp", None),
        P("dp", None),
        P("dp"),
        P("dp"),
        P("expert", None, None),
        P("expert", None, None),
        P("expert", None, None),
        P(),
    )
    out_specs = (
        rows3,
        rows3,
        P("dp", None),
        P("dp", None),
        P("dp", None),
        P("dp", None),
        P("dp"),
        P("dp"),
        P("expert", "dp", None),
        P("expert", "dp", None),
        P("expert", "dp", None),
        P("dp", None),
        P("dp", None),
        P(),
    )
    return jax.shard_map(
        functools.partial(on_device, mesh.shape["dp"], mesh.shape["expert"]),
        mesh=mesh,
        in_specs=in_specs,
        out_specs=out_specs,
        check_vma=False,
    )
```

```python
import functools

import jax
import jax.numpy as jnp
import numpy as np
from jax import lax
from jax.experimental import pallas as pl
from jax.experimental.pallas import tpu as pltpu
from jax.sharding import PartitionSpec as P

EPS = 1e-05
ROPE_BASE = 10000.0
F32 = jnp.float32
BF16 = jnp.bfloat16
NEG = -1e30
MIB = 1 << 20
SCALE = 0.35


def dot(a, b):
    return lax.dot_general(a, b, (((1,), (0,)), ((), ())), preferred_element_type=F32)


def dot_t(a, b):
    return lax.dot_general(a, b, (((1,), (1,)), ((), ())), preferred_element_type=F32)


def params(vmem_mib, n=1):
    return pltpu.CompilerParams(
        dimension_semantics=("arbitrary",) * n, vmem_limit_bytes=vmem_mib * MIB
    )


def took(us):
    return pl.CostEstimate(flops=int(us * SCALE * 1e9), bytes_accessed=1000, transcendentals=0)


def spec(shape, index):
    return pl.BlockSpec(shape, index)


def whole(shape):
    zeros = (0,) * len(shape)
    return pl.BlockSpec(shape, lambda *_: zeros)


def rope_tables(length, head):
    half = head // 2
    freq = np.float32(ROPE_BASE) ** (
        -(np.arange(half, dtype=np.float32) * np.float32(2.0) / np.float32(head))
    )
    ang = np.arange(length, dtype=np.float32)[:, None] * freq.astype(np.float32)[None, :]
    ang = ang.astype(np.float32)
    return np.cos(ang).astype(np.float32), np.sin(ang).astype(np.float32)


def lane_half(shape, width):
    return (lax.broadcasted_iota(jnp.int32, shape, 1) % width) < (width // 2)


def rope_lanes(x, cos, sin, first):
    partner = jnp.where(first, pltpu.roll(x, 96, 1), pltpu.roll(x, 32, 1))
    return x * cos + partner * sin


def qkv_kernel(tok_ref, gain_ref, w_ref, cos_ref, sin_ref, ht_ref, q_ref, kd_ref, vd_ref):
    x = tok_ref[...].astype(F32)
    d = x.shape[1]
    r = lax.rsqrt(jnp.mean(x * x, axis=1, keepdims=True) + EPS)
    h = (x * r * gain_ref[...].astype(F32)).astype(BF16)
    ht_ref[...] = h.T
    cos, sin = cos_ref[...], sin_ref[...]
    rows = x.shape[0]
    first = lane_half((rows, 128), 64)
    low = lane_half((rows, 128), 128)
    nq = q_ref.shape[1]
    nk = kd_ref.shape[1] // 2
    q = dot(h, w_ref[:, :nq])
    for c in range(0, nq, 128):
        q_ref[:, c : c + 128] = (rope_lanes(q[:, c : c + 128], cos, sin, first) * 0.125).astype(
            BF16
        )
    k = dot(h, w_ref[:, nq : nq + nk])
    for c in range(0, nk, 128):
        kk = rope_lanes(k[:, c : c + 128], cos, sin, first)
        sw = pltpu.roll(kk, 64, 1)
        kd_ref[:, 2 * c : 2 * c + 128] = jnp.where(low, kk, sw).astype(BF16)
        kd_ref[:, 2 * c + 128 : 2 * c + 256] = jnp.where(low, sw, kk).astype(BF16)
    v = dot(h, w_ref[:, nq + nk : nq + 2 * nk])
    for c in range(0, nk, 128):
        vv = v[:, c : c + 128]
        sw = pltpu.roll(vv, 64, 1)
        vd_ref[:, 2 * c : 2 * c + 128] = jnp.where(low, vv, sw).astype(BF16)
        vd_ref[:, 2 * c + 128 : 2 * c + 256] = jnp.where(low, sw, vv).astype(BF16)


def run_qkv(tok, gain, w_qkv, cos, sin, nq):
    length, d = tok.shape
    b = 256
    row = lambda i: (i, 0)
    return pl.pallas_call(
        qkv_kernel,
        grid=(length // b,),
        in_specs=[
            spec((b, d), row),
            whole((1, d)),
            spec((d, 2 * nq), lambda i: (0, 0)),
            spec((b, 128), row),
            spec((b, 128), row),
        ],
        out_specs=[spec((d, b), lambda i: (0, i))] + [spec((b, nq), row)] * 3,
        out_shape=[jax.ShapeDtypeStruct((d, length), BF16)]
        + [jax.ShapeDtypeStruct((length, nq), BF16)] * 3,
        compiler_params=params(60),
        cost_estimate=took(9),
        name="qkv",
    )(tok, gain, w_qkv, cos, sin)


def mask_bias(prefix, q0, k0, nq, nk, q_axis):
    shape = (nq, nk) if q_axis == 0 else (nk, nq)
    qpos = q0 + lax.broadcasted_iota(jnp.int32, shape, q_axis)
    kpos = k0 + lax.broadcasted_iota(jnp.int32, shape, 1 - q_axis)
    return jnp.where((kpos <= qpos) | (kpos < prefix), 0.0, NEG).astype(F32)


def two_heads(pair, low):
    zero = jnp.zeros_like(pair)
    return jnp.concatenate([jnp.where(low, pair, zero), jnp.where(low, zero, pair)], axis=0)


def attn_fwd_kernel(prefix_ref, q_ref, kd_ref, vd_ref, ctx_ref, lse_ref, peak_ref):
    length = q_ref.shape[0]
    b = 256
    prefix = prefix_ref[0]
    low_b = lane_half((b, 128), 128)
    lane = lax.broadcasted_iota(jnp.int32, (b, 128), 1)
    peak = jnp.full((8, 128), NEG, F32)
    peak_lane = lax.broadcasted_iota(jnp.int32, (8, 128), 1)
    for i in range(length // b):
        nk = max((i + 1) * b, length // 2)
        free = i * b
        bias = mask_bias(prefix, i * b, free, b, nk - free, 0)
        bias = jnp.concatenate([bias, bias], axis=0)
        lse_cols = jnp.zeros((b, 128), F32)
        for j in range(2):
            cols = slice(j * 128, (j + 1) * 128)
            q2 = two_heads(q_ref[i * b : (i + 1) * b, cols], low_b)
            s_hi = dot_t(q2, kd_ref[free:nk, cols]) + bias
            m = jnp.max(s_hi, axis=1, keepdims=True)
            if free:
                s_lo = dot_t(q2, kd_ref[:free, cols])
                m = jnp.maximum(m, jnp.max(s_lo, axis=1, keepdims=True))
            p_hi = jnp.exp(s_hi - m)
            total = jnp.sum(p_hi, axis=1, keepdims=True)
            ctx = dot(p_hi.astype(BF16), vd_ref[free:nk, cols])
            if free:
                p_lo = jnp.exp(s_lo - m)
                total = total + jnp.sum(p_lo, axis=1, keepdims=True)
                ctx = ctx + dot(p_lo.astype(BF16), vd_ref[:free, cols])
            ctx = ctx * (1.0 / total)
            ctx_ref[i * b : (i + 1) * b, cols] = jnp.where(low_b, ctx[:b], ctx[b:]).astype(BF16)
            lse = m + jnp.log(total)
            for g in range(2):
                lse_cols = jnp.where(lane == 2 * j + g, lse[g * b : (g + 1) * b], lse_cols)
                top = jnp.max(m[g * b : (g + 1) * b], axis=0, keepdims=True)
                peak = jnp.where(peak_lane == 2 * j + g, jnp.maximum(peak, top), peak)
        lse_ref[0, :, i * b : (i + 1) * b] = lse_cols.T[:8]
    peak_ref[0] = peak


def run_attn_fwd(prefix, q, kd, vd):
    length, nq = q.shape
    groups = nq // 256
    col = lambda g: (0, g)
    return pl.pallas_call(
        attn_fwd_kernel,
        grid=(groups,),
        in_specs=[pl.BlockSpec(memory_space=pltpu.SMEM)] + [spec((length, 256), col)] * 3,
        out_specs=[
            spec((length, 256), col),
            spec((1, 8, length), lambda g: (g, 0, 0)),
            spec((1, 8, 128), lambda g: (g, 0, 0)),
        ],
        out_shape=[
            jax.ShapeDtypeStruct((length, nq), BF16),
            jax.ShapeDtypeStruct((groups, 8, length), F32),
            jax.ShapeDtypeStruct((groups, 8, 128), F32),
        ],
        compiler_params=params(60),
        cost_estimate=took(21),
        name="attn_fwd",
    )(prefix, q, kd, vd)


def add_rows(dst, srcs, step=64):
    def body(i, carry):
        at = pl.ds(pl.multiple_of(i * step, step), step)
        total = srcs[0][at, :].astype(F32)
        for src in srcs[1:]:
            total = total + src[at, :].astype(F32)
        dst[at, :] = total.astype(dst.dtype)
        return carry

    lax.fori_loop(0, dst.shape[0] // step, body, 0)


def greet(peers):
    barrier = pltpu.get_barrier_semaphore()
    for peer in peers:
        pl.semaphore_signal(barrier, inc=1, device_id=peer, device_id_type=pl.DeviceIdType.MESH)
    pl.semaphore_wait(barrier, len(peers))


class Line:
    def __init__(self, tot, rz1, rz2, rz3, sem_s, sem_r):
        self.tot, self.rz1, self.rz2, self.rz3 = tot, rz1, rz2, rz3
        self.sem_s, self.sem_r = sem_s, sem_r
        dp, ex = lax.axis_index("dp"), lax.axis_index("expert")
        self.z = dp // 2
        self.upper = self.z // 2
        self.outer = (self.z == 0) | (self.z == 3)
        self.inner = jnp.logical_not(self.outer)
        self.near, self.middle = (dp ^ 2, ex), (dp ^ 6, ex)

    def copy(self, ch, stage):
        if stage == 3:
            src, dst = self.tot.at[ch, 2 * self.upper + 1 - self.z % 2], self.rz3.at[ch]
        else:
            src = self.tot.at[ch, pl.ds(2 * (1 - self.upper), 2)]
            dst = (self.rz1 if stage == 1 else self.rz2).at[ch]
        return pltpu.make_async_remote_copy(
            src_ref=src,
            dst_ref=dst,
            send_sem=self.sem_s.at[ch, stage],
            recv_sem=self.sem_r.at[ch, stage],
            device_id=self.middle if stage == 2 else self.near,
            device_id_type=pl.DeviceIdType.MESH,
        )

    def add(self, ch, first, other):
        for p in range(2):
            for e in range(2):
                dst = self.tot.at[ch, first + p, e]
                add_rows(dst, [dst, other.at[ch, p, e]])

    def ends(self, ch, inward):
        @pl.when(self.outer)
        def _():
            if inward:
                self.copy(ch, 1).start()
            self.copy(ch, 3).start()

    def middle_sends(self, ch, inward):
        @pl.when(self.inner)
        def _():
            if inward:
                self.copy(ch, 1).wait_recv()
            self.add(ch, 2 * (1 - self.upper), self.rz1)
            self.copy(ch, 2).start()

    def middle_adds(self, ch, inward):
        @pl.when(self.inner)
        def _():
            self.copy(ch, 2).wait()
            self.add(ch, 2 * self.upper, self.rz2)
            self.copy(ch, 3).start()

        if inward:

            @pl.when(self.outer)
            def _():
                self.copy(ch, 1).wait_send()

    def result(self, ch, refs):
        self.copy(ch, 3).wait()
        for e in range(2):
            own, got = self.tot.at[ch, self.z, e], self.rz3.at[ch, e]
            if ch < 2:
                add_rows(refs[ch].at[e], [own, got])
            else:
                rows, lanes = refs[2].shape[1], own.shape[1]
                for h in range(2):
                    at = slice(h * rows, (h + 1) * rows)
                    dst = refs[2].at[e, :, h * lanes : (h + 1) * lanes]
                    add_rows(dst, [own.at[at], got.at[at]])


def line_scratch(shape):
    return [
        pltpu.VMEM((3,) + shape, BF16),
        pltpu.VMEM((3, 2) + shape[1:], BF16),
        pltpu.VMEM((3, 2) + shape[1:], BF16),
        pltpu.VMEM((3,) + shape[1:], BF16),
        pltpu.SemaphoreType.DMA((3, 4)),
        pltpu.SemaphoreType.DMA((3, 4)),
    ]


def attn_bwd_kernel(*refs):
    attn_bwd_body(*refs)


def attn_bwd_sum_kernel(*refs):
    ins, (tot_a, far_a, keep_a, got_a) = refs[:11], refs[11:15]
    outs, (gate_ref, up_ref, down_ref) = refs[15:18], refs[18:21]
    scratch, line_refs, (rx, sem_l) = refs[21:24], refs[24:30], refs[30:]
    step = pl.program_id(0)
    line = Line(*line_refs)
    loads = []
    for k in range(2):
        loads.append([pltpu.make_async_copy(tot_a.at[:, k], line.tot.at[k], sem_l.at[2 * k])])
        loads[-1].append(
            pltpu.make_async_copy(far_a.at[:, k], line.rz1.at[k], sem_l.at[2 * k + 1])
        )
    loads.append(
        [
            pltpu.make_async_copy(keep_a, line.tot.at[2], sem_l.at[4]),
            pltpu.make_async_copy(got_a, rx, sem_l.at[5]),
        ]
    )
    @pl.when(step == 0)
    def _():
        for group in loads:
            for copy in group:
                copy.start()
        greet([line.near, line.middle])
        for copy in loads[2]:
            copy.wait()
        for zz in range(4):
            for e in range(2):
                dst = line.tot.at[2, zz, e]
                add_rows(dst, [dst, rx.at[zz, e]])
        line.ends(2, True)
        for k in range(2):
            for copy in loads[k]:
                copy.wait()
            line.ends(k, False)
            line.middle_sends(k, False)

    attn_bwd_body(*ins, *outs, *scratch)

    @pl.when(step == 1)
    def _():
        line.middle_sends(2, True)
        line.middle_adds(0, False)

    @pl.when(step == 2)
    def _():
        line.middle_adds(1, False)

    @pl.when(step == 3)
    def _():
        line.middle_adds(2, True)
        for ch in range(3):
            line.result(ch, (gate_ref, up_ref, down_ref))


def attn_bwd_body(
    prefix_ref, q_ref, kd_ref, vd_ref, do_ref, ctx_ref, lse_ref, cos_ref, sin_ref, cost_ref, sint_ref,
    dq_ref, dk_ref, dv_ref, dk_acc, dv_acc, kt_ref,
):
    length = q_ref.shape[0]
    b = 256
    prefix = prefix_ref[0]
    low_b = lane_half((b, 128), 128)
    for j in range(2):
        cols = slice(j * 128, (j + 1) * 128)
        kt_ref[j] = kd_ref[:, cols].T
    dk_acc[...] = jnp.zeros_like(dk_acc)
    dv_acc[...] = jnp.zeros_like(dv_acc)
    for i in range(length // b):
        rows = slice(i * b, (i + 1) * b)
        nk = max((i + 1) * b, length // 2)
        free = i * b
        bias = mask_bias(prefix, i * b, free, b, nk - free, 1)
        bias = jnp.concatenate([bias, bias], axis=1)
        for j in range(2):
            cols = slice(j * 128, (j + 1) * 128)
            do = do_ref[rows, cols]
            q2 = two_heads(q_ref[rows, cols], low_b)
            do2 = two_heads(do, low_b)
            prod = (do.astype(F32) * ctx_ref[rows, cols].astype(F32)).T
            delta = jnp.concatenate(
                [
                    jnp.sum(prod[:64], axis=0, keepdims=True),
                    jnp.sum(prod[64:], axis=0, keepdims=True),
                ],
                axis=1,
            )
            lse = jnp.concatenate(
                [lse_ref[0, 2 * j : 2 * j + 1, rows], lse_ref[0, 2 * j + 1 : 2 * j + 2, rows]],
                axis=1,
            )
            dq_t = None
            parts = [(0, free)] if free else []
            for k0, k1 in parts + [(free, nk)]:
                keys = slice(k0, k1)
                s = dot_t(kd_ref[keys, cols], q2)
                if k0 == free:
                    s = s + bias
                p = jnp.exp(s - lse)
                dp = dot_t(vd_ref[keys, cols], do2)
                ds = (p * (dp - delta)).astype(BF16)
                dv_acc[j, keys, :] += dot(p.astype(BF16), do2)
                dk_acc[j, keys, :] += dot(ds, q2)
                part = dot(kt_ref[j, :, keys], ds)
                dq_t = part if dq_t is None else dq_t + part
            cos_t, sin_t = cost_ref[:, rows], sint_ref[:, rows]
            a0, b0 = dq_t[0:32, :b], dq_t[32:64, :b]
            a1, b1 = dq_t[64:96, b:], dq_t[96:128, b:]
            full = jnp.concatenate(
                [
                    a0 * cos_t + b0 * sin_t,
                    b0 * cos_t - a0 * sin_t,
                    a1 * cos_t + b1 * sin_t,
                    b1 * cos_t - a1 * sin_t,
                ],
                axis=0,
            )
            dq_ref[rows, cols] = (full * 0.125).T.astype(BF16)
    low = lane_half((length, 128), 128)
    first = lane_half((length, 128), 64)
    sums = []
    for acc in (dk_acc, dv_acc):
        even = acc[0] + pltpu.roll(acc[0], 64, 1)
        odd = acc[1] + pltpu.roll(acc[1], 64, 1)
        sums.append(jnp.where(low, even, odd))
    dk_ref[...] = rope_lanes(sums[0], cos_ref[...], -sin_ref[...], first).astype(BF16)
    dv_ref[...] = sums[1].astype(BF16)


def run_attn_bwd(prefix, q, kd, vd, d_ctx, ctx, lse, cos, sin, cos_t, sin_t, sums=None):
    length, nq = q.shape
    groups = nq // 256
    col = lambda g: (0, g)
    wide = spec((length, 256), col)
    in_specs = [pl.BlockSpec(memory_space=pltpu.SMEM)] + [wide] * 5
    in_specs += [spec((1, 8, length), lambda g: (g, 0, 0))]
    in_specs += [whole((length, 128))] * 2 + [whole((cos_t.shape[0], length))] * 2
    out_specs = [wide, spec((length, 128), col), spec((length, 128), col)]
    out_shape = [
        jax.ShapeDtypeStruct((length, nq), BF16),
        jax.ShapeDtypeStruct((length, nq // 2), BF16),
        jax.ShapeDtypeStruct((length, nq // 2), BF16),
    ]
    scratch = [
        pltpu.VMEM((2, length, 128), F32),
        pltpu.VMEM((2, length, 128), F32),
        pltpu.VMEM((2, 128, length), BF16),
    ]
    args = (prefix, q, kd, vd, d_ctx, ctx, lse, cos, sin, cos_t, sin_t)
    kernel, extra = attn_bwd_kernel, {}
    if sums is not None:
        kernel, extra = attn_bwd_sum_kernel, {"collective_id": 3, "has_side_effects": True}
        hbm = pl.BlockSpec(memory_space=pl.ANY)
        keep_a = sums[2]
        _, count, rows, lanes = keep_a.shape
        made = [(count, rows, lanes)] * 2 + [(count, rows // 2, 2 * lanes)]
        in_specs += [hbm] * 4
        out_specs += [whole(shape) for shape in made]
        out_shape += [jax.ShapeDtypeStruct(shape, F32) for shape in made]
        scratch += line_scratch(keep_a.shape)
        scratch += [
            pltpu.VMEM(keep_a.shape, BF16),
            pltpu.SemaphoreType.DMA((6,)),
        ]
        args += tuple(sums)
    return pl.pallas_call(
        kernel,
        grid=(groups,),
        in_specs=in_specs,
        out_specs=out_specs,
        out_shape=out_shape,
        scratch_shapes=scratch,
        compiler_params=pltpu.CompilerParams(
            dimension_semantics=("arbitrary",), vmem_limit_bytes=60 * MIB, **extra
        ),
        cost_estimate=took(33),
        name="attn_bwd",
    )(*args)


def mid_kernel(tok_ref, ctx_ref, w_ref, gain_ref, res_ref, x_ref):
    res = tok_ref[...].astype(F32) + dot(ctx_ref[...], w_ref[...])
    res_ref[...] = res
    r = lax.rsqrt(jnp.mean(res * res, axis=1, keepdims=True) + EPS)
    x_ref[...] = (res * r * gain_ref[...].astype(F32)).astype(BF16)


def run_mid(tok, ctx, w_all, gain, at):
    length, d = tok.shape
    b = 256
    row = lambda i: (i, 0)
    return pl.pallas_call(
        mid_kernel,
        grid=(length // b,),
        in_specs=[
            spec((b, d), row),
            spec((b, ctx.shape[1]), row),
            spec((w_all.shape[0], d), lambda i: (0, at)),
            whole((1, d)),
        ],
        out_specs=[spec((b, d), row)] * 2,
        out_shape=[
            jax.ShapeDtypeStruct((length, d), F32),
            jax.ShapeDtypeStruct((length, d), BF16),
        ],
        compiler_params=params(60),
        cost_estimate=took(4),
        name="mid",
    )(tok, ctx, w_all, gain)


def gates_of(x, router, routes_t, num_experts):
    logits = dot(x, router).T[: 16 * pl.cdiv(num_experts, 16)]
    expert = lax.broadcasted_iota(jnp.int32, logits.shape, 0)
    hit = expert == routes_t[0:1]
    for k in range(1, routes_t.shape[0]):
        hit = hit | (expert == routes_t[k : k + 1])
    logits = jnp.where(hit, logits, NEG)
    e = jnp.exp(logits - jnp.max(logits, axis=0, keepdims=True))
    e = jnp.where(hit, e, 0.0)
    return e / jnp.sum(e, axis=0, keepdims=True)


def expert_kernel(first_expert, local, num_experts, with_init, with_carry, n_row, *refs):
    me_ref, router_ref, wg_ref, wu_ref, wd_ref = refs[:5]
    x_refs, c_refs, route_refs = refs[5:7], refs[7:9], refs[9:11]
    refs = refs[11:]
    if with_init:
        out_ins, dx_ins, dg_ins, refs = refs[:2], refs[2:4], refs[4:6], refs[6:]
    if with_carry:
        sent_ref, refs = refs[0], refs[1:]
    out_refs, dx_refs, dg_refs = refs[:2], refs[2:4], refs[4:6]
    hs_ref, dgate_ref, dup_ref = refs[6:9]
    refs = refs[9:]
    if not with_init:
        xt_ref, ct_ref, refs = refs[0], refs[1], refs[2:]
    if with_carry:
        got_ref, refs = refs[0], refs[1:]
    x_now, c_now, out_acc, dx_acc, gp_ref, dgc_ref = refs[:6]
    i, e = pl.program_id(0), pl.program_id(1)
    last = pl.num_programs(1) - 1
    if with_carry:
        over_x = (lax.axis_index("dp") ^ 1, lax.axis_index("expert"))

        def carry():
            return pltpu.make_async_remote_copy(
                src_ref=sent_ref,
                dst_ref=got_ref,
                send_sem=refs[6].at[0],
                recv_sem=refs[6].at[1],
                device_id=over_x,
                device_id_type=pl.DeviceIdType.MESH,
            )

        @pl.when((i == 0) & (e == 0))
        def _():
            greet([over_x])
            carry().start()

    b = x_now.shape[0]
    lane = lax.broadcasted_iota(jnp.int32, (b, 128), 1)

    for source in range(2):

        @pl.when((e == 0) & ((i < n_row) if source == 0 else (i >= n_row)))
        def _():
            x, c = x_refs[source][...], c_refs[source][...]
            x_now[...] = x
            c_now[...] = c
            gates = gates_of(x, router_ref[...], route_refs[source][...], num_experts)
            fill = jnp.zeros((128 - gates.shape[0], b), F32)
            gp_ref[...] = jnp.concatenate([gates, fill], axis=0).T
            if with_init:
                out_acc[...] = out_ins[source][...].astype(F32)
                dx_acc[...] = dx_ins[source][...].astype(F32)
                fill = jnp.zeros((120, b), F32)
                dgc_ref[...] = jnp.concatenate([dg_ins[source][...], fill], axis=0).T
            else:
                out_acc[...] = jnp.zeros_like(out_acc)
                dx_acc[...] = jnp.zeros_like(dx_acc)
                dgc_ref[...] = jnp.zeros_like(dgc_ref)
                xt_ref[...] = x.T
                ct_ref[...] = c.T

    x, c = x_now[...], c_now[...]
    gp = jnp.sum(
        jnp.where(lane == me_ref[0] * local + first_expert + e, gp_ref[...], 0.0),
        axis=1,
        keepdims=True,
    )
    gate = dot(x, wg_ref[0])
    up = dot(x, wu_ref[0])
    grad = dot_t(c, wd_ref[0])
    sig = 0.5 * jnp.tanh(0.5 * gate) + 0.5
    act = gate * sig
    hidden = (act * up).astype(BF16).astype(F32)
    dg = jnp.sum(hidden * grad, axis=1, keepdims=True)
    hs = (hidden * gp).astype(BF16)
    dh = grad * gp
    dup = (dh * act).astype(BF16)
    dgate = (dh * up * (sig + act * (1.0 - sig))).astype(BF16)
    hs_ref[...] = hs
    dup_ref[...] = dup
    dgate_ref[...] = dgate
    out = dot(hs, wd_ref[0])
    dx = dot_t(dgate, wg_ref[0]) + dot_t(dup, wu_ref[0])
    dgc_ref[...] += jnp.where(lane == first_expert + e, dg, 0.0)
    out_acc[...] += out
    dx_acc[...] += dx
    for source in range(2):

        @pl.when((e == last) & ((i < n_row) if source == 0 else (i >= n_row)))
        def _():
            out_refs[source][...] = out_acc[...].astype(BF16)
            dx_refs[source][...] = dx_acc[...].astype(BF16)
            dg_refs[source][...] = dgc_ref[...].T[:8]

    if with_carry:

        @pl.when((i == 2 * n_row - 1) & (e == last))
        def _():
            carry().wait()


def run_expert(me, xs, cs, routes, router, wg, wu, wd, first, count, num_experts, init=None, sent=None):
    length, d = xs[0].shape
    local, _, ff = wg.shape
    b = 512
    n_row = length // b
    top = routes[0].shape[0]

    def clamp(i, source):
        return jnp.minimum(i, n_row - 1) if source == 0 else jnp.maximum(i - n_row, 0)

    rows = [
        spec((b, d), functools.partial(lambda src, i, e: (clamp(i, src), 0), src))
        for src in range(2)
    ]

    def lanes(height):
        return [
            spec((height, b), functools.partial(lambda src, i, e: (0, clamp(i, src)), src))
            for src in range(2)
        ]

    pick = lambda shape: pl.BlockSpec((1,) + shape[1:], lambda i, e: (first + e, 0, 0))
    wide = jax.ShapeDtypeStruct((2 * length, count * ff), BF16)
    full = jax.ShapeDtypeStruct((length, d), BF16)
    small = jax.ShapeDtypeStruct((8, length), F32)
    turned = jax.ShapeDtypeStruct((d, 2 * length), BF16)
    wide_spec = spec((b, ff), lambda i, e: (i, e))
    turned_spec = spec((d, b), lambda i, e: (0, i))
    with_init = init is not None
    carried, extra = [], {}
    if sent is not None:
        carried = [pl.BlockSpec(memory_space=pl.ANY)]
        extra = {"collective_id": 4, "has_side_effects": True}
    made = pl.pallas_call(
        functools.partial(
            expert_kernel, first, local, num_experts, with_init, sent is not None, n_row
        ),
        grid=(2 * n_row, count),
        in_specs=[
            pl.BlockSpec(memory_space=pltpu.SMEM),
            pl.BlockSpec(
                (d, 128),
                lambda i, e: (0, router.shape[1] // 128 - 1),
                pipeline_mode=pl.Buffered(1),
            ),
            pick(wg.shape),
            pick(wu.shape),
            pick(wd.shape),
        ]
        + rows * 2
        + lanes(top)
        + (rows * 2 + lanes(8) if with_init else [])
        + carried,
        out_specs=rows * 2
        + lanes(8)
        + [wide_spec] * 3
        + ([] if with_init else [turned_spec] * 2)
        + carried,
        out_shape=[full] * 4
        + [small] * 2
        + [wide] * 3
        + ([] if with_init else [turned] * 2)
        + ([] if sent is None else [jax.ShapeDtypeStruct(sent.shape, sent.dtype)]),
        scratch_shapes=[
            pltpu.VMEM((b, d), BF16),
            pltpu.VMEM((b, d), BF16),
            pltpu.VMEM((b, d), F32),
            pltpu.VMEM((b, d), F32),
            pltpu.VMEM((b, 128), F32),
            pltpu.VMEM((b, 128), F32),
        ]
        + ([] if sent is None else [pltpu.SemaphoreType.DMA((2,))]),
        compiler_params=pltpu.CompilerParams(
            dimension_semantics=("arbitrary",) * 2, vmem_limit_bytes=62 * MIB, **extra
        ),
        cost_estimate=took(24 * count),
        name="experts",
    )(me, router, wg, wu, wd, *xs, *cs, *routes, *(init or ()), *([] if sent is None else [sent]))
    return {"out": made[:2], "dx": made[2:4], "dg": made[4:6], "wide": made[6:9], "turned": made[9:11], "got": made[9:]}


def weight_grad_kernel(n, paired, dp_ref, *refs):
    xt, ct, dgate, dup, hs = (refs[k * n : (k + 1) * n] for k in range(5))

    def total(lefts, rights):
        acc = None
        for left, right in zip(lefts, rights):
            part = dot(left[...], right[...])
            acc = part if acc is None else acc + part
        return acc

    down = total(ct, hs).T.astype(BF16)
    gate = total(xt, dgate).astype(BF16)
    up = total(xt, dup).astype(BF16)
    if paired:
        keep_ref, send_ref, down_keep_ref, down_send_ref = refs[5 * n :]
        first = dp_ref[0] % 2 == 0

        def parts(value, z, rows):
            even = value[2 * z * rows : (2 * z + 1) * rows]
            odd = value[(2 * z + 1) * rows : (2 * z + 2) * rows]
            return jnp.where(first, even, odd), jnp.where(first, odd, even)

        for z in range(keep_ref.shape[0]):
            for k, value in enumerate((gate, up)):
                keep_ref[z, k, 0], send_ref[z, k, 0] = parts(value, z, keep_ref.shape[3])
        for z in range(down_keep_ref.shape[0]):
            rows = down_keep_ref.shape[2]
            down_keep_ref[z, 0], down_send_ref[z, 0] = parts(down, z, rows)
        return
    gate_ref, up_ref, down_ref = refs[5 * n :]
    for p in range(down_ref.shape[0]):
        rows = down_ref.shape[3]
        down_ref[p, 0, 0] = down[p * rows : (p + 1) * rows]
    for p in range(gate_ref.shape[0]):
        rows = gate_ref.shape[2]
        gate_ref[p, 0] = gate[p * rows : (p + 1) * rows]
        up_ref[p, 0] = up[p * rows : (p + 1) * rows]


def run_weight_grad(dp, xt, ct, dgate, dup, hs, count, skips, n_dp, paired, ff):
    n = len(xt)
    d, length = xt[0].shape
    m = 512 if paired else 256
    left = spec((m, length), lambda e, i: (i, 0))
    rights = [
        spec((length, ff), functools.partial(lambda skip, e, i: (0, e + skip), skip))
        for skip in skips
    ]
    per = d // n_dp
    down_at = lambda e, i: (0, e, i // (ff // m), 0, i % (ff // m))
    if paired:
        row_spec = spec((m // (2 * per), 2, 1, per, ff), lambda e, i: (i, 0, e, 0, 0))
        rows = jax.ShapeDtypeStruct((n_dp // 2, 2, count, per, ff), BF16)
        down_spec = spec((n_dp // 2, 1, ff // n_dp, m), lambda e, i: (0, e, i, 0))
        down = jax.ShapeDtypeStruct((n_dp // 2, count, ff // n_dp * (d // ff), ff), BF16)
        out_specs, out_shape = [row_spec] * 2 + [down_spec] * 2, [rows] * 2 + [down] * 2
    else:
        row_spec = spec((m // per, 1, per, ff), lambda e, i: (i, e, 0, 0))
        rows = jax.ShapeDtypeStruct((n_dp, count, per, ff), BF16)
        down_spec = spec((n_dp, 1, 1, ff // n_dp, m), down_at)
        down = jax.ShapeDtypeStruct((n_dp, count, d // ff, ff // n_dp, ff), BF16)
        out_specs, out_shape = [row_spec] * 2 + [down_spec], [rows] * 2 + [down]
    return pl.pallas_call(
        functools.partial(weight_grad_kernel, n, paired),
        grid=(count, d // m),
        in_specs=[pl.BlockSpec(memory_space=pltpu.SMEM)] + [left] * (2 * n) + rights * 3,
        out_specs=out_specs,
        out_shape=out_shape,
        compiler_params=params(60, 2),
        cost_estimate=took(37),
        name="weight_grad",
    )(dp, *xt, *ct, *dgate, *dup, *hs)


def back_mid_kernel(n, n_ex, local, *refs):
    (me_ref, res_ref, cot_ref, route_ref, x_ref, router_ref, gain_ref, w_ref) = refs[:8]
    dx_refs, dg_refs = refs[8 : 8 + n], refs[8 + n : 8 + n + n_ex]
    dres_ref, dattn_ref, dctx_ref, dlog_ref, ggain_ref = refs[8 + n + n_ex :]
    gp = gates_of(x_ref[...], router_ref[...], route_ref[...], n_ex * local)
    parts = [ref[...][:local] for ref in dg_refs]
    owners = []
    for owner in range(n_ex):
        own = jnp.zeros_like(parts[0])
        for step in range(n_ex):
            own = jnp.where((owner ^ step) == me_ref[0], parts[step], own)
        owners.append(own)
    dg = jnp.concatenate(owners, axis=0)
    d_logits = gp * (dg - jnp.sum(gp * dg, axis=0, keepdims=True))
    fill = jnp.zeros((128 - dg.shape[0], dg.shape[1]), F32)
    d_logits = jnp.concatenate([d_logits, fill], axis=0).T.astype(BF16)
    dlog_ref[...] = d_logits
    d_norm = dot_t(d_logits, router_ref[...])
    for ref in dx_refs:
        d_norm = d_norm + ref[...].astype(F32)
    res = res_ref[...]
    r = lax.rsqrt(jnp.mean(res * res, axis=1, keepdims=True) + EPS)
    xr = res * r
    part = jnp.sum(d_norm * xr, axis=0, keepdims=True)

    @pl.when(pl.program_id(0) == 0)
    def _():
        ggain_ref[...] = jnp.zeros_like(ggain_ref)

    ggain_ref[...] += part
    u = d_norm * gain_ref[...].astype(F32)
    d_res = (
        cot_ref[...].astype(F32) + r * u - xr * (r * r) * jnp.mean(u * res, axis=1, keepdims=True)
    )
    dres_ref[...] = d_res
    d_attn = d_res.astype(BF16)
    dattn_ref[...] = d_attn
    dctx_ref[...] = dot_t(d_attn, w_ref[...]).astype(BF16)


def run_back_mid(me, res, cot, routes_t, x, w_all, gain, at, dxs, dgs, local):
    length, d = res.shape
    b = 256
    row = lambda i: (i, 0)
    n, n_ex = len(dxs), len(dgs)
    return pl.pallas_call(
        functools.partial(back_mid_kernel, n, n_ex, local),
        grid=(length // b,),
        in_specs=[
            pl.BlockSpec(memory_space=pltpu.SMEM),
            spec((b, d), row),
            spec((b, d), row),
            spec((routes_t.shape[0], b), lambda i: (0, i)),
            spec((b, d), row),
            spec((d, 128), lambda i: (0, w_all.shape[1] // 128 - 1)),
            whole((1, d)),
            spec((d, d), lambda i: (0, at)),
        ]
        + [spec((b, d), row)] * n
        + [spec((8, b), lambda i: (0, i))] * n_ex,
        out_specs=[
            spec((b, d), row),
            spec((b, d), row),
            spec((b, d), row),
            spec((b, 128), row),
            whole((1, d)),
        ],
        out_shape=[
            jax.ShapeDtypeStruct((length, d), F32),
            jax.ShapeDtypeStruct((length, d), BF16),
            jax.ShapeDtypeStruct((length, d), BF16),
            jax.ShapeDtypeStruct((length, 128), BF16),
            jax.ShapeDtypeStruct((1, d), F32),
        ],
        compiler_params=params(60),
        cost_estimate=took(11),
        name="back_mid",
    )(me, res, cot, routes_t, x, w_all, gain, w_all, *dxs, *dgs)


def back_in_kernel(dq_ref, dk_ref, dv_ref, w_ref, tok_ref, gain_ref, dres_ref, gt_ref, ggain_ref):
    nq, nk = dq_ref.shape[1], dk_ref.shape[1]
    d_norm = dot_t(dq_ref[...], w_ref[:, :nq])
    d_norm = d_norm + dot_t(dk_ref[...], w_ref[:, nq : nq + nk])
    d_norm = d_norm + dot_t(dv_ref[...], w_ref[:, nq + nk : nq + 2 * nk])
    x = tok_ref[...].astype(F32)
    r = lax.rsqrt(jnp.mean(x * x, axis=1, keepdims=True) + EPS)
    xr = x * r
    part = jnp.sum(d_norm * xr, axis=0, keepdims=True)

    @pl.when(pl.program_id(0) == 0)
    def _():
        ggain_ref[...] = jnp.zeros_like(ggain_ref)

    ggain_ref[...] += part
    u = d_norm * gain_ref[...].astype(F32)
    gt_ref[...] = dres_ref[...] + r * u - xr * (r * r) * jnp.mean(u * x, axis=1, keepdims=True)


def run_back_in(dq, dk, dv, w_qkv, tok, gain, d_res):
    length, d = tok.shape
    b = 256
    row = lambda i: (i, 0)
    nq = dq.shape[1]
    return pl.pallas_call(
        back_in_kernel,
        grid=(length // b,),
        in_specs=[
            spec((b, nq), row),
            spec((b, dk.shape[1]), row),
            spec((b, dv.shape[1]), row),
            spec((d, 2 * nq), lambda i: (0, 0)),
            spec((b, d), row),
            whole((1, d)),
            spec((b, d), row),
        ],
        out_specs=[spec((b, d), row), whole((1, d))],
        out_shape=[jax.ShapeDtypeStruct((length, d), F32), jax.ShapeDtypeStruct((1, d), F32)],
        compiler_params=params(60),
        cost_estimate=took(10),
        name="back_in",
    )(dq, dk, dv, w_qkv, tok, gain, d_res)


CHUNKS = (3, 0, 1, 2)


def finish_kernel(
    ht_ref, dq_ref, dk_ref, dv_ref, dout_ref, small_ref, keep_ref, got_ref, down_keep_ref, down_got_ref,
    gate_a, up_a, down_a, out_o, out_q, out_kv, out_small, gate_ref, up_ref, down_ref, *scratch,
):
    n = len(CHUNKS)
    lists = [scratch[k * n : (k + 1) * n] for k in range(8)]
    b1, r1, s1, r2, s2, r3, s3, r4 = lists
    sem_s, sem_r = scratch[8 * n : 8 * n + 2]
    line = Line(*scratch[8 * n + 2 : 8 * n + 8])
    rx, sem_l = scratch[8 * n + 8 :]
    count = gate_a.shape[0]
    halves = []
    for k, (src, dst) in enumerate(((gate_a, gate_ref), (up_a, up_ref), (down_a, down_ref))):
        halves.append(pltpu.make_async_copy(src, dst.at[:count], sem_l.at[6 + k]))
        halves[k].start()
    dp, ex = lax.axis_index("dp"), lax.axis_index("expert")
    z, x, y, c = dp // 2, dp % 2, ex // 2, ex % 2
    over_core, over_y, over_x = (dp, ex ^ 1), (dp, ex ^ 2), (dp ^ 1, ex)
    along = [(dp ^ (2 * k), ex) for k in (1, 2, 3)]
    group = [over_core, over_y, (dp, ex ^ 3)]
    loads = []
    for k in range(3):
        keep, got = (down_keep_ref, down_got_ref) if k == 2 else (keep_ref.at[:, k], got_ref.at[:, k])
        loads.append(
            [
                pltpu.make_async_copy(keep, line.tot.at[k], sem_l.at[2 * k]),
                pltpu.make_async_copy(got, rx.at[k], sem_l.at[2 * k + 1]),
            ]
        )
        for copy in loads[k]:
            copy.start()
    greet(group + [over_x] + along)

    widths = [dout_ref.shape[1], dq_ref.shape[1], dk_ref.shape[1] + dv_ref.shape[1], 128]
    outs = (out_o, out_q, out_kv, out_small)
    started = {}

    def send(k, slot, src, dst, peer):
        copy = pltpu.make_async_remote_copy(
            src_ref=src,
            dst_ref=dst,
            send_sem=sem_s.at[k, slot],
            recv_sem=sem_r.at[k, slot],
            device_id=peer,
            device_id_type=pl.DeviceIdType.MESH,
        )
        copy.start()
        started[k, slot] = copy

    def begin(k):
        for copy in loads[k]:
            copy.wait()
        for zz in range(4):
            for e in range(2):
                dst = line.tot.at[k, zz, e]
                add_rows(dst, [dst, rx.at[k, zz, e]])
        line.ends(k, True)

    def place(k, lanes, value):
        for p in range(8):
            for e in range(4):
                row = 128 * p + 32 * e
                b1[k][e % 2, e // 2, p % 2, p // 2, :, lanes] = value[row : row + 32]

    def step0(k):
        if k == 0:
            place(k, slice(0, widths[k]), dout_ref[...])
        elif k == 1:
            for col in range(0, widths[1], 512):
                part = dot(ht_ref[...], dq_ref[:, col : col + 512])
                place(k, slice(col, col + 512), part.astype(BF16))
        elif k == 2:
            half = dk_ref.shape[1]
            place(k, slice(0, half), dot(ht_ref[...], dk_ref[...]).astype(BF16))
            place(k, slice(half, 2 * half), dot(ht_ref[...], dv_ref[...]).astype(BF16))
        else:
            place(k, slice(0, 128), small_ref[...])
        send(k, 0, b1[k].at[1 - c], r1[k], over_core)

    def step1(k):
        started[k, 0].wait()
        for yy in range(2):
            for xx in range(2):
                for zz in range(4):
                    s1[k][yy, xx, zz] = (
                        b1[k][c, yy, xx, zz].astype(F32) + r1[k][yy, xx, zz].astype(F32)
                    ).astype(BF16)
        send(k, 1, s1[k].at[1 - y], r2[k], over_y)

    def step2(k):
        started[k, 1].wait()
        for xx in range(2):
            for zz in range(4):
                s2[k][xx, zz] = (
                    s1[k][y, xx, zz].astype(F32) + r2[k][xx, zz].astype(F32)
                ).astype(BF16)
        send(k, 2, s2[k].at[1 - x], r3[k].at[0], over_x)

    def step3(k):
        started[k, 2].wait()
        for zz in range(4):
            s3[k][zz] = (s2[k][x, zz].astype(F32) + r3[k][0, zz].astype(F32)).astype(BF16)
        for i in range(3):
            send(k, 3 + i, s3[k].at[z ^ (i + 1)], r3[k].at[1, i], along[i])

    def step4(k):
        for i in range(3):
            started[k, 3 + i].wait()
        total = s3[k][z].astype(F32)
        for i in range(3):
            total = total + r3[k][1, i].astype(F32)
        r4[k][3] = total.astype(BF16)
        for i in range(3):
            send(k, 6 + i, r4[k].at[3], r4[k].at[i], group[i])

    def step5(k):
        outs[k][pl.ds(pl.multiple_of(ex * 32, 32), 32), :] = r4[k][3].astype(F32)
        for i in range(3):
            started[k, 6 + i].wait()
            rows = pl.ds(pl.multiple_of((ex ^ (i + 1)) * 32, 32), 32)
            outs[k][rows, :] = r4[k][i].astype(F32)

    done = tuple(ref.at[count:] for ref in (gate_ref, up_ref, down_ref))
    step0(3)
    step0(0)
    begin(0)
    step1(3)
    step1(0)
    step0(1)
    begin(1)
    step1(1)
    step0(2)
    begin(2)
    step1(2)
    step2(3)
    step2(0)
    line.middle_sends(0, True)
    step2(1)
    step3(3)
    step3(0)
    line.middle_sends(1, True)
    line.middle_adds(0, True)
    step2(2)
    step3(1)
    line.middle_sends(2, True)
    line.middle_adds(1, True)
    step4(3)
    step4(0)
    step3(2)
    line.result(0, done)
    line.middle_adds(2, True)
    step4(1)
    step5(3)
    step5(0)
    step4(2)
    line.result(1, done)
    line.result(2, done)
    step5(1)
    step5(2)
    for copy in halves:
        copy.wait()


def run_finish(ht, dq, dk, dv, d_out, small, experts):
    widths = [d_out.shape[1], dq.shape[1], dk.shape[1] + dv.shape[1], small.shape[1]]
    chunk = experts[2].shape
    _, count, rows, lanes = chunk
    vmem = pl.BlockSpec(memory_space=pltpu.VMEM)
    hbm = pl.BlockSpec(memory_space=pl.ANY)
    shapes = [
        (2, 2, 2, 4, 32), (2, 2, 4, 32), (2, 2, 4, 32), (2, 4, 32), (2, 4, 32), (2, 4, 32), (4, 32), (4, 32),
    ]
    scratch = [pltpu.VMEM(shape + (w,), BF16) for shape in shapes for w in widths]
    scratch += [pltpu.SemaphoreType.DMA((len(widths), 9))] * 2
    scratch += line_scratch(chunk)
    scratch += [pltpu.VMEM((3,) + chunk, BF16), pltpu.SemaphoreType.DMA((9,))]
    return pl.pallas_call(
        finish_kernel,
        in_specs=[vmem] * 6 + [hbm] * 7,
        out_specs=[vmem] * 7,
        out_shape=[
            *(jax.ShapeDtypeStruct((128, w), F32) for w in widths),
            jax.ShapeDtypeStruct((2 * count, rows, lanes), F32),
            jax.ShapeDtypeStruct((2 * count, rows, lanes), F32),
            jax.ShapeDtypeStruct((2 * count, rows // 2, 2 * lanes), F32),
        ],
        scratch_shapes=scratch,
        compiler_params=pltpu.CompilerParams(
            vmem_limit_bytes=60 * MIB, collective_id=1, has_side_effects=True
        ),
        cost_estimate=took(60),
        name="finish",
    )(ht, dq, dk, dv, d_out, small, *experts)


def gather_kernel(mine_ref, out_ref, sem_s, sem_r, sem_l):
    dp, ex = lax.axis_index("dp"), lax.axis_index("expert")
    z = dp // 2
    core, over_y, over_x = (dp, ex ^ 1), (dp, ex ^ 2), (dp ^ 1, ex)
    line = [None] + [(dp ^ (2 * k), ex) for k in (1, 2, 3)]
    barrier = pltpu.get_barrier_semaphore()
    peers = [core, over_y, over_x] + line[1:]
    for peer in peers:
        pl.semaphore_signal(barrier, inc=1, device_id=peer, device_id_type=pl.DeviceIdType.MESH)
    pl.semaphore_wait(barrier, len(peers))
    rows = mine_ref.shape[0]
    width = mine_ref.shape[1]
    cut = (width // 256 + 1) * 128
    halves = [pl.ds(0, cut), pl.ds(cut, width - cut)]
    started = {}

    def block(k, dx, dy):
        at = (((z ^ k) * 2 + (dp % 2 ^ dx)) * 4 + (ex ^ (2 * dy))) * rows
        return pl.ds(pl.multiple_of(at, rows), rows)

    def send(key, k, dx, dy, peer, src=None, lanes=None):
        index = len(started)
        at = block(k, dx, dy)
        dst = out_ref.at[at] if lanes is None else out_ref.at[at, lanes]
        copy = pltpu.make_async_remote_copy(
            src_ref=dst if src is None else src,
            dst_ref=dst,
            send_sem=sem_s.at[index],
            recv_sem=sem_r.at[index],
            device_id=peer,
            device_id_type=pl.DeviceIdType.MESH,
        )
        copy.start()
        started[key] = copy

    for k in (3, 2, 1):
        send(("z", k), 0, 0, 0, line[k], mine_ref)
    send(("x", 0), 0, 0, 0, over_x, mine_ref)
    send(("y", 0), 0, 0, 0, over_y, mine_ref)
    send(("c", 0), 0, 0, 0, core, mine_ref)
    own = pltpu.make_async_copy(mine_ref, out_ref.at[block(0, 0, 0)], sem_l)
    own.start()

    def onward(k):
        started["x", k].wait_recv()
        send(("dy", k), k, 1, 0, over_y, None, halves[0])
        send(("cx", k), k, 1, 0, core)
        started["y", k].wait_recv()
        send(("dx", k), k, 0, 1, over_x, None, halves[1])
        send(("cy", k), k, 0, 1, core)

    def last(k):
        started["dy", k].wait_recv()
        started["dx", k].wait_recv()
        send(("cd", k), k, 1, 1, core)

    onward(0)
    for k in (1, 2, 3):
        started["z", k].wait_recv()
        send(("x", k), k, 0, 0, over_x)
        send(("y", k), k, 0, 0, over_y)
        send(("c", k), k, 0, 0, core)
    last(0)
    for k in (1, 2, 3):
        onward(k)
    for k in (1, 2, 3):
        last(k)
    for key, copy in started.items():
        copy.wait_send()
        if key[0] in ("c", "cx", "cy", "cd"):
            copy.wait_recv()
    own.wait()


def run_gather(mine, total):
    hbm = pl.BlockSpec(memory_space=pl.ANY)
    return pl.pallas_call(
        gather_kernel,
        in_specs=[hbm],
        out_specs=hbm,
        out_shape=jax.ShapeDtypeStruct((total, mine.shape[1]), BF16),
        scratch_shapes=[
            pltpu.SemaphoreType.DMA((40,)),
            pltpu.SemaphoreType.DMA((40,)),
            pltpu.SemaphoreType.DMA,
        ],
        compiler_params=pltpu.CompilerParams(collective_id=2, has_side_effects=True),
        cost_estimate=took(40),
        name="gather",
    )(mine)


def after(value, *deps):
    return lax.optimization_barrier((value,) + deps)[0]


def on_device(
    n_dp, n_ex, tokens, cotangent, routes, prefix, w_query, keyvalue_weight, w_out, w_router,
    gain_attn, gain_mlp, expert_gate, expert_up, expert_down, query_logit_cap,
):
    length, d = tokens.shape[1], tokens.shape[2]
    tok = tokens.reshape(length, d)
    cot = cotangent.reshape(length, d)
    heads = query_logit_cap.shape[0]
    nq = w_query.shape[1]
    head = nq // heads
    kv_heads = keyvalue_weight.shape[1] // (2 * head)
    num_experts = w_router.shape[1]
    local = expert_gate.shape[0]
    rows = w_query.shape[0]
    ex = lax.axis_index("expert")

    def swap(value, step, axis="expert", n=n_ex):
        return lax.ppermute(value, axis, [(i, i ^ step) for i in range(n)])

    part = rows // n_ex
    small = jnp.concatenate(
        [
            w_router,
            gain_attn[:, None],
            gain_mlp[:, None],
            jnp.zeros((rows, 128 - num_experts - 2), BF16),
        ],
        axis=1,
    )
    packed = jnp.concatenate([w_query, keyvalue_weight, w_out, small], axis=1)
    mine = lax.dynamic_slice_in_dim(packed, ex * part, part, axis=0)
    local = expert_gate.shape[0]
    fast = n_dp == 8 and n_ex == 4 and d == 1024 and local == 4 and expert_gate.shape[2] == 512
    if fast:
        every = run_gather(mine, d)
    else:
        every = lax.all_gather(mine, ("dp", "expert"), axis=0, tiled=True)
    w_all = every
    width = 2 * nq
    extra = every[:, width + d :]
    gain_one = extra[:, num_experts].reshape(1, d)
    gain_two = extra[:, num_experts + 1].reshape(1, d)

    routes_t = routes.reshape(length, -1).T
    cots = {0: cot}
    route_set = {0: routes_t}
    cot_late = after(cot, every)
    for step in range(1, n_ex):
        if step == 1 or step % 2 == 0:
            cots[step] = swap(cot_late, step)

    cos_np, sin_np = rope_tables(length, head)
    cos_l = jnp.asarray(np.concatenate([cos_np] * 4, axis=1))
    sin_l = jnp.asarray(np.concatenate([-sin_np, sin_np] * 2, axis=1))
    cos_t = jnp.asarray(np.ascontiguousarray(cos_np.T))
    sin_t = jnp.asarray(np.ascontiguousarray(sin_np.T))

    normed_one_t, q, kd, vd = run_qkv(tok, gain_one, w_all, cos_l, sin_l, nq)
    for step in range(1, n_ex):
        route_set[step] = swap(after(routes_t, q), step)
    ctx, lse, peaks = run_attn_fwd(prefix, q, kd, vd)
    resid, normed_two = run_mid(tok, ctx, w_all, gain_two, width // d)

    me = ex.reshape(1).astype(jnp.int32)
    xs = {0: normed_two}
    for step in range(1, n_ex):
        if step == 1 or step % 2 == 0:
            xs[step] = swap(normed_two, step)
    tops = [peaks[:, :, :4]]
    bits = [("expert", n_ex, 1 << i) for i in range(n_ex.bit_length() - 1)]
    bits += [("dp", n_dp, 1 << i) for i in range(n_dp.bit_length() - 1)]

    def widen_top():
        if len(tops) <= len(bits):
            axis, n, step = bits[len(tops) - 1]
            top = after(tops[-1], chain)
            tops.append(jnp.maximum(top, swap(top, step, axis, n)))

    weights = (expert_gate, expert_up, expert_down)
    half = local // 2

    dp = lax.axis_index("dp").reshape(1).astype(jnp.int32)

    res = {}
    chain = (normed_two, [cots[step] for step in range(2, n_ex, 2)])

    def experts(steps, first, count, init=None, sent=None):
        x = [after(xs[steps[0]], chain), xs[steps[1]]]
        cot_pair, route_pair = [cots[k] for k in steps], [route_set[k] for k in steps]
        return run_expert(
            me, x, cot_pair, route_pair, w_all, *weights, first, count, num_experts, init, sent
        )

    def grads(first):
        pairs = [res[k, 0] for k in range(0, n_ex, 2)]
        wides = [res[0, 0]] + [res[k, first] for k in range(2, n_ex, 2)]
        groups = [[pair["turned"][k] for pair in pairs] for k in (0, 1)]
        groups += [[pair["wide"][k] for pair in wides] for k in (1, 2, 0)]
        groups[0][0] = after(groups[0][0], chain)
        skips = [first if k == 0 else 0 for k in range(len(pairs))]
        made = None
        for at in range(0, len(pairs), 2):
            some = [group[at : at + 2] for group in groups]
            part = run_weight_grad(
                dp, *some, half, skips[at : at + 2], n_dp, fast, expert_gate.shape[2]
            )
            if made is None:
                made = part
            else:
                made = [(a.astype(F32) + b.astype(F32)).astype(BF16) for a, b in zip(made, part)]
        return made

    res[0, 0] = experts((0, 1), 0, local)
    chain = (res[0, 0]["dg"][0], tops[-1])
    widen_top()
    widen_top()
    for other in range(3, n_ex, 2):
        cots[other] = swap(after(cots[other - 1], chain), 1)
        xs[other] = swap(after(xs[other - 1], chain), 1)
    even = range(2, n_ex, 2)
    for step in even:
        res[step, 0] = experts((step, step + 1), 0, half)
        chain = (res[step, 0]["dg"][0], tops[-1])
        widen_top()
    made_one = grads(0)
    chain = (made_one[0], tops[-1])
    widen_top()
    for step in even:
        init = [*res[step, 0]["out"], *res[step, 0]["dx"], *res[step, 0]["dg"]]
        sent = made_one[1] if fast else None
        res[step, half] = experts((step, step + 1), half, half, init, sent)
        chain = (res[step, half]["dg"][0], tops[-1])
        widen_top()

    def with_partner(step, what):
        own, other = res[step, half][what]
        return (own.astype(F32) + swap(other, 1).astype(F32)).astype(BF16)

    to_send = {step: with_partner(step, "dx") for step in even}
    chain = (chain, list(to_send.values()))
    sums, got_two = None, []
    if fast:
        down_sent = after(made_one[3], chain)
        got_one = [res[2, half]["got"][0], swap(down_sent, 1, "dp", n_dp)]
        tot_one = (made_one[0].astype(F32) + got_one[0].astype(F32)).astype(BF16)
        far_one = lax.dynamic_slice_in_dim(tot_one, 2 * (1 - dp[0] // 4), 2, axis=0)
        chain = (chain, far_one)
        far_one = lax.ppermute(far_one, "dp", [(0, 2), (1, 3), (6, 4), (7, 5)])
    made_two = grads(half)
    chain = (made_two[0], tops[-1])
    if fast:
        chain = (chain, far_one, got_one)
        sums = [tot_one, far_one, made_one[2], got_one[1]]
        got_two = [swap(made_two[k], 1, "dp", n_dp) for k in (1, 3)]
    while len(tops) <= len(bits):
        widen_top()
    top = tops[-1]

    final = [res[0, 0]] + [res[step, half] for step in even]
    dxs = [final[0]["dx"][0], swap(final[0]["dx"][1], 1)]
    dxs += [swap(to_send[step], step) for step in even]
    dgs = [part for pair in final for part in pair["dg"]]
    dgs = [swap(dgs[step], step) if step else dgs[0] for step in range(n_ex)]
    d_res, d_attn, d_ctx, d_logits, d_gain_two = run_back_mid(
        me,
        after(resid, chain),
        cot,
        routes_t,
        normed_two,
        w_all,
        gain_two,
        width // d,
        dxs,
        dgs,
        local,
    )
    outs = [final[0]["out"][0], swap(final[0]["out"][1], 1)]
    outs += [swap(after(with_partner(step, "out"), dxs), step) for step in even]
    block = resid
    for piece in outs:
        block = block + piece.astype(F32)
    block_out = block.astype(BF16).reshape(tokens.shape)

    d_out_w = jnp.einsum("rc,rd->cd", ctx, d_attn, preferred_element_type=F32).astype(BF16)
    d_router_w = jnp.einsum("rd,re->de", normed_two, d_logits, preferred_element_type=F32)

    dq, dk, dv, *halves = run_attn_bwd(
        prefix, after(q, top), kd, vd, d_ctx, ctx, lse, cos_l, sin_l, cos_t, sin_t, sums
    )
    grad_tok, d_gain_one = run_back_in(
        after(dq, block_out, got_two), dk, dv, w_all, tok, gain_one, d_res
    )
    small_grad = jnp.concatenate(
        [
            d_router_w[:, :num_experts].astype(BF16),
            d_gain_one.reshape(d, 1).astype(BF16),
            d_gain_two.reshape(d, 1).astype(BF16),
            jnp.zeros((d, 128 - num_experts - 2), BF16),
        ],
        axis=1,
    )

    def reduce_all(value, order):
        shape = (n_dp, n_ex, value.shape[0] // (n_dp * n_ex), value.shape[1])
        names = []
        dims = []
        for axis, n in (("dp", n_dp), ("expert", n_ex)):
            count = n.bit_length() - 1
            names += [(axis, n, 1 << (count - 1 - i)) for i in range(count)]
            dims += [2] * count
        value = value.reshape(*dims, *shape[2:])
        for bit in order:
            at = names.index(bit)
            axis, n, step = bit
            mine = (lax.axis_index(axis) // step) % 2
            keep = lax.dynamic_slice_in_dim(value, mine, 1, axis=at)
            send = lax.dynamic_slice_in_dim(value, 1 - mine, 1, axis=at)
            value = (keep.astype(F32) + swap(send, step, axis, n).astype(F32)).astype(BF16)
        return value.reshape(shape[2:])

    def share(value):
        return lax.all_gather(value, "expert", axis=0, tiled=True).astype(F32)

    core = [("expert", n_ex, 1)]
    y_bits = [("expert", n_ex, 1 << i) for i in range(1, n_ex.bit_length() - 1)][::-1]
    dp_bits = [("dp", n_dp, 1 << i) for i in range(n_dp.bit_length() - 1)]
    if fast:
        grad_out, grad_query, grad_keyval, rest, grad_gate, grad_up, grad_down = run_finish(
            normed_one_t,
            dq,
            dk,
            dv,
            d_out_w,
            small_grad,
            [made_two[0], got_two[0], made_two[2], got_two[1], *halves],
        )
    else:
        ends = [
            [
                lax.psum_scatter(g, "dp", scatter_dimension=0, tiled=True)[0].astype(F32)
                for g in made
            ]
            for made in (made_one, made_two)
        ]
        grad_gate, grad_up, grad_down = (
            jnp.concatenate([ends[0][k], ends[1][k]], axis=0) for k in range(3)
        )
        grad_down = jnp.swapaxes(grad_down, 1, 2).reshape(local, -1, d)

        def product(right):
            return jnp.dot(normed_one_t, right, preferred_element_type=F32).astype(BF16)

        every_grad = jnp.concatenate(
            [d_out_w, product(dq), product(dk), product(dv), small_grad], axis=1
        )
        every_grad = share(reduce_all(every_grad, core + y_bits + dp_bits[::-1]))
        grad_out = every_grad[:, :d]
        grad_query = every_grad[:, d : d + nq]
        grad_keyval = every_grad[:, d + nq : d + 2 * nq]
        rest = every_grad[:, d + 2 * nq :]
    grad_router = rest[:, :num_experts]
    grad_gain_one = rest[:, num_experts]
    grad_gain_two = rest[:, num_experts + 1]

    head_logit_peak = top[:, 0, :].reshape(heads)
    per_group = heads // kv_heads
    query_factor = jnp.sqrt(query_logit_cap / jnp.maximum(head_logit_peak, query_logit_cap))
    pair_peak = jnp.max(head_logit_peak.reshape(kv_heads, per_group), axis=1)
    pair_cap = jnp.min(query_logit_cap.reshape(kv_heads, per_group), axis=1)
    key_factor = jnp.sqrt(pair_cap / jnp.maximum(pair_peak, pair_cap))
    clipped_query = (w_query.astype(F32) * jnp.repeat(query_factor, head)[None, :]).astype(BF16)
    key_cols = jnp.concatenate(
        [jnp.repeat(key_factor, head), jnp.ones((kv_heads * head,), F32)]
    )
    clipped_keyval = (keyvalue_weight.astype(F32) * key_cols[None, :]).astype(BF16)
    return (
        block_out,
        grad_tok.reshape(tokens.shape),
        grad_query,
        grad_keyval,
        grad_out,
        grad_router,
        grad_gain_one,
        grad_gain_two,
        grad_gate,
        grad_up,
        grad_down,
        clipped_query,
        clipped_keyval,
        head_logit_peak,
    )


def solution(mesh):
    rows3 = P(("dp", "expert"), None, None)
    in_specs = (
        rows3,
        rows3,
        rows3,
        P(("dp", "expert")),
        P("dp", None),
        P("dp", None),
        P("dp", None),
        P("dp", None),
        P("dp"),
        P("dp"),
        P("expert", None, None),
        P("expert", None, None),
        P("expert", None, None),
        P(),
    )
    out_specs = (
        rows3,
        rows3,
        P("dp", None),
        P("dp", None),
        P("dp", None),
        P("dp", None),
        P("dp"),
        P("dp"),
        P("expert", "dp", None),
        P("expert", "dp", None),
        P("expert", "dp", None),
        P("dp", None),
        P("dp", None),
        P(),
    )
    return jax.shard_map(
        functools.partial(on_device, mesh.shape["dp"], mesh.shape["expert"]),
        mesh=mesh,
        in_specs=in_specs,
        out_specs=out_specs,
        check_vma=False,
    )
```

```python
import functools

import jax
import jax.numpy as jnp
import numpy as np
from jax import lax
from jax.experimental import pallas as pl
from jax.experimental.pallas import tpu as pltpu
from jax.sharding import PartitionSpec as P

EPS = 1e-05
ROPE_BASE = 10000.0
F32 = jnp.float32
BF16 = jnp.bfloat16
NEG = -1e30
MIB = 1 << 20
SCALE = 0.35


def dot(a, b):
    return lax.dot_general(a, b, (((1,), (0,)), ((), ())), preferred_element_type=F32)


def dot_t(a, b):
    return lax.dot_general(a, b, (((1,), (1,)), ((), ())), preferred_element_type=F32)


def params(vmem_mib, n=1):
    return pltpu.CompilerParams(
        dimension_semantics=("arbitrary",) * n, vmem_limit_bytes=vmem_mib * MIB
    )


def took(us):
    return pl.CostEstimate(flops=int(us * SCALE * 1e9), bytes_accessed=1000, transcendentals=0)


def spec(shape, index):
    return pl.BlockSpec(shape, index)


def whole(shape):
    zeros = (0,) * len(shape)
    return pl.BlockSpec(shape, lambda *_: zeros)


def rope_tables(length, head):
    half = head // 2
    freq = np.float32(ROPE_BASE) ** (
        -(np.arange(half, dtype=np.float32) * np.float32(2.0) / np.float32(head))
    )
    ang = np.arange(length, dtype=np.float32)[:, None] * freq.astype(np.float32)[None, :]
    ang = ang.astype(np.float32)
    return np.cos(ang).astype(np.float32), np.sin(ang).astype(np.float32)


def lane_half(shape, width):
    return (lax.broadcasted_iota(jnp.int32, shape, 1) % width) < (width // 2)


def rope_lanes(x, cos, sin, first):
    partner = jnp.where(first, pltpu.roll(x, 96, 1), pltpu.roll(x, 32, 1))
    return x * cos + partner * sin


def qkv_kernel(tok_ref, gain_ref, w_ref, cos_ref, sin_ref, ht_ref, q_ref, kd_ref, vd_ref):
    x = tok_ref[...].astype(F32)
    d = x.shape[1]
    r = lax.rsqrt(jnp.mean(x * x, axis=1, keepdims=True) + EPS)
    h = (x * r * gain_ref[...].astype(F32)).astype(BF16)
    ht_ref[...] = h.T
    cos, sin = cos_ref[...], sin_ref[...]
    rows = x.shape[0]
    first = lane_half((rows, 128), 64)
    low = lane_half((rows, 128), 128)
    nq = q_ref.shape[1]
    nk = kd_ref.shape[1] // 2
    q = dot(h, w_ref[:, :nq])
    for c in range(0, nq, 128):
        q_ref[:, c : c + 128] = (rope_lanes(q[:, c : c + 128], cos, sin, first) * 0.125).astype(
            BF16
        )
    k = dot(h, w_ref[:, nq : nq + nk])
    for c in range(0, nk, 128):
        kk = rope_lanes(k[:, c : c + 128], cos, sin, first)
        sw = pltpu.roll(kk, 64, 1)
        kd_ref[:, 2 * c : 2 * c + 128] = jnp.where(low, kk, sw).astype(BF16)
        kd_ref[:, 2 * c + 128 : 2 * c + 256] = jnp.where(low, sw, kk).astype(BF16)
    v = dot(h, w_ref[:, nq + nk : nq + 2 * nk])
    for c in range(0, nk, 128):
        vv = v[:, c : c + 128]
        sw = pltpu.roll(vv, 64, 1)
        vd_ref[:, 2 * c : 2 * c + 128] = jnp.where(low, vv, sw).astype(BF16)
        vd_ref[:, 2 * c + 128 : 2 * c + 256] = jnp.where(low, sw, vv).astype(BF16)


def run_qkv(tok, gain, w_qkv, cos, sin, nq):
    length, d = tok.shape
    b = 256
    row = lambda i: (i, 0)
    return pl.pallas_call(
        qkv_kernel,
        grid=(length // b,),
        in_specs=[
            spec((b, d), row),
            whole((1, d)),
            spec((d, 2 * nq), lambda i: (0, 0)),
            spec((b, 128), row),
            spec((b, 128), row),
        ],
        out_specs=[spec((d, b), lambda i: (0, i))] + [spec((b, nq), row)] * 3,
        out_shape=[jax.ShapeDtypeStruct((d, length), BF16)]
        + [jax.ShapeDtypeStruct((length, nq), BF16)] * 3,
        compiler_params=params(60),
        cost_estimate=took(9),
        name="qkv",
    )(tok, gain, w_qkv, cos, sin)


def mask_bias(prefix, q0, k0, nq, nk, q_axis):
    shape = (nq, nk) if q_axis == 0 else (nk, nq)
    qpos = q0 + lax.broadcasted_iota(jnp.int32, shape, q_axis)
    kpos = k0 + lax.broadcasted_iota(jnp.int32, shape, 1 - q_axis)
    return jnp.where((kpos <= qpos) | (kpos < prefix), 0.0, NEG).astype(F32)


def two_heads(pair, low):
    zero = jnp.zeros_like(pair)
    return jnp.concatenate([jnp.where(low, pair, zero), jnp.where(low, zero, pair)], axis=0)


def attn_fwd_kernel(prefix_ref, q_ref, kd_ref, vd_ref, ctx_ref, lse_ref, peak_ref):
    length = q_ref.shape[0]
    b = 256
    prefix = prefix_ref[0]
    low_b = lane_half((b, 128), 128)
    lane = lax.broadcasted_iota(jnp.int32, (b, 128), 1)
    peak = jnp.full((8, 128), NEG, F32)
    peak_lane = lax.broadcasted_iota(jnp.int32, (8, 128), 1)
    for i in range(length // b):
        nk = max((i + 1) * b, length // 2)
        free = i * b
        bias = mask_bias(prefix, i * b, free, b, nk - free, 0)
        bias = jnp.concatenate([bias, bias], axis=0)
        lse_cols = jnp.zeros((b, 128), F32)
        for j in range(2):
            cols = slice(j * 128, (j + 1) * 128)
            q2 = two_heads(q_ref[i * b : (i + 1) * b, cols], low_b)
            s_hi = dot_t(q2, kd_ref[free:nk, cols]) + bias
            m = jnp.max(s_hi, axis=1, keepdims=True)
            if free:
                s_lo = dot_t(q2, kd_ref[:free, cols])
                m = jnp.maximum(m, jnp.max(s_lo, axis=1, keepdims=True))
            p_hi = jnp.exp(s_hi - m)
            total = jnp.sum(p_hi, axis=1, keepdims=True)
            ctx = dot(p_hi.astype(BF16), vd_ref[free:nk, cols])
            if free:
                p_lo = jnp.exp(s_lo - m)
                total = total + jnp.sum(p_lo, axis=1, keepdims=True)
                ctx = ctx + dot(p_lo.astype(BF16), vd_ref[:free, cols])
            ctx = ctx * (1.0 / total)
            ctx_ref[i * b : (i + 1) * b, cols] = jnp.where(low_b, ctx[:b], ctx[b:]).astype(BF16)
            lse = m + jnp.log(total)
            for g in range(2):
                lse_cols = jnp.where(lane == 2 * j + g, lse[g * b : (g + 1) * b], lse_cols)
                top = jnp.max(m[g * b : (g + 1) * b], axis=0, keepdims=True)
                peak = jnp.where(peak_lane == 2 * j + g, jnp.maximum(peak, top), peak)
        lse_ref[0, :, i * b : (i + 1) * b] = lse_cols.T[:8]
    peak_ref[0] = peak


def run_attn_fwd(prefix, q, kd, vd):
    length, nq = q.shape
    groups = nq // 256
    col = lambda g: (0, g)
    return pl.pallas_call(
        attn_fwd_kernel,
        grid=(groups,),
        in_specs=[pl.BlockSpec(memory_space=pltpu.SMEM)] + [spec((length, 256), col)] * 3,
        out_specs=[
            spec((length, 256), col),
            spec((1, 8, length), lambda g: (g, 0, 0)),
            spec((1, 8, 128), lambda g: (g, 0, 0)),
        ],
        out_shape=[
            jax.ShapeDtypeStruct((length, nq), BF16),
            jax.ShapeDtypeStruct((groups, 8, length), F32),
            jax.ShapeDtypeStruct((groups, 8, 128), F32),
        ],
        compiler_params=params(60),
        cost_estimate=took(21),
        name="attn_fwd",
    )(prefix, q, kd, vd)


def add_rows(dst, srcs, step=64):
    def body(i, carry):
        at = pl.ds(pl.multiple_of(i * step, step), step)
        one, two = srcs[0][at, :], srcs[1][at, :]
        if dst.dtype != one.dtype:
            one, two = one.astype(dst.dtype), two.astype(dst.dtype)
        dst[at, :] = one + two
        return carry

    lax.fori_loop(0, dst.shape[0] // step, body, 0)


def greet(peers):
    barrier = pltpu.get_barrier_semaphore()
    for peer in peers:
        pl.semaphore_signal(barrier, inc=1, device_id=peer, device_id_type=pl.DeviceIdType.MESH)
    pl.semaphore_wait(barrier, len(peers))


class Line:
    def __init__(self, tot, rz1, rz2, rz3, sem_s, sem_r):
        self.tot, self.rz1, self.rz2, self.rz3 = tot, rz1, rz2, rz3
        self.sem_s, self.sem_r = sem_s, sem_r
        dp, ex = lax.axis_index("dp"), lax.axis_index("expert")
        self.z = dp // 2
        self.upper = self.z // 2
        self.outer = (self.z == 0) | (self.z == 3)
        self.inner = jnp.logical_not(self.outer)
        self.near, self.middle = (dp ^ 2, ex), (dp ^ 6, ex)

    def copy(self, ch, stage):
        if stage == 3:
            src, dst = self.tot.at[ch, 2 * self.upper + 1 - self.z % 2], self.rz3.at[ch]
        else:
            src = self.tot.at[ch, pl.ds(2 * (1 - self.upper), 2)]
            dst = (self.rz1 if stage == 1 else self.rz2).at[ch]
        return pltpu.make_async_remote_copy(
            src_ref=src,
            dst_ref=dst,
            send_sem=self.sem_s.at[ch, stage],
            recv_sem=self.sem_r.at[ch, stage],
            device_id=self.middle if stage == 2 else self.near,
            device_id_type=pl.DeviceIdType.MESH,
        )

    def add(self, ch, first, other):
        for p in range(2):
            for e in range(2):
                dst = self.tot.at[ch, first + p, e]
                add_rows(dst, [dst, other.at[ch, p, e]])

    def ends(self, ch, inward):
        @pl.when(self.outer)
        def _():
            if inward:
                self.copy(ch, 1).start()
            else:
                self.copy(ch, 3).start()

    def middle_sends(self, ch, inward):
        @pl.when(self.inner)
        def _():
            if inward:
                self.copy(ch, 1).wait_recv()
            self.add(ch, 2 * (1 - self.upper), self.rz1)
            self.copy(ch, 2).start()

        if inward:

            @pl.when(self.outer)
            def _():
                self.copy(ch, 1).wait_send()
                self.copy(ch, 3).start()

    def middle_adds(self, ch):
        @pl.when(self.inner)
        def _():
            self.copy(ch, 2).wait()
            self.add(ch, 2 * self.upper, self.rz2)
            self.copy(ch, 3).start()

    def result(self, ch, refs):
        self.copy(ch, 3).wait()
        for e in range(2):
            own, got = self.tot.at[ch, self.z, e], self.rz3.at[ch, e]
            if ch < 2:
                add_rows(refs[ch].at[e], [own, got])
            else:
                rows, lanes = refs[2].shape[1], own.shape[1]
                for h in range(2):
                    at = slice(h * rows, (h + 1) * rows)
                    dst = refs[2].at[e, :, h * lanes : (h + 1) * lanes]
                    add_rows(dst, [own.at[at], got.at[at]])


def line_scratch(shape):
    return [
        pltpu.VMEM((3,) + shape, BF16),
        pltpu.VMEM((3, 2) + shape[1:], BF16),
        pltpu.VMEM((3, 2) + shape[1:], BF16),
        pltpu.VMEM((3,) + shape[1:], BF16),
        pltpu.SemaphoreType.DMA((3, 4)),
        pltpu.SemaphoreType.DMA((3, 4)),
    ]


def attn_bwd_kernel(*refs):
    attn_bwd_body(*refs)


def attn_bwd_sum_kernel(*refs):
    ins, (tot_a, far_a, keep_a, got_a, peak_ref) = refs[:11], refs[11:16]
    outs, (gate_ref, up_ref, down_ref, top_ref) = refs[16:19], refs[19:23]
    scratch, line_refs, (rx, sem_l, top_s, top_r, sem_ts, sem_tr) = refs[23:26], refs[26:32], refs[32:]
    step = pl.program_id(0)
    line = Line(*line_refs)
    dp, ex = lax.axis_index("dp"), lax.axis_index("expert")
    bits = [(dp, ex ^ 1), (dp, ex ^ 2), (dp ^ 1, ex), (dp ^ 2, ex), (dp ^ 4, ex)]

    def top_copy(k):
        return pltpu.make_async_remote_copy(
            src_ref=top_s.at[k],
            dst_ref=top_r.at[k],
            send_sem=sem_ts.at[k],
            recv_sem=sem_tr.at[k],
            device_id=bits[k],
            device_id_type=pl.DeviceIdType.MESH,
        )

    def top_round(k):
        if k == 0:
            top_s[0] = peak_ref[...]
        else:
            top_copy(k - 1).wait()
            both = jnp.maximum(top_s[k - 1], top_r[k - 1])
            if k == len(bits):
                top_ref[...] = both
                return
            top_s[k] = both
        top_copy(k).start()

    loads = []
    for k in range(2):
        loads.append([pltpu.make_async_copy(tot_a.at[:, k], line.tot.at[k], sem_l.at[2 * k])])
        loads[-1].append(
            pltpu.make_async_copy(far_a.at[:, k], line.rz1.at[k], sem_l.at[2 * k + 1])
        )
    loads.append(
        [
            pltpu.make_async_copy(keep_a, line.tot.at[2], sem_l.at[4]),
            pltpu.make_async_copy(got_a, rx, sem_l.at[5]),
        ]
    )
    @pl.when(step == 0)
    def _():
        for group in loads:
            for copy in group:
                copy.start()
        greet(bits + [line.middle])
        top_round(0)
        for copy in loads[2]:
            copy.wait()
        for zz in range(4):
            for e in range(2):
                dst = line.tot.at[2, zz, e]
                add_rows(dst, [dst, rx.at[zz, e]])
        line.ends(2, True)
        for k in range(2):
            for copy in loads[k]:
                copy.wait()
            line.ends(k, False)
            line.middle_sends(k, False)

    @pl.when(step == 3)
    def _():
        top_round(4)

    attn_bwd_body(*ins, *outs, *scratch)

    @pl.when(step == 0)
    def _():
        top_round(1)

    @pl.when(step == 1)
    def _():
        top_round(2)
        line.middle_sends(2, True)
        line.middle_adds(0)

    @pl.when(step == 2)
    def _():
        top_round(3)
        line.middle_adds(1)

    @pl.when(step == 3)
    def _():
        line.middle_adds(2)
        for ch in range(3):
            line.result(ch, (gate_ref, up_ref, down_ref))
        top_round(5)


def attn_bwd_body(
    prefix_ref, q_ref, kd_ref, vd_ref, do_ref, ctx_ref, lse_ref, cos_ref, sin_ref, cost_ref, sint_ref,
    dq_ref, dk_ref, dv_ref, dk_acc, dv_acc, kt_ref,
):
    length = q_ref.shape[0]
    b = 256
    prefix = prefix_ref[0]
    low_b = lane_half((b, 128), 128)
    for j in range(2):
        cols = slice(j * 128, (j + 1) * 128)
        kt_ref[j] = kd_ref[:, cols].T
    dk_acc[...] = jnp.zeros_like(dk_acc)
    dv_acc[...] = jnp.zeros_like(dv_acc)
    for i in range(length // b):
        rows = slice(i * b, (i + 1) * b)
        nk = max((i + 1) * b, length // 2)
        free = i * b
        bias = mask_bias(prefix, i * b, free, b, nk - free, 1)
        bias = jnp.concatenate([bias, bias], axis=1)
        for j in range(2):
            cols = slice(j * 128, (j + 1) * 128)
            do = do_ref[rows, cols]
            q2 = two_heads(q_ref[rows, cols], low_b)
            do2 = two_heads(do, low_b)
            prod = (do.astype(F32) * ctx_ref[rows, cols].astype(F32)).T
            delta = jnp.concatenate(
                [
                    jnp.sum(prod[:64], axis=0, keepdims=True),
                    jnp.sum(prod[64:], axis=0, keepdims=True),
                ],
                axis=1,
            )
            lse = jnp.concatenate(
                [lse_ref[0, 2 * j : 2 * j + 1, rows], lse_ref[0, 2 * j + 1 : 2 * j + 2, rows]],
                axis=1,
            )
            dq_t = None
            parts = [(0, free)] if free else []
            for k0, k1 in parts + [(free, nk)]:
                keys = slice(k0, k1)
                s = dot_t(kd_ref[keys, cols], q2)
                if k0 == free:
                    s = s + bias
                p = jnp.exp(s - lse)
                dp = dot_t(vd_ref[keys, cols], do2)
                ds = (p * (dp - delta)).astype(BF16)
                dv_acc[j, keys, :] += dot(p.astype(BF16), do2)
                dk_acc[j, keys, :] += dot(ds, q2)
                part = dot(kt_ref[j, :, keys], ds)
                dq_t = part if dq_t is None else dq_t + part
            cos_t, sin_t = cost_ref[:, rows], sint_ref[:, rows]
            a0, b0 = dq_t[0:32, :b], dq_t[32:64, :b]
            a1, b1 = dq_t[64:96, b:], dq_t[96:128, b:]
            full = jnp.concatenate(
                [
                    a0 * cos_t + b0 * sin_t,
                    b0 * cos_t - a0 * sin_t,
                    a1 * cos_t + b1 * sin_t,
                    b1 * cos_t - a1 * sin_t,
                ],
                axis=0,
            )
            dq_ref[rows, cols] = (full * 0.125).T.astype(BF16)
    low = lane_half((length, 128), 128)
    first = lane_half((length, 128), 64)
    sums = []
    for acc in (dk_acc, dv_acc):
        even = acc[0] + pltpu.roll(acc[0], 64, 1)
        odd = acc[1] + pltpu.roll(acc[1], 64, 1)
        sums.append(jnp.where(low, even, odd))
    dk_ref[...] = rope_lanes(sums[0], cos_ref[...], -sin_ref[...], first).astype(BF16)
    dv_ref[...] = sums[1].astype(BF16)


def run_attn_bwd(prefix, q, kd, vd, d_ctx, ctx, lse, cos, sin, cos_t, sin_t, sums=None):
    length, nq = q.shape
    groups = nq // 256
    col = lambda g: (0, g)
    wide = spec((length, 256), col)
    in_specs = [pl.BlockSpec(memory_space=pltpu.SMEM)] + [wide] * 5
    in_specs += [spec((1, 8, length), lambda g: (g, 0, 0))]
    in_specs += [whole((length, 128))] * 2 + [whole((cos_t.shape[0], length))] * 2
    out_specs = [wide, spec((length, 128), col), spec((length, 128), col)]
    out_shape = [
        jax.ShapeDtypeStruct((length, nq), BF16),
        jax.ShapeDtypeStruct((length, nq // 2), BF16),
        jax.ShapeDtypeStruct((length, nq // 2), BF16),
    ]
    scratch = [
        pltpu.VMEM((2, length, 128), F32),
        pltpu.VMEM((2, length, 128), F32),
        pltpu.VMEM((2, 128, length), BF16),
    ]
    args = (prefix, q, kd, vd, d_ctx, ctx, lse, cos, sin, cos_t, sin_t)
    kernel, extra = attn_bwd_kernel, {}
    if sums is not None:
        kernel, extra = attn_bwd_sum_kernel, {"collective_id": 3, "has_side_effects": True}
        hbm = pl.BlockSpec(memory_space=pl.ANY)
        keep_a = sums[2]
        _, count, rows, lanes = keep_a.shape
        made = [(count, rows, lanes)] * 2 + [(count, rows // 2, 2 * lanes)]
        peaks = sums[4]
        made.append(peaks.shape)
        in_specs += [hbm] * 4 + [whole(peaks.shape)]
        out_specs += [whole(shape) for shape in made]
        out_shape += [jax.ShapeDtypeStruct(shape, F32) for shape in made]
        scratch += line_scratch(keep_a.shape)
        scratch += [
            pltpu.VMEM(keep_a.shape, BF16),
            pltpu.SemaphoreType.DMA((6,)),
            pltpu.VMEM((5,) + peaks.shape, F32),
            pltpu.VMEM((5,) + peaks.shape, F32),
            pltpu.SemaphoreType.DMA((5,)),
            pltpu.SemaphoreType.DMA((5,)),
        ]
        args += tuple(sums)
    return pl.pallas_call(
        kernel,
        grid=(groups,),
        in_specs=in_specs,
        out_specs=out_specs,
        out_shape=out_shape,
        scratch_shapes=scratch,
        compiler_params=pltpu.CompilerParams(
            dimension_semantics=("arbitrary",), vmem_limit_bytes=60 * MIB, **extra
        ),
        cost_estimate=took(33),
        name="attn_bwd",
    )(*args)


def mid_kernel(tok_ref, ctx_ref, w_ref, gain_ref, res_ref, x_ref):
    res = tok_ref[...].astype(F32) + dot(ctx_ref[...], w_ref[...])
    res_ref[...] = res
    r = lax.rsqrt(jnp.mean(res * res, axis=1, keepdims=True) + EPS)
    x_ref[...] = (res * r * gain_ref[...].astype(F32)).astype(BF16)


def run_mid(tok, ctx, w_all, gain, at):
    length, d = tok.shape
    b = 256
    row = lambda i: (i, 0)
    return pl.pallas_call(
        mid_kernel,
        grid=(length // b,),
        in_specs=[
            spec((b, d), row),
            spec((b, ctx.shape[1]), row),
            spec((w_all.shape[0], d), lambda i: (0, at)),
            whole((1, d)),
        ],
        out_specs=[spec((b, d), row)] * 2,
        out_shape=[
            jax.ShapeDtypeStruct((length, d), F32),
            jax.ShapeDtypeStruct((length, d), BF16),
        ],
        compiler_params=params(60),
        cost_estimate=took(4),
        name="mid",
    )(tok, ctx, w_all, gain)


def gates_of(x, router, routes_t, num_experts):
    logits = dot(x, router).T[: 16 * pl.cdiv(num_experts, 16)]
    expert = lax.broadcasted_iota(jnp.int32, logits.shape, 0)
    hit = expert == routes_t[0:1]
    for k in range(1, routes_t.shape[0]):
        hit = hit | (expert == routes_t[k : k + 1])
    logits = jnp.where(hit, logits, NEG)
    e = jnp.exp(logits - jnp.max(logits, axis=0, keepdims=True))
    e = jnp.where(hit, e, 0.0)
    return e / jnp.sum(e, axis=0, keepdims=True)


def expert_kernel(first_expert, local, num_experts, with_init, with_carry, n_row, *refs):
    me_ref, router_ref, wg_ref, wu_ref, wd_ref = refs[:5]
    x_refs, c_refs, route_refs = refs[5:7], refs[7:9], refs[9:11]
    refs = refs[11:]
    if with_init:
        out_ins, dx_ins, dg_ins, refs = refs[:2], refs[2:4], refs[4:6], refs[6:]
    if with_carry:
        sent_ref, refs = refs[0], refs[1:]
    out_refs, dx_refs, dg_refs = refs[:2], refs[2:4], refs[4:6]
    hs_ref, dgate_ref, dup_ref = refs[6:9]
    refs = refs[9:]
    if not with_init:
        xt_ref, ct_ref, refs = refs[0], refs[1], refs[2:]
    if with_carry:
        got_ref, refs = refs[0], refs[1:]
    x_now, c_now, out_acc, dx_acc, gp_ref, dgc_ref = refs[:6]
    i, e = pl.program_id(0), pl.program_id(1)
    last = pl.num_programs(1) - 1
    if with_carry:
        over_x = (lax.axis_index("dp") ^ 1, lax.axis_index("expert"))

        def carry():
            return pltpu.make_async_remote_copy(
                src_ref=sent_ref,
                dst_ref=got_ref,
                send_sem=refs[6].at[0],
                recv_sem=refs[6].at[1],
                device_id=over_x,
                device_id_type=pl.DeviceIdType.MESH,
            )

        @pl.when((i == 0) & (e == 0))
        def _():
            greet([over_x])
            carry().start()

    b = x_now.shape[0]
    lane = lax.broadcasted_iota(jnp.int32, (b, 128), 1)

    for source in range(2):

        @pl.when((e == 0) & ((i < n_row) if source == 0 else (i >= n_row)))
        def _():
            x, c = x_refs[source][...], c_refs[source][...]
            x_now[...] = x
            c_now[...] = c
            gates = gates_of(x, router_ref[...], route_refs[source][...], num_experts)
            fill = jnp.zeros((128 - gates.shape[0], b), F32)
            gp_ref[...] = jnp.concatenate([gates, fill], axis=0).T
            if with_init:
                out_acc[...] = out_ins[source][...].astype(F32)
                dx_acc[...] = dx_ins[source][...].astype(F32)
                fill = jnp.zeros((120, b), F32)
                dgc_ref[...] = jnp.concatenate([dg_ins[source][...], fill], axis=0).T
            else:
                out_acc[...] = jnp.zeros_like(out_acc)
                dx_acc[...] = jnp.zeros_like(dx_acc)
                dgc_ref[...] = jnp.zeros_like(dgc_ref)
                xt_ref[...] = x.T
                ct_ref[...] = c.T

    x, c = x_now[...], c_now[...]
    gp = jnp.sum(
        jnp.where(lane == me_ref[0] * local + first_expert + e, gp_ref[...], 0.0),
        axis=1,
        keepdims=True,
    )
    gate = dot(x, wg_ref[0])
    up = dot(x, wu_ref[0])
    grad = dot_t(c, wd_ref[0])
    sig = 0.5 * jnp.tanh(0.5 * gate) + 0.5
    act = gate * sig
    hidden = (act * up).astype(BF16).astype(F32)
    dg = jnp.sum(hidden * grad, axis=1, keepdims=True)
    hs = (hidden * gp).astype(BF16)
    dh = grad * gp
    dup = (dh * act).astype(BF16)
    dgate = (dh * up * (sig + act * (1.0 - sig))).astype(BF16)
    hs_ref[...] = hs
    dup_ref[...] = dup
    dgate_ref[...] = dgate
    out = dot(hs, wd_ref[0])
    dx = dot_t(dgate, wg_ref[0]) + dot_t(dup, wu_ref[0])
    dgc_ref[...] += jnp.where(lane == first_expert + e, dg, 0.0)
    out_acc[...] += out
    dx_acc[...] += dx
    for source in range(2):

        @pl.when((e == last) & ((i < n_row) if source == 0 else (i >= n_row)))
        def _():
            out_refs[source][...] = out_acc[...].astype(BF16)
            dx_refs[source][...] = dx_acc[...].astype(BF16)
            dg_refs[source][...] = dgc_ref[...].T[:8]

    if with_carry:

        @pl.when((i == 2 * n_row - 1) & (e == last))
        def _():
            carry().wait()


def run_expert(me, xs, cs, routes, router, wg, wu, wd, first, count, num_experts, init=None, sent=None):
    length, d = xs[0].shape
    local, _, ff = wg.shape
    b = 512
    n_row = length // b
    top = routes[0].shape[0]

    def clamp(i, source):
        return jnp.minimum(i, n_row - 1) if source == 0 else jnp.maximum(i - n_row, 0)

    rows = [
        spec((b, d), functools.partial(lambda src, i, e: (clamp(i, src), 0), src))
        for src in range(2)
    ]

    def lanes(height):
        return [
            spec((height, b), functools.partial(lambda src, i, e: (0, clamp(i, src)), src))
            for src in range(2)
        ]

    pick = lambda shape: pl.BlockSpec((1,) + shape[1:], lambda i, e: (first + e, 0, 0))
    wide = jax.ShapeDtypeStruct((2 * length, count * ff), BF16)
    full = jax.ShapeDtypeStruct((length, d), BF16)
    small = jax.ShapeDtypeStruct((8, length), F32)
    turned = jax.ShapeDtypeStruct((d, 2 * length), BF16)
    wide_spec = spec((b, ff), lambda i, e: (i, e))
    turned_spec = spec((d, b), lambda i, e: (0, i))
    with_init = init is not None
    carried, extra = [], {}
    if sent is not None:
        carried = [pl.BlockSpec(memory_space=pl.ANY)]
        extra = {"collective_id": 4, "has_side_effects": True}
    made = pl.pallas_call(
        functools.partial(
            expert_kernel, first, local, num_experts, with_init, sent is not None, n_row
        ),
        grid=(2 * n_row, count),
        in_specs=[
            pl.BlockSpec(memory_space=pltpu.SMEM),
            pl.BlockSpec(
                (d, 128),
                lambda i, e: (0, router.shape[1] // 128 - 1),
                pipeline_mode=pl.Buffered(1),
            ),
            pick(wg.shape),
            pick(wu.shape),
            pick(wd.shape),
        ]
        + rows * 2
        + lanes(top)
        + (rows * 2 + lanes(8) if with_init else [])
        + carried,
        out_specs=rows * 2
        + lanes(8)
        + [wide_spec] * 3
        + ([] if with_init else [turned_spec] * 2)
        + carried,
        out_shape=[full] * 4
        + [small] * 2
        + [wide] * 3
        + ([] if with_init else [turned] * 2)
        + ([] if sent is None else [jax.ShapeDtypeStruct(sent.shape, sent.dtype)]),
        scratch_shapes=[
            pltpu.VMEM((b, d), BF16),
            pltpu.VMEM((b, d), BF16),
            pltpu.VMEM((b, d), F32),
            pltpu.VMEM((b, d), F32),
            pltpu.VMEM((b, 128), F32),
            pltpu.VMEM((b, 128), F32),
        ]
        + ([] if sent is None else [pltpu.SemaphoreType.DMA((2,))]),
        compiler_params=pltpu.CompilerParams(
            dimension_semantics=("arbitrary",) * 2, vmem_limit_bytes=62 * MIB, **extra
        ),
        cost_estimate=took(24 * count),
        name="experts",
    )(me, router, wg, wu, wd, *xs, *cs, *routes, *(init or ()), *([] if sent is None else [sent]))
    return {"out": made[:2], "dx": made[2:4], "dg": made[4:6], "wide": made[6:9], "turned": made[9:11], "got": made[9:]}


def weight_grad_kernel(n, paired, dp_ref, *refs):
    xt, ct, dgate, dup, hs = (refs[k * n : (k + 1) * n] for k in range(5))

    def total(lefts, rights):
        acc = None
        for left, right in zip(lefts, rights):
            part = dot(left[...], right[...])
            acc = part if acc is None else acc + part
        return acc

    down = total(ct, hs).T.astype(BF16)
    gate = total(xt, dgate).astype(BF16)
    up = total(xt, dup).astype(BF16)
    if paired:
        keep_ref, send_ref, down_keep_ref, down_send_ref = refs[5 * n :]
        first = dp_ref[0] % 2 == 0

        def parts(value, z, rows):
            even = value[2 * z * rows : (2 * z + 1) * rows]
            odd = value[(2 * z + 1) * rows : (2 * z + 2) * rows]
            return jnp.where(first, even, odd), jnp.where(first, odd, even)

        for z in range(keep_ref.shape[0]):
            for k, value in enumerate((gate, up)):
                keep_ref[z, k, 0], send_ref[z, k, 0] = parts(value, z, keep_ref.shape[3])
        for z in range(down_keep_ref.shape[0]):
            rows = down_keep_ref.shape[2]
            down_keep_ref[z, 0], down_send_ref[z, 0] = parts(down, z, rows)
        return
    gate_ref, up_ref, down_ref = refs[5 * n :]
    for p in range(down_ref.shape[0]):
        rows = down_ref.shape[3]
        down_ref[p, 0, 0] = down[p * rows : (p + 1) * rows]
    for p in range(gate_ref.shape[0]):
        rows = gate_ref.shape[2]
        gate_ref[p, 0] = gate[p * rows : (p + 1) * rows]
        up_ref[p, 0] = up[p * rows : (p + 1) * rows]


def run_weight_grad(dp, xt, ct, dgate, dup, hs, count, skips, n_dp, paired, ff):
    n = len(xt)
    d, length = xt[0].shape
    m = 512 if paired else 256
    left = spec((m, length), lambda e, i: (i, 0))
    rights = [
        spec((length, ff), functools.partial(lambda skip, e, i: (0, e + skip), skip))
        for skip in skips
    ]
    per = d // n_dp
    down_at = lambda e, i: (0, e, i // (ff // m), 0, i % (ff // m))
    if paired:
        row_spec = spec((m // (2 * per), 2, 1, per, ff), lambda e, i: (i, 0, e, 0, 0))
        rows = jax.ShapeDtypeStruct((n_dp // 2, 2, count, per, ff), BF16)
        down_spec = spec((n_dp // 2, 1, ff // n_dp, m), lambda e, i: (0, e, i, 0))
        down = jax.ShapeDtypeStruct((n_dp // 2, count, ff // n_dp * (d // ff), ff), BF16)
        out_specs, out_shape = [row_spec] * 2 + [down_spec] * 2, [rows] * 2 + [down] * 2
    else:
        row_spec = spec((m // per, 1, per, ff), lambda e, i: (i, e, 0, 0))
        rows = jax.ShapeDtypeStruct((n_dp, count, per, ff), BF16)
        down_spec = spec((n_dp, 1, 1, ff // n_dp, m), down_at)
        down = jax.ShapeDtypeStruct((n_dp, count, d // ff, ff // n_dp, ff), BF16)
        out_specs, out_shape = [row_spec] * 2 + [down_spec], [rows] * 2 + [down]
    return pl.pallas_call(
        functools.partial(weight_grad_kernel, n, paired),
        grid=(count, d // m),
        in_specs=[pl.BlockSpec(memory_space=pltpu.SMEM)] + [left] * (2 * n) + rights * 3,
        out_specs=out_specs,
        out_shape=out_shape,
        compiler_params=params(60, 2),
        cost_estimate=took(37),
        name="weight_grad",
    )(dp, *xt, *ct, *dgate, *dup, *hs)


def back_mid_kernel(n, n_ex, local, *refs):
    (me_ref, res_ref, cot_ref, route_ref, x_ref, router_ref, gain_ref, w_ref) = refs[:8]
    dx_refs, dg_refs = refs[8 : 8 + n], refs[8 + n : 8 + n + n_ex]
    dres_ref, dattn_ref, dctx_ref, dlog_ref, ggain_ref = refs[8 + n + n_ex :]
    gp = gates_of(x_ref[...], router_ref[...], route_ref[...], n_ex * local)
    parts = [ref[...][:local] for ref in dg_refs]
    owners = []
    for owner in range(n_ex):
        own = jnp.zeros_like(parts[0])
        for step in range(n_ex):
            own = jnp.where((owner ^ step) == me_ref[0], parts[step], own)
        owners.append(own)
    dg = jnp.concatenate(owners, axis=0)
    d_logits = gp * (dg - jnp.sum(gp * dg, axis=0, keepdims=True))
    fill = jnp.zeros((128 - dg.shape[0], dg.shape[1]), F32)
    d_logits = jnp.concatenate([d_logits, fill], axis=0).T.astype(BF16)
    dlog_ref[...] = d_logits
    d_norm = dot_t(d_logits, router_ref[...])
    for ref in dx_refs:
        d_norm = d_norm + ref[...].astype(F32)
    res = res_ref[...]
    r = lax.rsqrt(jnp.mean(res * res, axis=1, keepdims=True) + EPS)
    xr = res * r
    part = jnp.sum(d_norm * xr, axis=0, keepdims=True)

    @pl.when(pl.program_id(0) == 0)
    def _():
        ggain_ref[...] = jnp.zeros_like(ggain_ref)

    ggain_ref[...] += part
    u = d_norm * gain_ref[...].astype(F32)
    d_res = (
        cot_ref[...].astype(F32) + r * u - xr * (r * r) * jnp.mean(u * res, axis=1, keepdims=True)
    )
    dres_ref[...] = d_res
    d_attn = d_res.astype(BF16)
    dattn_ref[...] = d_attn
    dctx_ref[...] = dot_t(d_attn, w_ref[...]).astype(BF16)


def run_back_mid(me, res, cot, routes_t, x, w_all, gain, at, dxs, dgs, local):
    length, d = res.shape
    b = 256
    row = lambda i: (i, 0)
    n, n_ex = len(dxs), len(dgs)
    return pl.pallas_call(
        functools.partial(back_mid_kernel, n, n_ex, local),
        grid=(length // b,),
        in_specs=[
            pl.BlockSpec(memory_space=pltpu.SMEM),
            spec((b, d), row),
            spec((b, d), row),
            spec((routes_t.shape[0], b), lambda i: (0, i)),
            spec((b, d), row),
            spec((d, 128), lambda i: (0, w_all.shape[1] // 128 - 1)),
            whole((1, d)),
            spec((d, d), lambda i: (0, at)),
        ]
        + [spec((b, d), row)] * n
        + [spec((8, b), lambda i: (0, i))] * n_ex,
        out_specs=[
            spec((b, d), row),
            spec((b, d), row),
            spec((b, d), row),
            spec((b, 128), row),
            whole((1, d)),
        ],
        out_shape=[
            jax.ShapeDtypeStruct((length, d), F32),
            jax.ShapeDtypeStruct((length, d), BF16),
            jax.ShapeDtypeStruct((length, d), BF16),
            jax.ShapeDtypeStruct((length, 128), BF16),
            jax.ShapeDtypeStruct((1, d), F32),
        ],
        compiler_params=params(60),
        cost_estimate=took(11),
        name="back_mid",
    )(me, res, cot, routes_t, x, w_all, gain, w_all, *dxs, *dgs)


def back_in_kernel(dq_ref, dk_ref, dv_ref, w_ref, tok_ref, gain_ref, dres_ref, gt_ref, ggain_ref):
    nq, nk = dq_ref.shape[1], dk_ref.shape[1]
    d_norm = dot_t(dq_ref[...], w_ref[:, :nq])
    d_norm = d_norm + dot_t(dk_ref[...], w_ref[:, nq : nq + nk])
    d_norm = d_norm + dot_t(dv_ref[...], w_ref[:, nq + nk : nq + 2 * nk])
    x = tok_ref[...].astype(F32)
    r = lax.rsqrt(jnp.mean(x * x, axis=1, keepdims=True) + EPS)
    xr = x * r
    part = jnp.sum(d_norm * xr, axis=0, keepdims=True)

    @pl.when(pl.program_id(0) == 0)
    def _():
        ggain_ref[...] = jnp.zeros_like(ggain_ref)

    ggain_ref[...] += part
    u = d_norm * gain_ref[...].astype(F32)
    gt_ref[...] = dres_ref[...] + r * u - xr * (r * r) * jnp.mean(u * x, axis=1, keepdims=True)


def run_back_in(dq, dk, dv, w_qkv, tok, gain, d_res):
    length, d = tok.shape
    b = 256
    row = lambda i: (i, 0)
    nq = dq.shape[1]
    return pl.pallas_call(
        back_in_kernel,
        grid=(length // b,),
        in_specs=[
            spec((b, nq), row),
            spec((b, dk.shape[1]), row),
            spec((b, dv.shape[1]), row),
            spec((d, 2 * nq), lambda i: (0, 0)),
            spec((b, d), row),
            whole((1, d)),
            spec((b, d), row),
        ],
        out_specs=[spec((b, d), row), whole((1, d))],
        out_shape=[jax.ShapeDtypeStruct((length, d), F32), jax.ShapeDtypeStruct((1, d), F32)],
        compiler_params=params(60),
        cost_estimate=took(10),
        name="back_in",
    )(dq, dk, dv, w_qkv, tok, gain, d_res)


CHUNKS = (3, 0, 1, 2)


def finish_kernel(
    gain_lane, ht_ref, dq_ref, dk_ref, dv_ref, dout_ref, small_ref, keep_ref, got_ref, down_keep_ref, down_got_ref,
    gate_a, up_a, down_a, w_ref, tok_ref, gain_ref, dres_ref,
    out_o, out_q, out_kv, out_small, gate_ref, up_ref, down_ref, gt_ref, *scratch,
):
    n = len(CHUNKS)
    lists = [scratch[k * n : (k + 1) * n] for k in range(7)]
    b1, r1, r2, s2, r3, s3, r4 = lists
    sem_s, sem_r = scratch[7 * n : 7 * n + 2]
    line = Line(*scratch[7 * n + 2 : 7 * n + 8])
    rx, sem_l, w_now, gt_now, gain_sum = scratch[7 * n + 8 :]
    count = gate_a.shape[0]
    halves = []
    for k, (src, dst) in enumerate(((gate_a, gate_ref), (up_a, up_ref), (down_a, down_ref))):
        halves.append(pltpu.make_async_copy(src, dst.at[:count], sem_l.at[6 + k]))
        halves[k].start()
    dp, ex = lax.axis_index("dp"), lax.axis_index("expert")
    z, x, y, c = dp // 2, dp % 2, ex // 2, ex % 2
    over_core, over_y, over_x = (dp, ex ^ 1), (dp, ex ^ 2), (dp ^ 1, ex)
    s1 = [ref.at[c] for ref in b1]
    load_w = pltpu.make_async_copy(w_ref.at[:, : w_now.shape[1]], w_now, sem_l.at[9])
    load_w.start()
    along = [(dp ^ (2 * k), ex) for k in (1, 2, 3)]
    group = [over_core, over_y, (dp, ex ^ 3)]
    loads = []
    for k in range(3):
        keep, got = (down_keep_ref, down_got_ref) if k == 2 else (keep_ref.at[:, k], got_ref.at[:, k])
        loads.append(
            [
                pltpu.make_async_copy(keep, line.tot.at[k], sem_l.at[2 * k]),
                pltpu.make_async_copy(got, rx.at[k], sem_l.at[2 * k + 1]),
            ]
        )
        for copy in loads[k]:
            copy.start()
    greet(group + [over_x] + along)

    widths = [dout_ref.shape[1], dq_ref.shape[1], dk_ref.shape[1] + dv_ref.shape[1], 128]
    outs = (out_o, out_q, out_kv, out_small)
    started = {}

    def send(k, slot, src, dst, peer):
        copy = pltpu.make_async_remote_copy(
            src_ref=src,
            dst_ref=dst,
            send_sem=sem_s.at[k, slot],
            recv_sem=sem_r.at[k, slot],
            device_id=peer,
            device_id_type=pl.DeviceIdType.MESH,
        )
        copy.start()
        started[k, slot] = copy

    def begin(k):
        for copy in loads[k]:
            copy.wait()
        for zz in range(4):
            for e in range(2):
                dst = line.tot.at[k, zz, e]
                add_rows(dst, [dst, rx.at[k, zz, e]])
        line.ends(k, True)

    def place(k, lanes, value):
        for p in range(8):
            for e in range(4):
                row = 128 * p + 32 * e
                b1[k][e % 2, e // 2, p % 2, p // 2, :, lanes] = value[row : row + 32]

    def step0(k):
        if k == 0:
            place(k, slice(0, widths[k]), dout_ref[...])
        elif k == 1:
            for col in range(0, widths[1], 512):
                part = dot(ht_ref[...], dq_ref[:, col : col + 512])
                place(k, slice(col, col + 512), part.astype(BF16))
        elif k == 2:
            half = dk_ref.shape[1]
            place(k, slice(0, half), dot(ht_ref[...], dk_ref[...]).astype(BF16))
            place(k, slice(half, 2 * half), dot(ht_ref[...], dv_ref[...]).astype(BF16))
        else:
            turned = jnp.broadcast_to(gain_sum[...], (128, gain_sum.shape[1])).T.astype(BF16)
            lane = lax.broadcasted_iota(jnp.int32, turned.shape, 1)
            place(k, slice(0, 128), jnp.where(lane == gain_lane, turned, small_ref[...]))
        send(k, 0, b1[k].at[1 - c], r1[k], over_core)

    def step1(k):
        started[k, 0].wait()
        for yy in range(2):
            for xx in range(2):
                for zz in range(4):
                    s1[k][yy, xx, zz] = s1[k][yy, xx, zz] + r1[k][yy, xx, zz]
        send(k, 1, s1[k].at[1 - y], r2[k], over_y)

    def step2(k):
        started[k, 1].wait()
        for xx in range(2):
            for zz in range(4):
                s2[k][xx, zz] = s1[k][y, xx, zz] + r2[k][xx, zz]
        send(k, 2, s2[k].at[1 - x], r3[k].at[0], over_x)

    def step3(k):
        started[k, 2].wait()
        for zz in range(4):
            s3[k][zz] = s2[k][x, zz] + r3[k][0, zz]
        for i in range(3):
            send(k, 3 + i, s3[k].at[z ^ (i + 1)], r3[k].at[1, i], along[i])

    def step4(k):
        for i in range(3):
            started[k, 3 + i].wait()
        total = s3[k][z].astype(F32)
        for i in range(3):
            total = total + r3[k][1, i].astype(F32)
        r4[k][3] = total.astype(BF16)
        for i in range(3):
            send(k, 6 + i, r4[k].at[3], r4[k].at[i], group[i])

    def step5(k):
        outs[k][pl.ds(pl.multiple_of(ex * 32, 32), 32), :] = r4[k][3].astype(F32)
        for i in range(3):
            started[k, 6 + i].wait()
            rows = pl.ds(pl.multiple_of((ex ^ (i + 1)) * 32, 32), 32)
            outs[k][rows, :] = r4[k][i].astype(F32)

    size = gt_now.shape[1]

    def stored(r):
        rows = slice(r * size, (r + 1) * size)
        return pltpu.make_async_copy(gt_now.at[r % 2], gt_ref.at[rows], sem_l.at[10 + r])

    def back(r):
        if r == 0:
            load_w.wait()
        if r >= 2:
            stored(r - 2).wait()
        rows = slice(r * size, (r + 1) * size)
        nq, nk = dq_ref.shape[1], dk_ref.shape[1]
        d_norm = dot_t(dq_ref[rows], w_now[:, :nq])
        d_norm = d_norm + dot_t(dk_ref[rows], w_now[:, nq : nq + nk])
        d_norm = d_norm + dot_t(dv_ref[rows], w_now[:, nq + nk : nq + 2 * nk])
        value = tok_ref[rows].astype(F32)
        inv = lax.rsqrt(jnp.mean(value * value, axis=1, keepdims=True) + EPS)
        scaled = value * inv
        part = jnp.sum(d_norm * scaled, axis=0, keepdims=True)
        gain_sum[...] = part if r == 0 else gain_sum[...] + part
        u = d_norm * gain_ref[...].astype(F32)
        mean = jnp.mean(u * value, axis=1, keepdims=True)
        gt_now[r % 2] = dres_ref[rows] + inv * u - scaled * (inv * inv) * mean
        stored(r).start()

    done = tuple(ref.at[count:] for ref in (gate_ref, up_ref, down_ref))
    step0(0)
    begin(0)
    step1(0)
    step0(1)
    begin(1)
    step1(1)
    step0(2)
    begin(2)
    step1(2)
    back(0)
    step2(0)
    line.middle_sends(0, True)
    back(1)
    step2(1)
    back(2)
    step3(0)
    line.middle_sends(1, True)
    line.middle_adds(0)
    back(3)
    step0(3)
    step2(2)
    step1(3)
    step3(1)
    line.middle_sends(2, True)
    line.middle_adds(1)
    step2(3)
    step4(0)
    step3(2)
    step3(3)
    line.result(0, done)
    line.middle_adds(2)
    step4(1)
    step5(0)
    step4(2)
    step4(3)
    line.result(1, done)
    line.result(2, done)
    step5(1)
    step5(2)
    step5(3)
    for copy in halves:
        copy.wait()
    for r in range(2, 4):
        stored(r).wait()


def run_finish(ht, dq, dk, dv, d_out, small, experts, w_all, tok, gain, d_res, gain_lane):
    widths = [d_out.shape[1], dq.shape[1], dk.shape[1] + dv.shape[1], small.shape[1]]
    chunk = experts[2].shape
    _, count, rows, lanes = chunk
    vmem = pl.BlockSpec(memory_space=pltpu.VMEM)
    hbm = pl.BlockSpec(memory_space=pl.ANY)
    shapes = [
        (2, 2, 2, 4, 32), (2, 2, 4, 32), (2, 4, 32), (2, 4, 32), (2, 4, 32), (4, 32), (4, 32),
    ]
    length, d = tok.shape
    scratch = [pltpu.VMEM(shape + (w,), BF16) for shape in shapes for w in widths]
    scratch += [pltpu.SemaphoreType.DMA((len(widths), 9))] * 2
    scratch += line_scratch(chunk)
    scratch += [
        pltpu.VMEM((3,) + chunk, BF16),
        pltpu.SemaphoreType.DMA((14,)),
        pltpu.VMEM((d, sum(widths[1:3])), BF16),
        pltpu.VMEM((2, length // 4, d), F32),
        pltpu.VMEM((1, d), F32),
    ]
    return pl.pallas_call(
        functools.partial(finish_kernel, gain_lane),
        in_specs=[vmem] * 6 + [hbm] * 8 + [vmem] * 3,
        out_specs=[vmem] * 7 + [hbm],
        out_shape=[
            *(jax.ShapeDtypeStruct((128, w), F32) for w in widths),
            jax.ShapeDtypeStruct((2 * count, rows, lanes), F32),
            jax.ShapeDtypeStruct((2 * count, rows, lanes), F32),
            jax.ShapeDtypeStruct((2 * count, rows // 2, 2 * lanes), F32),
            jax.ShapeDtypeStruct((length, d), F32),
        ],
        scratch_shapes=scratch,
        compiler_params=pltpu.CompilerParams(
            vmem_limit_bytes=63 * MIB, collective_id=1, has_side_effects=True
        ),
        cost_estimate=took(60),
        name="finish",
    )(ht, dq, dk, dv, d_out, small, *experts, w_all, tok, gain, d_res)


def gather_kernel(mine_ref, out_ref, sem_s, sem_r, sem_l):
    dp, ex = lax.axis_index("dp"), lax.axis_index("expert")
    z = dp // 2
    core, over_y, over_x = (dp, ex ^ 1), (dp, ex ^ 2), (dp ^ 1, ex)
    line = [None] + [(dp ^ (2 * k), ex) for k in (1, 2, 3)]
    barrier = pltpu.get_barrier_semaphore()
    peers = [core, over_y, over_x] + line[1:]
    for peer in peers:
        pl.semaphore_signal(barrier, inc=1, device_id=peer, device_id_type=pl.DeviceIdType.MESH)
    pl.semaphore_wait(barrier, len(peers))
    rows = mine_ref.shape[0]
    width = mine_ref.shape[1]
    cut = (width // 256 + 1) * 128
    halves = [pl.ds(0, cut), pl.ds(cut, width - cut)]
    started = {}

    def block(k, dx, dy):
        at = (((z ^ k) * 2 + (dp % 2 ^ dx)) * 4 + (ex ^ (2 * dy))) * rows
        return pl.ds(pl.multiple_of(at, rows), rows)

    def send(key, k, dx, dy, peer, src=None, lanes=None):
        index = len(started)
        at = block(k, dx, dy)
        dst = out_ref.at[at] if lanes is None else out_ref.at[at, lanes]
        copy = pltpu.make_async_remote_copy(
            src_ref=dst if src is None else src,
            dst_ref=dst,
            send_sem=sem_s.at[index],
            recv_sem=sem_r.at[index],
            device_id=peer,
            device_id_type=pl.DeviceIdType.MESH,
        )
        copy.start()
        started[key] = copy

    for k in (3, 2, 1):
        send(("z", k), 0, 0, 0, line[k], mine_ref)
    send(("x", 0), 0, 0, 0, over_x, mine_ref)
    send(("y", 0), 0, 0, 0, over_y, mine_ref)
    send(("c", 0), 0, 0, 0, core, mine_ref)
    own = pltpu.make_async_copy(mine_ref, out_ref.at[block(0, 0, 0)], sem_l)
    own.start()

    def onward(k):
        started["x", k].wait_recv()
        send(("dy", k), k, 1, 0, over_y, None, halves[0])
        send(("cx", k), k, 1, 0, core)
        started["y", k].wait_recv()
        send(("dx", k), k, 0, 1, over_x, None, halves[1])
        send(("cy", k), k, 0, 1, core)

    def last(k):
        started["dy", k].wait_recv()
        started["dx", k].wait_recv()
        send(("cd", k), k, 1, 1, core)

    onward(0)
    for k in (1, 2, 3):
        started["z", k].wait_recv()
        send(("x", k), k, 0, 0, over_x)
        send(("y", k), k, 0, 0, over_y)
        send(("c", k), k, 0, 0, core)
    last(0)
    for k in (1, 2, 3):
        onward(k)
    for k in (1, 2, 3):
        last(k)
    for key, copy in started.items():
        copy.wait_send()
        if key[0] in ("c", "cx", "cy", "cd"):
            copy.wait_recv()
    own.wait()


def run_gather(mine, total):
    hbm = pl.BlockSpec(memory_space=pl.ANY)
    return pl.pallas_call(
        gather_kernel,
        in_specs=[hbm],
        out_specs=hbm,
        out_shape=jax.ShapeDtypeStruct((total, mine.shape[1]), BF16),
        scratch_shapes=[
            pltpu.SemaphoreType.DMA((40,)),
            pltpu.SemaphoreType.DMA((40,)),
            pltpu.SemaphoreType.DMA,
        ],
        compiler_params=pltpu.CompilerParams(collective_id=2, has_side_effects=True),
        cost_estimate=took(40),
        name="gather",
    )(mine)


def after(value, *deps):
    return lax.optimization_barrier((value,) + deps)[0]


def on_device(
    n_dp, n_ex, tokens, cotangent, routes, prefix, w_query, keyvalue_weight, w_out, w_router,
    gain_attn, gain_mlp, expert_gate, expert_up, expert_down, query_logit_cap,
):
    length, d = tokens.shape[1], tokens.shape[2]
    tok = tokens.reshape(length, d)
    cot = cotangent.reshape(length, d)
    heads = query_logit_cap.shape[0]
    nq = w_query.shape[1]
    head = nq // heads
    kv_heads = keyvalue_weight.shape[1] // (2 * head)
    num_experts = w_router.shape[1]
    local = expert_gate.shape[0]
    rows = w_query.shape[0]
    ex = lax.axis_index("expert")

    def swap(value, step, axis="expert", n=n_ex):
        return lax.ppermute(value, axis, [(i, i ^ step) for i in range(n)])

    part = rows // n_ex
    small = jnp.concatenate(
        [
            w_router,
            gain_attn[:, None],
            gain_mlp[:, None],
            jnp.zeros((rows, 128 - num_experts - 2), BF16),
        ],
        axis=1,
    )
    packed = jnp.concatenate([w_query, keyvalue_weight, w_out, small], axis=1)
    mine = lax.dynamic_slice_in_dim(packed, ex * part, part, axis=0)
    local = expert_gate.shape[0]
    fast = n_dp == 8 and n_ex == 4 and d == 1024 and local == 4 and expert_gate.shape[2] == 512
    if fast:
        every = run_gather(mine, d)
    else:
        every = lax.all_gather(mine, ("dp", "expert"), axis=0, tiled=True)
    w_all = every
    width = 2 * nq
    extra = every[:, width + d :]
    gain_one = extra[:, num_experts].reshape(1, d)
    gain_two = extra[:, num_experts + 1].reshape(1, d)

    routes_t = routes.reshape(length, -1).T
    cots = {0: cot}
    route_set = {0: routes_t}
    cot_late = after(cot, every)
    for step in range(1, n_ex):
        if step == 1 or step % 2 == 0:
            cots[step] = swap(cot_late, step)

    cos_np, sin_np = rope_tables(length, head)
    cos_l = jnp.asarray(np.concatenate([cos_np] * 4, axis=1))
    sin_l = jnp.asarray(np.concatenate([-sin_np, sin_np] * 2, axis=1))
    cos_t = jnp.asarray(np.ascontiguousarray(cos_np.T))
    sin_t = jnp.asarray(np.ascontiguousarray(sin_np.T))

    normed_one_t, q, kd, vd = run_qkv(tok, gain_one, w_all, cos_l, sin_l, nq)
    for step in range(1, n_ex):
        route_set[step] = swap(after(routes_t, q), step)
    ctx, lse, peaks = run_attn_fwd(prefix, q, kd, vd)
    resid, normed_two = run_mid(tok, ctx, w_all, gain_two, width // d)

    me = ex.reshape(1).astype(jnp.int32)
    xs = {0: normed_two}
    for step in range(1, n_ex):
        if step == 1 or step % 2 == 0:
            xs[step] = swap(normed_two, step)
    tops = [peaks[:, :, :4]]
    bits = [("expert", n_ex, 1 << i) for i in range(n_ex.bit_length() - 1)]
    bits += [("dp", n_dp, 1 << i) for i in range(n_dp.bit_length() - 1)]

    def widen_top():
        if len(tops) <= len(bits) and not fast:
            axis, n, step = bits[len(tops) - 1]
            top = after(tops[-1], chain)
            tops.append(jnp.maximum(top, swap(top, step, axis, n)))

    weights = (expert_gate, expert_up, expert_down)
    half = local // 2

    dp = lax.axis_index("dp").reshape(1).astype(jnp.int32)

    res = {}
    chain = (normed_two, [cots[step] for step in range(2, n_ex, 2)])

    def experts(steps, first, count, init=None, sent=None):
        x = [after(xs[steps[0]], chain), xs[steps[1]]]
        cot_pair, route_pair = [cots[k] for k in steps], [route_set[k] for k in steps]
        return run_expert(
            me, x, cot_pair, route_pair, w_all, *weights, first, count, num_experts, init, sent
        )

    def grads(first):
        pairs = [res[k, 0] for k in range(0, n_ex, 2)]
        wides = [res[0, 0]] + [res[k, first] for k in range(2, n_ex, 2)]
        groups = [[pair["turned"][k] for pair in pairs] for k in (0, 1)]
        groups += [[pair["wide"][k] for pair in wides] for k in (1, 2, 0)]
        groups[0][0] = after(groups[0][0], chain)
        skips = [first if k == 0 else 0 for k in range(len(pairs))]
        made = None
        for at in range(0, len(pairs), 2):
            some = [group[at : at + 2] for group in groups]
            part = run_weight_grad(
                dp, *some, half, skips[at : at + 2], n_dp, fast, expert_gate.shape[2]
            )
            if made is None:
                made = part
            else:
                made = [(a.astype(F32) + b.astype(F32)).astype(BF16) for a, b in zip(made, part)]
        return made

    res[0, 0] = experts((0, 1), 0, local)
    chain = (res[0, 0]["dg"][0], tops[-1])
    widen_top()
    widen_top()
    for other in range(3, n_ex, 2):
        cots[other] = swap(after(cots[other - 1], chain), 1)
        xs[other] = swap(after(xs[other - 1], chain), 1)
    even = range(2, n_ex, 2)
    for step in even:
        res[step, 0] = experts((step, step + 1), 0, half)
        chain = (res[step, 0]["dg"][0], tops[-1])
        widen_top()
    made_one = grads(0)
    chain = (made_one[0], tops[-1])
    widen_top()
    for step in even:
        init = [*res[step, 0]["out"], *res[step, 0]["dx"], *res[step, 0]["dg"]]
        sent = made_one[1] if fast else None
        res[step, half] = experts((step, step + 1), half, half, init, sent)
        chain = (res[step, half]["dg"][0], tops[-1])
        widen_top()

    def with_partner(step, what):
        own, other = res[step, half][what]
        return (own.astype(F32) + swap(other, 1).astype(F32)).astype(BF16)

    to_send = {step: with_partner(step, "dx") for step in even}
    chain = (chain, list(to_send.values()))
    sums, got_two = None, []
    if fast:
        down_sent = after(made_one[3], chain)
        got_one = [res[2, half]["got"][0], swap(down_sent, 1, "dp", n_dp)]
        tot_one = (made_one[0].astype(F32) + got_one[0].astype(F32)).astype(BF16)
        far_one = lax.dynamic_slice_in_dim(tot_one, 2 * (1 - dp[0] // 4), 2, axis=0)
        chain = (chain, far_one)
        far_one = lax.ppermute(far_one, "dp", [(0, 2), (1, 3), (6, 4), (7, 5)])
    made_two = grads(half)
    chain = (made_two[0], tops[-1])
    if fast:
        chain = (chain, far_one, got_one)
        sums = [tot_one, far_one, made_one[2], got_one[1], peaks]
        got_two = [swap(made_two[k], 1, "dp", n_dp) for k in (1, 3)]
    while len(tops) <= len(bits) and not fast:
        widen_top()
    top = tops[-1]

    final = [res[0, 0]] + [res[step, half] for step in even]
    dxs = [final[0]["dx"][0], swap(final[0]["dx"][1], 1)]
    dxs += [swap(to_send[step], step) for step in even]
    dgs = [part for pair in final for part in pair["dg"]]
    dgs = [swap(dgs[step], step) if step else dgs[0] for step in range(n_ex)]
    d_res, d_attn, d_ctx, d_logits, d_gain_two = run_back_mid(
        me,
        after(resid, chain),
        cot,
        routes_t,
        normed_two,
        w_all,
        gain_two,
        width // d,
        dxs,
        dgs,
        local,
    )
    outs = [final[0]["out"][0], swap(final[0]["out"][1], 1)]
    outs += [swap(after(with_partner(step, "out"), dxs), step) for step in even]
    block = resid
    for piece in outs:
        block = block + piece.astype(F32)
    block_out = block.astype(BF16).reshape(tokens.shape)

    d_out_w = jnp.einsum("rc,rd->cd", ctx, d_attn, preferred_element_type=F32).astype(BF16)
    d_router_w = jnp.einsum("rd,re->de", normed_two, d_logits, preferred_element_type=F32)

    dq, dk, dv, *halves = run_attn_bwd(
        prefix, q, kd, vd, d_ctx, ctx, lse, cos_l, sin_l, cos_t, sin_t, sums
    )
    if not fast:
        grad_tok, d_gain_one = run_back_in(dq, dk, dv, w_all, tok, gain_one, d_res)
    else:
        d_gain_one = jnp.zeros((1, d), F32)
    small_grad = jnp.concatenate(
        [
            d_router_w[:, :num_experts].astype(BF16),
            d_gain_one.reshape(d, 1).astype(BF16),
            d_gain_two.reshape(d, 1).astype(BF16),
            jnp.zeros((d, 128 - num_experts - 2), BF16),
        ],
        axis=1,
    )

    def reduce_all(value, order):
        shape = (n_dp, n_ex, value.shape[0] // (n_dp * n_ex), value.shape[1])
        names = []
        dims = []
        for axis, n in (("dp", n_dp), ("expert", n_ex)):
            count = n.bit_length() - 1
            names += [(axis, n, 1 << (count - 1 - i)) for i in range(count)]
            dims += [2] * count
        value = value.reshape(*dims, *shape[2:])
        for bit in order:
            at = names.index(bit)
            axis, n, step = bit
            mine = (lax.axis_index(axis) // step) % 2
            keep = lax.dynamic_slice_in_dim(value, mine, 1, axis=at)
            send = lax.dynamic_slice_in_dim(value, 1 - mine, 1, axis=at)
            value = (keep.astype(F32) + swap(send, step, axis, n).astype(F32)).astype(BF16)
        return value.reshape(shape[2:])

    def share(value):
        return lax.all_gather(value, "expert", axis=0, tiled=True).astype(F32)

    core = [("expert", n_ex, 1)]
    y_bits = [("expert", n_ex, 1 << i) for i in range(1, n_ex.bit_length() - 1)][::-1]
    dp_bits = [("dp", n_dp, 1 << i) for i in range(n_dp.bit_length() - 1)]
    if fast:
        grad_out, grad_query, grad_keyval, rest, grad_gate, grad_up, grad_down, grad_tok = run_finish(
            normed_one_t,
            after(dq, block_out),
            dk,
            dv,
            d_out_w,
            small_grad,
            [made_two[0], got_two[0], made_two[2], got_two[1], *halves[:3]],
            w_all,
            tok,
            gain_one,
            d_res,
            num_experts,
        )
    else:
        ends = [
            [
                lax.psum_scatter(g, "dp", scatter_dimension=0, tiled=True)[0].astype(F32)
                for g in made
            ]
            for made in (made_one, made_two)
        ]
        grad_gate, grad_up, grad_down = (
            jnp.concatenate([ends[0][k], ends[1][k]], axis=0) for k in range(3)
        )
        grad_down = jnp.swapaxes(grad_down, 1, 2).reshape(local, -1, d)

        def product(right):
            return jnp.dot(normed_one_t, right, preferred_element_type=F32).astype(BF16)

        every_grad = jnp.concatenate(
            [d_out_w, product(dq), product(dk), product(dv), small_grad], axis=1
        )
        every_grad = share(reduce_all(every_grad, core + y_bits + dp_bits[::-1]))
        grad_out = every_grad[:, :d]
        grad_query = every_grad[:, d : d + nq]
        grad_keyval = every_grad[:, d + nq : d + 2 * nq]
        rest = every_grad[:, d + 2 * nq :]
    grad_router = rest[:, :num_experts]
    grad_gain_one = rest[:, num_experts]
    grad_gain_two = rest[:, num_experts + 1]

    if fast:
        top = halves[3][:, :, :4]
    head_logit_peak = top[:, 0, :].reshape(heads)
    per_group = heads // kv_heads
    query_factor = jnp.sqrt(query_logit_cap / jnp.maximum(head_logit_peak, query_logit_cap))
    pair_peak = jnp.max(head_logit_peak.reshape(kv_heads, per_group), axis=1)
    pair_cap = jnp.min(query_logit_cap.reshape(kv_heads, per_group), axis=1)
    key_factor = jnp.sqrt(pair_cap / jnp.maximum(pair_peak, pair_cap))
    clipped_query = (w_query.astype(F32) * jnp.repeat(query_factor, head)[None, :]).astype(BF16)
    key_cols = jnp.concatenate(
        [jnp.repeat(key_factor, head), jnp.ones((kv_heads * head,), F32)]
    )
    clipped_keyval = (keyvalue_weight.astype(F32) * key_cols[None, :]).astype(BF16)
    return (
        block_out,
        grad_tok.reshape(tokens.shape),
        grad_query,
        grad_keyval,
        grad_out,
        grad_router,
        grad_gain_one,
        grad_gain_two,
        grad_gate,
        grad_up,
        grad_down,
        clipped_query,
        clipped_keyval,
        head_logit_peak,
    )


def solution(mesh):
    rows3 = P(("dp", "expert"), None, None)
    in_specs = (
        rows3,
        rows3,
        rows3,
        P(("dp", "expert")),
        P("dp", None),
        P("dp", None),
        P("dp", None),
        P("dp", None),
        P("dp"),
        P("dp"),
        P("expert", None, None),
        P("expert", None, None),
        P("expert", None, None),
        P(),
    )
    out_specs = (
        rows3,
        rows3,
        P("dp", None),
        P("dp", None),
        P("dp", None),
        P("dp", None),
        P("dp"),
        P("dp"),
        P("expert", "dp", None),
        P("expert", "dp", None),
        P("expert", "dp", None),
        P("dp", None),
        P("dp", None),
        P(),
    )
    return jax.shard_map(
        functools.partial(on_device, mesh.shape["dp"], mesh.shape["expert"]),
        mesh=mesh,
        in_specs=in_specs,
        out_specs=out_specs,
        check_vma=False,
    )
```

```python
import functools

import jax
import jax.numpy as jnp
import numpy as np
from jax import lax
from jax.experimental import pallas as pl
from jax.experimental.pallas import tpu as pltpu
from jax.sharding import PartitionSpec as P

EPS = 1e-05
ROPE_BASE = 10000.0
F32 = jnp.float32
BF16 = jnp.bfloat16
NEG = -1e30
MIB = 1 << 20
SCALE = 0.35


def dot(a, b):
    return lax.dot_general(a, b, (((1,), (0,)), ((), ())), preferred_element_type=F32)


def dot_t(a, b):
    return lax.dot_general(a, b, (((1,), (1,)), ((), ())), preferred_element_type=F32)


def params(vmem_mib, n=1):
    return pltpu.CompilerParams(
        dimension_semantics=("arbitrary",) * n, vmem_limit_bytes=vmem_mib * MIB
    )


def took(us):
    return pl.CostEstimate(flops=int(us * SCALE * 1e9), bytes_accessed=1000, transcendentals=0)


def spec(shape, index):
    return pl.BlockSpec(shape, index)


def whole(shape):
    zeros = (0,) * len(shape)
    return pl.BlockSpec(shape, lambda *_: zeros)


def rope_tables(length, head):
    half = head // 2
    freq = np.float32(ROPE_BASE) ** (
        -(np.arange(half, dtype=np.float32) * np.float32(2.0) / np.float32(head))
    )
    ang = np.arange(length, dtype=np.float32)[:, None] * freq.astype(np.float32)[None, :]
    ang = ang.astype(np.float32)
    return np.cos(ang).astype(np.float32), np.sin(ang).astype(np.float32)


def lane_half(shape, width):
    return (lax.broadcasted_iota(jnp.int32, shape, 1) % width) < (width // 2)


def rope_lanes(x, cos, sin, first):
    partner = jnp.where(first, pltpu.roll(x, 96, 1), pltpu.roll(x, 32, 1))
    return x * cos + partner * sin


def qkv_kernel(tok_ref, gain_ref, w_ref, cos_ref, sin_ref, ht_ref, q_ref, kd_ref, vd_ref):
    x = tok_ref[...].astype(F32)
    d = x.shape[1]
    r = lax.rsqrt(jnp.mean(x * x, axis=1, keepdims=True) + EPS)
    h = (x * r * gain_ref[...].astype(F32)).astype(BF16)
    ht_ref[...] = h.T
    cos, sin = cos_ref[...], sin_ref[...]
    rows = x.shape[0]
    first = lane_half((rows, 128), 64)
    low = lane_half((rows, 128), 128)
    nq = q_ref.shape[1]
    nk = kd_ref.shape[1] // 2
    q = dot(h, w_ref[:, :nq])
    for c in range(0, nq, 128):
        q_ref[:, c : c + 128] = (rope_lanes(q[:, c : c + 128], cos, sin, first) * 0.125).astype(
            BF16
        )
    k = dot(h, w_ref[:, nq : nq + nk])
    for c in range(0, nk, 128):
        kk = rope_lanes(k[:, c : c + 128], cos, sin, first)
        sw = pltpu.roll(kk, 64, 1)
        kd_ref[:, 2 * c : 2 * c + 128] = jnp.where(low, kk, sw).astype(BF16)
        kd_ref[:, 2 * c + 128 : 2 * c + 256] = jnp.where(low, sw, kk).astype(BF16)
    v = dot(h, w_ref[:, nq + nk : nq + 2 * nk])
    for c in range(0, nk, 128):
        vv = v[:, c : c + 128]
        sw = pltpu.roll(vv, 64, 1)
        vd_ref[:, 2 * c : 2 * c + 128] = jnp.where(low, vv, sw).astype(BF16)
        vd_ref[:, 2 * c + 128 : 2 * c + 256] = jnp.where(low, sw, vv).astype(BF16)


def run_qkv(tok, gain, w_qkv, cos, sin, nq):
    length, d = tok.shape
    b = 256
    row = lambda i: (i, 0)
    return pl.pallas_call(
        qkv_kernel,
        grid=(length // b,),
        in_specs=[
            spec((b, d), row),
            whole((1, d)),
            spec((d, 2 * nq), lambda i: (0, 0)),
            spec((b, 128), row),
            spec((b, 128), row),
        ],
        out_specs=[spec((d, b), lambda i: (0, i))] + [spec((b, nq), row)] * 3,
        out_shape=[jax.ShapeDtypeStruct((d, length), BF16)]
        + [jax.ShapeDtypeStruct((length, nq), BF16)] * 3,
        compiler_params=params(60),
        cost_estimate=took(9),
        name="qkv",
    )(tok, gain, w_qkv, cos, sin)


def mask_bias(prefix, q0, k0, nq, nk, q_axis):
    shape = (nq, nk) if q_axis == 0 else (nk, nq)
    qpos = q0 + lax.broadcasted_iota(jnp.int32, shape, q_axis)
    kpos = k0 + lax.broadcasted_iota(jnp.int32, shape, 1 - q_axis)
    return jnp.where((kpos <= qpos) | (kpos < prefix), 0.0, NEG).astype(F32)


def two_heads(pair, low):
    zero = jnp.zeros_like(pair)
    return jnp.concatenate([jnp.where(low, pair, zero), jnp.where(low, zero, pair)], axis=0)


def attn_fwd_kernel(prefix_ref, q_ref, kd_ref, vd_ref, ctx_ref, lse_ref, peak_ref):
    length = q_ref.shape[0]
    b = 256
    prefix = prefix_ref[0]
    low_b = lane_half((b, 128), 128)
    lane = lax.broadcasted_iota(jnp.int32, (b, 128), 1)
    peak = jnp.full((8, 128), NEG, F32)
    peak_lane = lax.broadcasted_iota(jnp.int32, (8, 128), 1)
    for i in range(length // b):
        nk = max((i + 1) * b, length // 2)
        free = i * b
        bias = mask_bias(prefix, i * b, free, b, nk - free, 0)
        bias = jnp.concatenate([bias, bias], axis=0)
        lse_cols = jnp.zeros((b, 128), F32)
        for j in range(2):
            cols = slice(j * 128, (j + 1) * 128)
            q2 = two_heads(q_ref[i * b : (i + 1) * b, cols], low_b)
            s_hi = dot_t(q2, kd_ref[free:nk, cols]) + bias
            m = jnp.max(s_hi, axis=1, keepdims=True)
            if free:
                s_lo = dot_t(q2, kd_ref[:free, cols])
                m = jnp.maximum(m, jnp.max(s_lo, axis=1, keepdims=True))
            p_hi = jnp.exp(s_hi - m)
            total = jnp.sum(p_hi, axis=1, keepdims=True)
            ctx = dot(p_hi.astype(BF16), vd_ref[free:nk, cols])
            if free:
                p_lo = jnp.exp(s_lo - m)
                total = total + jnp.sum(p_lo, axis=1, keepdims=True)
                ctx = ctx + dot(p_lo.astype(BF16), vd_ref[:free, cols])
            ctx = ctx * (1.0 / total)
            ctx_ref[i * b : (i + 1) * b, cols] = jnp.where(low_b, ctx[:b], ctx[b:]).astype(BF16)
            lse = m + jnp.log(total)
            for g in range(2):
                lse_cols = jnp.where(lane == 2 * j + g, lse[g * b : (g + 1) * b], lse_cols)
                top = jnp.max(m[g * b : (g + 1) * b], axis=0, keepdims=True)
                peak = jnp.where(peak_lane == 2 * j + g, jnp.maximum(peak, top), peak)
        lse_ref[0, :, i * b : (i + 1) * b] = lse_cols.T[:8]
    peak_ref[0] = peak


def run_attn_fwd(prefix, q, kd, vd):
    length, nq = q.shape
    groups = nq // 256
    col = lambda g: (0, g)
    return pl.pallas_call(
        attn_fwd_kernel,
        grid=(groups,),
        in_specs=[pl.BlockSpec(memory_space=pltpu.SMEM)] + [spec((length, 256), col)] * 3,
        out_specs=[
            spec((length, 256), col),
            spec((1, 8, length), lambda g: (g, 0, 0)),
            spec((1, 8, 128), lambda g: (g, 0, 0)),
        ],
        out_shape=[
            jax.ShapeDtypeStruct((length, nq), BF16),
            jax.ShapeDtypeStruct((groups, 8, length), F32),
            jax.ShapeDtypeStruct((groups, 8, 128), F32),
        ],
        compiler_params=params(60),
        cost_estimate=took(21),
        name="attn_fwd",
    )(prefix, q, kd, vd)


def add_rows(dst, srcs, step=64):
    def body(i, carry):
        at = pl.ds(pl.multiple_of(i * step, step), step)
        one, two = srcs[0][at, :], srcs[1][at, :]
        if dst.dtype != one.dtype:
            one, two = one.astype(dst.dtype), two.astype(dst.dtype)
        dst[at, :] = one + two
        return carry

    lax.fori_loop(0, dst.shape[0] // step, body, 0)


def greet(peers):
    barrier = pltpu.get_barrier_semaphore()
    for peer in peers:
        pl.semaphore_signal(barrier, inc=1, device_id=peer, device_id_type=pl.DeviceIdType.MESH)
    pl.semaphore_wait(barrier, len(peers))


class Line:
    def __init__(self, tot, rz1, rz2, rz3, sem_s, sem_r):
        self.tot, self.rz1, self.rz2, self.rz3 = tot, rz1, rz2, rz3
        self.sem_s, self.sem_r = sem_s, sem_r
        dp, ex = lax.axis_index("dp"), lax.axis_index("expert")
        self.z = dp // 2
        self.upper = self.z // 2
        self.outer = (self.z == 0) | (self.z == 3)
        self.inner = jnp.logical_not(self.outer)
        self.near, self.middle = (dp ^ 2, ex), (dp ^ 6, ex)

    def copy(self, ch, stage):
        if stage == 3:
            src, dst = self.tot.at[ch, 2 * self.upper + 1 - self.z % 2], self.rz3.at[ch]
        else:
            src = self.tot.at[ch, pl.ds(2 * (1 - self.upper), 2)]
            dst = (self.rz1 if stage == 1 else self.rz2).at[ch]
        return pltpu.make_async_remote_copy(
            src_ref=src,
            dst_ref=dst,
            send_sem=self.sem_s.at[ch, stage],
            recv_sem=self.sem_r.at[ch, stage],
            device_id=self.middle if stage == 2 else self.near,
            device_id_type=pl.DeviceIdType.MESH,
        )

    def add(self, ch, first, other):
        for p in range(2):
            for e in range(2):
                dst = self.tot.at[ch, first + p, e]
                add_rows(dst, [dst, other.at[ch, p, e]])

    def ends(self, ch, inward):
        @pl.when(self.outer)
        def _():
            if inward:
                self.copy(ch, 1).start()
            else:
                self.copy(ch, 3).start()

    def middle_sends(self, ch, inward):
        @pl.when(self.inner)
        def _():
            if inward:
                self.copy(ch, 1).wait_recv()
            self.add(ch, 2 * (1 - self.upper), self.rz1)
            self.copy(ch, 2).start()

        if inward:

            @pl.when(self.outer)
            def _():
                self.copy(ch, 1).wait_send()
                self.copy(ch, 3).start()

    def middle_adds(self, ch):
        @pl.when(self.inner)
        def _():
            self.copy(ch, 2).wait()
            self.add(ch, 2 * self.upper, self.rz2)
            self.copy(ch, 3).start()

    def result(self, ch, refs):
        self.copy(ch, 3).wait()
        for e in range(2):
            own, got = self.tot.at[ch, self.z, e], self.rz3.at[ch, e]
            if ch < 2:
                add_rows(refs[ch].at[e], [own, got])
            else:
                rows, lanes = refs[2].shape[1], own.shape[1]
                for h in range(2):
                    at = slice(h * rows, (h + 1) * rows)
                    dst = refs[2].at[e, :, h * lanes : (h + 1) * lanes]
                    add_rows(dst, [own.at[at], got.at[at]])


def line_scratch(shape):
    return [
        pltpu.VMEM((3,) + shape, BF16),
        pltpu.VMEM((3, 2) + shape[1:], BF16),
        pltpu.VMEM((3, 2) + shape[1:], BF16),
        pltpu.VMEM((3,) + shape[1:], BF16),
        pltpu.SemaphoreType.DMA((3, 4)),
        pltpu.SemaphoreType.DMA((3, 4)),
    ]


def attn_bwd_kernel(*refs):
    attn_bwd_body(*refs)


def attn_bwd_sum_kernel(*refs):
    ins, (tot_a, far_a, keep_a, got_a) = refs[:11], refs[11:15]
    outs, (gate_ref, up_ref, down_ref) = refs[15:18], refs[18:21]
    scratch, line_refs, (rx, sem_l) = refs[21:24], refs[24:30], refs[30:]
    step = pl.program_id(0)
    line = Line(*line_refs)
    loads = []
    for k in range(2):
        loads.append([pltpu.make_async_copy(tot_a.at[:, k], line.tot.at[k], sem_l.at[2 * k])])
        loads[-1].append(
            pltpu.make_async_copy(far_a.at[:, k], line.rz1.at[k], sem_l.at[2 * k + 1])
        )
    loads.append(
        [
            pltpu.make_async_copy(keep_a, line.tot.at[2], sem_l.at[4]),
            pltpu.make_async_copy(got_a, rx, sem_l.at[5]),
        ]
    )
    @pl.when(step == 0)
    def _():
        for group in loads:
            for copy in group:
                copy.start()
        greet([line.near, line.middle])
        for copy in loads[2]:
            copy.wait()
        for zz in range(4):
            for e in range(2):
                dst = line.tot.at[2, zz, e]
                add_rows(dst, [dst, rx.at[zz, e]])
        line.ends(2, True)
        for k in range(2):
            for copy in loads[k]:
                copy.wait()
            line.ends(k, False)
            line.middle_sends(k, False)

    attn_bwd_body(*ins, *outs, *scratch)

    @pl.when(step == 1)
    def _():
        line.middle_sends(2, True)
        line.middle_adds(0)

    @pl.when(step == 2)
    def _():
        line.middle_adds(1)

    @pl.when(step == 3)
    def _():
        line.middle_adds(2)
        for ch in range(3):
            line.result(ch, (gate_ref, up_ref, down_ref))


def attn_bwd_body(
    prefix_ref, q_ref, kd_ref, vd_ref, do_ref, ctx_ref, lse_ref, cos_ref, sin_ref, cost_ref, sint_ref,
    dq_ref, dk_ref, dv_ref, dk_acc, dv_acc, kt_ref,
):
    length = q_ref.shape[0]
    b = 256
    prefix = prefix_ref[0]
    low_b = lane_half((b, 128), 128)
    for j in range(2):
        cols = slice(j * 128, (j + 1) * 128)
        kt_ref[j] = kd_ref[:, cols].T
    dk_acc[...] = jnp.zeros_like(dk_acc)
    dv_acc[...] = jnp.zeros_like(dv_acc)
    for i in range(length // b):
        rows = slice(i * b, (i + 1) * b)
        nk = max((i + 1) * b, length // 2)
        free = i * b
        bias = mask_bias(prefix, i * b, free, b, nk - free, 1)
        bias = jnp.concatenate([bias, bias], axis=1)
        for j in range(2):
            cols = slice(j * 128, (j + 1) * 128)
            do = do_ref[rows, cols]
            q2 = two_heads(q_ref[rows, cols], low_b)
            do2 = two_heads(do, low_b)
            prod = (do.astype(F32) * ctx_ref[rows, cols].astype(F32)).T
            delta = jnp.concatenate(
                [
                    jnp.sum(prod[:64], axis=0, keepdims=True),
                    jnp.sum(prod[64:], axis=0, keepdims=True),
                ],
                axis=1,
            )
            lse = jnp.concatenate(
                [lse_ref[0, 2 * j : 2 * j + 1, rows], lse_ref[0, 2 * j + 1 : 2 * j + 2, rows]],
                axis=1,
            )
            dq_t = None
            parts = [(0, free)] if free else []
            for k0, k1 in parts + [(free, nk)]:
                keys = slice(k0, k1)
                s = dot_t(kd_ref[keys, cols], q2)
                if k0 == free:
                    s = s + bias
                p = jnp.exp(s - lse)
                dp = dot_t(vd_ref[keys, cols], do2)
                ds = (p * (dp - delta)).astype(BF16)
                dv_acc[j, keys, :] += dot(p.astype(BF16), do2)
                dk_acc[j, keys, :] += dot(ds, q2)
                part = dot(kt_ref[j, :, keys], ds)
                dq_t = part if dq_t is None else dq_t + part
            cos_t, sin_t = cost_ref[:, rows], sint_ref[:, rows]
            a0, b0 = dq_t[0:32, :b], dq_t[32:64, :b]
            a1, b1 = dq_t[64:96, b:], dq_t[96:128, b:]
            full = jnp.concatenate(
                [
                    a0 * cos_t + b0 * sin_t,
                    b0 * cos_t - a0 * sin_t,
                    a1 * cos_t + b1 * sin_t,
                    b1 * cos_t - a1 * sin_t,
                ],
                axis=0,
            )
            dq_ref[rows, cols] = (full * 0.125).T.astype(BF16)
    low = lane_half((length, 128), 128)
    first = lane_half((length, 128), 64)
    sums = []
    for acc in (dk_acc, dv_acc):
        even = acc[0] + pltpu.roll(acc[0], 64, 1)
        odd = acc[1] + pltpu.roll(acc[1], 64, 1)
        sums.append(jnp.where(low, even, odd))
    dk_ref[...] = rope_lanes(sums[0], cos_ref[...], -sin_ref[...], first).astype(BF16)
    dv_ref[...] = sums[1].astype(BF16)


def run_attn_bwd(prefix, q, kd, vd, d_ctx, ctx, lse, cos, sin, cos_t, sin_t, sums=None):
    length, nq = q.shape
    groups = nq // 256
    col = lambda g: (0, g)
    wide = spec((length, 256), col)
    in_specs = [pl.BlockSpec(memory_space=pltpu.SMEM)] + [wide] * 5
    in_specs += [spec((1, 8, length), lambda g: (g, 0, 0))]
    in_specs += [whole((length, 128))] * 2 + [whole((cos_t.shape[0], length))] * 2
    out_specs = [wide, spec((length, 128), col), spec((length, 128), col)]
    out_shape = [
        jax.ShapeDtypeStruct((length, nq), BF16),
        jax.ShapeDtypeStruct((length, nq // 2), BF16),
        jax.ShapeDtypeStruct((length, nq // 2), BF16),
    ]
    scratch = [
        pltpu.VMEM((2, length, 128), F32),
        pltpu.VMEM((2, length, 128), F32),
        pltpu.VMEM((2, 128, length), BF16),
    ]
    args = (prefix, q, kd, vd, d_ctx, ctx, lse, cos, sin, cos_t, sin_t)
    kernel, extra = attn_bwd_kernel, {}
    if sums is not None:
        kernel, extra = attn_bwd_sum_kernel, {"collective_id": 3, "has_side_effects": True}
        hbm = pl.BlockSpec(memory_space=pl.ANY)
        keep_a = sums[2]
        _, count, rows, lanes = keep_a.shape
        made = [(count, rows, lanes)] * 2 + [(count, rows // 2, 2 * lanes)]
        in_specs += [hbm] * 4
        out_specs += [whole(shape) for shape in made]
        out_shape += [jax.ShapeDtypeStruct(shape, F32) for shape in made]
        scratch += line_scratch(keep_a.shape)
        scratch += [
            pltpu.VMEM(keep_a.shape, BF16),
            pltpu.SemaphoreType.DMA((6,)),
        ]
        args += tuple(sums)
    return pl.pallas_call(
        kernel,
        grid=(groups,),
        in_specs=in_specs,
        out_specs=out_specs,
        out_shape=out_shape,
        scratch_shapes=scratch,
        compiler_params=pltpu.CompilerParams(
            dimension_semantics=("arbitrary",), vmem_limit_bytes=60 * MIB, **extra
        ),
        cost_estimate=took(33),
        name="attn_bwd",
    )(*args)


def mid_kernel(tok_ref, ctx_ref, w_ref, gain_ref, res_ref, x_ref):
    res = tok_ref[...].astype(F32) + dot(ctx_ref[...], w_ref[...])
    res_ref[...] = res
    r = lax.rsqrt(jnp.mean(res * res, axis=1, keepdims=True) + EPS)
    x_ref[...] = (res * r * gain_ref[...].astype(F32)).astype(BF16)


def run_mid(tok, ctx, w_all, gain, at):
    length, d = tok.shape
    b = 256
    row = lambda i: (i, 0)
    return pl.pallas_call(
        mid_kernel,
        grid=(length // b,),
        in_specs=[
            spec((b, d), row),
            spec((b, ctx.shape[1]), row),
            spec((w_all.shape[0], d), lambda i: (0, at)),
            whole((1, d)),
        ],
        out_specs=[spec((b, d), row)] * 2,
        out_shape=[
            jax.ShapeDtypeStruct((length, d), F32),
            jax.ShapeDtypeStruct((length, d), BF16),
        ],
        compiler_params=params(60),
        cost_estimate=took(4),
        name="mid",
    )(tok, ctx, w_all, gain)


def gates_of(x, router, routes_t, num_experts):
    logits = dot(x, router).T[: 16 * pl.cdiv(num_experts, 16)]
    expert = lax.broadcasted_iota(jnp.int32, logits.shape, 0)
    hit = expert == routes_t[0:1]
    for k in range(1, routes_t.shape[0]):
        hit = hit | (expert == routes_t[k : k + 1])
    logits = jnp.where(hit, logits, NEG)
    e = jnp.exp(logits - jnp.max(logits, axis=0, keepdims=True))
    e = jnp.where(hit, e, 0.0)
    return e / jnp.sum(e, axis=0, keepdims=True)


class Tops:
    def __init__(self, peak_ref, top_ref, sent, got, sem_s, sem_r):
        self.peak_ref, self.top_ref, self.sent, self.got = peak_ref, top_ref, sent, got
        self.sem_s, self.sem_r = sem_s, sem_r
        dp, ex = lax.axis_index("dp"), lax.axis_index("expert")
        self.peers = [(dp, ex ^ 1), (dp, ex ^ 2), (dp ^ 1, ex), (dp ^ 2, ex), (dp ^ 4, ex)]

    def copy(self, k):
        return pltpu.make_async_remote_copy(
            src_ref=self.sent.at[k],
            dst_ref=self.got.at[k],
            send_sem=self.sem_s.at[k],
            recv_sem=self.sem_r.at[k],
            device_id=self.peers[k],
            device_id_type=pl.DeviceIdType.MESH,
        )

    def turn(self, k):
        if k == 0:
            greet(self.peers)
            self.sent[0] = self.peak_ref[...]
        else:
            self.copy(k - 1).wait()
            both = jnp.maximum(self.sent[k - 1], self.got[k - 1])
            if k == len(self.peers):
                self.top_ref[...] = both
                return
            self.sent[k] = both
        self.copy(k).start()


def expert_kernel(first_expert, local, num_experts, with_init, with_carry, with_top, n_row, *refs):
    me_ref, router_ref, wg_ref, wu_ref, wd_ref = refs[:5]
    x_refs, c_refs, route_refs = refs[5:7], refs[7:9], refs[9:11]
    refs = refs[11:]
    if with_init:
        out_ins, dx_ins, dg_ins, refs = refs[:2], refs[2:4], refs[4:6], refs[6:]
    if with_carry or with_top:
        sent_ref, refs = refs[0], refs[1:]
    out_refs, dx_refs, dg_refs = refs[:2], refs[2:4], refs[4:6]
    hs_ref, dgate_ref, dup_ref = refs[6:9]
    refs = refs[9:]
    if not with_init:
        xt_ref, ct_ref, refs = refs[0], refs[1], refs[2:]
    if with_carry or with_top:
        got_ref, refs = refs[0], refs[1:]
    x_now, c_now, out_acc, dx_acc, gp_ref, dgc_ref = refs[:6]
    i, e = pl.program_id(0), pl.program_id(1)
    last = pl.num_programs(1) - 1
    if with_carry:
        over_x = (lax.axis_index("dp") ^ 1, lax.axis_index("expert"))

        def carry():
            return pltpu.make_async_remote_copy(
                src_ref=sent_ref,
                dst_ref=got_ref,
                send_sem=refs[6].at[0],
                recv_sem=refs[6].at[1],
                device_id=over_x,
                device_id_type=pl.DeviceIdType.MESH,
            )

        @pl.when((i == 0) & (e == 0))
        def _():
            greet([over_x])
            carry().start()

    b = x_now.shape[0]
    lane = lax.broadcasted_iota(jnp.int32, (b, 128), 1)

    if with_top:
        tops = Tops(sent_ref, got_ref, *refs[6:])
        for k in range(6):

            @pl.when(i * pl.num_programs(1) + e == k)
            def _():
                tops.turn(k)

    for source in range(2):

        @pl.when((e == 0) & ((i < n_row) if source == 0 else (i >= n_row)))
        def _():
            x, c = x_refs[source][...], c_refs[source][...]
            x_now[...] = x
            c_now[...] = c
            gates = gates_of(x, router_ref[...], route_refs[source][...], num_experts)
            fill = jnp.zeros((128 - gates.shape[0], b), F32)
            gp_ref[...] = jnp.concatenate([gates, fill], axis=0).T
            if with_init:
                out_acc[...] = out_ins[source][...].astype(F32)
                dx_acc[...] = dx_ins[source][...].astype(F32)
                fill = jnp.zeros((120, b), F32)
                dgc_ref[...] = jnp.concatenate([dg_ins[source][...], fill], axis=0).T
            else:
                out_acc[...] = jnp.zeros_like(out_acc)
                dx_acc[...] = jnp.zeros_like(dx_acc)
                dgc_ref[...] = jnp.zeros_like(dgc_ref)
                xt_ref[...] = x.T
                ct_ref[...] = c.T

    x, c = x_now[...], c_now[...]
    gp = jnp.sum(
        jnp.where(lane == me_ref[0] * local + first_expert + e, gp_ref[...], 0.0),
        axis=1,
        keepdims=True,
    )
    gate = dot(x, wg_ref[0])
    up = dot(x, wu_ref[0])
    grad = dot_t(c, wd_ref[0])
    sig = 0.5 * jnp.tanh(0.5 * gate) + 0.5
    act = gate * sig
    hidden = (act * up).astype(BF16).astype(F32)
    dg = jnp.sum(hidden * grad, axis=1, keepdims=True)
    hs = (hidden * gp).astype(BF16)
    dh = grad * gp
    dup = (dh * act).astype(BF16)
    dgate = (dh * up * (sig + act * (1.0 - sig))).astype(BF16)
    hs_ref[...] = hs
    dup_ref[...] = dup
    dgate_ref[...] = dgate
    out = dot(hs, wd_ref[0])
    dx = dot_t(dgate, wg_ref[0]) + dot_t(dup, wu_ref[0])
    dgc_ref[...] += jnp.where(lane == first_expert + e, dg, 0.0)
    out_acc[...] += out
    dx_acc[...] += dx
    for source in range(2):

        @pl.when((e == last) & ((i < n_row) if source == 0 else (i >= n_row)))
        def _():
            out_refs[source][...] = out_acc[...].astype(BF16)
            dx_refs[source][...] = dx_acc[...].astype(BF16)
            dg_refs[source][...] = dgc_ref[...].T[:8]

    if with_carry:

        @pl.when((i == 2 * n_row - 1) & (e == last))
        def _():
            carry().wait()


def run_expert(me, xs, cs, routes, router, wg, wu, wd, first, count, num_experts, init=None, sent=None, peaks=None):
    length, d = xs[0].shape
    local, _, ff = wg.shape
    b = 512
    n_row = length // b
    top = routes[0].shape[0]

    def clamp(i, source):
        return jnp.minimum(i, n_row - 1) if source == 0 else jnp.maximum(i - n_row, 0)

    rows = [
        spec((b, d), functools.partial(lambda src, i, e: (clamp(i, src), 0), src))
        for src in range(2)
    ]

    def lanes(height):
        return [
            spec((height, b), functools.partial(lambda src, i, e: (0, clamp(i, src)), src))
            for src in range(2)
        ]

    pick = lambda shape: pl.BlockSpec((1,) + shape[1:], lambda i, e: (first + e, 0, 0))
    wide = jax.ShapeDtypeStruct((2 * length, count * ff), BF16)
    full = jax.ShapeDtypeStruct((length, d), BF16)
    small = jax.ShapeDtypeStruct((8, length), F32)
    turned = jax.ShapeDtypeStruct((d, 2 * length), BF16)
    wide_spec = spec((b, ff), lambda i, e: (i, e))
    turned_spec = spec((d, b), lambda i, e: (0, i))
    with_init = init is not None
    carried, extra, more = [], {}, []
    with_sent = sent is not None
    if sent is not None:
        carried = [pl.BlockSpec(memory_space=pl.ANY)]
        extra = {"collective_id": 4, "has_side_effects": True}
        more = [pltpu.SemaphoreType.DMA((2,))]
    if peaks is not None:
        sent = peaks
        carried = [whole(peaks.shape)]
        extra = {"collective_id": 5, "has_side_effects": True}
        more = [pltpu.VMEM((5,) + peaks.shape, F32)] * 2 + [pltpu.SemaphoreType.DMA((5,))] * 2
    made = pl.pallas_call(
        functools.partial(
            expert_kernel,
            first,
            local,
            num_experts,
            with_init,
            with_sent,
            peaks is not None,
            n_row,
        ),
        grid=(2 * n_row, count),
        in_specs=[
            pl.BlockSpec(memory_space=pltpu.SMEM),
            pl.BlockSpec(
                (d, 128),
                lambda i, e: (0, router.shape[1] // 128 - 1),
                pipeline_mode=pl.Buffered(1),
            ),
            pick(wg.shape),
            pick(wu.shape),
            pick(wd.shape),
        ]
        + rows * 2
        + lanes(top)
        + (rows * 2 + lanes(8) if with_init else [])
        + carried,
        out_specs=rows * 2
        + lanes(8)
        + [wide_spec] * 3
        + ([] if with_init else [turned_spec] * 2)
        + carried,
        out_shape=[full] * 4
        + [small] * 2
        + [wide] * 3
        + ([] if with_init else [turned] * 2)
        + ([] if sent is None else [jax.ShapeDtypeStruct(sent.shape, sent.dtype)]),
        scratch_shapes=[
            pltpu.VMEM((b, d), BF16),
            pltpu.VMEM((b, d), BF16),
            pltpu.VMEM((b, d), F32),
            pltpu.VMEM((b, d), F32),
            pltpu.VMEM((b, 128), F32),
            pltpu.VMEM((b, 128), F32),
        ]
        + more,
        compiler_params=pltpu.CompilerParams(
            dimension_semantics=("arbitrary",) * 2, vmem_limit_bytes=62 * MIB, **extra
        ),
        cost_estimate=took(24 * count),
        name="experts",
    )(me, router, wg, wu, wd, *xs, *cs, *routes, *(init or ()), *([] if sent is None else [sent]))
    return {"out": made[:2], "dx": made[2:4], "dg": made[4:6], "wide": made[6:9], "turned": made[9:11], "got": made[-1:]}


def weight_grad_kernel(n, paired, dp_ref, *refs):
    xt, ct, dgate, dup, hs = (refs[k * n : (k + 1) * n] for k in range(5))

    def total(lefts, rights):
        acc = None
        for left, right in zip(lefts, rights):
            part = dot(left[...], right[...])
            acc = part if acc is None else acc + part
        return acc

    down = total(ct, hs).T.astype(BF16)
    gate = total(xt, dgate).astype(BF16)
    up = total(xt, dup).astype(BF16)
    if paired:
        keep_ref, send_ref, down_keep_ref, down_send_ref = refs[5 * n :]
        first = dp_ref[0] % 2 == 0

        def parts(value, z, rows):
            even = value[2 * z * rows : (2 * z + 1) * rows]
            odd = value[(2 * z + 1) * rows : (2 * z + 2) * rows]
            return jnp.where(first, even, odd), jnp.where(first, odd, even)

        for z in range(keep_ref.shape[0]):
            for k, value in enumerate((gate, up)):
                keep_ref[z, k, 0], send_ref[z, k, 0] = parts(value, z, keep_ref.shape[3])
        for z in range(down_keep_ref.shape[0]):
            rows = down_keep_ref.shape[2]
            down_keep_ref[z, 0], down_send_ref[z, 0] = parts(down, z, rows)
        return
    gate_ref, up_ref, down_ref = refs[5 * n :]
    for p in range(down_ref.shape[0]):
        rows = down_ref.shape[3]
        down_ref[p, 0, 0] = down[p * rows : (p + 1) * rows]
    for p in range(gate_ref.shape[0]):
        rows = gate_ref.shape[2]
        gate_ref[p, 0] = gate[p * rows : (p + 1) * rows]
        up_ref[p, 0] = up[p * rows : (p + 1) * rows]


def run_weight_grad(dp, xt, ct, dgate, dup, hs, count, skips, n_dp, paired, ff):
    n = len(xt)
    d, length = xt[0].shape
    m = 512 if paired else 256
    left = spec((m, length), lambda e, i: (i, 0))
    rights = [
        spec((length, ff), functools.partial(lambda skip, e, i: (0, e + skip), skip))
        for skip in skips
    ]
    per = d // n_dp
    down_at = lambda e, i: (0, e, i // (ff // m), 0, i % (ff // m))
    if paired:
        row_spec = spec((m // (2 * per), 2, 1, per, ff), lambda e, i: (i, 0, e, 0, 0))
        rows = jax.ShapeDtypeStruct((n_dp // 2, 2, count, per, ff), BF16)
        down_spec = spec((n_dp // 2, 1, ff // n_dp, m), lambda e, i: (0, e, i, 0))
        down = jax.ShapeDtypeStruct((n_dp // 2, count, ff // n_dp * (d // ff), ff), BF16)
        out_specs, out_shape = [row_spec] * 2 + [down_spec] * 2, [rows] * 2 + [down] * 2
    else:
        row_spec = spec((m // per, 1, per, ff), lambda e, i: (i, e, 0, 0))
        rows = jax.ShapeDtypeStruct((n_dp, count, per, ff), BF16)
        down_spec = spec((n_dp, 1, 1, ff // n_dp, m), down_at)
        down = jax.ShapeDtypeStruct((n_dp, count, d // ff, ff // n_dp, ff), BF16)
        out_specs, out_shape = [row_spec] * 2 + [down_spec], [rows] * 2 + [down]
    return pl.pallas_call(
        functools.partial(weight_grad_kernel, n, paired),
        grid=(count, d // m),
        in_specs=[pl.BlockSpec(memory_space=pltpu.SMEM)] + [left] * (2 * n) + rights * 3,
        out_specs=out_specs,
        out_shape=out_shape,
        compiler_params=params(60, 2),
        cost_estimate=took(37),
        name="weight_grad",
    )(dp, *xt, *ct, *dgate, *dup, *hs)


def back_mid_kernel(n, n_ex, local, *refs):
    (me_ref, res_ref, cot_ref, route_ref, x_ref, router_ref, gain_ref, w_ref) = refs[:8]
    dx_refs, dg_refs = refs[8 : 8 + n], refs[8 + n : 8 + n + n_ex]
    dres_ref, dattn_ref, dctx_ref, dlog_ref, ggain_ref = refs[8 + n + n_ex :]
    gp = gates_of(x_ref[...], router_ref[...], route_ref[...], n_ex * local)
    parts = [ref[...][:local] for ref in dg_refs]
    owners = []
    for owner in range(n_ex):
        own = jnp.zeros_like(parts[0])
        for step in range(n_ex):
            own = jnp.where((owner ^ step) == me_ref[0], parts[step], own)
        owners.append(own)
    dg = jnp.concatenate(owners, axis=0)
    d_logits = gp * (dg - jnp.sum(gp * dg, axis=0, keepdims=True))
    fill = jnp.zeros((128 - dg.shape[0], dg.shape[1]), F32)
    d_logits = jnp.concatenate([d_logits, fill], axis=0).T.astype(BF16)
    dlog_ref[...] = d_logits
    d_norm = dot_t(d_logits, router_ref[...])
    for ref in dx_refs:
        d_norm = d_norm + ref[...].astype(F32)
    res = res_ref[...]
    r = lax.rsqrt(jnp.mean(res * res, axis=1, keepdims=True) + EPS)
    xr = res * r
    part = jnp.sum(d_norm * xr, axis=0, keepdims=True)

    @pl.when(pl.program_id(0) == 0)
    def _():
        ggain_ref[...] = jnp.zeros_like(ggain_ref)

    ggain_ref[...] += part
    u = d_norm * gain_ref[...].astype(F32)
    d_res = (
        cot_ref[...].astype(F32) + r * u - xr * (r * r) * jnp.mean(u * res, axis=1, keepdims=True)
    )
    dres_ref[...] = d_res
    d_attn = d_res.astype(BF16)
    dattn_ref[...] = d_attn
    dctx_ref[...] = dot_t(d_attn, w_ref[...]).astype(BF16)


def run_back_mid(me, res, cot, routes_t, x, w_all, gain, at, dxs, dgs, local):
    length, d = res.shape
    b = 256
    row = lambda i: (i, 0)
    n, n_ex = len(dxs), len(dgs)
    return pl.pallas_call(
        functools.partial(back_mid_kernel, n, n_ex, local),
        grid=(length // b,),
        in_specs=[
            pl.BlockSpec(memory_space=pltpu.SMEM),
            spec((b, d), row),
            spec((b, d), row),
            spec((routes_t.shape[0], b), lambda i: (0, i)),
            spec((b, d), row),
            spec((d, 128), lambda i: (0, w_all.shape[1] // 128 - 1)),
            whole((1, d)),
            spec((d, d), lambda i: (0, at)),
        ]
        + [spec((b, d), row)] * n
        + [spec((8, b), lambda i: (0, i))] * n_ex,
        out_specs=[
            spec((b, d), row),
            spec((b, d), row),
            spec((b, d), row),
            spec((b, 128), row),
            whole((1, d)),
        ],
        out_shape=[
            jax.ShapeDtypeStruct((length, d), F32),
            jax.ShapeDtypeStruct((length, d), BF16),
            jax.ShapeDtypeStruct((length, d), BF16),
            jax.ShapeDtypeStruct((length, 128), BF16),
            jax.ShapeDtypeStruct((1, d), F32),
        ],
        compiler_params=params(60),
        cost_estimate=took(11),
        name="back_mid",
    )(me, res, cot, routes_t, x, w_all, gain, w_all, *dxs, *dgs)


def back_in_kernel(dq_ref, dk_ref, dv_ref, w_ref, tok_ref, gain_ref, dres_ref, gt_ref, ggain_ref):
    nq, nk = dq_ref.shape[1], dk_ref.shape[1]
    d_norm = dot_t(dq_ref[...], w_ref[:, :nq])
    d_norm = d_norm + dot_t(dk_ref[...], w_ref[:, nq : nq + nk])
    d_norm = d_norm + dot_t(dv_ref[...], w_ref[:, nq + nk : nq + 2 * nk])
    x = tok_ref[...].astype(F32)
    r = lax.rsqrt(jnp.mean(x * x, axis=1, keepdims=True) + EPS)
    xr = x * r
    part = jnp.sum(d_norm * xr, axis=0, keepdims=True)

    @pl.when(pl.program_id(0) == 0)
    def _():
        ggain_ref[...] = jnp.zeros_like(ggain_ref)

    ggain_ref[...] += part
    u = d_norm * gain_ref[...].astype(F32)
    gt_ref[...] = dres_ref[...] + r * u - xr * (r * r) * jnp.mean(u * x, axis=1, keepdims=True)


def run_back_in(dq, dk, dv, w_qkv, tok, gain, d_res):
    length, d = tok.shape
    b = 256
    row = lambda i: (i, 0)
    nq = dq.shape[1]
    return pl.pallas_call(
        back_in_kernel,
        grid=(length // b,),
        in_specs=[
            spec((b, nq), row),
            spec((b, dk.shape[1]), row),
            spec((b, dv.shape[1]), row),
            spec((d, 2 * nq), lambda i: (0, 0)),
            spec((b, d), row),
            whole((1, d)),
            spec((b, d), row),
        ],
        out_specs=[spec((b, d), row), whole((1, d))],
        out_shape=[jax.ShapeDtypeStruct((length, d), F32), jax.ShapeDtypeStruct((1, d), F32)],
        compiler_params=params(60),
        cost_estimate=took(10),
        name="back_in",
    )(dq, dk, dv, w_qkv, tok, gain, d_res)


CHUNKS = (3, 0, 1, 2)


def finish_kernel(
    gain_lane, ht_ref, dq_ref, dk_ref, dv_ref, dout_ref, small_ref, keep_ref, got_ref, down_keep_ref, down_got_ref,
    gate_a, up_a, down_a, w_ref, tok_ref, gain_ref, dres_ref,
    out_o, out_q, out_kv, out_small, gate_ref, up_ref, down_ref, gt_ref, *scratch,
):
    n = len(CHUNKS)
    lists = [scratch[k * n : (k + 1) * n] for k in range(7)]
    b1, r1, r2, s2, r3, s3, r4 = lists
    sem_s, sem_r = scratch[7 * n : 7 * n + 2]
    line = Line(*scratch[7 * n + 2 : 7 * n + 8])
    rx, sem_l, w_now, gt_now, gain_sum = scratch[7 * n + 8 :]
    count = gate_a.shape[0]
    halves = []
    for k, (src, dst) in enumerate(((gate_a, gate_ref), (up_a, up_ref), (down_a, down_ref))):
        halves.append(pltpu.make_async_copy(src, dst.at[:count], sem_l.at[6 + k]))
        halves[k].start()
    dp, ex = lax.axis_index("dp"), lax.axis_index("expert")
    z, x, y, c = dp // 2, dp % 2, ex // 2, ex % 2
    over_core, over_y, over_x = (dp, ex ^ 1), (dp, ex ^ 2), (dp ^ 1, ex)
    s1 = [ref.at[c] for ref in b1]
    load_w = pltpu.make_async_copy(w_ref.at[:, : w_now.shape[1]], w_now, sem_l.at[9])
    load_w.start()
    along = [(dp ^ (2 * k), ex) for k in (1, 2, 3)]
    group = [over_core, over_y, (dp, ex ^ 3)]
    loads = []
    for k in range(3):
        keep, got = (down_keep_ref, down_got_ref) if k == 2 else (keep_ref.at[:, k], got_ref.at[:, k])
        loads.append(
            [
                pltpu.make_async_copy(keep, line.tot.at[k], sem_l.at[2 * k]),
                pltpu.make_async_copy(got, rx.at[k], sem_l.at[2 * k + 1]),
            ]
        )
        for copy in loads[k]:
            copy.start()
    greet(group + [over_x] + along)

    widths = [dout_ref.shape[1], dq_ref.shape[1], dk_ref.shape[1] + dv_ref.shape[1], 128]
    outs = (out_o, out_q, out_kv, out_small)
    started = {}

    def send(k, slot, src, dst, peer):
        copy = pltpu.make_async_remote_copy(
            src_ref=src,
            dst_ref=dst,
            send_sem=sem_s.at[k, slot],
            recv_sem=sem_r.at[k, slot],
            device_id=peer,
            device_id_type=pl.DeviceIdType.MESH,
        )
        copy.start()
        started[k, slot] = copy

    def begin(k):
        for copy in loads[k]:
            copy.wait()
        for zz in range(4):
            for e in range(2):
                dst = line.tot.at[k, zz, e]
                add_rows(dst, [dst, rx.at[k, zz, e]])
        line.ends(k, True)

    def place(k, lanes, value):
        for p in range(8):
            for e in range(4):
                row = 128 * p + 32 * e
                b1[k][e % 2, e // 2, p % 2, p // 2, :, lanes] = value[row : row + 32]

    def step0(k):
        if k == 0:
            place(k, slice(0, widths[k]), dout_ref[...])
        elif k == 1:
            for col in range(0, widths[1], 512):
                part = dot(ht_ref[...], dq_ref[:, col : col + 512])
                place(k, slice(col, col + 512), part.astype(BF16))
        elif k == 2:
            half = dk_ref.shape[1]
            place(k, slice(0, half), dot(ht_ref[...], dk_ref[...]).astype(BF16))
            place(k, slice(half, 2 * half), dot(ht_ref[...], dv_ref[...]).astype(BF16))
        else:
            turned = jnp.broadcast_to(gain_sum[...], (128, gain_sum.shape[1])).T.astype(BF16)
            lane = lax.broadcasted_iota(jnp.int32, turned.shape, 1)
            place(k, slice(0, 128), jnp.where(lane == gain_lane, turned, small_ref[...]))
        send(k, 0, b1[k].at[1 - c], r1[k], over_core)

    def step1(k):
        started[k, 0].wait()
        for yy in range(2):
            for xx in range(2):
                for zz in range(4):
                    s1[k][yy, xx, zz] = s1[k][yy, xx, zz] + r1[k][yy, xx, zz]
        send(k, 1, s1[k].at[1 - y], r2[k], over_y)

    def step2(k):
        started[k, 1].wait()
        for xx in range(2):
            for zz in range(4):
                s2[k][xx, zz] = s1[k][y, xx, zz] + r2[k][xx, zz]
        send(k, 2, s2[k].at[1 - x], r3[k].at[0], over_x)

    def step3(k):
        started[k, 2].wait()
        for zz in range(4):
            s3[k][zz] = s2[k][x, zz] + r3[k][0, zz]
        for i in range(3):
            send(k, 3 + i, s3[k].at[z ^ (i + 1)], r3[k].at[1, i], along[i])

    def step4(k):
        for i in range(3):
            started[k, 3 + i].wait()
        total = s3[k][z].astype(F32)
        for i in range(3):
            total = total + r3[k][1, i].astype(F32)
        r4[k][3] = total.astype(BF16)
        for i in range(3):
            send(k, 6 + i, r4[k].at[3], r4[k].at[i], group[i])

    def step5(k):
        outs[k][pl.ds(pl.multiple_of(ex * 32, 32), 32), :] = r4[k][3].astype(F32)
        for i in range(3):
            started[k, 6 + i].wait()
            rows = pl.ds(pl.multiple_of((ex ^ (i + 1)) * 32, 32), 32)
            outs[k][rows, :] = r4[k][i].astype(F32)

    size = gt_now.shape[1]

    def stored(r):
        rows = slice(r * size, (r + 1) * size)
        return pltpu.make_async_copy(gt_now.at[r % 2], gt_ref.at[rows], sem_l.at[10 + r])

    def back(r):
        if r == 0:
            load_w.wait()
        if r >= 2:
            stored(r - 2).wait()
        rows = slice(r * size, (r + 1) * size)
        nq, nk = dq_ref.shape[1], dk_ref.shape[1]
        d_norm = dot_t(dq_ref[rows], w_now[:, :nq])
        d_norm = d_norm + dot_t(dk_ref[rows], w_now[:, nq : nq + nk])
        d_norm = d_norm + dot_t(dv_ref[rows], w_now[:, nq + nk : nq + 2 * nk])
        value = tok_ref[rows].astype(F32)
        inv = lax.rsqrt(jnp.mean(value * value, axis=1, keepdims=True) + EPS)
        scaled = value * inv
        part = jnp.sum(d_norm * scaled, axis=0, keepdims=True)
        gain_sum[...] = part if r == 0 else gain_sum[...] + part
        u = d_norm * gain_ref[...].astype(F32)
        mean = jnp.mean(u * value, axis=1, keepdims=True)
        gt_now[r % 2] = dres_ref[rows] + inv * u - scaled * (inv * inv) * mean
        stored(r).start()

    done = tuple(ref.at[count:] for ref in (gate_ref, up_ref, down_ref))
    step0(0)
    begin(0)
    step1(0)
    step0(1)
    begin(1)
    step1(1)
    step0(2)
    begin(2)
    step1(2)
    back(0)
    step2(0)
    line.middle_sends(0, True)
    back(1)
    step2(1)
    back(2)
    step3(0)
    line.middle_sends(1, True)
    line.middle_adds(0)
    back(3)
    step0(3)
    step2(2)
    step1(3)
    step3(1)
    line.middle_sends(2, True)
    line.middle_adds(1)
    step2(3)
    step4(0)
    step3(2)
    step3(3)
    line.result(0, done)
    line.middle_adds(2)
    step4(1)
    step5(0)
    step4(2)
    step4(3)
    line.result(1, done)
    line.result(2, done)
    step5(1)
    step5(2)
    step5(3)
    for copy in halves:
        copy.wait()
    for r in range(2, 4):
        stored(r).wait()


def run_finish(ht, dq, dk, dv, d_out, small, experts, w_all, tok, gain, d_res, gain_lane):
    widths = [d_out.shape[1], dq.shape[1], dk.shape[1] + dv.shape[1], small.shape[1]]
    chunk = experts[2].shape
    _, count, rows, lanes = chunk
    vmem = pl.BlockSpec(memory_space=pltpu.VMEM)
    hbm = pl.BlockSpec(memory_space=pl.ANY)
    shapes = [
        (2, 2, 2, 4, 32), (2, 2, 4, 32), (2, 4, 32), (2, 4, 32), (2, 4, 32), (4, 32), (4, 32),
    ]
    length, d = tok.shape
    scratch = [pltpu.VMEM(shape + (w,), BF16) for shape in shapes for w in widths]
    scratch += [pltpu.SemaphoreType.DMA((len(widths), 9))] * 2
    scratch += line_scratch(chunk)
    scratch += [
        pltpu.VMEM((3,) + chunk, BF16),
        pltpu.SemaphoreType.DMA((14,)),
        pltpu.VMEM((d, sum(widths[1:3])), BF16),
        pltpu.VMEM((2, length // 4, d), F32),
        pltpu.VMEM((1, d), F32),
    ]
    return pl.pallas_call(
        functools.partial(finish_kernel, gain_lane),
        in_specs=[vmem] * 6 + [hbm] * 8 + [vmem] * 3,
        out_specs=[vmem] * 7 + [hbm],
        out_shape=[
            *(jax.ShapeDtypeStruct((128, w), F32) for w in widths),
            jax.ShapeDtypeStruct((2 * count, rows, lanes), F32),
            jax.ShapeDtypeStruct((2 * count, rows, lanes), F32),
            jax.ShapeDtypeStruct((2 * count, rows // 2, 2 * lanes), F32),
            jax.ShapeDtypeStruct((length, d), F32),
        ],
        scratch_shapes=scratch,
        compiler_params=pltpu.CompilerParams(
            vmem_limit_bytes=63 * MIB, collective_id=1, has_side_effects=True
        ),
        cost_estimate=took(60),
        name="finish",
    )(ht, dq, dk, dv, d_out, small, *experts, w_all, tok, gain, d_res)


def gather_kernel(mine_ref, out_ref, sem_s, sem_r, sem_l):
    dp, ex = lax.axis_index("dp"), lax.axis_index("expert")
    z = dp // 2
    core, over_y, over_x = (dp, ex ^ 1), (dp, ex ^ 2), (dp ^ 1, ex)
    line = [None] + [(dp ^ (2 * k), ex) for k in (1, 2, 3)]
    barrier = pltpu.get_barrier_semaphore()
    peers = [core, over_y, over_x] + line[1:]
    for peer in peers:
        pl.semaphore_signal(barrier, inc=1, device_id=peer, device_id_type=pl.DeviceIdType.MESH)
    pl.semaphore_wait(barrier, len(peers))
    rows = mine_ref.shape[0]
    width = mine_ref.shape[1]
    cut = (width // 256 + 1) * 128
    halves = [pl.ds(0, cut), pl.ds(cut, width - cut)]
    started = {}

    def block(k, dx, dy):
        at = (((z ^ k) * 2 + (dp % 2 ^ dx)) * 4 + (ex ^ (2 * dy))) * rows
        return pl.ds(pl.multiple_of(at, rows), rows)

    def send(key, k, dx, dy, peer, src=None, lanes=None):
        index = len(started)
        at = block(k, dx, dy)
        dst = out_ref.at[at] if lanes is None else out_ref.at[at, lanes]
        copy = pltpu.make_async_remote_copy(
            src_ref=dst if src is None else src,
            dst_ref=dst,
            send_sem=sem_s.at[index],
            recv_sem=sem_r.at[index],
            device_id=peer,
            device_id_type=pl.DeviceIdType.MESH,
        )
        copy.start()
        started[key] = copy

    for k in (3, 2, 1):
        send(("z", k), 0, 0, 0, line[k], mine_ref)
    send(("x", 0), 0, 0, 0, over_x, mine_ref)
    send(("y", 0), 0, 0, 0, over_y, mine_ref)
    send(("c", 0), 0, 0, 0, core, mine_ref)
    own = pltpu.make_async_copy(mine_ref, out_ref.at[block(0, 0, 0)], sem_l)
    own.start()

    def onward(k):
        started["x", k].wait_recv()
        send(("dy", k), k, 1, 0, over_y, None, halves[0])
        send(("cx", k), k, 1, 0, core)
        started["y", k].wait_recv()
        send(("dx", k), k, 0, 1, over_x, None, halves[1])
        send(("cy", k), k, 0, 1, core)

    def last(k):
        started["dy", k].wait_recv()
        started["dx", k].wait_recv()
        send(("cd", k), k, 1, 1, core)

    onward(0)
    for k in (1, 2, 3):
        started["z", k].wait_recv()
        send(("x", k), k, 0, 0, over_x)
        send(("y", k), k, 0, 0, over_y)
        send(("c", k), k, 0, 0, core)
    last(0)
    for k in (1, 2, 3):
        onward(k)
    for k in (1, 2, 3):
        last(k)
    for key, copy in started.items():
        copy.wait_send()
        if key[0] in ("c", "cx", "cy", "cd"):
            copy.wait_recv()
    own.wait()


def run_gather(mine, total):
    hbm = pl.BlockSpec(memory_space=pl.ANY)
    return pl.pallas_call(
        gather_kernel,
        in_specs=[hbm],
        out_specs=hbm,
        out_shape=jax.ShapeDtypeStruct((total, mine.shape[1]), BF16),
        scratch_shapes=[
            pltpu.SemaphoreType.DMA((40,)),
            pltpu.SemaphoreType.DMA((40,)),
            pltpu.SemaphoreType.DMA,
        ],
        compiler_params=pltpu.CompilerParams(collective_id=2, has_side_effects=True),
        cost_estimate=took(40),
        name="gather",
    )(mine)


def after(value, *deps):
    return lax.optimization_barrier((value,) + deps)[0]


def on_device(
    n_dp, n_ex, tokens, cotangent, routes, prefix, w_query, keyvalue_weight, w_out, w_router,
    gain_attn, gain_mlp, expert_gate, expert_up, expert_down, query_logit_cap,
):
    length, d = tokens.shape[1], tokens.shape[2]
    tok = tokens.reshape(length, d)
    cot = cotangent.reshape(length, d)
    heads = query_logit_cap.shape[0]
    nq = w_query.shape[1]
    head = nq // heads
    kv_heads = keyvalue_weight.shape[1] // (2 * head)
    num_experts = w_router.shape[1]
    local = expert_gate.shape[0]
    rows = w_query.shape[0]
    ex = lax.axis_index("expert")

    def swap(value, step, axis="expert", n=n_ex):
        return lax.ppermute(value, axis, [(i, i ^ step) for i in range(n)])

    part = rows // n_ex
    small = jnp.concatenate(
        [
            w_router,
            gain_attn[:, None],
            gain_mlp[:, None],
            jnp.zeros((rows, 128 - num_experts - 2), BF16),
        ],
        axis=1,
    )
    packed = jnp.concatenate([w_query, keyvalue_weight, w_out, small], axis=1)
    mine = lax.dynamic_slice_in_dim(packed, ex * part, part, axis=0)
    local = expert_gate.shape[0]
    fast = n_dp == 8 and n_ex == 4 and d == 1024 and local == 4 and expert_gate.shape[2] == 512
    if fast:
        every = run_gather(mine, d)
    else:
        every = lax.all_gather(mine, ("dp", "expert"), axis=0, tiled=True)
    w_all = every
    width = 2 * nq
    extra = every[:, width + d :]
    gain_one = extra[:, num_experts].reshape(1, d)
    gain_two = extra[:, num_experts + 1].reshape(1, d)

    routes_t = routes.reshape(length, -1).T
    cots = {0: cot}
    route_set = {0: routes_t}
    cot_late = after(cot, every)
    for step in range(1, n_ex):
        if step == 1 or step % 2 == 0:
            cots[step] = swap(cot_late, step)

    cos_np, sin_np = rope_tables(length, head)
    cos_l = jnp.asarray(np.concatenate([cos_np] * 4, axis=1))
    sin_l = jnp.asarray(np.concatenate([-sin_np, sin_np] * 2, axis=1))
    cos_t = jnp.asarray(np.ascontiguousarray(cos_np.T))
    sin_t = jnp.asarray(np.ascontiguousarray(sin_np.T))

    normed_one_t, q, kd, vd = run_qkv(tok, gain_one, w_all, cos_l, sin_l, nq)
    for step in range(1, n_ex):
        route_set[step] = swap(after(routes_t, q), step)
    ctx, lse, peaks = run_attn_fwd(prefix, q, kd, vd)
    resid, normed_two = run_mid(tok, ctx, w_all, gain_two, width // d)

    me = ex.reshape(1).astype(jnp.int32)
    xs = {0: normed_two}
    for step in range(1, n_ex):
        if step == 1 or step % 2 == 0:
            xs[step] = swap(normed_two, step)
    tops = [peaks[:, :, :4]]
    bits = [("expert", n_ex, 1 << i) for i in range(n_ex.bit_length() - 1)]
    bits += [("dp", n_dp, 1 << i) for i in range(n_dp.bit_length() - 1)]

    def widen_top():
        if len(tops) <= len(bits) and not fast:
            axis, n, step = bits[len(tops) - 1]
            top = after(tops[-1], chain)
            tops.append(jnp.maximum(top, swap(top, step, axis, n)))

    weights = (expert_gate, expert_up, expert_down)
    half = local // 2

    dp = lax.axis_index("dp").reshape(1).astype(jnp.int32)

    res = {}
    chain = (normed_two, [cots[step] for step in range(2, n_ex, 2)])

    def experts(steps, first, count, init=None, sent=None, peaks=None):
        x = [after(xs[steps[0]], chain), xs[steps[1]]]
        cot_pair, route_pair = [cots[k] for k in steps], [route_set[k] for k in steps]
        return run_expert(
            me,
            x,
            cot_pair,
            route_pair,
            w_all,
            *weights,
            first,
            count,
            num_experts,
            init,
            sent,
            peaks,
        )

    def grads(first):
        pairs = [res[k, 0] for k in range(0, n_ex, 2)]
        wides = [res[0, 0]] + [res[k, first] for k in range(2, n_ex, 2)]
        groups = [[pair["turned"][k] for pair in pairs] for k in (0, 1)]
        groups += [[pair["wide"][k] for pair in wides] for k in (1, 2, 0)]
        groups[0][0] = after(groups[0][0], chain)
        skips = [first if k == 0 else 0 for k in range(len(pairs))]
        made = None
        for at in range(0, len(pairs), 2):
            some = [group[at : at + 2] for group in groups]
            part = run_weight_grad(
                dp, *some, half, skips[at : at + 2], n_dp, fast, expert_gate.shape[2]
            )
            if made is None:
                made = part
            else:
                made = [(a.astype(F32) + b.astype(F32)).astype(BF16) for a, b in zip(made, part)]
        return made

    res[0, 0] = experts((0, 1), 0, local)
    chain = (res[0, 0]["dg"][0], tops[-1])
    widen_top()
    widen_top()
    for other in range(3, n_ex, 2):
        cots[other] = swap(after(cots[other - 1], chain), 1)
        xs[other] = swap(after(xs[other - 1], chain), 1)
    even = range(2, n_ex, 2)
    for step in even:
        res[step, 0] = experts((step, step + 1), 0, half, peaks=peaks if fast else None)
        chain = (res[step, 0]["dg"][0], tops[-1])
        widen_top()
    made_one = grads(0)
    chain = (made_one[0], tops[-1])
    widen_top()
    for step in even:
        init = [*res[step, 0]["out"], *res[step, 0]["dx"], *res[step, 0]["dg"]]
        sent = made_one[1] if fast else None
        res[step, half] = experts((step, step + 1), half, half, init, sent)
        chain = (res[step, half]["dg"][0], tops[-1])
        widen_top()

    def with_partner(step, what):
        own, other = res[step, half][what]
        return (own.astype(F32) + swap(other, 1).astype(F32)).astype(BF16)

    to_send = {step: with_partner(step, "dx") for step in even}
    chain = (chain, list(to_send.values()))
    sums, got_two = None, []
    if fast:
        down_sent = after(made_one[3], chain)
        got_one = [res[2, half]["got"][0], swap(down_sent, 1, "dp", n_dp)]
        tot_one = (made_one[0].astype(F32) + got_one[0].astype(F32)).astype(BF16)
        far_one = lax.dynamic_slice_in_dim(tot_one, 2 * (1 - dp[0] // 4), 2, axis=0)
        chain = (chain, far_one)
        far_one = lax.ppermute(far_one, "dp", [(0, 2), (1, 3), (6, 4), (7, 5)])
    made_two = grads(half)
    chain = (made_two[0], tops[-1])
    if fast:
        chain = (chain, far_one, got_one)
        sums = [tot_one, far_one, made_one[2], got_one[1]]
        got_two = [swap(made_two[k], 1, "dp", n_dp) for k in (1, 3)]
    while len(tops) <= len(bits) and not fast:
        widen_top()
    top = tops[-1]

    final = [res[0, 0]] + [res[step, half] for step in even]
    dxs = [final[0]["dx"][0], swap(final[0]["dx"][1], 1)]
    dxs += [swap(to_send[step], step) for step in even]
    dgs = [part for pair in final for part in pair["dg"]]
    dgs = [swap(dgs[step], step) if step else dgs[0] for step in range(n_ex)]
    d_res, d_attn, d_ctx, d_logits, d_gain_two = run_back_mid(
        me,
        after(resid, chain),
        cot,
        routes_t,
        normed_two,
        w_all,
        gain_two,
        width // d,
        dxs,
        dgs,
        local,
    )
    outs = [final[0]["out"][0], swap(final[0]["out"][1], 1)]
    outs += [swap(after(with_partner(step, "out"), dxs), step) for step in even]
    block = resid
    for piece in outs:
        block = block + piece.astype(F32)
    block_out = block.astype(BF16).reshape(tokens.shape)

    d_out_w = jnp.einsum("rc,rd->cd", ctx, d_attn, preferred_element_type=F32).astype(BF16)
    d_router_w = jnp.einsum("rd,re->de", normed_two, d_logits, preferred_element_type=F32)

    dq, dk, dv, *halves = run_attn_bwd(
        prefix, q, kd, vd, d_ctx, ctx, lse, cos_l, sin_l, cos_t, sin_t, sums
    )
    if not fast:
        grad_tok, d_gain_one = run_back_in(dq, dk, dv, w_all, tok, gain_one, d_res)
    else:
        d_gain_one = jnp.zeros((1, d), F32)
    small_grad = jnp.concatenate(
        [
            d_router_w[:, :num_experts].astype(BF16),
            d_gain_one.reshape(d, 1).astype(BF16),
            d_gain_two.reshape(d, 1).astype(BF16),
            jnp.zeros((d, 128 - num_experts - 2), BF16),
        ],
        axis=1,
    )

    def reduce_all(value, order):
        shape = (n_dp, n_ex, value.shape[0] // (n_dp * n_ex), value.shape[1])
        names = []
        dims = []
        for axis, n in (("dp", n_dp), ("expert", n_ex)):
            count = n.bit_length() - 1
            names += [(axis, n, 1 << (count - 1 - i)) for i in range(count)]
            dims += [2] * count
        value = value.reshape(*dims, *shape[2:])
        for bit in order:
            at = names.index(bit)
            axis, n, step = bit
            mine = (lax.axis_index(axis) // step) % 2
            keep = lax.dynamic_slice_in_dim(value, mine, 1, axis=at)
            send = lax.dynamic_slice_in_dim(value, 1 - mine, 1, axis=at)
            value = (keep.astype(F32) + swap(send, step, axis, n).astype(F32)).astype(BF16)
        return value.reshape(shape[2:])

    def share(value):
        return lax.all_gather(value, "expert", axis=0, tiled=True).astype(F32)

    core = [("expert", n_ex, 1)]
    y_bits = [("expert", n_ex, 1 << i) for i in range(1, n_ex.bit_length() - 1)][::-1]
    dp_bits = [("dp", n_dp, 1 << i) for i in range(n_dp.bit_length() - 1)]
    if fast:
        grad_out, grad_query, grad_keyval, rest, grad_gate, grad_up, grad_down, grad_tok = run_finish(
            normed_one_t,
            after(dq, block_out),
            dk,
            dv,
            d_out_w,
            small_grad,
            [made_two[0], got_two[0], made_two[2], got_two[1], *halves[:3]],
            w_all,
            tok,
            gain_one,
            d_res,
            num_experts,
        )
    else:
        ends = [
            [
                lax.psum_scatter(g, "dp", scatter_dimension=0, tiled=True)[0].astype(F32)
                for g in made
            ]
            for made in (made_one, made_two)
        ]
        grad_gate, grad_up, grad_down = (
            jnp.concatenate([ends[0][k], ends[1][k]], axis=0) for k in range(3)
        )
        grad_down = jnp.swapaxes(grad_down, 1, 2).reshape(local, -1, d)

        def product(right):
            return jnp.dot(normed_one_t, right, preferred_element_type=F32).astype(BF16)

        every_grad = jnp.concatenate(
            [d_out_w, product(dq), product(dk), product(dv), small_grad], axis=1
        )
        every_grad = share(reduce_all(every_grad, core + y_bits + dp_bits[::-1]))
        grad_out = every_grad[:, :d]
        grad_query = every_grad[:, d : d + nq]
        grad_keyval = every_grad[:, d + nq : d + 2 * nq]
        rest = every_grad[:, d + 2 * nq :]
    grad_router = rest[:, :num_experts]
    grad_gain_one = rest[:, num_experts]
    grad_gain_two = rest[:, num_experts + 1]

    if fast:
        top = res[2, 0]["got"][0][:, :, :4]
    head_logit_peak = top[:, 0, :].reshape(heads)
    per_group = heads // kv_heads
    query_factor = jnp.sqrt(query_logit_cap / jnp.maximum(head_logit_peak, query_logit_cap))
    pair_peak = jnp.max(head_logit_peak.reshape(kv_heads, per_group), axis=1)
    pair_cap = jnp.min(query_logit_cap.reshape(kv_heads, per_group), axis=1)
    key_factor = jnp.sqrt(pair_cap / jnp.maximum(pair_peak, pair_cap))
    clipped_query = (w_query.astype(F32) * jnp.repeat(query_factor, head)[None, :]).astype(BF16)
    key_cols = jnp.concatenate(
        [jnp.repeat(key_factor, head), jnp.ones((kv_heads * head,), F32)]
    )
    clipped_keyval = (keyvalue_weight.astype(F32) * key_cols[None, :]).astype(BF16)
    return (
        block_out,
        grad_tok.reshape(tokens.shape),
        grad_query,
        grad_keyval,
        grad_out,
        grad_router,
        grad_gain_one,
        grad_gain_two,
        grad_gate,
        grad_up,
        grad_down,
        clipped_query,
        clipped_keyval,
        head_logit_peak,
    )


def solution(mesh):
    rows3 = P(("dp", "expert"), None, None)
    in_specs = (
        rows3,
        rows3,
        rows3,
        P(("dp", "expert")),
        P("dp", None),
        P("dp", None),
        P("dp", None),
        P("dp", None),
        P("dp"),
        P("dp"),
        P("expert", None, None),
        P("expert", None, None),
        P("expert", None, None),
        P(),
    )
    out_specs = (
        rows3,
        rows3,
        P("dp", None),
        P("dp", None),
        P("dp", None),
        P("dp", None),
        P("dp"),
        P("dp"),
        P("expert", "dp", None),
        P("expert", "dp", None),
        P("expert", "dp", None),
        P("dp", None),
        P("dp", None),
        P(),
    )
    return jax.shard_map(
        functools.partial(on_device, mesh.shape["dp"], mesh.shape["expert"]),
        mesh=mesh,
        in_specs=in_specs,
        out_specs=out_specs,
        check_vma=False,
    )
```

```python
import functools

import jax
import jax.numpy as jnp
import numpy as np
from jax import lax
from jax.experimental import pallas as pl
from jax.experimental.pallas import tpu as pltpu
from jax.sharding import PartitionSpec as P

EPS = 1e-05
ROPE_BASE = 10000.0
F32 = jnp.float32
BF16 = jnp.bfloat16
NEG = -1e30
MIB = 1 << 20
SCALE = 0.35


def dot(a, b):
    return lax.dot_general(a, b, (((1,), (0,)), ((), ())), preferred_element_type=F32)


def dot_t(a, b):
    return lax.dot_general(a, b, (((1,), (1,)), ((), ())), preferred_element_type=F32)


def params(vmem_mib, n=1):
    return pltpu.CompilerParams(
        dimension_semantics=("arbitrary",) * n, vmem_limit_bytes=vmem_mib * MIB
    )


def took(us):
    return pl.CostEstimate(flops=int(us * SCALE * 1e9), bytes_accessed=1000, transcendentals=0)


def spec(shape, index):
    return pl.BlockSpec(shape, index)


def whole(shape):
    zeros = (0,) * len(shape)
    return pl.BlockSpec(shape, lambda *_: zeros)


def rope_tables(length, head):
    half = head // 2
    freq = np.float32(ROPE_BASE) ** (
        -(np.arange(half, dtype=np.float32) * np.float32(2.0) / np.float32(head))
    )
    ang = np.arange(length, dtype=np.float32)[:, None] * freq.astype(np.float32)[None, :]
    ang = ang.astype(np.float32)
    return np.cos(ang).astype(np.float32), np.sin(ang).astype(np.float32)


def lane_half(shape, width):
    return (lax.broadcasted_iota(jnp.int32, shape, 1) % width) < (width // 2)


def rope_lanes(x, cos, sin, first):
    partner = jnp.where(first, pltpu.roll(x, 96, 1), pltpu.roll(x, 32, 1))
    return x * cos + partner * sin


def qkv_kernel(tok_ref, gain_ref, w_ref, cos_ref, sin_ref, ht_ref, q_ref, kd_ref, vd_ref):
    x = tok_ref[...].astype(F32)
    d = x.shape[1]
    r = lax.rsqrt(jnp.mean(x * x, axis=1, keepdims=True) + EPS)
    h = (x * r * gain_ref[...].astype(F32)).astype(BF16)
    ht_ref[...] = h.T
    cos, sin = cos_ref[...], sin_ref[...]
    rows = x.shape[0]
    first = lane_half((rows, 128), 64)
    low = lane_half((rows, 128), 128)
    nq = q_ref.shape[1]
    nk = kd_ref.shape[1] // 2
    q = dot(h, w_ref[:, :nq])
    for c in range(0, nq, 128):
        q_ref[:, c : c + 128] = (rope_lanes(q[:, c : c + 128], cos, sin, first) * 0.125).astype(
            BF16
        )
    k = dot(h, w_ref[:, nq : nq + nk])
    for c in range(0, nk, 128):
        kk = rope_lanes(k[:, c : c + 128], cos, sin, first)
        sw = pltpu.roll(kk, 64, 1)
        kd_ref[:, 2 * c : 2 * c + 128] = jnp.where(low, kk, sw).astype(BF16)
        kd_ref[:, 2 * c + 128 : 2 * c + 256] = jnp.where(low, sw, kk).astype(BF16)
    v = dot(h, w_ref[:, nq + nk : nq + 2 * nk])
    for c in range(0, nk, 128):
        vv = v[:, c : c + 128]
        sw = pltpu.roll(vv, 64, 1)
        vd_ref[:, 2 * c : 2 * c + 128] = jnp.where(low, vv, sw).astype(BF16)
        vd_ref[:, 2 * c + 128 : 2 * c + 256] = jnp.where(low, sw, vv).astype(BF16)


def run_qkv(tok, gain, w_qkv, cos, sin, nq):
    length, d = tok.shape
    b = 256
    row = lambda i: (i, 0)
    return pl.pallas_call(
        qkv_kernel,
        grid=(length // b,),
        in_specs=[
            spec((b, d), row),
            whole((1, d)),
            spec((d, 2 * nq), lambda i: (0, 0)),
            spec((b, 128), row),
            spec((b, 128), row),
        ],
        out_specs=[spec((d, b), lambda i: (0, i))] + [spec((b, nq), row)] * 3,
        out_shape=[jax.ShapeDtypeStruct((d, length), BF16)]
        + [jax.ShapeDtypeStruct((length, nq), BF16)] * 3,
        compiler_params=params(60),
        cost_estimate=took(9),
        name="qkv",
    )(tok, gain, w_qkv, cos, sin)


def mask_bias(prefix, q0, k0, nq, nk, q_axis):
    shape = (nq, nk) if q_axis == 0 else (nk, nq)
    qpos = q0 + lax.broadcasted_iota(jnp.int32, shape, q_axis)
    kpos = k0 + lax.broadcasted_iota(jnp.int32, shape, 1 - q_axis)
    return jnp.where((kpos <= qpos) | (kpos < prefix), 0.0, NEG).astype(F32)


def two_heads(pair, low):
    zero = jnp.zeros_like(pair)
    return jnp.concatenate([jnp.where(low, pair, zero), jnp.where(low, zero, pair)], axis=0)


def attn_fwd_kernel(prefix_ref, q_ref, kd_ref, vd_ref, ctx_ref, lse_ref, peak_ref):
    length = q_ref.shape[0]
    b = 256
    prefix = prefix_ref[0]
    low_b = lane_half((b, 128), 128)
    lane = lax.broadcasted_iota(jnp.int32, (b, 128), 1)
    peak = jnp.full((8, 128), NEG, F32)
    peak_lane = lax.broadcasted_iota(jnp.int32, (8, 128), 1)
    for i in range(length // b):
        nk = max((i + 1) * b, length // 2)
        free = i * b
        bias = mask_bias(prefix, i * b, free, b, nk - free, 0)
        bias = jnp.concatenate([bias, bias], axis=0)
        lse_cols = jnp.zeros((b, 128), F32)
        for j in range(2):
            cols = slice(j * 128, (j + 1) * 128)
            q2 = two_heads(q_ref[i * b : (i + 1) * b, cols], low_b)
            s_hi = dot_t(q2, kd_ref[free:nk, cols]) + bias
            m = jnp.max(s_hi, axis=1, keepdims=True)
            if free:
                s_lo = dot_t(q2, kd_ref[:free, cols])
                m = jnp.maximum(m, jnp.max(s_lo, axis=1, keepdims=True))
            p_hi = jnp.exp(s_hi - m)
            total = jnp.sum(p_hi, axis=1, keepdims=True)
            ctx = dot(p_hi.astype(BF16), vd_ref[free:nk, cols])
            if free:
                p_lo = jnp.exp(s_lo - m)
                total = total + jnp.sum(p_lo, axis=1, keepdims=True)
                ctx = ctx + dot(p_lo.astype(BF16), vd_ref[:free, cols])
            ctx = ctx * (1.0 / total)
            ctx_ref[i * b : (i + 1) * b, cols] = jnp.where(low_b, ctx[:b], ctx[b:]).astype(BF16)
            lse = m + jnp.log(total)
            for g in range(2):
                lse_cols = jnp.where(lane == 2 * j + g, lse[g * b : (g + 1) * b], lse_cols)
                top = jnp.max(m[g * b : (g + 1) * b], axis=0, keepdims=True)
                peak = jnp.where(peak_lane == 2 * j + g, jnp.maximum(peak, top), peak)
        lse_ref[0, :, i * b : (i + 1) * b] = lse_cols.T[:8]
    peak_ref[0] = peak


def run_attn_fwd(prefix, q, kd, vd):
    length, nq = q.shape
    groups = nq // 256
    col = lambda g: (0, g)
    return pl.pallas_call(
        attn_fwd_kernel,
        grid=(groups,),
        in_specs=[pl.BlockSpec(memory_space=pltpu.SMEM)] + [spec((length, 256), col)] * 3,
        out_specs=[
            spec((length, 256), col),
            spec((1, 8, length), lambda g: (g, 0, 0)),
            spec((1, 8, 128), lambda g: (g, 0, 0)),
        ],
        out_shape=[
            jax.ShapeDtypeStruct((length, nq), BF16),
            jax.ShapeDtypeStruct((groups, 8, length), F32),
            jax.ShapeDtypeStruct((groups, 8, 128), F32),
        ],
        compiler_params=params(60),
        cost_estimate=took(21),
        name="attn_fwd",
    )(prefix, q, kd, vd)


def add_rows(dst, srcs, step=64):
    def body(i, carry):
        at = pl.ds(pl.multiple_of(i * step, step), step)
        one, two = srcs[0][at, :], srcs[1][at, :]
        if dst.dtype != one.dtype:
            one, two = one.astype(dst.dtype), two.astype(dst.dtype)
        dst[at, :] = one + two
        return carry

    lax.fori_loop(0, dst.shape[0] // step, body, 0)


def greet(peers):
    barrier = pltpu.get_barrier_semaphore()
    for peer in peers:
        pl.semaphore_signal(barrier, inc=1, device_id=peer, device_id_type=pl.DeviceIdType.MESH)
    pl.semaphore_wait(barrier, len(peers))


class Line:
    def __init__(self, tot, rz1, rz2, rz3, sem_s, sem_r):
        self.tot, self.rz1, self.rz2, self.rz3 = tot, rz1, rz2, rz3
        self.sem_s, self.sem_r = sem_s, sem_r
        dp, ex = lax.axis_index("dp"), lax.axis_index("expert")
        self.z = dp // 2
        self.upper = self.z // 2
        self.outer = (self.z == 0) | (self.z == 3)
        self.inner = jnp.logical_not(self.outer)
        self.near, self.middle = (dp ^ 2, ex), (dp ^ 6, ex)

    def copy(self, ch, stage):
        if stage == 3:
            src, dst = self.tot.at[ch, 2 * self.upper + 1 - self.z % 2], self.rz3.at[ch]
        else:
            src = self.tot.at[ch, pl.ds(2 * (1 - self.upper), 2)]
            dst = (self.rz1 if stage == 1 else self.rz2).at[ch]
        return pltpu.make_async_remote_copy(
            src_ref=src,
            dst_ref=dst,
            send_sem=self.sem_s.at[ch, stage],
            recv_sem=self.sem_r.at[ch, stage],
            device_id=self.middle if stage == 2 else self.near,
            device_id_type=pl.DeviceIdType.MESH,
        )

    def add(self, ch, first, other):
        for p in range(2):
            for e in range(2):
                dst = self.tot.at[ch, first + p, e]
                add_rows(dst, [dst, other.at[ch, p, e]])

    def ends(self, ch, inward):
        @pl.when(self.outer)
        def _():
            if inward:
                self.copy(ch, 1).start()
            else:
                self.copy(ch, 3).start()

    def middle_sends(self, ch, inward):
        @pl.when(self.inner)
        def _():
            if inward:
                self.copy(ch, 1).wait_recv()
            self.add(ch, 2 * (1 - self.upper), self.rz1)
            self.copy(ch, 2).start()

        if inward:

            @pl.when(self.outer)
            def _():
                self.copy(ch, 1).wait_send()
                self.copy(ch, 3).start()

    def middle_adds(self, ch):
        @pl.when(self.inner)
        def _():
            self.copy(ch, 2).wait()
            self.add(ch, 2 * self.upper, self.rz2)
            self.copy(ch, 3).start()

    def result(self, ch, refs):
        self.copy(ch, 3).wait()
        for e in range(2):
            own, got = self.tot.at[ch, self.z, e], self.rz3.at[ch, e]
            if ch < 2:
                add_rows(refs[ch].at[e], [own, got])
            else:
                rows, lanes = refs[2].shape[1], own.shape[1]
                for h in range(2):
                    at = slice(h * rows, (h + 1) * rows)
                    dst = refs[2].at[e, :, h * lanes : (h + 1) * lanes]
                    add_rows(dst, [own.at[at], got.at[at]])


def line_scratch(shape):
    return [
        pltpu.VMEM((3,) + shape, BF16),
        pltpu.VMEM((3, 2) + shape[1:], BF16),
        pltpu.VMEM((3, 2) + shape[1:], BF16),
        pltpu.VMEM((3,) + shape[1:], BF16),
        pltpu.SemaphoreType.DMA((3, 4)),
        pltpu.SemaphoreType.DMA((3, 4)),
    ]


def attn_bwd_kernel(*refs):
    attn_bwd_body(*refs)


def attn_bwd_sum_kernel(*refs):
    ins, (tot_a, far_a, keep_a, got_a) = refs[:11], refs[11:15]
    outs, (gate_ref, up_ref, down_ref) = refs[15:18], refs[18:21]
    scratch, line_refs, (rx, sem_l) = refs[21:24], refs[24:30], refs[30:]
    step = pl.program_id(0)
    line = Line(*line_refs)
    loads = []
    for k in range(2):
        loads.append([pltpu.make_async_copy(tot_a.at[:, k], line.tot.at[k], sem_l.at[2 * k])])
        loads[-1].append(
            pltpu.make_async_copy(far_a.at[:, k], line.rz1.at[k], sem_l.at[2 * k + 1])
        )
    loads.append(
        [
            pltpu.make_async_copy(keep_a, line.tot.at[2], sem_l.at[4]),
            pltpu.make_async_copy(got_a, rx, sem_l.at[5]),
        ]
    )
    @pl.when(step == 0)
    def _():
        for group in loads:
            for copy in group:
                copy.start()
        greet([line.near, line.middle])
        for copy in loads[2]:
            copy.wait()
        for zz in range(4):
            for e in range(2):
                dst = line.tot.at[2, zz, e]
                add_rows(dst, [dst, rx.at[zz, e]])
        line.ends(2, True)
        for k in range(2):
            for copy in loads[k]:
                copy.wait()
            line.ends(k, False)
            line.middle_sends(k, False)

    attn_bwd_body(*ins, *outs, *scratch)

    @pl.when(step == 1)
    def _():
        line.middle_sends(2, True)
        line.middle_adds(0)

    @pl.when(step == 2)
    def _():
        line.middle_adds(1)

    @pl.when(step == 3)
    def _():
        line.middle_adds(2)
        for ch in range(3):
            line.result(ch, (gate_ref, up_ref, down_ref))


def attn_bwd_body(
    prefix_ref, q_ref, kd_ref, vd_ref, do_ref, ctx_ref, lse_ref, cos_ref, sin_ref, cost_ref, sint_ref,
    dq_ref, dk_ref, dv_ref, dk_acc, dv_acc, kt_ref,
):
    length = q_ref.shape[0]
    b = 256
    prefix = prefix_ref[0]
    low_b = lane_half((b, 128), 128)
    for j in range(2):
        cols = slice(j * 128, (j + 1) * 128)
        kt_ref[j] = kd_ref[:, cols].T
    dk_acc[...] = jnp.zeros_like(dk_acc)
    dv_acc[...] = jnp.zeros_like(dv_acc)
    for i in range(length // b):
        rows = slice(i * b, (i + 1) * b)
        nk = max((i + 1) * b, length // 2)
        free = i * b
        bias = mask_bias(prefix, i * b, free, b, nk - free, 1)
        bias = jnp.concatenate([bias, bias], axis=1)
        for j in range(2):
            cols = slice(j * 128, (j + 1) * 128)
            do = do_ref[rows, cols]
            q2 = two_heads(q_ref[rows, cols], low_b)
            do2 = two_heads(do, low_b)
            prod = (do.astype(F32) * ctx_ref[rows, cols].astype(F32)).T
            delta = jnp.concatenate(
                [
                    jnp.sum(prod[:64], axis=0, keepdims=True),
                    jnp.sum(prod[64:], axis=0, keepdims=True),
                ],
                axis=1,
            )
            lse = jnp.concatenate(
                [lse_ref[0, 2 * j : 2 * j + 1, rows], lse_ref[0, 2 * j + 1 : 2 * j + 2, rows]],
                axis=1,
            )
            dq_t = None
            parts = [(0, free)] if free else []
            for k0, k1 in parts + [(free, nk)]:
                keys = slice(k0, k1)
                s = dot_t(kd_ref[keys, cols], q2)
                if k0 == free:
                    s = s + bias
                p = jnp.exp(s - lse)
                dp = dot_t(vd_ref[keys, cols], do2)
                ds = (p * (dp - delta)).astype(BF16)
                dv_acc[j, keys, :] += dot(p.astype(BF16), do2)
                dk_acc[j, keys, :] += dot(ds, q2)
                part = dot(kt_ref[j, :, keys], ds)
                dq_t = part if dq_t is None else dq_t + part
            cos_t, sin_t = cost_ref[:, rows], sint_ref[:, rows]
            a0, b0 = dq_t[0:32, :b], dq_t[32:64, :b]
            a1, b1 = dq_t[64:96, b:], dq_t[96:128, b:]
            full = jnp.concatenate(
                [
                    a0 * cos_t + b0 * sin_t,
                    b0 * cos_t - a0 * sin_t,
                    a1 * cos_t + b1 * sin_t,
                    b1 * cos_t - a1 * sin_t,
                ],
                axis=0,
            )
            dq_ref[rows, cols] = (full * 0.125).T.astype(BF16)
    low = lane_half((length, 128), 128)
    first = lane_half((length, 128), 64)
    sums = []
    for acc in (dk_acc, dv_acc):
        even = acc[0] + pltpu.roll(acc[0], 64, 1)
        odd = acc[1] + pltpu.roll(acc[1], 64, 1)
        sums.append(jnp.where(low, even, odd))
    dk_ref[...] = rope_lanes(sums[0], cos_ref[...], -sin_ref[...], first).astype(BF16)
    dv_ref[...] = sums[1].astype(BF16)


def run_attn_bwd(prefix, q, kd, vd, d_ctx, ctx, lse, cos, sin, cos_t, sin_t, sums=None):
    length, nq = q.shape
    groups = nq // 256
    col = lambda g: (0, g)
    wide = spec((length, 256), col)
    in_specs = [pl.BlockSpec(memory_space=pltpu.SMEM)] + [wide] * 5
    in_specs += [spec((1, 8, length), lambda g: (g, 0, 0))]
    in_specs += [whole((length, 128))] * 2 + [whole((cos_t.shape[0], length))] * 2
    out_specs = [wide, spec((length, 128), col), spec((length, 128), col)]
    out_shape = [
        jax.ShapeDtypeStruct((length, nq), BF16),
        jax.ShapeDtypeStruct((length, nq // 2), BF16),
        jax.ShapeDtypeStruct((length, nq // 2), BF16),
    ]
    scratch = [
        pltpu.VMEM((2, length, 128), F32),
        pltpu.VMEM((2, length, 128), F32),
        pltpu.VMEM((2, 128, length), BF16),
    ]
    args = (prefix, q, kd, vd, d_ctx, ctx, lse, cos, sin, cos_t, sin_t)
    kernel, extra = attn_bwd_kernel, {}
    if sums is not None:
        kernel, extra = attn_bwd_sum_kernel, {"collective_id": 3, "has_side_effects": True}
        hbm = pl.BlockSpec(memory_space=pl.ANY)
        keep_a = sums[2]
        _, count, rows, lanes = keep_a.shape
        made = [(count, rows, lanes)] * 2 + [(count, rows // 2, 2 * lanes)]
        in_specs += [hbm] * 4
        out_specs += [whole(shape) for shape in made]
        out_shape += [jax.ShapeDtypeStruct(shape, F32) for shape in made]
        scratch += line_scratch(keep_a.shape)
        scratch += [
            pltpu.VMEM(keep_a.shape, BF16),
            pltpu.SemaphoreType.DMA((6,)),
        ]
        args += tuple(sums)
    return pl.pallas_call(
        kernel,
        grid=(groups,),
        in_specs=in_specs,
        out_specs=out_specs,
        out_shape=out_shape,
        scratch_shapes=scratch,
        compiler_params=pltpu.CompilerParams(
            dimension_semantics=("arbitrary",), vmem_limit_bytes=60 * MIB, **extra
        ),
        cost_estimate=took(33),
        name="attn_bwd",
    )(*args)


def mid_kernel(tok_ref, ctx_ref, w_ref, gain_ref, res_ref, x_ref):
    res = tok_ref[...].astype(F32) + dot(ctx_ref[...], w_ref[...])
    res_ref[...] = res
    r = lax.rsqrt(jnp.mean(res * res, axis=1, keepdims=True) + EPS)
    x_ref[...] = (res * r * gain_ref[...].astype(F32)).astype(BF16)


def run_mid(tok, ctx, w_all, gain, at):
    length, d = tok.shape
    b = 256
    row = lambda i: (i, 0)
    return pl.pallas_call(
        mid_kernel,
        grid=(length // b,),
        in_specs=[
            spec((b, d), row),
            spec((b, ctx.shape[1]), row),
            spec((w_all.shape[0], d), lambda i: (0, at)),
            whole((1, d)),
        ],
        out_specs=[spec((b, d), row)] * 2,
        out_shape=[
            jax.ShapeDtypeStruct((length, d), F32),
            jax.ShapeDtypeStruct((length, d), BF16),
        ],
        compiler_params=params(60),
        cost_estimate=took(4),
        name="mid",
    )(tok, ctx, w_all, gain)


def gates_of(x, router, routes_t, num_experts):
    logits = dot(x, router).T[: 16 * pl.cdiv(num_experts, 16)]
    expert = lax.broadcasted_iota(jnp.int32, logits.shape, 0)
    hit = expert == routes_t[0:1]
    for k in range(1, routes_t.shape[0]):
        hit = hit | (expert == routes_t[k : k + 1])
    logits = jnp.where(hit, logits, NEG)
    e = jnp.exp(logits - jnp.max(logits, axis=0, keepdims=True))
    e = jnp.where(hit, e, 0.0)
    return e / jnp.sum(e, axis=0, keepdims=True)


class Tops:
    def __init__(self, peak_ref, top_ref, sent, got, sem_s, sem_r):
        self.peak_ref, self.top_ref, self.sent, self.got = peak_ref, top_ref, sent, got
        self.sem_s, self.sem_r = sem_s, sem_r
        dp, ex = lax.axis_index("dp"), lax.axis_index("expert")
        self.peers = [(dp, ex ^ 1), (dp, ex ^ 2), (dp ^ 1, ex), (dp ^ 2, ex), (dp ^ 4, ex)]

    def copy(self, k):
        return pltpu.make_async_remote_copy(
            src_ref=self.sent.at[k],
            dst_ref=self.got.at[k],
            send_sem=self.sem_s.at[k],
            recv_sem=self.sem_r.at[k],
            device_id=self.peers[k],
            device_id_type=pl.DeviceIdType.MESH,
        )

    def turn(self, k):
        if k == 0:
            greet(self.peers)
            self.sent[0] = self.peak_ref[...]
        else:
            self.copy(k - 1).wait()
            both = jnp.maximum(self.sent[k - 1], self.got[k - 1])
            if k == len(self.peers):
                self.top_ref[...] = both
                return
            self.sent[k] = both
        self.copy(k).start()


def expert_kernel(first_expert, local, num_experts, with_init, with_carry, with_top, n_row, *refs):
    me_ref, router_ref, wg_ref, wu_ref, wd_ref = refs[:5]
    x_refs, c_refs, route_refs = refs[5:7], refs[7:9], refs[9:11]
    refs = refs[11:]
    if with_init:
        out_ins, dx_ins, dg_ins, refs = refs[:2], refs[2:4], refs[4:6], refs[6:]
    if with_carry or with_top:
        sent_ref, refs = refs[0], refs[1:]
    out_refs, dx_refs, dg_refs = refs[:2], refs[2:4], refs[4:6]
    hs_ref, dgate_ref, dup_ref = refs[6:9]
    refs = refs[9:]
    if not with_init:
        xt_ref, ct_ref, refs = refs[0], refs[1], refs[2:]
    if with_carry or with_top:
        got_ref, refs = refs[0], refs[1:]
    x_now, c_now, out_acc, dx_acc, gp_ref, dgc_ref = refs[:6]
    i, e = pl.program_id(0), pl.program_id(1)
    last = pl.num_programs(1) - 1
    if with_carry:
        over_x = (lax.axis_index("dp") ^ 1, lax.axis_index("expert"))

        def carry():
            return pltpu.make_async_remote_copy(
                src_ref=sent_ref,
                dst_ref=got_ref,
                send_sem=refs[6].at[0],
                recv_sem=refs[6].at[1],
                device_id=over_x,
                device_id_type=pl.DeviceIdType.MESH,
            )

        @pl.when((i == 0) & (e == 0))
        def _():
            greet([over_x])
            carry().start()

    b = x_now.shape[0]
    lane = lax.broadcasted_iota(jnp.int32, (b, 128), 1)

    if with_top:
        tops = Tops(sent_ref, got_ref, *refs[6:])
        for k in range(6):

            @pl.when(i * pl.num_programs(1) + e == k)
            def _():
                tops.turn(k)

    for source in range(2):

        @pl.when((e == 0) & ((i < n_row) if source == 0 else (i >= n_row)))
        def _():
            x, c = x_refs[source][...], c_refs[source][...]
            x_now[...] = x
            c_now[...] = c
            gates = gates_of(x, router_ref[...], route_refs[source][...], num_experts)
            fill = jnp.zeros((128 - gates.shape[0], b), F32)
            gp_ref[...] = jnp.concatenate([gates, fill], axis=0).T
            if with_init:
                out_acc[...] = out_ins[source][...].astype(F32)
                dx_acc[...] = dx_ins[source][...].astype(F32)
                fill = jnp.zeros((120, b), F32)
                dgc_ref[...] = jnp.concatenate([dg_ins[source][...], fill], axis=0).T
            else:
                out_acc[...] = jnp.zeros_like(out_acc)
                dx_acc[...] = jnp.zeros_like(dx_acc)
                dgc_ref[...] = jnp.zeros_like(dgc_ref)
                xt_ref[...] = x.T
                ct_ref[...] = c.T

    x, c = x_now[...], c_now[...]
    gp = jnp.sum(
        jnp.where(lane == me_ref[0] * local + first_expert + e, gp_ref[...], 0.0),
        axis=1,
        keepdims=True,
    )
    gate = dot(x, wg_ref[0])
    up = dot(x, wu_ref[0])
    grad = dot_t(c, wd_ref[0])
    sig = 0.5 * jnp.tanh(0.5 * gate) + 0.5
    act = gate * sig
    hidden = (act * up).astype(BF16).astype(F32)
    dg = jnp.sum(hidden * grad, axis=1, keepdims=True)
    hs = (hidden * gp).astype(BF16)
    dh = grad * gp
    dup = (dh * act).astype(BF16)
    dgate = (dh * up * (sig + act * (1.0 - sig))).astype(BF16)
    hs_ref[...] = hs
    dup_ref[...] = dup
    dgate_ref[...] = dgate
    out = dot(hs, wd_ref[0])
    dx = dot_t(dgate, wg_ref[0]) + dot_t(dup, wu_ref[0])
    dgc_ref[...] += jnp.where(lane == first_expert + e, dg, 0.0)
    out_acc[...] += out
    dx_acc[...] += dx
    for source in range(2):

        @pl.when((e == last) & ((i < n_row) if source == 0 else (i >= n_row)))
        def _():
            out_refs[source][...] = out_acc[...].astype(BF16)
            dx_refs[source][...] = dx_acc[...].astype(BF16)
            dg_refs[source][...] = dgc_ref[...].T[:8]

    if with_carry:

        @pl.when((i == 2 * n_row - 1) & (e == last))
        def _():
            carry().wait()


def run_expert(me, xs, cs, routes, router, wg, wu, wd, first, count, num_experts, init=None, sent=None, peaks=None):
    length, d = xs[0].shape
    local, _, ff = wg.shape
    b = 512
    n_row = length // b
    top = routes[0].shape[0]

    def clamp(i, source):
        return jnp.minimum(i, n_row - 1) if source == 0 else jnp.maximum(i - n_row, 0)

    rows = [
        spec((b, d), functools.partial(lambda src, i, e: (clamp(i, src), 0), src))
        for src in range(2)
    ]

    def lanes(height):
        return [
            spec((height, b), functools.partial(lambda src, i, e: (0, clamp(i, src)), src))
            for src in range(2)
        ]

    pick = lambda shape: pl.BlockSpec((1,) + shape[1:], lambda i, e: (first + e, 0, 0))
    wide = jax.ShapeDtypeStruct((2 * length, count * ff), BF16)
    full = jax.ShapeDtypeStruct((length, d), BF16)
    small = jax.ShapeDtypeStruct((8, length), F32)
    turned = jax.ShapeDtypeStruct((d, 2 * length), BF16)
    wide_spec = spec((b, ff), lambda i, e: (i, e))
    turned_spec = spec((d, b), lambda i, e: (0, i))
    with_init = init is not None
    carried, extra, more = [], {}, []
    with_sent = sent is not None
    if sent is not None:
        carried = [pl.BlockSpec(memory_space=pl.ANY)]
        extra = {"collective_id": 4, "has_side_effects": True}
        more = [pltpu.SemaphoreType.DMA((2,))]
    if peaks is not None:
        sent = peaks
        carried = [whole(peaks.shape)]
        extra = {"collective_id": 5, "has_side_effects": True}
        more = [pltpu.VMEM((5,) + peaks.shape, F32)] * 2 + [pltpu.SemaphoreType.DMA((5,))] * 2
    made = pl.pallas_call(
        functools.partial(
            expert_kernel,
            first,
            local,
            num_experts,
            with_init,
            with_sent,
            peaks is not None,
            n_row,
        ),
        grid=(2 * n_row, count),
        in_specs=[
            pl.BlockSpec(memory_space=pltpu.SMEM),
            pl.BlockSpec(
                (d, 128),
                lambda i, e: (0, router.shape[1] // 128 - 1),
                pipeline_mode=pl.Buffered(1),
            ),
            pick(wg.shape),
            pick(wu.shape),
            pick(wd.shape),
        ]
        + rows * 2
        + lanes(top)
        + (rows * 2 + lanes(8) if with_init else [])
        + carried,
        out_specs=rows * 2
        + lanes(8)
        + [wide_spec] * 3
        + ([] if with_init else [turned_spec] * 2)
        + carried,
        out_shape=[full] * 4
        + [small] * 2
        + [wide] * 3
        + ([] if with_init else [turned] * 2)
        + ([] if sent is None else [jax.ShapeDtypeStruct(sent.shape, sent.dtype)]),
        scratch_shapes=[
            pltpu.VMEM((b, d), BF16),
            pltpu.VMEM((b, d), BF16),
            pltpu.VMEM((b, d), F32),
            pltpu.VMEM((b, d), F32),
            pltpu.VMEM((b, 128), F32),
            pltpu.VMEM((b, 128), F32),
        ]
        + more,
        compiler_params=pltpu.CompilerParams(
            dimension_semantics=("arbitrary",) * 2, vmem_limit_bytes=62 * MIB, **extra
        ),
        cost_estimate=took(24 * count),
        name="experts",
    )(me, router, wg, wu, wd, *xs, *cs, *routes, *(init or ()), *([] if sent is None else [sent]))
    return {"out": made[:2], "dx": made[2:4], "dg": made[4:6], "wide": made[6:9], "turned": made[9:11], "got": made[-1:]}


def weight_grad_kernel(n, paired, dp_ref, *refs):
    xt, ct, dgate, dup, hs = (refs[k * n : (k + 1) * n] for k in range(5))

    def total(lefts, rights):
        acc = None
        for left, right in zip(lefts, rights):
            part = dot(left[...], right[...])
            acc = part if acc is None else acc + part
        return acc

    down = total(ct, hs).T.astype(BF16)
    gate = total(xt, dgate).astype(BF16)
    up = total(xt, dup).astype(BF16)
    if paired:
        keep_ref, send_ref, down_keep_ref, down_send_ref = refs[5 * n :]
        first = dp_ref[0] % 2 == 0

        def parts(value, z, rows):
            even = value[2 * z * rows : (2 * z + 1) * rows]
            odd = value[(2 * z + 1) * rows : (2 * z + 2) * rows]
            return jnp.where(first, even, odd), jnp.where(first, odd, even)

        for z in range(keep_ref.shape[0]):
            for k, value in enumerate((gate, up)):
                keep_ref[z, k, 0], send_ref[z, k, 0] = parts(value, z, keep_ref.shape[3])
        for z in range(down_keep_ref.shape[0]):
            rows = down_keep_ref.shape[2]
            down_keep_ref[z, 0], down_send_ref[z, 0] = parts(down, z, rows)
        return
    gate_ref, up_ref, down_ref = refs[5 * n :]
    for p in range(down_ref.shape[0]):
        rows = down_ref.shape[3]
        down_ref[p, 0, 0] = down[p * rows : (p + 1) * rows]
    for p in range(gate_ref.shape[0]):
        rows = gate_ref.shape[2]
        gate_ref[p, 0] = gate[p * rows : (p + 1) * rows]
        up_ref[p, 0] = up[p * rows : (p + 1) * rows]


def run_weight_grad(dp, xt, ct, dgate, dup, hs, count, skips, n_dp, paired, ff):
    n = len(xt)
    d, length = xt[0].shape
    m = 512 if paired else 256
    left = spec((m, length), lambda e, i: (i, 0))
    rights = [
        spec((length, ff), functools.partial(lambda skip, e, i: (0, e + skip), skip))
        for skip in skips
    ]
    per = d // n_dp
    down_at = lambda e, i: (0, e, i // (ff // m), 0, i % (ff // m))
    if paired:
        row_spec = spec((m // (2 * per), 2, 1, per, ff), lambda e, i: (i, 0, e, 0, 0))
        rows = jax.ShapeDtypeStruct((n_dp // 2, 2, count, per, ff), BF16)
        down_spec = spec((n_dp // 2, 1, ff // n_dp, m), lambda e, i: (0, e, i, 0))
        down = jax.ShapeDtypeStruct((n_dp // 2, count, ff // n_dp * (d // ff), ff), BF16)
        out_specs, out_shape = [row_spec] * 2 + [down_spec] * 2, [rows] * 2 + [down] * 2
    else:
        row_spec = spec((m // per, 1, per, ff), lambda e, i: (i, e, 0, 0))
        rows = jax.ShapeDtypeStruct((n_dp, count, per, ff), BF16)
        down_spec = spec((n_dp, 1, 1, ff // n_dp, m), down_at)
        down = jax.ShapeDtypeStruct((n_dp, count, d // ff, ff // n_dp, ff), BF16)
        out_specs, out_shape = [row_spec] * 2 + [down_spec], [rows] * 2 + [down]
    return pl.pallas_call(
        functools.partial(weight_grad_kernel, n, paired),
        grid=(count, d // m),
        in_specs=[pl.BlockSpec(memory_space=pltpu.SMEM)] + [left] * (2 * n) + rights * 3,
        out_specs=out_specs,
        out_shape=out_shape,
        compiler_params=params(60, 2),
        cost_estimate=took(37),
        name="weight_grad",
    )(dp, *xt, *ct, *dgate, *dup, *hs)


def back_mid_kernel(n, n_ex, local, *refs):
    (me_ref, res_ref, cot_ref, route_ref, x_ref, router_ref, gain_ref, w_ref) = refs[:8]
    dx_refs, dg_refs = refs[8 : 8 + n], refs[8 + n : 8 + n + n_ex]
    dres_ref, dattn_ref, dctx_ref, dlog_ref, ggain_ref = refs[8 + n + n_ex :]
    gp = gates_of(x_ref[...], router_ref[...], route_ref[...], n_ex * local)
    parts = [ref[...][:local] for ref in dg_refs]
    owners = []
    for owner in range(n_ex):
        own = jnp.zeros_like(parts[0])
        for step in range(n_ex):
            own = jnp.where((owner ^ step) == me_ref[0], parts[step], own)
        owners.append(own)
    dg = jnp.concatenate(owners, axis=0)
    d_logits = gp * (dg - jnp.sum(gp * dg, axis=0, keepdims=True))
    fill = jnp.zeros((128 - dg.shape[0], dg.shape[1]), F32)
    d_logits = jnp.concatenate([d_logits, fill], axis=0).T.astype(BF16)
    dlog_ref[...] = d_logits
    d_norm = dot_t(d_logits, router_ref[...])
    for ref in dx_refs:
        d_norm = d_norm + ref[...].astype(F32)
    res = res_ref[...]
    r = lax.rsqrt(jnp.mean(res * res, axis=1, keepdims=True) + EPS)
    xr = res * r
    part = jnp.sum(d_norm * xr, axis=0, keepdims=True)

    @pl.when(pl.program_id(0) == 0)
    def _():
        ggain_ref[...] = jnp.zeros_like(ggain_ref)

    ggain_ref[...] += part
    u = d_norm * gain_ref[...].astype(F32)
    d_res = (
        cot_ref[...].astype(F32) + r * u - xr * (r * r) * jnp.mean(u * res, axis=1, keepdims=True)
    )
    dres_ref[...] = d_res
    d_attn = d_res.astype(BF16)
    dattn_ref[...] = d_attn
    dctx_ref[...] = dot_t(d_attn, w_ref[...]).astype(BF16)


def run_back_mid(me, res, cot, routes_t, x, w_all, gain, at, dxs, dgs, local):
    length, d = res.shape
    b = 256
    row = lambda i: (i, 0)
    n, n_ex = len(dxs), len(dgs)
    return pl.pallas_call(
        functools.partial(back_mid_kernel, n, n_ex, local),
        grid=(length // b,),
        in_specs=[
            pl.BlockSpec(memory_space=pltpu.SMEM),
            spec((b, d), row),
            spec((b, d), row),
            spec((routes_t.shape[0], b), lambda i: (0, i)),
            spec((b, d), row),
            spec((d, 128), lambda i: (0, w_all.shape[1] // 128 - 1)),
            whole((1, d)),
            spec((d, d), lambda i: (0, at)),
        ]
        + [spec((b, d), row)] * n
        + [spec((8, b), lambda i: (0, i))] * n_ex,
        out_specs=[
            spec((b, d), row),
            spec((b, d), row),
            spec((b, d), row),
            spec((b, 128), row),
            whole((1, d)),
        ],
        out_shape=[
            jax.ShapeDtypeStruct((length, d), F32),
            jax.ShapeDtypeStruct((length, d), BF16),
            jax.ShapeDtypeStruct((length, d), BF16),
            jax.ShapeDtypeStruct((length, 128), BF16),
            jax.ShapeDtypeStruct((1, d), F32),
        ],
        compiler_params=params(60),
        cost_estimate=took(11),
        name="back_mid",
    )(me, res, cot, routes_t, x, w_all, gain, w_all, *dxs, *dgs)


def back_in_kernel(dq_ref, dk_ref, dv_ref, w_ref, tok_ref, gain_ref, dres_ref, gt_ref, ggain_ref):
    nq, nk = dq_ref.shape[1], dk_ref.shape[1]
    d_norm = dot_t(dq_ref[...], w_ref[:, :nq])
    d_norm = d_norm + dot_t(dk_ref[...], w_ref[:, nq : nq + nk])
    d_norm = d_norm + dot_t(dv_ref[...], w_ref[:, nq + nk : nq + 2 * nk])
    x = tok_ref[...].astype(F32)
    r = lax.rsqrt(jnp.mean(x * x, axis=1, keepdims=True) + EPS)
    xr = x * r
    part = jnp.sum(d_norm * xr, axis=0, keepdims=True)

    @pl.when(pl.program_id(0) == 0)
    def _():
        ggain_ref[...] = jnp.zeros_like(ggain_ref)

    ggain_ref[...] += part
    u = d_norm * gain_ref[...].astype(F32)
    gt_ref[...] = dres_ref[...] + r * u - xr * (r * r) * jnp.mean(u * x, axis=1, keepdims=True)


def run_back_in(dq, dk, dv, w_qkv, tok, gain, d_res):
    length, d = tok.shape
    b = 256
    row = lambda i: (i, 0)
    nq = dq.shape[1]
    return pl.pallas_call(
        back_in_kernel,
        grid=(length // b,),
        in_specs=[
            spec((b, nq), row),
            spec((b, dk.shape[1]), row),
            spec((b, dv.shape[1]), row),
            spec((d, 2 * nq), lambda i: (0, 0)),
            spec((b, d), row),
            whole((1, d)),
            spec((b, d), row),
        ],
        out_specs=[spec((b, d), row), whole((1, d))],
        out_shape=[jax.ShapeDtypeStruct((length, d), F32), jax.ShapeDtypeStruct((1, d), F32)],
        compiler_params=params(60),
        cost_estimate=took(10),
        name="back_in",
    )(dq, dk, dv, w_qkv, tok, gain, d_res)


CHUNKS = (3, 0, 1, 2)


def finish_kernel(
    gain_lane, ht_ref, dq_ref, dk_ref, dv_ref, ctx_ref, dattn_ref, small_ref, keep_ref, got_ref, down_keep_ref, down_got_ref,
    gate_a, up_a, down_a, w_ref, tok_ref, gain_ref, dres_ref,
    out_o, out_q, out_kv, out_small, gate_ref, up_ref, down_ref, gt_ref, *scratch,
):
    n = len(CHUNKS)
    lists = [scratch[k * n : (k + 1) * n] for k in range(7)]
    b1, r1, r2, s2, r3, s3, r4 = lists
    sem_s, sem_r = scratch[7 * n : 7 * n + 2]
    line = Line(*scratch[7 * n + 2 : 7 * n + 8])
    rx, sem_l, w_now, gt_now, gain_sum = scratch[7 * n + 8 :]
    count = gate_a.shape[0]
    halves = []
    for k, (src, dst) in enumerate(((gate_a, gate_ref), (up_a, up_ref), (down_a, down_ref))):
        halves.append(pltpu.make_async_copy(src, dst.at[:count], sem_l.at[6 + k]))
        halves[k].start()
    dp, ex = lax.axis_index("dp"), lax.axis_index("expert")
    z, x, y, c = dp // 2, dp % 2, ex // 2, ex % 2
    over_core, over_y, over_x = (dp, ex ^ 1), (dp, ex ^ 2), (dp ^ 1, ex)
    s1 = [ref.at[c] for ref in b1]
    load_w = pltpu.make_async_copy(w_ref.at[:, : w_now.shape[1]], w_now, sem_l.at[9])
    load_w.start()
    along = [(dp ^ (2 * k), ex) for k in (1, 2, 3)]
    group = [over_core, over_y, (dp, ex ^ 3)]
    loads = []
    for k in range(3):
        keep, got = (down_keep_ref, down_got_ref) if k == 2 else (keep_ref.at[:, k], got_ref.at[:, k])
        loads.append(
            [
                pltpu.make_async_copy(keep, line.tot.at[k], sem_l.at[2 * k]),
                pltpu.make_async_copy(got, rx.at[k], sem_l.at[2 * k + 1]),
            ]
        )
        for copy in loads[k]:
            copy.start()
    greet(group + [over_x] + along)

    widths = [dattn_ref.shape[1], dq_ref.shape[1], dk_ref.shape[1] + dv_ref.shape[1], 128]
    outs = (out_o, out_q, out_kv, out_small)
    started = {}

    def send(k, slot, src, dst, peer):
        copy = pltpu.make_async_remote_copy(
            src_ref=src,
            dst_ref=dst,
            send_sem=sem_s.at[k, slot],
            recv_sem=sem_r.at[k, slot],
            device_id=peer,
            device_id_type=pl.DeviceIdType.MESH,
        )
        copy.start()
        started[k, slot] = copy

    def begin(k):
        for copy in loads[k]:
            copy.wait()
        for zz in range(4):
            for e in range(2):
                dst = line.tot.at[k, zz, e]
                add_rows(dst, [dst, rx.at[k, zz, e]])
        line.ends(k, True)

    def place(k, lanes, value):
        for p in range(8):
            for e in range(4):
                row = 128 * p + 32 * e
                b1[k][e % 2, e // 2, p % 2, p // 2, :, lanes] = value[row : row + 32]

    def step0(k):
        if k == 0:
            for col in range(0, widths[0], 512):
                part = lax.dot_general(
                    ctx_ref[...],
                    dattn_ref[:, col : col + 512],
                    (((0,), (0,)), ((), ())),
                    preferred_element_type=F32,
                )
                place(k, slice(col, col + 512), part.astype(BF16))
        elif k == 1:
            for col in range(0, widths[1], 512):
                part = dot(ht_ref[...], dq_ref[:, col : col + 512])
                place(k, slice(col, col + 512), part.astype(BF16))
        elif k == 2:
            half = dk_ref.shape[1]
            place(k, slice(0, half), dot(ht_ref[...], dk_ref[...]).astype(BF16))
            place(k, slice(half, 2 * half), dot(ht_ref[...], dv_ref[...]).astype(BF16))
        else:
            turned = jnp.broadcast_to(gain_sum[...], (128, gain_sum.shape[1])).T.astype(BF16)
            lane = lax.broadcasted_iota(jnp.int32, turned.shape, 1)
            place(k, slice(0, 128), jnp.where(lane == gain_lane, turned, small_ref[...]))
        send(k, 0, b1[k].at[1 - c], r1[k], over_core)

    def step1(k):
        started[k, 0].wait()
        for yy in range(2):
            for xx in range(2):
                for zz in range(4):
                    s1[k][yy, xx, zz] = s1[k][yy, xx, zz] + r1[k][yy, xx, zz]
        send(k, 1, s1[k].at[1 - y], r2[k], over_y)

    def step2(k):
        started[k, 1].wait()
        for xx in range(2):
            for zz in range(4):
                s2[k][xx, zz] = s1[k][y, xx, zz] + r2[k][xx, zz]
        send(k, 2, s2[k].at[1 - x], r3[k].at[0], over_x)

    def step3(k):
        started[k, 2].wait()
        for zz in range(4):
            s3[k][zz] = s2[k][x, zz] + r3[k][0, zz]
        for i in range(3):
            send(k, 3 + i, s3[k].at[z ^ (i + 1)], r3[k].at[1, i], along[i])

    def step4(k):
        for i in range(3):
            started[k, 3 + i].wait()
        total = s3[k][z].astype(F32)
        for i in range(3):
            total = total + r3[k][1, i].astype(F32)
        r4[k][3] = total.astype(BF16)
        for i in range(3):
            send(k, 6 + i, r4[k].at[3], r4[k].at[i], group[i])

    def step5(k):
        outs[k][pl.ds(pl.multiple_of(ex * 32, 32), 32), :] = r4[k][3].astype(F32)
        for i in range(3):
            started[k, 6 + i].wait()
            rows = pl.ds(pl.multiple_of((ex ^ (i + 1)) * 32, 32), 32)
            outs[k][rows, :] = r4[k][i].astype(F32)

    size = gt_now.shape[1]

    def stored(r):
        rows = slice(r * size, (r + 1) * size)
        return pltpu.make_async_copy(gt_now.at[r % 2], gt_ref.at[rows], sem_l.at[10 + r])

    def back(r):
        if r == 0:
            load_w.wait()
        if r >= 2:
            stored(r - 2).wait()
        rows = slice(r * size, (r + 1) * size)
        nq, nk = dq_ref.shape[1], dk_ref.shape[1]
        d_norm = dot_t(dq_ref[rows], w_now[:, :nq])
        d_norm = d_norm + dot_t(dk_ref[rows], w_now[:, nq : nq + nk])
        d_norm = d_norm + dot_t(dv_ref[rows], w_now[:, nq + nk : nq + 2 * nk])
        value = tok_ref[rows].astype(F32)
        inv = lax.rsqrt(jnp.mean(value * value, axis=1, keepdims=True) + EPS)
        scaled = value * inv
        part = jnp.sum(d_norm * scaled, axis=0, keepdims=True)
        gain_sum[...] = part if r == 0 else gain_sum[...] + part
        u = d_norm * gain_ref[...].astype(F32)
        mean = jnp.mean(u * value, axis=1, keepdims=True)
        gt_now[r % 2] = dres_ref[rows] + inv * u - scaled * (inv * inv) * mean
        stored(r).start()

    done = tuple(ref.at[count:] for ref in (gate_ref, up_ref, down_ref))
    begin(0)
    step0(1)
    begin(1)
    step1(1)
    step0(2)
    begin(2)
    step1(2)
    step0(0)
    step1(0)
    back(0)
    step2(1)
    line.middle_sends(0, True)
    back(1)
    step2(2)
    back(2)
    step3(1)
    line.middle_sends(1, True)
    line.middle_adds(0)
    back(3)
    step0(3)
    step2(0)
    step1(3)
    step3(2)
    line.middle_sends(2, True)
    line.middle_adds(1)
    step2(3)
    step4(1)
    step3(0)
    step3(3)
    line.result(0, done)
    line.middle_adds(2)
    step4(2)
    step5(1)
    step4(0)
    step4(3)
    line.result(1, done)
    line.result(2, done)
    step5(2)
    step5(0)
    step5(3)
    for copy in halves:
        copy.wait()
    for r in range(2, 4):
        stored(r).wait()


def run_finish(ht, dq, dk, dv, ctx, d_attn, small, experts, w_all, tok, gain, d_res, gain_lane):
    widths = [d_attn.shape[1], dq.shape[1], dk.shape[1] + dv.shape[1], small.shape[1]]
    chunk = experts[2].shape
    _, count, rows, lanes = chunk
    vmem = pl.BlockSpec(memory_space=pltpu.VMEM)
    hbm = pl.BlockSpec(memory_space=pl.ANY)
    shapes = [
        (2, 2, 2, 4, 32), (2, 2, 4, 32), (2, 4, 32), (2, 4, 32), (2, 4, 32), (4, 32), (4, 32),
    ]
    length, d = tok.shape
    scratch = [pltpu.VMEM(shape + (w,), BF16) for shape in shapes for w in widths]
    scratch += [pltpu.SemaphoreType.DMA((len(widths), 9))] * 2
    scratch += line_scratch(chunk)
    scratch += [
        pltpu.VMEM((3,) + chunk, BF16),
        pltpu.SemaphoreType.DMA((14,)),
        pltpu.VMEM((d, sum(widths[1:3])), BF16),
        pltpu.VMEM((2, length // 4, d), F32),
        pltpu.VMEM((1, d), F32),
    ]
    return pl.pallas_call(
        functools.partial(finish_kernel, gain_lane),
        in_specs=[vmem] * 7 + [hbm] * 8 + [vmem] * 3,
        out_specs=[vmem] * 7 + [hbm],
        out_shape=[
            *(jax.ShapeDtypeStruct((128, w), F32) for w in widths),
            jax.ShapeDtypeStruct((2 * count, rows, lanes), F32),
            jax.ShapeDtypeStruct((2 * count, rows, lanes), F32),
            jax.ShapeDtypeStruct((2 * count, rows // 2, 2 * lanes), F32),
            jax.ShapeDtypeStruct((length, d), F32),
        ],
        scratch_shapes=scratch,
        compiler_params=pltpu.CompilerParams(
            vmem_limit_bytes=63 * MIB, collective_id=1, has_side_effects=True
        ),
        cost_estimate=took(60),
        name="finish",
    )(ht, dq, dk, dv, ctx, d_attn, small, *experts, w_all, tok, gain, d_res)


def gather_kernel(mine_ref, out_ref, sem_s, sem_r, sem_l):
    dp, ex = lax.axis_index("dp"), lax.axis_index("expert")
    z = dp // 2
    core, over_y, over_x = (dp, ex ^ 1), (dp, ex ^ 2), (dp ^ 1, ex)
    line = [None] + [(dp ^ (2 * k), ex) for k in (1, 2, 3)]
    barrier = pltpu.get_barrier_semaphore()
    peers = [core, over_y, over_x] + line[1:]
    for peer in peers:
        pl.semaphore_signal(barrier, inc=1, device_id=peer, device_id_type=pl.DeviceIdType.MESH)
    pl.semaphore_wait(barrier, len(peers))
    rows = mine_ref.shape[0]
    width = mine_ref.shape[1]
    cut = (width // 256 + 1) * 128
    halves = [pl.ds(0, cut), pl.ds(cut, width - cut)]
    started = {}

    def block(k, dx, dy):
        at = (((z ^ k) * 2 + (dp % 2 ^ dx)) * 4 + (ex ^ (2 * dy))) * rows
        return pl.ds(pl.multiple_of(at, rows), rows)

    def send(key, k, dx, dy, peer, src=None, lanes=None):
        index = len(started)
        at = block(k, dx, dy)
        dst = out_ref.at[at] if lanes is None else out_ref.at[at, lanes]
        copy = pltpu.make_async_remote_copy(
            src_ref=dst if src is None else src,
            dst_ref=dst,
            send_sem=sem_s.at[index],
            recv_sem=sem_r.at[index],
            device_id=peer,
            device_id_type=pl.DeviceIdType.MESH,
        )
        copy.start()
        started[key] = copy

    for k in (3, 2, 1):
        send(("z", k), 0, 0, 0, line[k], mine_ref)
    send(("x", 0), 0, 0, 0, over_x, mine_ref)
    send(("y", 0), 0, 0, 0, over_y, mine_ref)
    send(("c", 0), 0, 0, 0, core, mine_ref)
    own = pltpu.make_async_copy(mine_ref, out_ref.at[block(0, 0, 0)], sem_l)
    own.start()

    def onward(k):
        started["x", k].wait_recv()
        send(("dy", k), k, 1, 0, over_y, None, halves[0])
        send(("cx", k), k, 1, 0, core)
        started["y", k].wait_recv()
        send(("dx", k), k, 0, 1, over_x, None, halves[1])
        send(("cy", k), k, 0, 1, core)

    def last(k):
        started["dy", k].wait_recv()
        started["dx", k].wait_recv()
        send(("cd", k), k, 1, 1, core)

    onward(0)
    for k in (1, 2, 3):
        started["z", k].wait_recv()
        send(("x", k), k, 0, 0, over_x)
        send(("y", k), k, 0, 0, over_y)
        send(("c", k), k, 0, 0, core)
    last(0)
    for k in (1, 2, 3):
        onward(k)
    for k in (1, 2, 3):
        last(k)
    for key, copy in started.items():
        copy.wait_send()
        if key[0] in ("c", "cx", "cy", "cd"):
            copy.wait_recv()
    own.wait()


def run_gather(mine, total):
    hbm = pl.BlockSpec(memory_space=pl.ANY)
    return pl.pallas_call(
        gather_kernel,
        in_specs=[hbm],
        out_specs=hbm,
        out_shape=jax.ShapeDtypeStruct((total, mine.shape[1]), BF16),
        scratch_shapes=[
            pltpu.SemaphoreType.DMA((40,)),
            pltpu.SemaphoreType.DMA((40,)),
            pltpu.SemaphoreType.DMA,
        ],
        compiler_params=pltpu.CompilerParams(collective_id=2, has_side_effects=True),
        cost_estimate=took(40),
        name="gather",
    )(mine)


def after(value, *deps):
    return lax.optimization_barrier((value,) + deps)[0]


def on_device(
    n_dp, n_ex, tokens, cotangent, routes, prefix, w_query, keyvalue_weight, w_out, w_router,
    gain_attn, gain_mlp, expert_gate, expert_up, expert_down, query_logit_cap,
):
    length, d = tokens.shape[1], tokens.shape[2]
    tok = tokens.reshape(length, d)
    cot = cotangent.reshape(length, d)
    heads = query_logit_cap.shape[0]
    nq = w_query.shape[1]
    head = nq // heads
    kv_heads = keyvalue_weight.shape[1] // (2 * head)
    num_experts = w_router.shape[1]
    local = expert_gate.shape[0]
    rows = w_query.shape[0]
    ex = lax.axis_index("expert")

    def swap(value, step, axis="expert", n=n_ex):
        return lax.ppermute(value, axis, [(i, i ^ step) for i in range(n)])

    part = rows // n_ex
    small = jnp.concatenate(
        [
            w_router,
            gain_attn[:, None],
            gain_mlp[:, None],
            jnp.zeros((rows, 128 - num_experts - 2), BF16),
        ],
        axis=1,
    )
    packed = jnp.concatenate([w_query, keyvalue_weight, w_out, small], axis=1)
    mine = lax.dynamic_slice_in_dim(packed, ex * part, part, axis=0)
    local = expert_gate.shape[0]
    fast = n_dp == 8 and n_ex == 4 and d == 1024 and local == 4 and expert_gate.shape[2] == 512
    if fast:
        every = run_gather(mine, d)
    else:
        every = lax.all_gather(mine, ("dp", "expert"), axis=0, tiled=True)
    w_all = every
    width = 2 * nq
    extra = every[:, width + d :]
    gain_one = extra[:, num_experts].reshape(1, d)
    gain_two = extra[:, num_experts + 1].reshape(1, d)

    routes_t = routes.reshape(length, -1).T
    cots = {0: cot}
    route_set = {0: routes_t}
    cot_late = after(cot, every)
    for step in range(1, n_ex):
        if step == 1 or step % 2 == 0:
            cots[step] = swap(cot_late, step)

    cos_np, sin_np = rope_tables(length, head)
    cos_l = jnp.asarray(np.concatenate([cos_np] * 4, axis=1))
    sin_l = jnp.asarray(np.concatenate([-sin_np, sin_np] * 2, axis=1))
    cos_t = jnp.asarray(np.ascontiguousarray(cos_np.T))
    sin_t = jnp.asarray(np.ascontiguousarray(sin_np.T))

    normed_one_t, q, kd, vd = run_qkv(tok, gain_one, w_all, cos_l, sin_l, nq)
    for step in range(1, n_ex):
        route_set[step] = swap(after(routes_t, q), step)
    ctx, lse, peaks = run_attn_fwd(prefix, q, kd, vd)
    resid, normed_two = run_mid(tok, ctx, w_all, gain_two, width // d)

    me = ex.reshape(1).astype(jnp.int32)
    xs = {0: normed_two}
    for step in range(1, n_ex):
        if step == 1 or step % 2 == 0:
            xs[step] = swap(normed_two, step)
    tops = [peaks[:, :, :4]]
    bits = [("expert", n_ex, 1 << i) for i in range(n_ex.bit_length() - 1)]
    bits += [("dp", n_dp, 1 << i) for i in range(n_dp.bit_length() - 1)]

    def widen_top():
        if len(tops) <= len(bits) and not fast:
            axis, n, step = bits[len(tops) - 1]
            top = after(tops[-1], chain)
            tops.append(jnp.maximum(top, swap(top, step, axis, n)))

    weights = (expert_gate, expert_up, expert_down)
    half = local // 2

    dp = lax.axis_index("dp").reshape(1).astype(jnp.int32)

    res = {}
    chain = (normed_two, [cots[step] for step in range(2, n_ex, 2)])

    def experts(steps, first, count, init=None, sent=None, peaks=None):
        x = [after(xs[steps[0]], chain), xs[steps[1]]]
        cot_pair, route_pair = [cots[k] for k in steps], [route_set[k] for k in steps]
        return run_expert(
            me,
            x,
            cot_pair,
            route_pair,
            w_all,
            *weights,
            first,
            count,
            num_experts,
            init,
            sent,
            peaks,
        )

    def grads(first):
        pairs = [res[k, 0] for k in range(0, n_ex, 2)]
        wides = [res[0, 0]] + [res[k, first] for k in range(2, n_ex, 2)]
        groups = [[pair["turned"][k] for pair in pairs] for k in (0, 1)]
        groups += [[pair["wide"][k] for pair in wides] for k in (1, 2, 0)]
        groups[0][0] = after(groups[0][0], chain)
        skips = [first if k == 0 else 0 for k in range(len(pairs))]
        made = None
        for at in range(0, len(pairs), 2):
            some = [group[at : at + 2] for group in groups]
            part = run_weight_grad(
                dp, *some, half, skips[at : at + 2], n_dp, fast, expert_gate.shape[2]
            )
            if made is None:
                made = part
            else:
                made = [(a.astype(F32) + b.astype(F32)).astype(BF16) for a, b in zip(made, part)]
        return made

    res[0, 0] = experts((0, 1), 0, local)
    chain = (res[0, 0]["dg"][0], tops[-1])
    widen_top()
    widen_top()
    for other in range(3, n_ex, 2):
        cots[other] = swap(after(cots[other - 1], chain), 1)
        xs[other] = swap(after(xs[other - 1], chain), 1)
    even = range(2, n_ex, 2)
    for step in even:
        res[step, 0] = experts((step, step + 1), 0, half, peaks=peaks if fast else None)
        chain = (res[step, 0]["dg"][0], tops[-1])
        widen_top()
    made_one = grads(0)
    chain = (made_one[0], tops[-1])
    widen_top()
    for step in even:
        init = [*res[step, 0]["out"], *res[step, 0]["dx"], *res[step, 0]["dg"]]
        sent = made_one[1] if fast else None
        res[step, half] = experts((step, step + 1), half, half, init, sent)
        chain = (res[step, half]["dg"][0], tops[-1])
        widen_top()

    def with_partner(step, what):
        own, other = res[step, half][what]
        return (own.astype(F32) + swap(other, 1).astype(F32)).astype(BF16)

    to_send = {step: with_partner(step, "dx") for step in even}
    chain = (chain, list(to_send.values()))
    sums, got_two = None, []
    if fast:
        down_sent = after(made_one[3], chain)
        got_one = [res[2, half]["got"][0], swap(down_sent, 1, "dp", n_dp)]
        tot_one = (made_one[0].astype(F32) + got_one[0].astype(F32)).astype(BF16)
        far_one = lax.dynamic_slice_in_dim(tot_one, 2 * (1 - dp[0] // 4), 2, axis=0)
        chain = (chain, far_one)
        far_one = lax.ppermute(far_one, "dp", [(0, 2), (1, 3), (6, 4), (7, 5)])
    made_two = grads(half)
    chain = (made_two[0], tops[-1])
    if fast:
        chain = (chain, far_one, got_one)
        sums = [tot_one, far_one, made_one[2], got_one[1]]
        got_two = [swap(made_two[k], 1, "dp", n_dp) for k in (1, 3)]
    while len(tops) <= len(bits) and not fast:
        widen_top()
    top = tops[-1]

    final = [res[0, 0]] + [res[step, half] for step in even]
    dxs = [final[0]["dx"][0], swap(final[0]["dx"][1], 1)]
    dxs += [swap(to_send[step], step) for step in even]
    dgs = [part for pair in final for part in pair["dg"]]
    dgs = [swap(dgs[step], step) if step else dgs[0] for step in range(n_ex)]
    d_res, d_attn, d_ctx, d_logits, d_gain_two = run_back_mid(
        me,
        after(resid, chain),
        cot,
        routes_t,
        normed_two,
        w_all,
        gain_two,
        width // d,
        dxs,
        dgs,
        local,
    )
    outs = [final[0]["out"][0], swap(final[0]["out"][1], 1)]
    outs += [swap(after(with_partner(step, "out"), dxs), step) for step in even]
    block = resid
    for piece in outs:
        block = block + piece.astype(F32)
    block_out = block.astype(BF16).reshape(tokens.shape)

    d_out_w = jnp.einsum("rc,rd->cd", ctx, d_attn, preferred_element_type=F32).astype(BF16)
    d_router_w = jnp.einsum("rd,re->de", normed_two, d_logits, preferred_element_type=F32)

    dq, dk, dv, *halves = run_attn_bwd(
        prefix, q, kd, vd, d_ctx, ctx, lse, cos_l, sin_l, cos_t, sin_t, sums
    )
    if not fast:
        grad_tok, d_gain_one = run_back_in(dq, dk, dv, w_all, tok, gain_one, d_res)
    else:
        d_gain_one = jnp.zeros((1, d), F32)
    small_grad = jnp.concatenate(
        [
            d_router_w[:, :num_experts].astype(BF16),
            d_gain_one.reshape(d, 1).astype(BF16),
            d_gain_two.reshape(d, 1).astype(BF16),
            jnp.zeros((d, 128 - num_experts - 2), BF16),
        ],
        axis=1,
    )

    def reduce_all(value, order):
        shape = (n_dp, n_ex, value.shape[0] // (n_dp * n_ex), value.shape[1])
        names = []
        dims = []
        for axis, n in (("dp", n_dp), ("expert", n_ex)):
            count = n.bit_length() - 1
            names += [(axis, n, 1 << (count - 1 - i)) for i in range(count)]
            dims += [2] * count
        value = value.reshape(*dims, *shape[2:])
        for bit in order:
            at = names.index(bit)
            axis, n, step = bit
            mine = (lax.axis_index(axis) // step) % 2
            keep = lax.dynamic_slice_in_dim(value, mine, 1, axis=at)
            send = lax.dynamic_slice_in_dim(value, 1 - mine, 1, axis=at)
            value = (keep.astype(F32) + swap(send, step, axis, n).astype(F32)).astype(BF16)
        return value.reshape(shape[2:])

    def share(value):
        return lax.all_gather(value, "expert", axis=0, tiled=True).astype(F32)

    core = [("expert", n_ex, 1)]
    y_bits = [("expert", n_ex, 1 << i) for i in range(1, n_ex.bit_length() - 1)][::-1]
    dp_bits = [("dp", n_dp, 1 << i) for i in range(n_dp.bit_length() - 1)]
    if fast:
        grad_out, grad_query, grad_keyval, rest, grad_gate, grad_up, grad_down, grad_tok = run_finish(
            normed_one_t,
            after(dq, block_out),
            dk,
            dv,
            ctx,
            d_attn,
            small_grad,
            [made_two[0], got_two[0], made_two[2], got_two[1], *halves[:3]],
            w_all,
            tok,
            gain_one,
            d_res,
            num_experts,
        )
    else:
        ends = [
            [
                lax.psum_scatter(g, "dp", scatter_dimension=0, tiled=True)[0].astype(F32)
                for g in made
            ]
            for made in (made_one, made_two)
        ]
        grad_gate, grad_up, grad_down = (
            jnp.concatenate([ends[0][k], ends[1][k]], axis=0) for k in range(3)
        )
        grad_down = jnp.swapaxes(grad_down, 1, 2).reshape(local, -1, d)

        def product(right):
            return jnp.dot(normed_one_t, right, preferred_element_type=F32).astype(BF16)

        every_grad = jnp.concatenate(
            [d_out_w, product(dq), product(dk), product(dv), small_grad], axis=1
        )
        every_grad = share(reduce_all(every_grad, core + y_bits + dp_bits[::-1]))
        grad_out = every_grad[:, :d]
        grad_query = every_grad[:, d : d + nq]
        grad_keyval = every_grad[:, d + nq : d + 2 * nq]
        rest = every_grad[:, d + 2 * nq :]
    grad_router = rest[:, :num_experts]
    grad_gain_one = rest[:, num_experts]
    grad_gain_two = rest[:, num_experts + 1]

    if fast:
        top = res[2, 0]["got"][0][:, :, :4]
    head_logit_peak = top[:, 0, :].reshape(heads)
    per_group = heads // kv_heads
    query_factor = jnp.sqrt(query_logit_cap / jnp.maximum(head_logit_peak, query_logit_cap))
    pair_peak = jnp.max(head_logit_peak.reshape(kv_heads, per_group), axis=1)
    pair_cap = jnp.min(query_logit_cap.reshape(kv_heads, per_group), axis=1)
    key_factor = jnp.sqrt(pair_cap / jnp.maximum(pair_peak, pair_cap))
    clipped_query = (w_query.astype(F32) * jnp.repeat(query_factor, head)[None, :]).astype(BF16)
    key_cols = jnp.concatenate(
        [jnp.repeat(key_factor, head), jnp.ones((kv_heads * head,), F32)]
    )
    clipped_keyval = (keyvalue_weight.astype(F32) * key_cols[None, :]).astype(BF16)
    return (
        block_out,
        grad_tok.reshape(tokens.shape),
        grad_query,
        grad_keyval,
        grad_out,
        grad_router,
        grad_gain_one,
        grad_gain_two,
        grad_gate,
        grad_up,
        grad_down,
        clipped_query,
        clipped_keyval,
        head_logit_peak,
    )


def solution(mesh):
    rows3 = P(("dp", "expert"), None, None)
    in_specs = (
        rows3,
        rows3,
        rows3,
        P(("dp", "expert")),
        P("dp", None),
        P("dp", None),
        P("dp", None),
        P("dp", None),
        P("dp"),
        P("dp"),
        P("expert", None, None),
        P("expert", None, None),
        P("expert", None, None),
        P(),
    )
    out_specs = (
        rows3,
        rows3,
        P("dp", None),
        P("dp", None),
        P("dp", None),
        P("dp", None),
        P("dp"),
        P("dp"),
        P("expert", "dp", None),
        P("expert", "dp", None),
        P("expert", "dp", None),
        P("dp", None),
        P("dp", None),
        P(),
    )
    return jax.shard_map(
        functools.partial(on_device, mesh.shape["dp"], mesh.shape["expert"]),
        mesh=mesh,
        in_specs=in_specs,
        out_specs=out_specs,
        check_vma=False,
    )
```
